32 devices in a mesh: group: 2 (over x), pool: 8 (over z, y), tp: 2 (over core).
Axes of the slice: x: 2, y: 2, z: 4, core: 2. Of those that a mesh axis runs over, the one named last changes fastest.
Arguments:
- prompt_kv: bfloat16 [256, 2, 4, 128, 128], P(('group', 'pool'), None, 'tp'), parts along dimension 0, may hold values from -6 to 6
- prompt_lengths: int32 [16, 4], P(('group', 'pool')), parts along dimension 0, may hold values from 1 to 1664, as said below
- page_slot: int32 [256], P(('group', 'pool')), parts along dimension 0, may hold values from 0 to 383, as said below
- cache_kv: bfloat16 [768, 2, 4, 128, 128], P(('group', 'pool'), None, 'tp'), parts along dimension 0, may hold values from -6 to 6
- cache_fill: int32 [768], P(('group', 'pool')), parts along dimension 0, may hold values from 0 to 128, as said below
- page_table: int32 [256, 3], P(('group', 'pool')), parts along dimension 0, may hold values from 0 to 47, as said below
- context_lengths: int32 [256], P(('group', 'pool')), parts along dimension 0, may hold values from 1 to 384
- queries: bfloat16 [2, 256, 4096], P(None, ('group', 'pool'), 'tp'), parts along dimension 1
- new_kv: bfloat16 [2, 256, 2, 4, 128], P(None, ('group', 'pool'), None, 'tp'), parts along dimension 1, may hold values from -6 to 6
- out_weight: bfloat16 [4096, 8192], P('tp', 'pool'), may hold values from -0.09375 to 0.09375
Outputs:
- projected: bfloat16 [2, 256, 8192], P(None, 'group', ('pool', 'tp')), parts along dimension 1
The draws below stay inside these ranges and needn't reach their ends.
There are 2 independent parts, one for each index of `group`. The reference program is written for one: setup_inputs(seed, part) draws one part's arguments, and reference() takes and returns one part's arrays. A program takes and returns all parts, laid end to end along the dimension named above; an argument that names none is the same for every part. Nothing has to cross between parts.
Inputs may be any that keep to these rules, and one draw needn't show every extreme that they name: `prompt_lengths`: each device's prompts take exactly 16 pages in all. `page_slot`: slots are distinct; each lands in a slot whose cache_fill is 0; every device receives exactly 16 pages; a device sends 0 or exactly 2 pages to each device. `cache_fill`: exactly 16 slots of each device are 0. `page_table`: each device's table uses each of its slots once.
All inputs are finite; a program needn't handle non-finite values.
Results may differ from the reference program's by a relative error of at most 0.0067.
Values may be sent and summed in bfloat16 or wider, within the bound.
No kernel may reach another device: no remote copies, remote signals or barrier semaphores. Data moves between devices by JAX's collectives and lax.ppermute only.
A program may use at most 128 MiB of HBM per device.

```python
import jax
import jax.numpy as jnp
from jax import lax

D = 8192
QH = 32
KVH = 4
HD = 128
PAGE = 128
PF_PAGES = 16
ROWS = 16
MAXP = 3
STEPS = 2
PROMPTS = 4
PAIR = 2
CACHE = 48
PAGES_ALL = 128
ROWS_ALL = 128
SLOTS = 384
N_POOL = 8


def slot_orders(key):
    key = jax.random.fold_in(key, 100)
    keys = jax.random.split(key, N_POOL)
    return jax.vmap(lambda k: jax.random.permutation(k, ROWS * MAXP))(keys)


def draw_page_slot(key, part):
    orders = slot_orders(key)
    key = jax.random.fold_in(key, 1)
    shifts = jax.random.permutation(key, N_POOL)[:PF_PAGES // PAIR]
    sender = jnp.arange(N_POOL)[:, None]
    page = jnp.arange(PF_PAGES)[None, :]
    target = (sender + shifts[page // PAIR]) % N_POOL
    local = orders[target, page]
    return (target * (ROWS * MAXP) + local).reshape(-1).astype(jnp.int32)


def draw_cache_fill(key, part):
    orders = slot_orders(key)
    key = jax.random.fold_in(key, 2)
    fill = jax.random.randint(key, (N_POOL, ROWS * MAXP), 1, PAGE + 1)
    rank = jnp.argsort(orders, axis=1)
    return jnp.where(rank < PF_PAGES, 0, fill).reshape(-1).astype(jnp.int32)


def draw_page_table(key, part):
    key = jax.random.fold_in(key, 3)
    keys = jax.random.split(key, N_POOL)
    perms = jax.vmap(lambda k: jax.random.permutation(k, ROWS * MAXP))(keys)
    return perms.reshape(N_POOL * ROWS, MAXP).astype(jnp.int32)


def draw_context_lengths(key, part):
    key = jax.random.fold_in(key, 4)
    first_key, second_key = jax.random.split(key)
    lengths = jax.random.randint(first_key, (N_POOL, ROWS), 1, MAXP * PAGE + 1)
    longest = jax.random.randint(second_key, (N_POOL, 1), 0, ROWS)
    lengths = jnp.where(jnp.arange(ROWS)[None, :] == longest, MAXP * PAGE, lengths)
    return lengths.reshape(-1).astype(jnp.int32)


def draw_prompt_lengths(key, part):
    key = jax.random.fold_in(key, 5)
    first_key, second_key, third_key = jax.random.split(key, 3)
    keys = jax.random.split(first_key, N_POOL)
    cuts = jax.vmap(lambda k: jnp.sort(jax.random.permutation(k, PF_PAGES - 1)[:PROMPTS - 1] + 1))(keys).astype(jnp.int32)
    heavy = jax.random.randint(third_key, (), 0, N_POOL)
    packed = jnp.broadcast_to(jnp.arange(1, PROMPTS, dtype=jnp.int32)[None, :], cuts.shape)
    is_heavy = jnp.arange(N_POOL)[:, None] == heavy
    cuts = jnp.where(is_heavy, packed, cuts)
    bounds = jnp.concatenate([jnp.zeros((N_POOL, 1), jnp.int32), cuts, jnp.full((N_POOL, 1), PF_PAGES, jnp.int32)], 1)
    counts = bounds[:, 1:] - bounds[:, :-1]
    tail = jax.random.randint(second_key, (N_POOL, PROMPTS), 1, PAGE + 1)
    last = jnp.arange(PROMPTS)[None, :] == PROMPTS - 1
    lead = jnp.arange(PROMPTS)[None, :] == 0
    tail = jnp.where(is_heavy & last, PAGE, tail)
    tail = jnp.where(is_heavy & lead, 1, tail)
    return ((counts - 1) * PAGE + tail).astype(jnp.int32)


def draw_queries(key, part):
    key = jax.random.fold_in(key, 6)
    first_key = jax.random.fold_in(key, 0)
    values = jax.random.normal(first_key, (STEPS, N_POOL * ROWS, QH * HD), jnp.float32)
    return values.astype(jnp.bfloat16)


def shard_levels(own_key, extent, cuts, smallest, high):
    def one(axis_at, parts):
        steps = jax.random.uniform(jax.random.fold_in(jax.random.fold_in(own_key, 6), axis_at), (parts,), jnp.float32, smallest / len(cuts), high / len(cuts))
        return jnp.repeat(jnp.exp(steps), extent[axis_at] // parts).reshape((-1,) + (1,) * (len(extent) - axis_at - 1))

    gain = one(*cuts[0])
    for cut in cuts[1:]:
        gain = gain * one(*cut)
    return gain


def centred(rng, extent, deviation, reach, shards=(), held_as=jnp.bfloat16):
    loudness = shard_levels(rng, extent, shards, -0.22, 0.18) if shards else 1.0
    array = jax.random.normal(rng, extent, jnp.float32) * deviation * loudness
    return jnp.minimum(jnp.maximum(array, -reach), reach).astype(held_as)


def setup_inputs(seed: int = 0, part: int = 0) -> dict:
    splits = jax.random.split(jax.random.key(seed), 11)
    part_keys = jax.random.split(jax.random.fold_in(splits[10], part), 11)
    prompt_kv = centred(part_keys[0], (PAGES_ALL, 2, KVH, PAGE, HD), 1.0, 6.0, ((0, 8), (2, 2)))
    prompt_lengths = draw_prompt_lengths(jax.random.fold_in(jax.random.fold_in(splits[10], part), 71), part)
    page_slot = draw_page_slot(jax.random.fold_in(jax.random.fold_in(splits[10], part), 71), part)
    cache_kv = centred(part_keys[3], (SLOTS, 2, KVH, PAGE, HD), 1.0, 6.0, ((0, 8), (2, 2)))
    cache_fill = draw_cache_fill(jax.random.fold_in(jax.random.fold_in(splits[10], part), 71), part)
    page_table = draw_page_table(jax.random.fold_in(jax.random.fold_in(splits[10], part), 71), part)
    context_lengths = draw_context_lengths(jax.random.fold_in(jax.random.fold_in(splits[10], part), 71), part)
    queries = draw_queries(jax.random.fold_in(jax.random.fold_in(splits[10], part), 71), part)
    new_kv = centred(part_keys[8], (STEPS, ROWS_ALL, 2, KVH, HD), 1.0, 6.0, ((1, 8), (3, 2)))
    out_weight = centred(splits[9], (QH * HD, D), (QH * HD) ** -0.5, 0.09375, ((0, 2), (1, 8)))
    return dict(prompt_kv=prompt_kv, prompt_lengths=prompt_lengths, page_slot=page_slot, cache_kv=cache_kv, cache_fill=cache_fill, page_table=page_table, context_lengths=context_lengths, queries=queries, new_kv=new_kv, out_weight=out_weight)


rope_base = 500000.0


def rotate(x, pos):
    half = x.shape[-1] // 2
    freq = rope_base ** (-(jnp.arange(half, dtype=jnp.float32) * 2.0) / x.shape[-1])
    angle = pos[..., None].astype(jnp.float32) * freq
    first, second = x[..., :half], x[..., half:]
    return jnp.concatenate([first * jnp.cos(angle) - second * jnp.sin(angle), second * jnp.cos(angle) + first * jnp.sin(angle)], -1)


def attend_one(args):
    cache, fills, table, lengths, queries, new_kv = args
    rows, most = table.shape
    steps = queries.shape[0]
    context = cache[table]
    page_fill = fills[table]
    offset = jnp.arange(most)[:, None] * PAGE + jnp.arange(PAGE)[None, :]
    valid = (offset[None] < lengths[:, None, None]) & (jnp.arange(PAGE)[None, None, :] < page_fill[:, :, None])
    grouped = queries.reshape(steps, rows, KVH, QH // KVH, HD).astype(jnp.float32)
    scale = HD ** -0.5
    old = jnp.einsum('srkgd,rjktd->srkgjt', grouped, context[:, :, 0].astype(jnp.float32)) * scale
    old = jnp.where(valid[None, :, None, None], old, -jnp.inf)
    position = lengths[None, :] + jnp.arange(steps)[:, None]
    fresh_keys = rotate(new_kv[:, :, 0].astype(jnp.float32), position[:, :, None]).astype(jnp.bfloat16)
    fresh = jnp.einsum('srkgd,urkd->srkgu', grouped, fresh_keys.astype(jnp.float32)) * scale
    causal = jnp.arange(steps)[None, :] <= jnp.arange(steps)[:, None]
    fresh = jnp.where(causal[:, None, None, None, :], fresh, -jnp.inf)
    top = jnp.maximum(jnp.max(old, axis=(4, 5)), jnp.max(fresh, axis=4))
    old_w = jnp.exp(old - top[..., None, None])
    fresh_w = jnp.exp(fresh - top[..., None])
    total = jnp.sum(old_w, axis=(4, 5)) + jnp.sum(fresh_w, axis=4)
    mixed = jnp.einsum('srkgjt,rjktd->srkgd', old_w.astype(jnp.bfloat16).astype(jnp.float32), context[:, :, 1].astype(jnp.float32))
    mixed = mixed + jnp.einsum('srkgu,urkd->srkgd', fresh_w.astype(jnp.bfloat16).astype(jnp.float32), new_kv[:, :, 1].astype(jnp.float32))
    return (mixed / total[..., None]).astype(jnp.bfloat16).reshape(steps, rows, QH * HD)


def reference(prompt_kv, prompt_lengths, page_slot, cache_kv, cache_fill, page_table, context_lengths, queries, new_kv, out_weight):
    counts = (prompt_lengths + PAGE - 1) // PAGE
    ends = jnp.cumsum(counts, axis=1)
    index = jnp.arange(PF_PAGES)
    owner = jnp.sum(ends[:, None, :] <= index[None, :, None], axis=2).astype(jnp.int32)
    first = jnp.take_along_axis(ends - counts, owner, 1)
    length = jnp.take_along_axis(prompt_lengths, owner, 1)
    start = ((index[None, :] - first) * PAGE).reshape(-1)
    fill = jnp.clip(length.reshape(-1) - start, 0, PAGE).astype(jnp.int32)
    positions = start[:, None] + jnp.arange(PAGE)[None, :]
    keys = rotate(prompt_kv[:, 0].astype(jnp.float32), positions[:, None, :]).astype(jnp.bfloat16)
    arrived = jnp.stack([keys, prompt_kv[:, 1]], 1)
    cache = cache_kv.at[page_slot].set(arrived)
    fills = cache_fill.at[page_slot].set(fill)
    steps = queries.shape[0]
    per_cache = cache.reshape(N_POOL, CACHE, 2, KVH, PAGE, HD)
    per_fill = fills.reshape(N_POOL, CACHE)
    per_table = page_table.reshape(N_POOL, ROWS, MAXP)
    per_len = context_lengths.reshape(N_POOL, ROWS)
    per_query = jnp.transpose(queries.reshape(steps, N_POOL, ROWS, QH * HD), (1, 0, 2, 3))
    per_new = jnp.transpose(new_kv.reshape(steps, N_POOL, ROWS, 2, KVH, HD), (1, 0, 2, 3, 4, 5))
    attention = lax.map(attend_one, (per_cache, per_fill, per_table, per_len, per_query, per_new))
    attention = jnp.transpose(attention, (1, 0, 2, 3)).reshape(steps, N_POOL * ROWS, QH * HD)
    projected = jnp.einsum('srh,hc->src', attention.astype(jnp.float32), out_weight.astype(jnp.float32))
    return projected.astype(jnp.bfloat16)
```

```python
import functools

import jax
import jax.numpy as jnp
import numpy as np
from jax import lax
from jax.experimental import pallas as pl
from jax.experimental.pallas import tpu as pltpu
from jax.sharding import PartitionSpec as P

ROPE_BASE = 500000.0
BF16, F32, I32 = jnp.bfloat16, jnp.float32, jnp.int32
SMEM = pl.BlockSpec(memory_space=pltpu.SMEM)
VMEM = pl.BlockSpec(memory_space=pltpu.VMEM)
ANY = pl.BlockSpec(memory_space=pl.ANY)
CONTRACT_LAST = (((1,), (1,)), ((), ()))
PARAMS = pltpu.CompilerParams(vmem_limit_bytes=32 * 2**20)


def tables(page_len, head_dim, pages):
    half = head_dim // 2
    freq = ROPE_BASE ** (-(np.arange(half) * 2.0) / head_dim)
    freq = np.concatenate([freq, freq])[None, :]
    sign = np.concatenate([-np.ones(half), np.ones(half)])[None, :]
    token = np.arange(page_len)[:, None] * freq
    first = np.arange(pages)[:, None] * page_len * freq
    out = (np.cos(token), sign * np.sin(token), np.cos(first), sign * np.sin(first), freq, sign)
    return [jnp.asarray(x, F32) for x in out]


def rope_kernel(page_len, per, len_ref, keys_ref, ct_ref, st_ref, cp_ref, sp_ref, out_ref):
    heads, head_dim = keys_ref.shape[2], keys_ref.shape[4]
    prompts = len_ref.shape[1]
    for i in range(per):
        number, _ = page_place(len_ref, prompts, page_len, pl.program_id(0) * per + i)
        c0, s0 = cp_ref[pl.ds(number, 1), :], sp_ref[pl.ds(number, 1), :]
        ct, st = ct_ref[...], st_ref[...]
        cos = c0 * ct - s0 * st
        sin = s0 * ct + c0 * st
        for k in range(heads):
            x = keys_ref[i, 0, k].astype(F32)
            out_ref[i, k] = (x * cos + pltpu.roll(x, head_dim // 2, 1) * sin).astype(BF16)


def page_place(len_ref, prompts, page_len, n):
    begin = jnp.int32(0)
    number, fill = jnp.int32(0), jnp.int32(0)
    for q in range(prompts):
        length = len_ref[0, q]
        count = (length + page_len - 1) // page_len
        here = (n >= begin) & (n < begin + count)
        number = jnp.where(here, n - begin, number)
        fill = jnp.where(here, jnp.clip(length - (n - begin) * page_len, 0, page_len), fill)
        begin = begin + count
    return number, fill


def rotated_keys(prompt_kv, prompt_lengths, tabs):
    pages, _, heads, page_len, head_dim = prompt_kv.shape
    per = 4
    ct, st, cp, sp, _, _ = tabs
    whole = lambda x: pl.BlockSpec(x.shape, lambda i: (0, 0))
    return pl.pallas_call(
        functools.partial(rope_kernel, page_len, per),
        grid=(pages // per,),
        out_shape=jax.ShapeDtypeStruct((pages, heads, page_len, head_dim), BF16),
        in_specs=[
            SMEM,
            pl.BlockSpec((per, 1, heads, page_len, head_dim), lambda i: (i, 0, 0, 0, 0)),
            whole(ct),
            whole(st),
            whole(cp),
            whole(sp),
        ],
        out_specs=pl.BlockSpec((per, heads, page_len, head_dim), lambda i: (i, 0, 0, 0)),
        compiler_params=PARAMS,
        cost_estimate=pl.CostEstimate(flops=6_000_000, bytes_accessed=2_000_000, transcendentals=0),
        name="rope_pages",
    )(prompt_lengths, prompt_kv, ct, st, cp, sp)


def spread_queries(q_ref, qf_ref, heads):
    steps, rows, width = q_ref.shape
    head_dim = qf_ref.shape[1]
    per = width // head_dim // heads
    block = heads * steps * per
    for s in range(steps):
        for h in range(heads * per):
            k, g = divmod(h, per)
            at = k * steps * per + s * per + g
            qf_ref[pl.ds(at, rows, stride=block), :] = q_ref[s, :, h * head_dim : (h + 1) * head_dim].astype(F32)


def query_kernel(npool, cache_pages, pair, heads, pages, *refs):
    me_ref, table_ref = refs[:2]
    metas = refs[2 : 2 + npool]
    q_ref = refs[2 + npool]
    outs = refs[3 + npool : 3 + 2 * npool]
    request_ref, inverse, qf = refs[3 + 2 * npool :]
    rows = q_ref.shape[1]
    most = table_ref.shape[0] // rows
    block = qf.shape[0] // rows
    for r in range(rows):
        for j in range(most):
            inverse[table_ref[r * most + j]] = r
    spread_queries(q_ref, qf, heads)
    base = me_ref[0] * cache_pages
    for t in range(npool):
        for p in range(pair):
            request_ref[t * pair + p] = -1

        def look(n, count):
            v = metas[t][0, n] - base
            hit = (v >= 0) & (v < cache_pages)

            @pl.when(hit)
            def _():
                request_ref[t * pair + count] = inverse[v]

            return count + hit.astype(I32)

        lax.fori_loop(0, pages, look, jnp.int32(0))
        for p in range(pair):
            r = jnp.maximum(request_ref[t * pair + p], 0)
            start = pl.multiple_of(r * block, block)
            outs[t][p * block : (p + 1) * block, :] = qf[pl.ds(start, block), :].astype(BF16)


def queries_out(me, table, metas, queries, pages, cache_pages, pair, heads, head_dim):
    npool = len(metas)
    steps, rows, width = queries.shape
    block = steps * width // head_dim
    payload = jax.ShapeDtypeStruct((pair * block, head_dim), BF16)
    out = pl.pallas_call(
        functools.partial(query_kernel, npool, cache_pages, pair, heads, pages),
        out_shape=[payload] * npool + [jax.ShapeDtypeStruct((npool * pair,), I32)],
        in_specs=[SMEM] * (2 + npool) + [VMEM],
        out_specs=[VMEM] * npool + [SMEM],
        scratch_shapes=[
            pltpu.SMEM((cache_pages,), I32),
            pltpu.VMEM((rows * block, head_dim), F32),
        ],
        compiler_params=PARAMS,
        cost_estimate=pl.CostEstimate(flops=1_000_000, bytes_accessed=500_000, transcendentals=0),
        name="queries_out",
    )(me, table, *metas, queries)
    return out[:npool], out[npool]


def softmax_parts(scores, mask):
    top = jnp.max(jnp.where(mask, scores, -jnp.inf), axis=1, keepdims=True)
    seen = top > -jnp.inf
    top = jnp.where(seen, top, 0.0)
    weights = jnp.where(mask, jnp.exp(scores - top), 0.0)
    return top, weights, jnp.sum(weights, axis=1, keepdims=True)


def local_kernel(
    page_len,
    heads,
    table_ref,
    context_ref,
    fill_ref,
    position_ref,
    q_ref,
    new_ref,
    freq_ref,
    sign_ref,
    cache_ref,
    o_ref,
    top_ref,
    total_ref,
    kv,
    sems,
    qf,
    kf,
    vf,
):
    steps, rows, width = q_ref.shape
    head_dim = qf.shape[1]
    most = table_ref.shape[0] // rows
    per = width // head_dim // heads
    block = heads * steps * per
    group = steps * per
    scale = head_dim ** (-0.5)

    def copy(n):
        return pltpu.make_async_copy(cache_ref.at[table_ref[n]], kv.at[n], sems.at[n])

    for n in range(rows * most):
        copy(n).start()
    spread_queries(q_ref, qf, heads)
    kf[...] = jnp.zeros_like(kf)
    vf[...] = jnp.zeros_like(vf)
    for u in range(steps):
        angle = (position_ref[...] + u).astype(F32) * freq_ref[...]
        cos, sin = jnp.cos(angle), jnp.sin(angle) * sign_ref[...]
        for k in range(heads):
            x = new_ref[u, :, k * head_dim : (k + 1) * head_dim].astype(F32)
            at = k * group + u
            kf[pl.ds(at, rows, stride=block), :] = x * cos + pltpu.roll(x, head_dim // 2, 1) * sin
            x = new_ref[u, :, (heads + k) * head_dim : (heads + k + 1) * head_dim].astype(F32)
            vf[pl.ds(at, rows, stride=block), :] = x
    column = lax.broadcasted_iota(I32, (group, page_len), 1)
    fresh_column = lax.broadcasted_iota(I32, (group, group), 1)
    fresh_step = lax.broadcasted_iota(I32, (group, group), 0) // per
    fresh_mask = (fresh_column <= fresh_step) & (fresh_column < steps)

    def request(r):
        for j in range(most):
            copy(r * most + j).wait()
        limits = [
            jnp.minimum(fill_ref[table_ref[r * most + j]], context_ref[r] - j * page_len) for j in range(most)
        ]
        mask = jnp.concatenate([column < limit for limit in limits] + [fresh_mask], axis=1)
        for k in range(heads):
            at = pl.multiple_of(r * block + k * group, group)
            q = qf[pl.ds(at, group), :].astype(BF16)
            fresh_k = kf[pl.ds(at, group), :].astype(BF16)
            fresh_v = vf[pl.ds(at, group), :].astype(BF16)
            keys = [kv[r * most + j, 0, k] for j in range(most)] + [fresh_k]
            values = [kv[r * most + j, 1, k] for j in range(most)] + [fresh_v]
            scores = [lax.dot_general(q, x, CONTRACT_LAST, preferred_element_type=F32) for x in keys]
            top, weights, total = softmax_parts(jnp.concatenate(scores, axis=1) * scale, mask)
            weights = weights.astype(BF16)
            mixed = jnp.zeros((group, head_dim), F32)
            begin = 0
            for x in values:
                part = weights[:, begin : begin + x.shape[0]]
                mixed = mixed + jnp.dot(part, x, preferred_element_type=F32)
                begin += x.shape[0]
            o_ref[pl.ds(at, group), :] = mixed
            top_ref[pl.ds(at, group), :] = jnp.broadcast_to(top, (group, head_dim))
            total_ref[pl.ds(at, group), :] = jnp.broadcast_to(total, (group, head_dim))

    together = 2

    @pl.loop(0, rows // together)
    def _(i):
        for u in range(together):
            request(i * together + u)


def local_attention(table, context, fills, queries, new_kv, cache_kv, tabs):
    steps, rows, width = queries.shape
    slots, _, heads, page_len, head_dim = cache_kv.shape
    block = steps * width // head_dim
    flat = jax.ShapeDtypeStruct((rows * block, head_dim), F32)
    freq, sign = tabs[4:]
    return pl.pallas_call(
        functools.partial(local_kernel, page_len, heads),
        out_shape=[flat] * 3,
        in_specs=[SMEM] * 3 + [VMEM] * 5 + [ANY],
        out_specs=[VMEM] * 3,
        scratch_shapes=[
            pltpu.VMEM((table.shape[0], 2, heads, page_len, head_dim), BF16),
            pltpu.SemaphoreType.DMA((table.shape[0],)),
            pltpu.VMEM((rows * block, head_dim), F32),
            pltpu.VMEM((rows * block, head_dim), F32),
            pltpu.VMEM((rows * block, head_dim), F32),
        ],
        compiler_params=PARAMS,
        cost_estimate=pl.CostEstimate(flops=110_000_000, bytes_accessed=7_000_000, transcendentals=300_000),
        name="local_attention",
    )(
        table,
        context,
        fills,
        context[:, None],
        queries,
        new_kv.reshape(steps, rows, 2 * heads * head_dim),
        freq,
        sign,
        cache_kv,
    )


def pieces(x):
    high = x.astype(BF16).astype(F32)
    middle = (x - high).astype(BF16).astype(F32)
    return [high, middle, x - high - middle]


def arrived_kernel(npool, cache_pages, pair, page_len, heads, *refs):
    me_ref, slot_ref, len_ref = refs[:3]
    metas = refs[3 : 3 + npool]
    queries = refs[3 + npool : 3 + 2 * npool]
    keys_ref, prompt_ref = refs[3 + 2 * npool : 5 + 2 * npool]
    outs = refs[5 + 2 * npool : 5 + 3 * npool]
    values, sem, page_of, slot_of, count_of = refs[5 + 3 * npool :]
    pages = slot_ref.shape[0]
    prompts = len_ref.shape[1]
    head_dim = keys_ref.shape[3]
    block = queries[0].shape[0] // pair
    group = block // heads
    scale = head_dim ** (-0.5)
    fetch = pltpu.make_async_copy(prompt_ref.at[:, 1], values, sem)
    fetch.start()
    for s in range(npool):
        count_of[s] = 0
        for p in range(pair):
            page_of[s * pair + p] = 0
            slot_of[s * pair + p] = -1

    def place(n, _):
        slot = slot_ref[n]
        target = slot // cache_pages
        s = lax.rem(target - me_ref[0] + npool, npool)
        at = s * pair + count_of[s]
        page_of[at] = n
        slot_of[at] = slot - target * cache_pages
        count_of[s] = count_of[s] + 1
        return 0

    lax.fori_loop(0, pages, place, 0)
    fetch.wait()
    column = lax.broadcasted_iota(I32, (group, page_len), 1)
    lane = lax.broadcasted_iota(I32, (group, head_dim), 1)
    for s in range(npool):
        meta = metas[(npool - s) % npool]
        for p in range(pair):
            n = page_of[s * pair + p]
            slot = slot_of[s * pair + p]
            _, fill = page_place(len_ref, prompts, page_len, n)
            left = jnp.sum(jnp.where(meta[1:2, :] == slot, meta[2:3, :], 0), axis=1, keepdims=True)
            mask = column < jnp.minimum(left, fill)
            for k in range(heads):
                at = p * block + k * group
                q = queries[s][at : at + group, :]
                scores = lax.dot_general(q, keys_ref[n, k], CONTRACT_LAST, preferred_element_type=F32)
                top, weights, total = softmax_parts(scores * scale, mask)
                mixed = jnp.dot(weights.astype(BF16), values[n, k], preferred_element_type=F32)
                stats = jnp.zeros((group, head_dim), F32)
                for i, x in enumerate(pieces(top) + pieces(total)):
                    stats = jnp.where(lane == i, x, stats)
                at = p * 2 * block + k * group
                outs[s][at : at + group, :] = mixed.astype(BF16)
                outs[s][at + block : at + block + group, :] = stats.astype(BF16)


def arrived_attention(me, page_slot, prompt_lengths, metas, queries, keys, prompt_kv, cache_pages, pair):
    npool = len(metas)
    pages, _, heads, page_len, head_dim = prompt_kv.shape
    payload = jax.ShapeDtypeStruct((2 * queries[0].shape[0], head_dim), BF16)
    return pl.pallas_call(
        functools.partial(arrived_kernel, npool, cache_pages, pair, page_len, heads),
        out_shape=[payload] * npool,
        in_specs=[SMEM] * 3 + [VMEM] * (2 * npool + 1) + [ANY],
        out_specs=[VMEM] * npool,
        scratch_shapes=[
            pltpu.VMEM((pages, heads, page_len, head_dim), BF16),
            pltpu.SemaphoreType.DMA,
            pltpu.SMEM((npool * pair,), I32),
            pltpu.SMEM((npool * pair,), I32),
            pltpu.SMEM((npool,), I32),
        ],
        compiler_params=PARAMS,
        cost_estimate=pl.CostEstimate(flops=40_000_000, bytes_accessed=4_000_000, transcendentals=70_000),
        name="arrived_attention",
    )(me, page_slot, prompt_lengths, *metas, *queries, keys, prompt_kv)


def merge_kernel(npool, pair, heads, *refs):
    request_ref = refs[0]
    parts = refs[1 : 1 + npool]
    o_ref, top_ref, total_ref, out_ref, mixed, top, total = refs[1 + npool :]
    steps, rows, width = out_ref.shape
    head_dim = o_ref.shape[1]
    per = width // head_dim // heads
    block = heads * steps * per
    mixed[...] = o_ref[...]
    top[...] = top_ref[...]
    total[...] = total_ref[...]
    for s in range(npool):
        for p in range(pair):
            r = request_ref[s * pair + p]
            at = pl.ds(pl.multiple_of(jnp.maximum(r, 0) * block, block), block)
            begin = p * 2 * block
            o = parts[s][begin : begin + block, :].astype(F32)
            stats = parts[s][begin + block : begin + 2 * block, :].astype(F32)
            m = stats[:, 0:1] + stats[:, 1:2] + stats[:, 2:3]
            l = stats[:, 3:4] + stats[:, 4:5] + stats[:, 5:6]
            seen = (l > 0.0) & (r >= 0)
            old = top[at, :]
            new = jnp.where(seen, jnp.maximum(old, m), old)
            a = jnp.exp(old - new)
            b = jnp.where(seen, jnp.exp(m - new), 0.0)
            top[at, :] = new
            total[at, :] = total[at, :] * a + l * b
            mixed[at, :] = mixed[at, :] * a + o * b
    for s in range(steps):
        for h in range(heads * per):
            k, g = divmod(h, per)
            at = pl.ds(k * steps * per + s * per + g, rows, stride=block)
            out_ref[s, :, h * head_dim : (h + 1) * head_dim] = (mixed[at, :] / total[at, :]).astype(BF16)


def merged(request, parts, local, steps, rows, width, heads, pair):
    npool = len(parts)
    flat = local[0].shape
    return pl.pallas_call(
        functools.partial(merge_kernel, npool, pair, heads),
        out_shape=jax.ShapeDtypeStruct((steps, rows, width), BF16),
        in_specs=[SMEM] + [VMEM] * (npool + 3),
        out_specs=VMEM,
        scratch_shapes=[pltpu.VMEM(flat, F32)] * 3,
        compiler_params=PARAMS,
        cost_estimate=pl.CostEstimate(flops=2_000_000, bytes_accessed=1_500_000, transcendentals=100_000),
        name="merge",
    )(request, *parts, *local)


def project_kernel(npool, scalars, *refs):
    blocks = refs[:npool]
    weight_ref, out_ref, lhs = refs[npool:]
    steps, rows, _ = blocks[0].shape

    @pl.when(pl.program_id(0) == 0)
    def _():
        for t in range(npool):
            owner = lax.rem(scalars[0] + npool - t, npool)
            at = pl.ds(pl.multiple_of(owner * rows, rows), rows)
            for s in range(steps):
                lhs[s, at, :] = blocks[t][s]

    for s in range(steps):
        out_ref[s] = jnp.dot(lhs[s], weight_ref[...], preferred_element_type=F32)


def projection(me, first_tile, blocks, weight, columns, tile):
    npool = len(blocks)
    steps, rows, width = blocks[0].shape
    whole = pl.BlockSpec((steps, rows, width), lambda i, sc: (0, 0, 0))
    return pl.pallas_call(
        functools.partial(project_kernel, npool),
        out_shape=jax.ShapeDtypeStruct((steps, npool * rows, columns), F32),
        grid_spec=pltpu.PrefetchScalarGridSpec(
            num_scalar_prefetch=1,
            grid=(columns // tile,),
            in_specs=[whole] * npool + [pl.BlockSpec((width, tile), lambda i, sc: (0, sc[1] + i))],
            out_specs=pl.BlockSpec((steps, npool * rows, tile), lambda i, sc: (0, 0, i)),
            scratch_shapes=[pltpu.VMEM((steps, npool * rows, width), BF16)],
        ),
        compiler_params=PARAMS,
        cost_estimate=pl.CostEstimate(
            flops=2 * steps * npool * rows * width * columns, bytes_accessed=4_000_000, transcendentals=0
        ),
        name="project",
    )(jnp.stack([me, first_tile]), *blocks, weight)


def shift(x, npool, by):
    return lax.ppermute(x, "pool", [(i, (i + by) % npool) for i in range(npool)])


def swap_halves(x):
    return lax.ppermute(x, "tp", [(0, 1), (1, 0)])


def shards(
    prompt_kv,
    prompt_lengths,
    page_slot,
    cache_kv,
    cache_fill,
    page_table,
    context_lengths,
    queries,
    new_kv,
    out_weight,
):
    npool = lax.axis_size("pool")
    me = lax.axis_index("pool").astype(I32)
    pages, _, heads, page_len, head_dim = prompt_kv.shape
    cache_pages = cache_kv.shape[0]
    steps, rows, width = queries.shape
    most = page_table.shape[1]
    pair = (pages + npool - 1) // npool
    tabs = tables(page_len, head_dim, pages)
    me1 = me[None]
    table = page_table.reshape(-1)

    left = jnp.clip(context_lengths[:, None] - page_len * jnp.arange(most, dtype=I32)[None, :], 0, page_len)
    lanes = 128
    row = lambda x, empty: jnp.pad(x, (0, lanes - x.shape[0]), constant_values=empty)[None]
    meta = jnp.concatenate(
        [row(page_slot, -1), row(table, -2), row(left.reshape(-1), 0), jnp.zeros((5, lanes), I32)], axis=0
    )
    metas = [meta] + [shift(meta, npool, t) for t in range(1, npool)]
    sent, request = queries_out(me1, table, metas, queries, pages, cache_pages, pair, heads, head_dim)
    got = [sent[0]] + [shift(sent[s], npool, -s) for s in range(1, npool)]
    keys = rotated_keys(prompt_kv, prompt_lengths, tabs)
    local = local_attention(table, context_lengths, cache_fill, queries, new_kv, cache_kv, tabs)
    parts = arrived_attention(me1, page_slot, prompt_lengths, metas, got, keys, prompt_kv, cache_pages, pair)
    parts = [parts[0]] + [shift(parts[t], npool, t) for t in range(1, npool)]
    attention = merged(request, parts, local, steps, rows, width, heads, pair)
    blocks = [attention] + [shift(attention, npool, t) for t in range(1, npool)]

    half = out_weight.shape[1] // 2
    tile = min(half, 256)
    mine = lax.axis_index("tp").astype(I32)
    other_terms = projection(me, (1 - mine) * (half // tile), blocks, out_weight, half, tile)
    other_terms = swap_halves(other_terms)
    terms = projection(me, mine * (half // tile), blocks, out_weight, half, tile)
    return (terms + other_terms).astype(BF16)


def solution(mesh):
    return jax.shard_map(
        shards,
        mesh=mesh,
        in_specs=(
            P(("group", "pool"), None, "tp", None, None),
            P(("group", "pool"), None),
            P(("group", "pool")),
            P(("group", "pool"), None, "tp", None, None),
            P(("group", "pool")),
            P(("group", "pool"), None),
            P(("group", "pool")),
            P(None, ("group", "pool"), "tp"),
            P(None, ("group", "pool"), None, "tp", None),
            P("tp", "pool"),
        ),
        out_specs=P(None, "group", ("pool", "tp")),
        check_vma=False,
    )
```

```python
import functools

import jax
import jax.numpy as jnp
import numpy as np
from jax import lax
from jax.experimental import pallas as pl
from jax.experimental.pallas import tpu as pltpu
from jax.sharding import PartitionSpec as P

ROPE_BASE = 500000.0
BF16, F32, I32 = jnp.bfloat16, jnp.float32, jnp.int32
SMEM = pl.BlockSpec(memory_space=pltpu.SMEM)
VMEM = pl.BlockSpec(memory_space=pltpu.VMEM)
ANY = pl.BlockSpec(memory_space=pl.ANY)
PARAMS = pltpu.CompilerParams(vmem_limit_bytes=60 * 2**20)
LANES = 128
CODES = 64
STAT_ROWS = 16
LEFT = 256


def tables(page_len, head_dim, pages):
    half = head_dim // 2
    freq = ROPE_BASE ** (-(np.arange(half) * 2.0) / head_dim)
    freq = np.concatenate([freq, freq])[None, :]
    sign = np.concatenate([-np.ones(half), np.ones(half)])[None, :]
    token = np.arange(page_len)[:, None] * freq
    first = np.arange(pages)[:, None] * page_len * freq
    out = (np.cos(token), sign * np.sin(token), np.cos(first), sign * np.sin(first), freq, sign)
    return [jnp.asarray(x, F32) for x in out]


def rope_kernel(page_len, per, len_ref, keys_ref, ct_ref, st_ref, cp_ref, sp_ref, out_ref):
    heads, head_dim = keys_ref.shape[2], keys_ref.shape[4]
    for i in range(per):
        number, _ = page_place(len_ref, page_len, pl.program_id(0) * per + i)
        c0, s0 = cp_ref[pl.ds(number, 1), :], sp_ref[pl.ds(number, 1), :]
        ct, st = ct_ref[...], st_ref[...]
        cos = c0 * ct - s0 * st
        sin = s0 * ct + c0 * st
        for k in range(heads):
            x = keys_ref[i, 0, k].astype(F32)
            out_ref[i, k] = (x * cos + pltpu.roll(x, head_dim // 2, 1) * sin).astype(BF16)


def page_place(len_ref, page_len, n):
    begin = jnp.int32(0)
    number, fill = jnp.int32(0), jnp.int32(0)
    for q in range(len_ref.shape[1]):
        length = len_ref[0, q]
        count = (length + page_len - 1) // page_len
        here = (n >= begin) & (n < begin + count)
        number = jnp.where(here, n - begin, number)
        fill = jnp.where(here, jnp.clip(length - (n - begin) * page_len, 0, page_len), fill)
        begin = begin + count
    return number, fill


def rotated_keys(prompt_kv, prompt_lengths, tabs):
    pages, _, heads, page_len, head_dim = prompt_kv.shape
    per = 4
    ct, st, cp, sp, _, _ = tabs
    whole = lambda x: pl.BlockSpec(x.shape, lambda i: (0, 0))
    return pl.pallas_call(
        functools.partial(rope_kernel, page_len, per),
        grid=(pages // per,),
        out_shape=jax.ShapeDtypeStruct((pages, heads, page_len, head_dim), BF16),
        in_specs=[
            SMEM,
            pl.BlockSpec((per, 1, heads, page_len, head_dim), lambda i: (i, 0, 0, 0, 0)),
            whole(ct),
            whole(st),
            whole(cp),
            whole(sp),
        ],
        out_specs=pl.BlockSpec((per, heads, page_len, head_dim), lambda i: (i, 0, 0, 0)),
        compiler_params=PARAMS,
        cost_estimate=pl.CostEstimate(flops=6_000_000, bytes_accessed=2_000_000, transcendentals=0),
        name="rope_pages",
    )(prompt_lengths, prompt_kv, ct, st, cp, sp)


def spread_queries(q_ref, qf_ref, heads):
    steps, rows, width = q_ref.shape
    head_dim = qf_ref.shape[1]
    per = width // head_dim // heads
    block = heads * steps * per
    for s in range(steps):
        for h in range(heads * per):
            k, g = divmod(h, per)
            at = k * steps * per + s * per + g
            qf_ref[pl.ds(at, rows, stride=block), :] = q_ref[s, :, h * head_dim : (h + 1) * head_dim].astype(F32)


def meta_kernel(npool, pair, cache_pages, page_len, slot_ref, len_ref, table_ref, context_ref, meta_ref, own_ref, count):
    items = npool * pair
    most, rows = table_ref.shape
    for e in range(npool):
        count[e] = 0
    for i in range(items):
        meta_ref[0, i] = -1
        own_ref[i] = 0
        own_ref[items + i] = 0
    for n in range(slot_ref.shape[0]):
        slot = slot_ref[n]
        target = slot // cache_pages
        at = target * pair + count[target]
        count[target] = count[target] + 1
        meta_ref[0, at] = slot - target * cache_pages
        _, fill = page_place(len_ref, page_len, n)
        own_ref[at] = n
        own_ref[items + at] = fill
    for r in range(rows):
        context = context_ref[r]
        for j in range(most):
            left = jnp.clip(context - j * page_len, 0, page_len)
            meta_ref[0, CODES + table_ref[j, r]] = r * LEFT + left


def meta_data(page_slot, prompt_lengths, table, context, npool, pair, cache_pages, page_len):
    return pl.pallas_call(
        functools.partial(meta_kernel, npool, pair, cache_pages, page_len),
        out_shape=[
            jax.ShapeDtypeStruct((1, LANES), I32),
            jax.ShapeDtypeStruct((2 * npool * pair,), I32),
        ],
        in_specs=[SMEM] * 4,
        out_specs=[SMEM] * 2,
        scratch_shapes=[pltpu.SMEM((npool,), I32)],
        compiler_params=PARAMS,
        cost_estimate=pl.CostEstimate(flops=1000, bytes_accessed=10_000, transcendentals=0),
        name="meta_data",
    )(page_slot, prompt_lengths, table, context)


def item_request(meta_ref, me, d, i):
    slot = meta_ref[d, i]
    code = meta_ref[me, CODES + jnp.maximum(slot, 0)]
    return jnp.where(slot >= 0, code // LEFT, 0), slot >= 0


def query_kernel(pair, heads, me_ref, meta_ref, q_ref, out_ref, qf):
    npool = out_ref.shape[0]
    rows = q_ref.shape[1]
    block = qf.shape[0] // rows
    me = me_ref[0]
    spread_queries(q_ref, qf, heads)
    for d in range(npool):
        for p in range(pair):
            r, _ = item_request(meta_ref, me, d, me * pair + p)
            at = pl.ds(pl.multiple_of(r * block, block), block)
            out_ref[d, p * block : (p + 1) * block, :] = qf[at, :].astype(BF16)


def queries_out(me, meta, queries, pair, heads, head_dim):
    npool = meta.shape[0]
    steps, rows, width = queries.shape
    block = steps * width // head_dim
    return pl.pallas_call(
        functools.partial(query_kernel, pair, heads),
        out_shape=jax.ShapeDtypeStruct((npool, pair * block, head_dim), BF16),
        in_specs=[SMEM, SMEM, VMEM],
        out_specs=VMEM,
        scratch_shapes=[pltpu.VMEM((rows * block, head_dim), F32)],
        compiler_params=PARAMS,
        cost_estimate=pl.CostEstimate(flops=100_000, bytes_accessed=500_000, transcendentals=0),
        name="queries_out",
    )(me, meta, queries)


def transposed_scores(queries, keys, group):
    turned = jnp.transpose(queries.astype(F32), (1, 0)).astype(BF16)
    chain = lax.broadcasted_iota(I32, turned.shape, 1) // group
    spread = [jnp.where(chain == c, turned, jnp.zeros_like(turned)) for c in range(len(keys))]
    scores = jnp.dot(
        jnp.concatenate(keys, axis=1), jnp.concatenate(spread, axis=0), preferred_element_type=F32
    )
    return scores * (queries.shape[1] ** -0.5)


def lane_values(scalars, lanes_each, shape):
    chain = lax.broadcasted_iota(I32, shape, 1) // lanes_each
    out = jnp.zeros(shape, I32)
    for i, x in enumerate(scalars):
        out = jnp.where(chain == i, x, out)
    return out


def local_kernel(
    page_len,
    heads,
    table_ref,
    context_ref,
    fill_ref,
    q_ref,
    new_ref,
    freq_ref,
    sign_ref,
    cache_ref,
    o_ref,
    stat_ref,
    kv,
    sems,
    qf,
    kf,
    vf,
    position,
):
    steps, rows, width = q_ref.shape
    head_dim = qf.shape[1]
    most = table_ref.shape[0]
    per = width // head_dim // heads
    group = steps * per
    block = heads * group
    together = LANES // block

    def copy(r, j):
        n = r * most + j
        return pltpu.make_async_copy(cache_ref.at[table_ref[j, r]], kv.at[n], sems.at[n])

    for r in range(rows):
        for j in range(most):
            copy(r, j).start()
    spread_queries(q_ref, qf, heads)
    kf[...] = jnp.zeros_like(kf)
    vf[...] = jnp.zeros_like(vf)
    for r in range(rows):
        position[r : r + 1, :] = jnp.full((1, head_dim), context_ref[r], I32)
    for u in range(steps):
        angle = (position[...] + u).astype(F32) * freq_ref[...]
        cos, sin = jnp.cos(angle), jnp.sin(angle) * sign_ref[...]
        for k in range(heads):
            x = new_ref[u, :, k * head_dim : (k + 1) * head_dim].astype(F32)
            at = k * group + u
            kf[pl.ds(at, rows, stride=block), :] = x * cos + pltpu.roll(x, head_dim // 2, 1) * sin
            x = new_ref[u, :, (heads + k) * head_dim : (heads + k + 1) * head_dim].astype(F32)
            vf[pl.ds(at, rows, stride=block), :] = x
    token = lax.broadcasted_iota(I32, (page_len, LANES), 0)
    fresh = lax.broadcasted_iota(I32, (group, LANES), 0)
    step = lax.broadcasted_iota(I32, (group, LANES), 1) % group // per
    fresh_mask = (fresh <= step) & (fresh < steps)

    for i in range(rows // together):
        requests = range(i * together, (i + 1) * together)
        chains = [(r, k) for r in requests for k in range(heads)]
        for r in requests:
            for j in range(most):
                copy(r, j).wait()
        queries = qf[i * LANES : (i + 1) * LANES, :]
        keys, values = [], []
        for r, k in chains:
            at = r * block + k * group
            page = lambda what: [kv[r * most + j, what, k] for j in range(most)]
            keys.append(jnp.concatenate(page(0) + [kf[at : at + group, :].astype(BF16)], axis=0))
            values.append(page(1) + [vf[at : at + group, :].astype(BF16)])
        scores = transposed_scores(queries, keys, group)
        mask = []
        for j in range(most):
            seen = [jnp.minimum(fill_ref[table_ref[j, r]], context_ref[r] - j * page_len) for r in requests]
            mask.append(token < lane_values(seen, block, (1, LANES)))
        parts = [
            jnp.where(m, scores[n * page_len : n * page_len + m.shape[0]], -jnp.inf)
            for n, m in enumerate(mask + [fresh_mask])
        ]
        top = functools.reduce(jnp.maximum, [jnp.max(x, axis=0, keepdims=True) for x in parts])
        parts = [jnp.exp(x - top) for x in parts]
        total = functools.reduce(jnp.add, [jnp.sum(x, axis=0, keepdims=True) for x in parts])
        stats = jnp.concatenate(
            [parts[most], jnp.broadcast_to(top, (8, LANES)), jnp.broadcast_to(total, (8, LANES))]
            + [jnp.zeros((LANES - group - 16, LANES), F32)],
            axis=0,
        )
        stats = jnp.transpose(stats, (1, 0))
        weights = [jnp.transpose(x, (1, 0)).astype(BF16) for x in parts[:most]]
        weights.append(stats[:, :group].astype(BF16))
        weights = jnp.concatenate(weights, axis=1)
        for c in range(len(chains)):
            at = i * LANES + c * group
            o_ref[at : at + group, :] = jnp.dot(
                weights[c * group : (c + 1) * group, :],
                jnp.concatenate(values[c], axis=0),
                preferred_element_type=F32,
            )
        stat_ref[i * LANES : (i + 1) * LANES, :] = stats


def local_attention(table, context, fills, queries, new_kv, cache_kv, tabs):
    steps, rows, width = queries.shape
    slots, _, heads, page_len, head_dim = cache_kv.shape
    block = steps * width // head_dim
    flat = (rows * block, head_dim)
    freq, sign = tabs[4:]
    return pl.pallas_call(
        functools.partial(local_kernel, page_len, heads),
        out_shape=[jax.ShapeDtypeStruct(flat, F32)] * 2,
        in_specs=[SMEM] * 3 + [VMEM] * 4 + [ANY],
        out_specs=[VMEM] * 2,
        scratch_shapes=[
            pltpu.VMEM((table.size, 2, heads, page_len, head_dim), BF16),
            pltpu.SemaphoreType.DMA((table.size,)),
            pltpu.VMEM(flat, F32),
            pltpu.VMEM(flat, F32),
            pltpu.VMEM(flat, F32),
            pltpu.VMEM((rows, head_dim), I32),
        ],
        compiler_params=PARAMS,
        cost_estimate=pl.CostEstimate(flops=800_000_000, bytes_accessed=12_000_000, transcendentals=400_000),
        name="local_attention",
    )(
        table,
        context,
        fills,
        queries,
        new_kv.reshape(steps, rows, 2 * heads * head_dim),
        freq,
        sign,
        cache_kv,
    )


def pieces(x):
    high = x.astype(BF16).astype(F32)
    middle = (x - high).astype(BF16).astype(F32)
    return [high, middle, x - high - middle]


def arrived_kernel(npool, pair, me_ref, meta_ref, own_ref, q_ref, keys_ref, prompt_ref, out_ref, values, sem):
    items = npool * pair
    _, heads, page_len, head_dim = keys_ref.shape
    block = q_ref.shape[0] // items
    group = block // heads
    together = LANES // block
    fetch = pltpu.make_async_copy(prompt_ref.at[:, 1], values, sem)
    fetch.start()
    fetch.wait()
    me = me_ref[0]
    token = lax.broadcasted_iota(I32, (page_len, LANES), 0)
    for i in range(items // together):
        own = range(i * together, (i + 1) * together)
        chains = [(own_ref[x], k) for x in own for k in range(heads)]
        seen = []
        for x in own:
            code = meta_ref[x // pair, CODES + jnp.maximum(meta_ref[me, x], 0)]
            seen.append(jnp.minimum(code % LEFT, own_ref[items + x]))
        scores = transposed_scores(
            q_ref[i * LANES : (i + 1) * LANES, :], [keys_ref[n, k] for n, k in chains], group
        )
        scores = jnp.where(token < lane_values(seen, block, (1, LANES)), scores, -jnp.inf)
        top = jnp.max(scores, axis=0, keepdims=True)
        top = jnp.where(top > -jnp.inf, top, 0.0)
        weights = jnp.exp(scores - top)
        stats = pieces(top) + pieces(jnp.sum(weights, axis=0, keepdims=True))
        stats = jnp.concatenate(stats + [jnp.zeros((STAT_ROWS - len(stats), LANES), F32)], axis=0).astype(BF16)
        weights = jnp.transpose(weights, (1, 0)).astype(BF16)
        for c, (n, k) in enumerate(chains):
            x, at = own[c // heads], (c % heads) * group
            at = (x % pair) * block + at
            out_ref[x // pair, at : at + group, :] = jnp.dot(
                weights[c * group : (c + 1) * group, :], values[n, k], preferred_element_type=F32
            ).astype(BF16)
        for e in sorted({x // pair for x in own}):
            out_ref[e, pair * block : pair * block + STAT_ROWS, :] = stats


def arrived_attention(me, meta, own, queries, keys, prompt_kv):
    npool, rows, head_dim = queries.shape
    pages, _, heads, page_len, _ = prompt_kv.shape
    pair = own.shape[0] // 2 // npool
    return pl.pallas_call(
        functools.partial(arrived_kernel, npool, pair),
        out_shape=jax.ShapeDtypeStruct((npool, rows + STAT_ROWS, head_dim), BF16),
        in_specs=[SMEM] * 3 + [VMEM] * 2 + [ANY],
        out_specs=VMEM,
        scratch_shapes=[
            pltpu.VMEM((pages, heads, page_len, head_dim), BF16),
            pltpu.SemaphoreType.DMA,
        ],
        compiler_params=PARAMS,
        cost_estimate=pl.CostEstimate(flops=200_000_000, bytes_accessed=4_000_000, transcendentals=70_000),
        name="arrived_attention",
    )(me, meta, own, queries.reshape(npool * rows, head_dim), keys, prompt_kv)


def merge_kernel(pair, heads, me_ref, meta_ref, parts_ref, o_ref, stat_ref, out_ref, mixed, top, total, turned):
    npool = parts_ref.shape[0]
    steps, rows, width = out_ref.shape
    head_dim = o_ref.shape[1]
    per = width // head_dim // heads
    group = steps * per
    block = heads * group
    me = me_ref[0]
    shape = top.shape
    mixed[...] = o_ref[...]
    top[...] = jnp.broadcast_to(stat_ref[:, group : group + 1], shape)
    total[...] = jnp.broadcast_to(stat_ref[:, group + 8 : group + 9], shape)
    tops, totals = [], []
    for d in range(npool):
        x = parts_ref[d, pair * block : pair * block + STAT_ROWS, :].astype(F32)
        tops.append(x[0:1] + x[1:2] + x[2:3])
        totals.append(x[3:4] + x[4:5] + x[5:6])
    empty = [jnp.zeros((LANES // 2 - npool, LANES), F32)]
    turned[...] = jnp.transpose(jnp.concatenate(tops + empty + totals + empty, axis=0), (1, 0))
    for d in range(npool):
        for p in range(pair):
            i = me * pair + p
            r, there = item_request(meta_ref, me, d, i)
            at = pl.ds(pl.multiple_of(r * block, block), block)
            lane = pl.ds(pl.multiple_of(lax.rem(i * block, LANES), block), block)
            m = jnp.broadcast_to(turned[lane, d : d + 1], (block, head_dim))
            l = jnp.broadcast_to(turned[lane, LANES // 2 + d : LANES // 2 + d + 1], (block, head_dim))
            seen = (l > 0.0) & there
            o = parts_ref[d, p * block : (p + 1) * block, :].astype(F32)
            old = top[at, :]
            new = jnp.where(seen, jnp.maximum(old, m), old)
            a = jnp.exp(old - new)
            b = jnp.where(seen, jnp.exp(m - new), 0.0)
            top[at, :] = new
            total[at, :] = total[at, :] * a + l * b
            mixed[at, :] = mixed[at, :] * a + o * b
    for s in range(steps):
        for h in range(heads * per):
            k, g = divmod(h, per)
            at = pl.ds(k * group + s * per + g, rows, stride=block)
            out_ref[s, :, h * head_dim : (h + 1) * head_dim] = (mixed[at, :] / total[at, :]).astype(BF16)


def merged(me, meta, parts, local, shape, heads, pair):
    flat = local[0].shape
    return pl.pallas_call(
        functools.partial(merge_kernel, pair, heads),
        out_shape=jax.ShapeDtypeStruct(shape, BF16),
        in_specs=[SMEM] * 2 + [VMEM] * 3,
        out_specs=VMEM,
        scratch_shapes=[pltpu.VMEM(flat, F32)] * 3 + [pltpu.VMEM((LANES, LANES), F32)],
        compiler_params=PARAMS,
        cost_estimate=pl.CostEstimate(flops=2_000_000, bytes_accessed=1_500_000, transcendentals=100_000),
        name="merge",
    )(me, meta, parts, *local)


def project_kernel(npool, scalars, *refs):
    blocks = refs[:npool]
    weight_ref, out_ref, lhs = refs[npool:]
    steps, rows, _ = blocks[0].shape

    @pl.when(pl.program_id(0) == 0)
    def _():
        for t in range(npool):
            owner = lax.rem(scalars[0] + npool - t, npool)
            at = pl.ds(pl.multiple_of(owner * rows, rows), rows)
            for s in range(steps):
                lhs[s, at, :] = blocks[t][s]

    for s in range(steps):
        out_ref[s] = jnp.dot(lhs[s], weight_ref[...], preferred_element_type=F32)


def projection(me, first_tile, blocks, weight, columns, tile):
    npool = len(blocks)
    steps, rows, width = blocks[0].shape
    whole = pl.BlockSpec((steps, rows, width), lambda i, sc: (0, 0, 0))
    return pl.pallas_call(
        functools.partial(project_kernel, npool),
        out_shape=jax.ShapeDtypeStruct((steps, npool * rows, columns), F32),
        grid_spec=pltpu.PrefetchScalarGridSpec(
            num_scalar_prefetch=1,
            grid=(columns // tile,),
            in_specs=[whole] * npool + [pl.BlockSpec((width, tile), lambda i, sc: (0, sc[1] + i))],
            out_specs=pl.BlockSpec((steps, npool * rows, tile), lambda i, sc: (0, 0, i)),
            scratch_shapes=[pltpu.VMEM((steps, npool * rows, width), BF16)],
        ),
        compiler_params=PARAMS,
        cost_estimate=pl.CostEstimate(
            flops=2 * steps * npool * rows * width * columns, bytes_accessed=4_000_000, transcendentals=0
        ),
        name="project",
    )(jnp.stack([me, first_tile]), *blocks, weight)


def shift(x, npool, by):
    return lax.ppermute(x, "pool", [(i, (i + by) % npool) for i in range(npool)])


def swap_halves(x):
    return lax.ppermute(x, "tp", [(0, 1), (1, 0)])


def shards(
    prompt_kv,
    prompt_lengths,
    page_slot,
    cache_kv,
    cache_fill,
    page_table,
    context_lengths,
    queries,
    new_kv,
    out_weight,
):
    npool = lax.axis_size("pool")
    me = lax.axis_index("pool").astype(I32)
    pages, _, heads, page_len, head_dim = prompt_kv.shape
    cache_pages = cache_kv.shape[0]
    pair = (pages + npool - 1) // npool
    tabs = tables(page_len, head_dim, pages)
    me1 = me[None]
    table = page_table.T

    mine, own = meta_data(page_slot, prompt_lengths, table, context_lengths, npool, pair, cache_pages, page_len)
    meta = lax.all_gather(mine, "pool", axis=0, tiled=True)
    keys = rotated_keys(prompt_kv, prompt_lengths, tabs)
    local = local_attention(table, context_lengths, cache_fill, queries, new_kv, cache_kv, tabs)
    sent = queries_out(me1, meta, queries, pair, heads, head_dim)
    got = lax.all_to_all(sent, "pool", split_axis=0, concat_axis=0, tiled=True)
    parts = arrived_attention(me1, meta, own, got, keys, prompt_kv)
    parts = lax.all_to_all(parts, "pool", split_axis=0, concat_axis=0, tiled=True)
    attention = merged(me1, meta, parts, local, queries.shape, heads, pair)
    blocks = [attention] + [shift(attention, npool, t) for t in range(1, npool)]

    half = out_weight.shape[1] // 2
    tile = min(half, 256)
    mine = lax.axis_index("tp").astype(I32)
    other_terms = projection(me, (1 - mine) * (half // tile), blocks, out_weight, half, tile)
    other_terms = swap_halves(other_terms)
    terms = projection(me, mine * (half // tile), blocks, out_weight, half, tile)
    return (terms + other_terms).astype(BF16)


def solution(mesh):
    return jax.shard_map(
        shards,
        mesh=mesh,
        in_specs=(
            P(("group", "pool"), None, "tp", None, None),
            P(("group", "pool"), None),
            P(("group", "pool")),
            P(("group", "pool"), None, "tp", None, None),
            P(("group", "pool")),
            P(("group", "pool"), None),
            P(("group", "pool")),
            P(None, ("group", "pool"), "tp"),
            P(None, ("group", "pool"), None, "tp", None),
            P("tp", "pool"),
        ),
        out_specs=P(None, "group", ("pool", "tp")),
        check_vma=False,
    )
```

```python
import functools

import jax
import jax.numpy as jnp
import numpy as np
from jax import lax
from jax.experimental import pallas as pl
from jax.experimental.pallas import tpu as pltpu
from jax.sharding import PartitionSpec as P

ROPE_BASE = 500000.0
BF16, F32, I32 = jnp.bfloat16, jnp.float32, jnp.int32
SMEM = pl.BlockSpec(memory_space=pltpu.SMEM)
VMEM = pl.BlockSpec(memory_space=pltpu.VMEM)
ANY = pl.BlockSpec(memory_space=pl.ANY)
SMALL = pltpu.CompilerParams(vmem_limit_bytes=24 * 2**20)
MIDDLE = pltpu.CompilerParams(vmem_limit_bytes=57 * 2**20)
LARGE = pltpu.CompilerParams(vmem_limit_bytes=59 * 2**20)
LANES = 128
CODES = 64
STAT_ROWS = 16
LEFT = 256


def tables(page_len, head_dim, pages):
    half = head_dim // 2
    freq = ROPE_BASE ** (-(np.arange(half) * 2.0) / head_dim)
    freq = np.concatenate([freq, freq])[None, :]
    sign = np.concatenate([-np.ones(half), np.ones(half)])[None, :]
    token = np.arange(page_len)[:, None] * freq
    first = np.arange(pages)[:, None] * page_len * freq
    out = (np.cos(token), sign * np.sin(token), np.cos(first), sign * np.sin(first), freq, sign)
    return [jnp.asarray(x, F32) for x in out]


def rope_kernel(
    npool, cache_pages, per, slot_ref, len_ref, keys_ref, ct_ref, st_ref, cp_ref, sp_ref, out_ref, own_ref, count
):
    _, _, heads, page_len, head_dim = keys_ref.shape

    @pl.when(pl.program_id(0) == 0)
    def _():
        items = own_ref.shape[0] // 2
        for e in range(npool):
            count[e] = 0
        for i in range(items):
            own_ref[i] = 0
            own_ref[items + i] = 0
        for n in range(slot_ref.shape[0]):
            target = slot_ref[n] // cache_pages
            at = target * (items // npool) + count[target]
            count[target] = count[target] + 1
            own_ref[at] = n
            own_ref[items + at] = page_place(len_ref, page_len, n)[1]

    for i in range(per):
        number, _ = page_place(len_ref, page_len, pl.program_id(0) * per + i)
        c0, s0 = cp_ref[pl.ds(number, 1), :], sp_ref[pl.ds(number, 1), :]
        ct, st = ct_ref[...], st_ref[...]
        cos = c0 * ct - s0 * st
        sin = s0 * ct + c0 * st
        for k in range(heads):
            x = keys_ref[i, 0, k].astype(F32)
            out_ref[i, k] = (x * cos + pltpu.roll(x, head_dim // 2, 1) * sin).astype(BF16)


def page_place(len_ref, page_len, n):
    begin = jnp.int32(0)
    number, fill = jnp.int32(0), jnp.int32(0)
    for q in range(len_ref.shape[1]):
        length = len_ref[0, q]
        count = (length + page_len - 1) // page_len
        here = (n >= begin) & (n < begin + count)
        number = jnp.where(here, n - begin, number)
        fill = jnp.where(here, jnp.clip(length - (n - begin) * page_len, 0, page_len), fill)
        begin = begin + count
    return number, fill


def rotated_keys(prompt_kv, page_slot, prompt_lengths, tabs, npool, pair, cache_pages):
    pages, _, heads, page_len, head_dim = prompt_kv.shape
    per = pages // 2
    ct, st, cp, sp, _, _ = tabs
    whole = lambda x: pl.BlockSpec(x.shape, lambda i: (0, 0))
    return pl.pallas_call(
        functools.partial(rope_kernel, npool, cache_pages, per),
        grid=(pages // per,),
        out_shape=[
            jax.ShapeDtypeStruct((pages, heads, page_len, head_dim), BF16),
            jax.ShapeDtypeStruct((2 * npool * pair,), I32),
        ],
        in_specs=[
            SMEM,
            SMEM,
            pl.BlockSpec((per, 1, heads, page_len, head_dim), lambda i: (i, 0, 0, 0, 0)),
            whole(ct),
            whole(st),
            whole(cp),
            whole(sp),
        ],
        out_specs=[pl.BlockSpec((per, heads, page_len, head_dim), lambda i: (i, 0, 0, 0)), SMEM],
        scratch_shapes=[pltpu.SMEM((npool,), I32)],
        compiler_params=LARGE,
        cost_estimate=pl.CostEstimate(flops=6_000_000, bytes_accessed=2_000_000, transcendentals=0),
        name="rope_pages",
    )(page_slot, prompt_lengths, prompt_kv, ct, st, cp, sp)


def spread_queries(q_ref, qf_ref, heads):
    steps, rows, width = q_ref.shape
    head_dim = qf_ref.shape[1]
    per = width // head_dim // heads
    block = heads * steps * per
    for s in range(steps):
        for h in range(heads * per):
            k, g = divmod(h, per)
            at = k * steps * per + s * per + g
            qf_ref[pl.ds(at, rows, stride=block), :] = q_ref[s, :, h * head_dim : (h + 1) * head_dim].astype(F32)


def meta_kernel(npool, pair, cache_pages, page_len, slot_ref, table_ref, context_ref, out_ref, row, count, sems):
    most, rows = table_ref.shape
    for e in range(npool):
        count[e] = 0
    for i in range(npool * pair):
        row[0, i] = -1
    for n in range(slot_ref.shape[0]):
        slot = slot_ref[n]
        target = slot // cache_pages
        row[0, target * pair + count[target]] = slot - target * cache_pages
        count[target] = count[target] + 1
    for r in range(rows):
        context = context_ref[r]
        for j in range(most):
            left = jnp.clip(context - j * page_len, 0, page_len)
            row[0, CODES + table_ref[j, r]] = r * LEFT + left
    copies = [pltpu.make_async_copy(row, out_ref.at[e], sems.at[e]) for e in range(npool)]
    for x in copies:
        x.start()
    for x in copies:
        x.wait()


def meta_data(page_slot, table, context, npool, pair, cache_pages, page_len):
    return pl.pallas_call(
        functools.partial(meta_kernel, npool, pair, cache_pages, page_len),
        out_shape=jax.ShapeDtypeStruct((npool, 1, LANES), I32),
        in_specs=[SMEM] * 3,
        out_specs=ANY,
        scratch_shapes=[
            pltpu.SMEM((1, LANES), I32),
            pltpu.SMEM((npool,), I32),
            pltpu.SemaphoreType.DMA((npool,)),
        ],
        compiler_params=SMALL,
        cost_estimate=pl.CostEstimate(flops=1000, bytes_accessed=10_000, transcendentals=0),
        name="meta_data",
    )(page_slot, table, context)


def item_request(meta_ref, me, d, i):
    slot = meta_ref[d, i]
    code = meta_ref[me, CODES + jnp.maximum(slot, 0)]
    return jnp.where(slot >= 0, code // LEFT, 0), slot >= 0


def query_kernel(pair, heads, me_ref, meta_ref, q_ref, out_ref, qf):
    npool = out_ref.shape[0]
    rows = q_ref.shape[1]
    block = qf.shape[0] // rows
    me = me_ref[0]
    spread_queries(q_ref, qf, heads)
    for d in range(npool):
        for p in range(pair):
            r, _ = item_request(meta_ref, me, d, me * pair + p)
            at = pl.ds(pl.multiple_of(r * block, block), block)
            out_ref[d, p * block : (p + 1) * block, :] = qf[at, :].astype(BF16)


def queries_out(me, meta, queries, pair, heads, head_dim):
    npool = meta.shape[0]
    steps, rows, width = queries.shape
    block = steps * width // head_dim
    return pl.pallas_call(
        functools.partial(query_kernel, pair, heads),
        out_shape=jax.ShapeDtypeStruct((npool, pair * block, head_dim), BF16),
        in_specs=[SMEM, SMEM, VMEM],
        out_specs=VMEM,
        scratch_shapes=[pltpu.VMEM((rows * block, head_dim), F32)],
        compiler_params=SMALL,
        cost_estimate=pl.CostEstimate(flops=100_000, bytes_accessed=500_000, transcendentals=0),
        name="queries_out",
    )(me, meta, queries)


def transposed_scores(queries, keys, group):
    turned = jnp.transpose(queries.astype(F32), (1, 0)).astype(BF16)
    chain = lax.broadcasted_iota(I32, turned.shape, 1) // group
    spread = [jnp.where(chain == c, turned, jnp.zeros_like(turned)) for c in range(len(keys))]
    scores = jnp.dot(
        jnp.concatenate(keys, axis=1), jnp.concatenate(spread, axis=0), preferred_element_type=F32
    )
    return scores * (queries.shape[1] ** -0.5)


def weighted_values(weights, values):
    heads, head_dim = len(values), values[0].shape[1]
    group = weights.shape[0] // heads
    out = jnp.dot(weights, jnp.concatenate(values, axis=1), preferred_element_type=F32)
    parts = [out[k * group : (k + 1) * group, k * head_dim : (k + 1) * head_dim] for k in range(heads)]
    return jnp.concatenate(parts, axis=0)


def lane_values(scalars, lanes_each, shape):
    chain = lax.broadcasted_iota(I32, shape, 1) // lanes_each
    out = jnp.zeros(shape, I32)
    for i, x in enumerate(scalars):
        out = jnp.where(chain == i, x, out)
    return out


def local_kernel(
    page_len,
    heads,
    table_ref,
    context_ref,
    fill_ref,
    q_ref,
    new_ref,
    freq_ref,
    sign_ref,
    cache_ref,
    o_ref,
    stat_ref,
    kv,
    sems,
    qf,
    kf,
    vf,
    position,
):
    steps, rows, width = q_ref.shape
    head_dim = qf.shape[1]
    most = table_ref.shape[0]
    per = width // head_dim // heads
    group = steps * per
    block = heads * group
    together = LANES // block

    def copy(r, j):
        n = r * most + j
        return pltpu.make_async_copy(cache_ref.at[table_ref[j, r]], kv.at[n], sems.at[n])

    for r in range(rows):
        for j in range(most):
            copy(r, j).start()
    spread_queries(q_ref, qf, heads)
    kf[...] = jnp.zeros_like(kf)
    vf[...] = jnp.zeros_like(vf)
    for r in range(rows):
        position[r : r + 1, :] = jnp.full((1, head_dim), context_ref[r], I32)
    for u in range(steps):
        angle = (position[...] + u).astype(F32) * freq_ref[...]
        cos, sin = jnp.cos(angle), jnp.sin(angle) * sign_ref[...]
        for k in range(heads):
            x = new_ref[u, :, k * head_dim : (k + 1) * head_dim].astype(F32)
            at = k * group + u
            kf[pl.ds(at, rows, stride=block), :] = x * cos + pltpu.roll(x, head_dim // 2, 1) * sin
            x = new_ref[u, :, (heads + k) * head_dim : (heads + k + 1) * head_dim].astype(F32)
            vf[pl.ds(at, rows, stride=block), :] = x
    token = lax.broadcasted_iota(I32, (page_len, LANES), 0)
    fresh = lax.broadcasted_iota(I32, (group, LANES), 0)
    step = lax.broadcasted_iota(I32, (group, LANES), 1) % group // per
    fresh_mask = (fresh <= step) & (fresh < steps)

    for i in range(rows // together):
        requests = range(i * together, (i + 1) * together)
        chains = [(r, k) for r in requests for k in range(heads)]
        for r in requests:
            for j in range(most):
                copy(r, j).wait()
        queries = qf[i * LANES : (i + 1) * LANES, :]
        keys, values = [], []
        for r, k in chains:
            at = r * block + k * group
            page = lambda what: [kv[r * most + j, what, k] for j in range(most)]
            keys.append(jnp.concatenate(page(0) + [kf[at : at + group, :].astype(BF16)], axis=0))
            values.append(page(1) + [vf[at : at + group, :].astype(BF16)])
        scores = transposed_scores(queries, keys, group)
        mask = []
        for j in range(most):
            seen = [jnp.minimum(fill_ref[table_ref[j, r]], context_ref[r] - j * page_len) for r in requests]
            mask.append(token < lane_values(seen, block, (1, LANES)))
        parts = [
            jnp.where(m, scores[n * page_len : n * page_len + m.shape[0]], -jnp.inf)
            for n, m in enumerate(mask + [fresh_mask])
        ]
        top = functools.reduce(jnp.maximum, [jnp.max(x, axis=0, keepdims=True) for x in parts])
        parts = [jnp.exp(x - top) for x in parts]
        total = functools.reduce(jnp.add, [jnp.sum(x, axis=0, keepdims=True) for x in parts])
        stats = jnp.concatenate(
            [parts[most], jnp.broadcast_to(top, (8, LANES)), jnp.broadcast_to(total, (8, LANES))]
            + [jnp.zeros((LANES - group - 16, LANES), F32)],
            axis=0,
        )
        stats = jnp.transpose(stats, (1, 0))
        weights = [jnp.transpose(x, (1, 0)).astype(BF16) for x in parts[:most]]
        weights.append(stats[:, :group].astype(BF16))
        weights = jnp.concatenate(weights, axis=1)
        for x in range(together):
            both = [jnp.concatenate(values[x * heads + k], axis=0) for k in range(heads)]
            both = weighted_values(weights[x * block : (x + 1) * block, :], both)
            o_ref[i * LANES + x * block : i * LANES + (x + 1) * block, :] = both
        stat_ref[i * LANES : (i + 1) * LANES, :] = stats


def local_attention(table, context, fills, queries, new_kv, cache_kv, tabs):
    steps, rows, width = queries.shape
    slots, _, heads, page_len, head_dim = cache_kv.shape
    block = steps * width // head_dim
    flat = (rows * block, head_dim)
    freq, sign = tabs[4:]
    return pl.pallas_call(
        functools.partial(local_kernel, page_len, heads),
        out_shape=[jax.ShapeDtypeStruct(flat, F32)] * 2,
        in_specs=[SMEM] * 3 + [VMEM] * 4 + [ANY],
        out_specs=[VMEM] * 2,
        scratch_shapes=[
            pltpu.VMEM((table.size, 2, heads, page_len, head_dim), BF16),
            pltpu.SemaphoreType.DMA((table.size,)),
            pltpu.VMEM(flat, F32),
            pltpu.VMEM(flat, F32),
            pltpu.VMEM(flat, F32),
            pltpu.VMEM((rows, head_dim), I32),
        ],
        compiler_params=MIDDLE,
        cost_estimate=pl.CostEstimate(flops=800_000_000, bytes_accessed=12_000_000, transcendentals=400_000),
        name="local_attention",
    )(
        table,
        context,
        fills,
        queries,
        new_kv.reshape(steps, rows, 2 * heads * head_dim),
        freq,
        sign,
        cache_kv,
    )


def pieces(x):
    high = x.astype(BF16).astype(F32)
    middle = (x - high).astype(BF16).astype(F32)
    return [high, middle, x - high - middle]


def arrived_kernel(npool, pair, me_ref, meta_ref, own_ref, q_ref, keys_ref, prompt_ref, out_ref, values, sem):
    items = npool * pair
    _, heads, page_len, head_dim = keys_ref.shape
    block = q_ref.shape[0] // items
    group = block // heads
    together = LANES // block
    fetch = pltpu.make_async_copy(prompt_ref.at[:, 1], values, sem)
    fetch.start()
    fetch.wait()
    me = me_ref[0]
    token = lax.broadcasted_iota(I32, (page_len, LANES), 0)
    for i in range(items // together):
        own = range(i * together, (i + 1) * together)
        chains = [(own_ref[x], k) for x in own for k in range(heads)]
        seen = []
        for x in own:
            code = meta_ref[x // pair, CODES + jnp.maximum(meta_ref[me, x], 0)]
            seen.append(jnp.minimum(code % LEFT, own_ref[items + x]))
        scores = transposed_scores(
            q_ref[i * LANES : (i + 1) * LANES, :], [keys_ref[n, k] for n, k in chains], group
        )
        scores = jnp.where(token < lane_values(seen, block, (1, LANES)), scores, -jnp.inf)
        top = jnp.max(scores, axis=0, keepdims=True)
        top = jnp.where(top > -jnp.inf, top, 0.0)
        weights = jnp.exp(scores - top)
        stats = pieces(top) + pieces(jnp.sum(weights, axis=0, keepdims=True))
        stats = jnp.concatenate(stats + [jnp.zeros((STAT_ROWS - len(stats), LANES), F32)], axis=0).astype(BF16)
        weights = jnp.transpose(weights, (1, 0)).astype(BF16)
        for c, x in enumerate(own):
            both = [values[own_ref[x], k] for k in range(heads)]
            both = weighted_values(weights[c * block : (c + 1) * block, :], both)
            at = (x % pair) * block
            out_ref[x // pair, at : at + block, :] = both.astype(BF16)
        for e in sorted({x // pair for x in own}):
            out_ref[e, pair * block : pair * block + STAT_ROWS, :] = stats


def arrived_attention(me, meta, own, queries, keys, prompt_kv):
    npool, rows, head_dim = queries.shape
    pages, _, heads, page_len, _ = prompt_kv.shape
    pair = own.shape[0] // 2 // npool
    return pl.pallas_call(
        functools.partial(arrived_kernel, npool, pair),
        out_shape=jax.ShapeDtypeStruct((npool, rows + STAT_ROWS, head_dim), BF16),
        in_specs=[SMEM] * 3 + [VMEM] * 2 + [ANY],
        out_specs=VMEM,
        scratch_shapes=[
            pltpu.VMEM((pages, heads, page_len, head_dim), BF16),
            pltpu.SemaphoreType.DMA,
        ],
        compiler_params=LARGE,
        cost_estimate=pl.CostEstimate(flops=200_000_000, bytes_accessed=4_000_000, transcendentals=70_000),
        name="arrived_attention",
    )(me, meta, own, queries.reshape(npool * rows, head_dim), keys, prompt_kv)


def merge_kernel(pair, heads, me_ref, meta_ref, parts_ref, o_ref, stat_ref, out_ref, mixed, top, total, turned):
    npool = parts_ref.shape[0]
    steps, rows, width = out_ref.shape
    head_dim = o_ref.shape[1]
    per = width // head_dim // heads
    group = steps * per
    block = heads * group
    me = me_ref[0]
    shape = top.shape
    mixed[...] = o_ref[...]
    top[...] = jnp.broadcast_to(stat_ref[:, group : group + 1], shape)
    total[...] = jnp.broadcast_to(stat_ref[:, group + 8 : group + 9], shape)
    tops, totals = [], []
    for d in range(npool):
        x = parts_ref[d, pair * block : pair * block + STAT_ROWS, :].astype(F32)
        tops.append(x[0:1] + x[1:2] + x[2:3])
        totals.append(x[3:4] + x[4:5] + x[5:6])
    empty = [jnp.zeros((LANES // 2 - npool, LANES), F32)]
    turned[...] = jnp.transpose(jnp.concatenate(tops + empty + totals + empty, axis=0), (1, 0))
    for d in range(npool):
        for p in range(pair):
            i = me * pair + p
            r, there = item_request(meta_ref, me, d, i)
            at = pl.ds(pl.multiple_of(r * block, block), block)
            lane = pl.ds(pl.multiple_of(lax.rem(i * block, LANES), block), block)
            m = jnp.broadcast_to(turned[lane, d : d + 1], (block, head_dim))
            l = jnp.broadcast_to(turned[lane, LANES // 2 + d : LANES // 2 + d + 1], (block, head_dim))
            seen = (l > 0.0) & there
            o = parts_ref[d, p * block : (p + 1) * block, :].astype(F32)
            old = top[at, :]
            new = jnp.where(seen, jnp.maximum(old, m), old)
            a = jnp.exp(old - new)
            b = jnp.where(seen, jnp.exp(m - new), 0.0)
            top[at, :] = new
            total[at, :] = total[at, :] * a + l * b
            mixed[at, :] = mixed[at, :] * a + o * b
    for s in range(steps):
        for h in range(heads * per):
            k, g = divmod(h, per)
            at = pl.ds(k * group + s * per + g, rows, stride=block)
            out_ref[s, :, h * head_dim : (h + 1) * head_dim] = (mixed[at, :] / total[at, :]).astype(BF16)


def merged(me, meta, parts, local, shape, heads, pair):
    flat = local[0].shape
    return pl.pallas_call(
        functools.partial(merge_kernel, pair, heads),
        out_shape=jax.ShapeDtypeStruct(shape, BF16),
        in_specs=[SMEM] * 2 + [VMEM] * 3,
        out_specs=VMEM,
        scratch_shapes=[pltpu.VMEM(flat, F32)] * 3 + [pltpu.VMEM((LANES, LANES), F32)],
        compiler_params=SMALL,
        cost_estimate=pl.CostEstimate(flops=2_000_000, bytes_accessed=1_500_000, transcendentals=100_000),
        name="merge",
    )(me, meta, parts, *local)


def project_kernel(npool, tile, place_ref, *refs):
    blocks = refs[:npool]
    weight_ref, out_ref, lhs, weight, sems, weight_sems = refs[npool:]
    steps, rows, _ = blocks[0].shape
    columns = weight.shape[1]
    every = npool * rows
    me, first = place_ref[0], pl.multiple_of(place_ref[1], LANES)
    fetch = []
    for i in range(columns // tile):
        at = pl.ds(i * tile, tile)
        source = weight_ref.at[:, pl.ds(first + i * tile, tile)]
        fetch.append(pltpu.make_async_copy(source, weight.at[:, at], weight_sems.at[i]))
        fetch[i].start()
    copies = []
    for x, (apart, flip) in enumerate(block_order(npool)):
        owner = owner_of(me, npool, apart, flip)
        for s in range(steps):
            at = pl.ds(pl.multiple_of(s * every + owner * rows, rows), rows)
            copies.append(pltpu.make_async_copy(blocks[x].at[s], lhs.at[at], sems.at[x * steps + s]))
            copies[-1].start()
    for x in copies:
        x.wait()
    for i in range(columns // tile):
        fetch[i].wait()
        at = slice(i * tile, (i + 1) * tile)
        terms = jnp.dot(lhs[...], weight[:, at], preferred_element_type=F32)
        for s in range(steps):
            out_ref[s, :, at] = terms[s * every : (s + 1) * every]


def projection(me, first, blocks, weight, columns):
    npool = len(blocks)
    steps, rows, width = blocks[0].shape
    tile = min(columns, 256)
    every = steps * npool * rows
    return pl.pallas_call(
        functools.partial(project_kernel, npool, tile),
        out_shape=jax.ShapeDtypeStruct((steps, npool * rows, columns), F32),
        in_specs=[SMEM] + [ANY] * (npool + 1),
        out_specs=VMEM,
        scratch_shapes=[
            pltpu.VMEM((every, width), BF16),
            pltpu.VMEM((width, columns), BF16),
            pltpu.SemaphoreType.DMA((npool * steps,)),
            pltpu.SemaphoreType.DMA((columns // tile,)),
        ],
        compiler_params=MIDDLE,
        cost_estimate=pl.CostEstimate(
            flops=2 * every * width * columns, bytes_accessed=4_000_000, transcendentals=0
        ),
        name="project",
    )(jnp.stack([me, first]), *blocks, weight)


def block_order(npool):
    return [(apart, flip) for flip in (0, 1) for apart in range(npool // 2)]


def owner_of(me, npool, apart, flip):
    half = npool // 2
    pair, side = me // 2, me % 2
    side = 1 - side if flip else side
    return lax.rem(pair + half - apart, half) * 2 + side


def gathered(x, npool):
    ahead = lambda x, by: lax.ppermute(x, "pool", [(i, (i + 2 * by) % npool) for i in range(npool)])
    across = lambda x: lax.ppermute(x, "pool", [(i, i ^ 1) for i in range(npool)])
    straight = [x] + [ahead(x, by) for by in range(1, npool // 2)]
    return straight + [across(y) for y in straight]


def swap_halves(x):
    return lax.ppermute(x, "tp", [(0, 1), (1, 0)])


def shards(
    prompt_kv,
    prompt_lengths,
    page_slot,
    cache_kv,
    cache_fill,
    page_table,
    context_lengths,
    queries,
    new_kv,
    out_weight,
):
    npool = lax.axis_size("pool")
    me = lax.axis_index("pool").astype(I32)
    pages, _, heads, page_len, head_dim = prompt_kv.shape
    cache_pages = cache_kv.shape[0]
    pair = (pages + npool - 1) // npool
    tabs = tables(page_len, head_dim, pages)
    me1 = me[None]
    table = page_table.T

    meta = meta_data(page_slot, table, context_lengths, npool, pair, cache_pages, page_len)
    meta = lax.all_to_all(meta, "pool", split_axis=0, concat_axis=0, tiled=True).reshape(npool, LANES)
    keys, own = rotated_keys(prompt_kv, page_slot, prompt_lengths, tabs, npool, pair, cache_pages)
    local = local_attention(table, context_lengths, cache_fill, queries, new_kv, cache_kv, tabs)
    sent = queries_out(me1, meta, queries, pair, heads, head_dim)
    got = lax.all_to_all(sent, "pool", split_axis=0, concat_axis=0, tiled=True)
    parts = arrived_attention(me1, meta, own, got, keys, prompt_kv)
    parts = lax.all_to_all(parts, "pool", split_axis=0, concat_axis=0, tiled=True)
    attention = merged(me1, meta, parts, local, queries.shape, heads, pair)
    blocks = gathered(attention, npool)
    half = out_weight.shape[1] // 2
    core = lax.axis_index("tp").astype(I32)
    other_terms = swap_halves(projection(me, (1 - core) * half, blocks, out_weight, half))
    terms = projection(me, core * half, blocks, out_weight, half)
    return (terms + other_terms).astype(BF16)


def solution(mesh):
    return jax.shard_map(
        shards,
        mesh=mesh,
        in_specs=(
            P(("group", "pool"), None, "tp", None, None),
            P(("group", "pool"), None),
            P(("group", "pool")),
            P(("group", "pool"), None, "tp", None, None),
            P(("group", "pool")),
            P(("group", "pool"), None),
            P(("group", "pool")),
            P(None, ("group", "pool"), "tp"),
            P(None, ("group", "pool"), None, "tp", None),
            P("tp", "pool"),
        ),
        out_specs=P(None, "group", ("pool", "tp")),
        check_vma=False,
    )
```

```python
import functools

import jax
import jax.numpy as jnp
import numpy as np
from jax import lax
from jax.experimental import pallas as pl
from jax.experimental.pallas import tpu as pltpu
from jax.sharding import PartitionSpec as P

ROPE_BASE = 500000.0
BF16, F32, I32 = jnp.bfloat16, jnp.float32, jnp.int32
SMEM = pl.BlockSpec(memory_space=pltpu.SMEM)
VMEM = pl.BlockSpec(memory_space=pltpu.VMEM)
ANY = pl.BlockSpec(memory_space=pl.ANY)
PARAMS = pltpu.CompilerParams(vmem_limit_bytes=60 * 2**20)
LANES = 128
CODES = 64
STAT_ROWS = 16
LEFT = 256


def tables(page_len, head_dim, pages):
    half = head_dim // 2
    freq = ROPE_BASE ** (-(np.arange(half) * 2.0) / head_dim)
    freq = np.concatenate([freq, freq])[None, :]
    sign = np.concatenate([-np.ones(half), np.ones(half)])[None, :]
    token = np.arange(page_len)[:, None] * freq
    first = np.arange(pages)[:, None] * page_len * freq
    out = (np.cos(token), sign * np.sin(token), np.cos(first), sign * np.sin(first), freq, sign)
    return [jnp.asarray(x, F32) for x in out]


def rope_kernel(
    npool, cache_pages, per, slot_ref, len_ref, keys_ref, ct_ref, st_ref, cp_ref, sp_ref, out_ref, own_ref, count
):
    _, _, heads, page_len, head_dim = keys_ref.shape

    @pl.when(pl.program_id(0) == 0)
    def _():
        items = own_ref.shape[0] // 2
        for e in range(npool):
            count[e] = 0
        for i in range(items):
            own_ref[i] = 0
            own_ref[items + i] = 0
        for n in range(slot_ref.shape[0]):
            target = slot_ref[n] // cache_pages
            at = target * (items // npool) + count[target]
            count[target] = count[target] + 1
            own_ref[at] = n
            own_ref[items + at] = page_place(len_ref, page_len, n)[1]

    for i in range(per):
        number, _ = page_place(len_ref, page_len, pl.program_id(0) * per + i)
        c0, s0 = cp_ref[pl.ds(number, 1), :], sp_ref[pl.ds(number, 1), :]
        ct, st = ct_ref[...], st_ref[...]
        cos = c0 * ct - s0 * st
        sin = s0 * ct + c0 * st
        for k in range(heads):
            x = keys_ref[i, 0, k].astype(F32)
            out_ref[i, k] = (x * cos + pltpu.roll(x, head_dim // 2, 1) * sin).astype(BF16)


def page_place(len_ref, page_len, n):
    begin = jnp.int32(0)
    number, fill = jnp.int32(0), jnp.int32(0)
    for q in range(len_ref.shape[1]):
        length = len_ref[0, q]
        count = (length + page_len - 1) // page_len
        here = (n >= begin) & (n < begin + count)
        number = jnp.where(here, n - begin, number)
        fill = jnp.where(here, jnp.clip(length - (n - begin) * page_len, 0, page_len), fill)
        begin = begin + count
    return number, fill


def rotated_keys(prompt_kv, page_slot, prompt_lengths, tabs, npool, pair, cache_pages):
    pages, _, heads, page_len, head_dim = prompt_kv.shape
    per = pages // 2
    ct, st, cp, sp, _, _ = tabs
    whole = lambda x: pl.BlockSpec(x.shape, lambda i: (0, 0))
    return pl.pallas_call(
        functools.partial(rope_kernel, npool, cache_pages, per),
        grid=(pages // per,),
        out_shape=[
            jax.ShapeDtypeStruct((pages, heads, page_len, head_dim), BF16),
            jax.ShapeDtypeStruct((2 * npool * pair,), I32),
        ],
        in_specs=[
            SMEM,
            SMEM,
            pl.BlockSpec((per, 1, heads, page_len, head_dim), lambda i: (i, 0, 0, 0, 0)),
            whole(ct),
            whole(st),
            whole(cp),
            whole(sp),
        ],
        out_specs=[pl.BlockSpec((per, heads, page_len, head_dim), lambda i: (i, 0, 0, 0)), SMEM],
        scratch_shapes=[pltpu.SMEM((npool,), I32)],
        compiler_params=PARAMS,
        cost_estimate=pl.CostEstimate(flops=6_000_000, bytes_accessed=2_000_000, transcendentals=0),
        name="rope_pages",
    )(page_slot, prompt_lengths, prompt_kv, ct, st, cp, sp)


def spread_queries(queries, heads, head_dim):
    steps, rows, width = queries.shape
    out = queries.reshape(steps, rows, heads, -1, head_dim).transpose(1, 2, 0, 3, 4)
    return out.reshape(rows, -1, head_dim)


def meta_kernel(npool, pair, cache_pages, page_len, slot_ref, table_ref, context_ref, out_ref, row, count, sems):
    most, rows = table_ref.shape
    for e in range(npool):
        count[e] = 0
    for i in range(npool * pair):
        row[0, i] = -1
    for n in range(slot_ref.shape[0]):
        slot = slot_ref[n]
        target = slot // cache_pages
        row[0, target * pair + count[target]] = slot - target * cache_pages
        count[target] = count[target] + 1
    for r in range(rows):
        context = context_ref[r]
        for j in range(most):
            left = jnp.clip(context - j * page_len, 0, page_len)
            row[0, CODES + table_ref[j, r]] = r * LEFT + left
    copies = [pltpu.make_async_copy(row, out_ref.at[e], sems.at[e]) for e in range(npool)]
    for x in copies:
        x.start()
    for x in copies:
        x.wait()


def meta_data(page_slot, table, context, npool, pair, cache_pages, page_len):
    return pl.pallas_call(
        functools.partial(meta_kernel, npool, pair, cache_pages, page_len),
        out_shape=jax.ShapeDtypeStruct((npool, 1, LANES), I32),
        in_specs=[SMEM] * 3,
        out_specs=ANY,
        scratch_shapes=[
            pltpu.SMEM((1, LANES), I32),
            pltpu.SMEM((npool,), I32),
            pltpu.SemaphoreType.DMA((npool,)),
        ],
        compiler_params=PARAMS,
        cost_estimate=pl.CostEstimate(flops=1000, bytes_accessed=10_000, transcendentals=0),
        name="meta_data",
    )(page_slot, table, context)


def item_request(meta_ref, me, d, i):
    slot = meta_ref[d, i]
    code = meta_ref[me, CODES + jnp.maximum(slot, 0)]
    return jnp.where(slot >= 0, code // LEFT, 0), slot >= 0


def transposed_scores(queries, keys, group):
    turned = jnp.transpose(queries.astype(F32), (1, 0)).astype(BF16)
    chain = lax.broadcasted_iota(I32, turned.shape, 1) // group
    spread = [jnp.where(chain == c, turned, jnp.zeros_like(turned)) for c in range(len(keys))]
    scores = jnp.dot(
        jnp.concatenate(keys, axis=1), jnp.concatenate(spread, axis=0), preferred_element_type=F32
    )
    return scores * (queries.shape[1] ** -0.5)


def weighted_values(weights, values):
    heads, head_dim = len(values), values[0].shape[1]
    group = weights.shape[0] // heads
    out = jnp.dot(weights, jnp.concatenate(values, axis=1), preferred_element_type=F32)
    parts = [out[k * group : (k + 1) * group, k * head_dim : (k + 1) * head_dim] for k in range(heads)]
    return jnp.concatenate(parts, axis=0)


def lane_values(scalars, lanes_each, shape):
    chain = lax.broadcasted_iota(I32, shape, 1) // lanes_each
    out = jnp.zeros(shape, I32)
    for i, x in enumerate(scalars):
        out = jnp.where(chain == i, x, out)
    return out


def local_kernel(
    page_len,
    heads,
    table_ref,
    context_ref,
    fill_ref,
    q_ref,
    new_ref,
    freq_ref,
    sign_ref,
    cache_ref,
    o_ref,
    stat_ref,
    kv,
    sems,
    kf,
    vf,
    position,
):
    rows, block, head_dim = q_ref.shape
    steps = new_ref.shape[0]
    most = table_ref.shape[0]
    group = block // heads
    per = group // steps
    together = LANES // block

    def copy(r, j):
        n = r * most + j
        return pltpu.make_async_copy(cache_ref.at[table_ref[j, r]], kv.at[n], sems.at[n])

    for r in range(rows):
        for j in range(most):
            copy(r, j).start()
    kf[...] = jnp.zeros_like(kf)
    vf[...] = jnp.zeros_like(vf)
    for r in range(rows):
        position[r : r + 1, :] = jnp.full((1, head_dim), context_ref[r], I32)
    for u in range(steps):
        angle = (position[...] + u).astype(F32) * freq_ref[...]
        cos, sin = jnp.cos(angle), jnp.sin(angle) * sign_ref[...]
        for k in range(heads):
            x = new_ref[u, :, k * head_dim : (k + 1) * head_dim].astype(F32)
            at = k * group + u
            kf[pl.ds(at, rows, stride=block), :] = x * cos + pltpu.roll(x, head_dim // 2, 1) * sin
            x = new_ref[u, :, (heads + k) * head_dim : (heads + k + 1) * head_dim].astype(F32)
            vf[pl.ds(at, rows, stride=block), :] = x
    token = lax.broadcasted_iota(I32, (page_len, LANES), 0)
    fresh = lax.broadcasted_iota(I32, (group, LANES), 0)
    step = lax.broadcasted_iota(I32, (group, LANES), 1) % group // per
    fresh_mask = (fresh <= step) & (fresh < steps)

    for i in range(rows // together):
        requests = range(i * together, (i + 1) * together)
        chains = [(r, k) for r in requests for k in range(heads)]
        for r in requests:
            for j in range(most):
                copy(r, j).wait()
        queries = q_ref[i * together : (i + 1) * together].reshape(LANES, head_dim)
        keys, values = [], []
        for r, k in chains:
            at = r * block + k * group
            page = lambda what: [kv[r * most + j, what, k] for j in range(most)]
            keys.append(jnp.concatenate(page(0) + [kf[at : at + group, :].astype(BF16)], axis=0))
            values.append(page(1) + [vf[at : at + group, :].astype(BF16)])
        scores = transposed_scores(queries, keys, group)
        mask = []
        for j in range(most):
            seen = [jnp.minimum(fill_ref[table_ref[j, r]], context_ref[r] - j * page_len) for r in requests]
            mask.append(token < lane_values(seen, block, (1, LANES)))
        parts = [
            jnp.where(m, scores[n * page_len : n * page_len + m.shape[0]], -jnp.inf)
            for n, m in enumerate(mask + [fresh_mask])
        ]
        top = functools.reduce(jnp.maximum, [jnp.max(x, axis=0, keepdims=True) for x in parts])
        parts = [jnp.exp(x - top) for x in parts]
        total = functools.reduce(jnp.add, [jnp.sum(x, axis=0, keepdims=True) for x in parts])
        stats = jnp.concatenate(
            [parts[most], jnp.broadcast_to(top, (8, LANES)), jnp.broadcast_to(total, (8, LANES))]
            + [jnp.zeros((LANES - group - 16, LANES), F32)],
            axis=0,
        )
        stats = jnp.transpose(stats, (1, 0))
        weights = [jnp.transpose(x, (1, 0)).astype(BF16) for x in parts[:most]]
        weights.append(stats[:, :group].astype(BF16))
        weights = jnp.concatenate(weights, axis=1)
        for x in range(together):
            both = [jnp.concatenate(values[x * heads + k], axis=0) for k in range(heads)]
            both = weighted_values(weights[x * block : (x + 1) * block, :], both)
            o_ref[i * LANES + x * block : i * LANES + (x + 1) * block, :] = both
        stat_ref[i * LANES : (i + 1) * LANES, :] = stats


def local_attention(table, context, fills, queries, new_kv, cache_kv, tabs):
    rows, block, _ = queries.shape
    steps = new_kv.shape[0]
    slots, _, heads, page_len, head_dim = cache_kv.shape
    flat = (rows * block, head_dim)
    freq, sign = tabs[4:]
    return pl.pallas_call(
        functools.partial(local_kernel, page_len, heads),
        out_shape=[jax.ShapeDtypeStruct(flat, F32)] * 2,
        in_specs=[SMEM] * 3 + [VMEM] * 4 + [ANY],
        out_specs=[VMEM] * 2,
        scratch_shapes=[
            pltpu.VMEM((table.size, 2, heads, page_len, head_dim), BF16),
            pltpu.SemaphoreType.DMA((table.size,)),
            pltpu.VMEM(flat, F32),
            pltpu.VMEM(flat, F32),
            pltpu.VMEM((rows, head_dim), I32),
        ],
        compiler_params=PARAMS,
        cost_estimate=pl.CostEstimate(flops=800_000_000, bytes_accessed=12_000_000, transcendentals=400_000),
        name="local_attention",
    )(
        table,
        context,
        fills,
        queries,
        new_kv.reshape(steps, rows, 2 * heads * head_dim),
        freq,
        sign,
        cache_kv,
    )


def pieces(x):
    high = x.astype(BF16).astype(F32)
    middle = (x - high).astype(BF16).astype(F32)
    return [high, middle, x - high - middle]


def arrived_kernel(npool, pair, me_ref, meta_ref, own_ref, *refs):
    blocks = refs[:npool]
    keys_ref, prompt_ref, out_ref, queries, values, sem, sems = refs[npool:]
    items = npool * pair
    _, heads, page_len, head_dim = keys_ref.shape
    block = queries.shape[0] // items
    group = block // heads
    together = LANES // block
    me = me_ref[0]
    owners = [owner_of(me, npool, apart, flip) for apart, flip in block_order(npool)]
    fetch, number, seen = [], [], []
    for x in range(items):
        e = owners[x // pair]
        at = e * pair + x % pair
        code = meta_ref[e, CODES + jnp.maximum(meta_ref[me, at], 0)]
        source = blocks[x // pair].at[code // LEFT]
        fetch.append(pltpu.make_async_copy(source, queries.at[pl.ds(x * block, block)], sems.at[x]))
        fetch[x].start()
        number.append(own_ref[at])
        seen.append(jnp.minimum(code % LEFT, own_ref[items + at]))
    page_values = pltpu.make_async_copy(prompt_ref.at[:, 1], values, sem)
    page_values.start()
    for x in fetch:
        x.wait()
    page_values.wait()
    token = lax.broadcasted_iota(I32, (page_len, LANES), 0)
    for i in range(items // together):
        own = range(i * together, (i + 1) * together)
        keys = [keys_ref[number[x], k] for x in own for k in range(heads)]
        scores = transposed_scores(queries[i * LANES : (i + 1) * LANES, :], keys, group)
        limit = lane_values([seen[x] for x in own], block, (1, LANES))
        scores = jnp.where(token < limit, scores, -jnp.inf)
        top = jnp.max(scores, axis=0, keepdims=True)
        top = jnp.where(top > -jnp.inf, top, 0.0)
        weights = jnp.exp(scores - top)
        stats = pieces(top) + pieces(jnp.sum(weights, axis=0, keepdims=True))
        stats = jnp.concatenate(stats + [jnp.zeros((STAT_ROWS - len(stats), LANES), F32)], axis=0).astype(BF16)
        weights = jnp.transpose(weights, (1, 0)).astype(BF16)
        for c, x in enumerate(own):
            both = [values[number[x], k] for k in range(heads)]
            both = weighted_values(weights[c * block : (c + 1) * block, :], both)
            at = (x % pair) * block
            out_ref[owners[x // pair], at : at + block, :] = both.astype(BF16)
        for place in sorted({x // pair for x in own}):
            out_ref[owners[place], pair * block : pair * block + STAT_ROWS, :] = stats


def arrived_attention(me, meta, own, blocks, keys, prompt_kv):
    npool = len(blocks)
    pages, _, heads, page_len, head_dim = prompt_kv.shape
    block = blocks[0].shape[1]
    items = own.shape[0] // 2
    pair = items // npool
    return pl.pallas_call(
        functools.partial(arrived_kernel, npool, pair),
        out_shape=jax.ShapeDtypeStruct((npool, pair * block + STAT_ROWS, head_dim), BF16),
        in_specs=[SMEM] * 3 + [ANY] * npool + [VMEM, ANY],
        out_specs=VMEM,
        scratch_shapes=[
            pltpu.VMEM((items * block, head_dim), BF16),
            pltpu.VMEM((pages, heads, page_len, head_dim), BF16),
            pltpu.SemaphoreType.DMA,
            pltpu.SemaphoreType.DMA((items,)),
        ],
        compiler_params=PARAMS,
        cost_estimate=pl.CostEstimate(flops=200_000_000, bytes_accessed=4_000_000, transcendentals=70_000),
        name="arrived_attention",
    )(me, meta, own, *[in_hbm(x) for x in blocks], keys, prompt_kv)


def item_request(meta_ref, me, d, i):
    slot = meta_ref[d, i]
    code = meta_ref[me, CODES + jnp.maximum(slot, 0)]
    return jnp.where(slot >= 0, code // LEFT, 0), slot >= 0


def merge_kernel(pair, heads, me_ref, meta_ref, parts_ref, o_ref, stat_ref, out_ref, mixed, top, total, turned):
    npool = parts_ref.shape[0]
    steps, rows, width = out_ref.shape
    head_dim = o_ref.shape[1]
    per = width // head_dim // heads
    group = steps * per
    block = heads * group
    me = me_ref[0]
    shape = top.shape
    mixed[...] = o_ref[...]
    top[...] = jnp.broadcast_to(stat_ref[:, group : group + 1], shape)
    total[...] = jnp.broadcast_to(stat_ref[:, group + 8 : group + 9], shape)
    tops, totals = [], []
    for d in range(npool):
        x = parts_ref[d, pair * block : pair * block + STAT_ROWS, :].astype(F32)
        tops.append(x[0:1] + x[1:2] + x[2:3])
        totals.append(x[3:4] + x[4:5] + x[5:6])
    empty = [jnp.zeros((LANES // 2 - npool, LANES), F32)]
    turned[...] = jnp.transpose(jnp.concatenate(tops + empty + totals + empty, axis=0), (1, 0))
    for d in range(npool):
        for p in range(pair):
            i = me * pair + p
            r, there = item_request(meta_ref, me, d, i)
            at = pl.ds(pl.multiple_of(r * block, block), block)
            place = place_of(me, npool, d) * pair + p
            lane = pl.ds(pl.multiple_of(lax.rem(place * block, LANES), block), block)
            m = jnp.broadcast_to(turned[lane, d : d + 1], (block, head_dim))
            l = jnp.broadcast_to(turned[lane, LANES // 2 + d : LANES // 2 + d + 1], (block, head_dim))
            seen = (l > 0.0) & there
            o = parts_ref[d, p * block : (p + 1) * block, :].astype(F32)
            old = top[at, :]
            new = jnp.where(seen, jnp.maximum(old, m), old)
            a = jnp.exp(old - new)
            b = jnp.where(seen, jnp.exp(m - new), 0.0)
            top[at, :] = new
            total[at, :] = total[at, :] * a + l * b
            mixed[at, :] = mixed[at, :] * a + o * b
    for s in range(steps):
        for h in range(heads * per):
            k, g = divmod(h, per)
            at = pl.ds(k * group + s * per + g, rows, stride=block)
            out_ref[s, :, h * head_dim : (h + 1) * head_dim] = (mixed[at, :] / total[at, :]).astype(BF16)


def merged(me, meta, parts, local, shape, heads, pair):
    flat = local[0].shape
    return pl.pallas_call(
        functools.partial(merge_kernel, pair, heads),
        out_shape=jax.ShapeDtypeStruct(shape, BF16),
        in_specs=[SMEM] * 2 + [VMEM] * 3,
        out_specs=VMEM,
        scratch_shapes=[pltpu.VMEM(flat, F32)] * 3 + [pltpu.VMEM((LANES, LANES), F32)],
        compiler_params=PARAMS,
        cost_estimate=pl.CostEstimate(flops=2_000_000, bytes_accessed=1_500_000, transcendentals=100_000),
        name="merge",
    )(me, meta, in_hbm(parts), *local)


def project_kernel(npool, chunk, place_ref, *refs):
    blocks = refs[:npool]
    weight_ref, mine_ref, other_ref, lhs, weight, total, sems, weight_sems = refs[npool:]
    steps, rows, _ = blocks[0].shape
    depth, columns = weight.shape
    half = columns // 2
    every = npool * rows
    me, core = place_ref[0], place_ref[1]
    fetch = []
    for i in range(depth // chunk):
        at = pl.ds(i * chunk, chunk)
        fetch.append(pltpu.make_async_copy(weight_ref.at[at], weight.at[at], weight_sems.at[i]))
        if i == 0:
            fetch[i].start()
    copies = []
    for x, (apart, flip) in enumerate(block_order(npool)):
        owner = owner_of(me, npool, apart, flip)
        for s in range(steps):
            at = pl.ds(pl.multiple_of(s * every + owner * rows, rows), rows)
            copies.append(pltpu.make_async_copy(blocks[x].at[s], lhs.at[at], sems.at[x * steps + s]))
            copies[-1].start()
    for x in fetch[1:]:
        x.start()
    for x in copies:
        x.wait()
    for i in range(depth // chunk):
        fetch[i].wait()
        at = slice(i * chunk, (i + 1) * chunk)
        terms = jnp.dot(lhs[:, at], weight[at, :], preferred_element_type=F32)
        total[...] = terms if i == 0 else total[...] + terms
    for s in range(steps):
        at = slice(s * every, (s + 1) * every)
        mine = pl.ds(pl.multiple_of(core * half, LANES), half)
        other = pl.ds(pl.multiple_of((1 - core) * half, LANES), half)
        mine_ref[s] = total[at, mine]
        other_ref[s] = total[at, other]


def projection(me, core, blocks, weight):
    npool = len(blocks)
    steps, rows, width = blocks[0].shape
    columns = weight.shape[1]
    every = steps * npool * rows
    chunk = 512
    return pl.pallas_call(
        functools.partial(project_kernel, npool, chunk),
        out_shape=[jax.ShapeDtypeStruct((steps, npool * rows, columns // 2), F32)] * 2,
        in_specs=[SMEM] + [ANY] * (npool + 1),
        out_specs=[VMEM] * 2,
        scratch_shapes=[
            pltpu.VMEM((every, width), BF16),
            pltpu.VMEM(weight.shape, BF16),
            pltpu.VMEM((every, columns), F32),
            pltpu.SemaphoreType.DMA((npool * steps,)),
            pltpu.SemaphoreType.DMA((width // chunk,)),
        ],
        compiler_params=PARAMS,
        cost_estimate=pl.CostEstimate(
            flops=2 * every * width * columns, bytes_accessed=6_000_000, transcendentals=0
        ),
        name="project",
    )(jnp.stack([me, core]), *[in_hbm(x) for x in blocks], weight)


def block_order(npool):
    return [(apart, flip) for flip in (0, 1) for apart in range(npool // 2)]


def owner_of(me, npool, apart, flip):
    half = npool // 2
    pair, side = me // 2, me % 2
    side = 1 - side if flip else side
    return lax.rem(pair + half - apart, half) * 2 + side


def place_of(me, npool, holder):
    half = npool // 2
    apart = lax.rem(holder // 2 - me // 2 + half, half)
    flip = lax.rem(me + holder, 2)
    return flip * half + apart


def in_hbm(x):
    return pltpu.with_memory_space_constraint(x, pltpu.HBM)


def gathered(x, npool):
    ahead = lambda x, by: lax.ppermute(x, "pool", [(i, (i + 2 * by) % npool) for i in range(npool)])
    across = lambda x: lax.ppermute(x, "pool", [(i, i ^ 1) for i in range(npool)])
    straight = [x] + [ahead(x, by) for by in range(1, npool // 2)]
    return straight + [across(y) for y in straight]


def swap_halves(x):
    return lax.ppermute(x, "tp", [(0, 1), (1, 0)])


def shards(
    prompt_kv,
    prompt_lengths,
    page_slot,
    cache_kv,
    cache_fill,
    page_table,
    context_lengths,
    queries,
    new_kv,
    out_weight,
):
    npool = lax.axis_size("pool")
    me = lax.axis_index("pool").astype(I32)
    pages, _, heads, page_len, head_dim = prompt_kv.shape
    cache_pages = cache_kv.shape[0]
    pair = (pages + npool - 1) // npool
    tabs = tables(page_len, head_dim, pages)
    me1 = me[None]
    table = page_table.T

    asked = spread_queries(queries, heads, head_dim)
    asked_all = gathered(asked, npool)
    meta = meta_data(page_slot, table, context_lengths, npool, pair, cache_pages, page_len)
    meta = lax.all_to_all(meta, "pool", split_axis=0, concat_axis=0, tiled=True).reshape(npool, LANES)
    meta = in_hbm(meta)
    keys, own = rotated_keys(prompt_kv, page_slot, prompt_lengths, tabs, npool, pair, cache_pages)
    local = local_attention(table, context_lengths, cache_fill, asked, new_kv, cache_kv, tabs)
    parts = arrived_attention(me1, meta, own, asked_all, keys, prompt_kv)
    parts = lax.all_to_all(parts, "pool", split_axis=0, concat_axis=0, tiled=True)
    attention = merged(me1, meta, parts, local, queries.shape, heads, pair)
    blocks = gathered(attention, npool)
    core = lax.axis_index("tp").astype(I32)
    terms, other_terms = projection(me, core, blocks, out_weight)
    other_terms = swap_halves(other_terms)
    return (terms + other_terms).astype(BF16)


def solution(mesh):
    return jax.shard_map(
        shards,
        mesh=mesh,
        in_specs=(
            P(("group", "pool"), None, "tp", None, None),
            P(("group", "pool"), None),
            P(("group", "pool")),
            P(("group", "pool"), None, "tp", None, None),
            P(("group", "pool")),
            P(("group", "pool"), None),
            P(("group", "pool")),
            P(None, ("group", "pool"), "tp"),
            P(None, ("group", "pool"), None, "tp", None),
            P("tp", "pool"),
        ),
        out_specs=P(None, "group", ("pool", "tp")),
        check_vma=False,
    )
```

```python
import functools

import jax
import jax.numpy as jnp
import numpy as np
from jax import lax
from jax.experimental import pallas as pl
from jax.experimental.pallas import tpu as pltpu
from jax.sharding import PartitionSpec as P

ROPE_BASE = 500000.0
BF16, F32, I32 = jnp.bfloat16, jnp.float32, jnp.int32
SMEM = pl.BlockSpec(memory_space=pltpu.SMEM)
VMEM = pl.BlockSpec(memory_space=pltpu.VMEM)
ANY = pl.BlockSpec(memory_space=pl.ANY)
PARAMS = pltpu.CompilerParams(vmem_limit_bytes=24 * 2**20)
LANES = 128
STAT_ROWS = 16


def tables(page_len, head_dim, pages):
    half = head_dim // 2
    freq = ROPE_BASE ** (-(np.arange(half) * 2.0) / head_dim)
    freq = np.concatenate([freq, freq])[None, :]
    sign = np.concatenate([-np.ones(half), np.ones(half)])[None, :]
    token = np.arange(page_len)[:, None] * freq
    first = np.arange(pages)[:, None] * page_len * freq
    out = (np.cos(token), sign * np.sin(token), np.cos(first), sign * np.sin(first), freq, sign)
    return [jnp.asarray(x, F32) for x in out]


def rope_kernel(
    npool, cache_pages, per, slot_ref, len_ref, keys_ref, ct_ref, st_ref, cp_ref, sp_ref, out_ref, own_ref, count
):
    _, _, heads, page_len, head_dim = keys_ref.shape

    @pl.when(pl.program_id(0) == 0)
    def _():
        items = own_ref.shape[0] // 3
        for e in range(npool):
            count[e] = 0
        for i in range(items):
            own_ref[i] = 0
            own_ref[items + i] = 0
            own_ref[2 * items + i] = -1
        for n in range(slot_ref.shape[0]):
            slot = slot_ref[n]
            target = slot // cache_pages
            at = target * (items // npool) + count[target]
            count[target] = count[target] + 1
            own_ref[at] = n
            own_ref[items + at] = page_place(len_ref, page_len, n)[1]
            own_ref[2 * items + at] = slot - target * cache_pages

    for i in range(per):
        number, _ = page_place(len_ref, page_len, pl.program_id(0) * per + i)
        c0, s0 = cp_ref[pl.ds(number, 1), :], sp_ref[pl.ds(number, 1), :]
        ct, st = ct_ref[...], st_ref[...]
        cos = c0 * ct - s0 * st
        sin = s0 * ct + c0 * st
        for k in range(heads):
            x = keys_ref[i, 0, k].astype(F32)
            out_ref[i, k] = (x * cos + pltpu.roll(x, head_dim // 2, 1) * sin).astype(BF16)


def page_place(len_ref, page_len, n):
    begin = jnp.int32(0)
    number, fill = jnp.int32(0), jnp.int32(0)
    for q in range(len_ref.shape[1]):
        length = len_ref[0, q]
        count = (length + page_len - 1) // page_len
        here = (n >= begin) & (n < begin + count)
        number = jnp.where(here, n - begin, number)
        fill = jnp.where(here, jnp.clip(length - (n - begin) * page_len, 0, page_len), fill)
        begin = begin + count
    return number, fill


def rotated_keys(prompt_kv, page_slot, prompt_lengths, tabs, npool, pair, cache_pages):
    pages, _, heads, page_len, head_dim = prompt_kv.shape
    per = pages // 2
    ct, st, cp, sp, _, _ = tabs
    whole = lambda x: pl.BlockSpec(x.shape, lambda i: (0, 0))
    return pl.pallas_call(
        functools.partial(rope_kernel, npool, cache_pages, per),
        grid=(pages // per,),
        out_shape=[
            jax.ShapeDtypeStruct((pages, heads, page_len, head_dim), BF16),
            jax.ShapeDtypeStruct((3 * npool * pair,), I32),
        ],
        in_specs=[
            SMEM,
            SMEM,
            pl.BlockSpec((per, 1, heads, page_len, head_dim), lambda i: (i, 0, 0, 0, 0)),
            whole(ct),
            whole(st),
            whole(cp),
            whole(sp),
        ],
        out_specs=[pl.BlockSpec((per, heads, page_len, head_dim), lambda i: (i, 0, 0, 0)), SMEM],
        scratch_shapes=[pltpu.SMEM((npool,), I32)],
        compiler_params=PARAMS,
        cost_estimate=pl.CostEstimate(flops=6_000_000, bytes_accessed=2_000_000, transcendentals=0),
        name="rope_pages",
    )(*[in_hbm(x) for x in (page_slot, prompt_lengths, prompt_kv, ct, st, cp, sp)])


def asked_kernel(page_len, heads, table_ref, context_ref, q_ref, out_ref, spread):
    most, rows = table_ref.shape
    steps, _, width = q_ref.shape
    block, head_dim = out_ref.shape[1:]
    per = width // head_dim // heads
    for s in range(steps):
        for h in range(heads * per):
            k, g = divmod(h, per)
            at = pl.ds(k * steps * per + s * per + g, rows, stride=block)
            spread[at, :] = q_ref[s, :, h * head_dim : (h + 1) * head_dim].astype(F32)
    for r in range(rows):
        out_ref[r] = spread[r * block : (r + 1) * block, :].astype(BF16)
    lane = lax.broadcasted_iota(I32, (block, LANES), 1)
    line = lax.broadcasted_iota(I32, (block, LANES), 0)
    request = jnp.zeros((block, LANES), I32)
    left = jnp.zeros((block, LANES), I32)
    for r in range(rows):
        context = context_ref[r]
        for j in range(most):
            here = lane == table_ref[j, r]
            request = jnp.where(here, r, request)
            left = jnp.where(here, jnp.clip(context - j * page_len, 0, page_len), left)
    out_ref[rows] = jnp.where(line == 0, request, left).astype(F32).astype(BF16)


def asked_queries(table, context, queries, page_len, heads, head_dim):
    steps, rows, width = queries.shape
    block = steps * width // head_dim
    return pl.pallas_call(
        functools.partial(asked_kernel, page_len, heads),
        out_shape=jax.ShapeDtypeStruct((rows + 1, block, head_dim), BF16),
        in_specs=[SMEM, SMEM, VMEM],
        out_specs=VMEM,
        scratch_shapes=[pltpu.VMEM((rows * block, head_dim), F32)],
        compiler_params=PARAMS,
        cost_estimate=pl.CostEstimate(flops=100_000, bytes_accessed=300_000, transcendentals=0),
        name="asked_queries",
    )(in_hbm(table), in_hbm(context), in_hbm(queries))


def read_scalar(x, pick):
    return jnp.max(jnp.where(pick, x, -2.0)).astype(I32)


def transposed_scores(queries, keys, group):
    turned = jnp.transpose(queries.astype(F32), (1, 0)).astype(BF16)
    chain = lax.broadcasted_iota(I32, (1, turned.shape[1]), 1) // group
    spread = [turned * jnp.where(chain == c, 1.0, 0.0).astype(BF16) for c in range(len(keys))]
    scores = jnp.dot(
        jnp.concatenate(keys, axis=1), jnp.concatenate(spread, axis=0), preferred_element_type=F32
    )
    return scores * (queries.shape[1] ** -0.5)


def weighted_values(weights, values):
    heads, head_dim = len(values), values[0].shape[1]
    group = weights.shape[0] // heads
    out = jnp.dot(weights, jnp.concatenate(values, axis=1), preferred_element_type=F32)
    parts = [out[k * group : (k + 1) * group, k * head_dim : (k + 1) * head_dim] for k in range(heads)]
    return jnp.concatenate(parts, axis=0)


def lane_values(scalars, lanes_each, shape):
    chain = lax.broadcasted_iota(I32, shape, 1) // lanes_each
    out = jnp.zeros(shape, I32)
    for i, x in enumerate(scalars):
        out = jnp.where(chain == i, x, out)
    return out


def local_kernel(
    page_len,
    heads,
    table_ref,
    context_ref,
    fill_ref,
    q_ref,
    new_ref,
    freq_ref,
    sign_ref,
    cache_ref,
    o_ref,
    stat_ref,
    kv,
    sems,
    kf,
    vf,
    position,
):
    rows, block, head_dim = q_ref.shape
    rows = rows - 1
    steps = new_ref.shape[0]
    most = table_ref.shape[0]
    group = block // heads
    per = group // steps
    together = LANES // block

    def copy(r, j):
        n = r * most + j
        return pltpu.make_async_copy(cache_ref.at[table_ref[j, r]], kv.at[n], sems.at[n])

    for r in range(rows):
        for j in range(most):
            copy(r, j).start()
    kf[...] = jnp.zeros_like(kf)
    vf[...] = jnp.zeros_like(vf)
    for r in range(rows):
        position[r : r + 1, :] = jnp.full((1, head_dim), context_ref[r], I32)
    for u in range(steps):
        angle = (position[...] + u).astype(F32) * freq_ref[...]
        cos, sin = jnp.cos(angle), jnp.sin(angle) * sign_ref[...]
        for k in range(heads):
            x = new_ref[u, :, k * head_dim : (k + 1) * head_dim].astype(F32)
            at = k * group + u
            kf[pl.ds(at, rows, stride=block), :] = x * cos + pltpu.roll(x, head_dim // 2, 1) * sin
            x = new_ref[u, :, (heads + k) * head_dim : (heads + k + 1) * head_dim].astype(F32)
            vf[pl.ds(at, rows, stride=block), :] = x
    token = lax.broadcasted_iota(I32, (page_len, LANES), 0)
    fresh = lax.broadcasted_iota(I32, (group, LANES), 0)
    step = lax.broadcasted_iota(I32, (group, LANES), 1) % group // per
    fresh_mask = (fresh <= step) & (fresh < steps)

    for i in range(rows // together):
        requests = range(i * together, (i + 1) * together)
        chains = [(r, k) for r in requests for k in range(heads)]
        if i % 2 == 0:
            for r in range(i * together, min(rows, (i + 2) * together)):
                for j in range(most):
                    copy(r, j).wait()
        queries = q_ref[i * together : (i + 1) * together].reshape(LANES, head_dim)
        keys, values = [], []
        for r, k in chains:
            at = r * block + k * group
            page = lambda what: [kv[r * most + j, what, k] for j in range(most)]
            keys.append(jnp.concatenate(page(0) + [kf[at : at + group, :].astype(BF16)], axis=0))
            values.append(page(1) + [vf[at : at + group, :].astype(BF16)])
        scores = transposed_scores(queries, keys, group)
        mask = []
        for j in range(most):
            seen = [jnp.minimum(fill_ref[table_ref[j, r]], context_ref[r] - j * page_len) for r in requests]
            mask.append(token < lane_values(seen, block, (1, LANES)))
        parts = [
            jnp.where(m, scores[n * page_len : n * page_len + m.shape[0]], -jnp.inf)
            for n, m in enumerate(mask + [fresh_mask])
        ]
        top = functools.reduce(jnp.maximum, [jnp.max(x, axis=0, keepdims=True) for x in parts])
        parts = [jnp.exp(x - top) for x in parts]
        total = functools.reduce(jnp.add, [jnp.sum(x, axis=0, keepdims=True) for x in parts])
        stats = jnp.concatenate(
            [parts[most], jnp.broadcast_to(top, (8, LANES)), jnp.broadcast_to(total, (8, LANES))]
            + [jnp.zeros((LANES - group - 16, LANES), F32)],
            axis=0,
        )
        stats = jnp.transpose(stats, (1, 0))
        weights = [jnp.transpose(x, (1, 0)).astype(BF16) for x in parts[:most]]
        weights.append(stats[:, :group].astype(BF16))
        weights = jnp.concatenate(weights, axis=1)
        for x in range(together):
            both = [jnp.concatenate(values[x * heads + k], axis=0) for k in range(heads)]
            both = weighted_values(weights[x * block : (x + 1) * block, :], both)
            o_ref[i * LANES + x * block : i * LANES + (x + 1) * block, :] = both
        stat_ref[i * LANES : (i + 1) * LANES, :] = stats


def local_attention(table, context, fills, queries, new_kv, cache_kv, tabs):
    rows, block, _ = queries.shape
    rows = rows - 1
    steps = new_kv.shape[0]
    slots, _, heads, page_len, head_dim = cache_kv.shape
    flat = (rows * block, head_dim)
    freq, sign = tabs[4:]
    return pl.pallas_call(
        functools.partial(local_kernel, page_len, heads),
        out_shape=[jax.ShapeDtypeStruct(flat, F32)] * 2,
        in_specs=[SMEM] * 3 + [VMEM] * 4 + [ANY],
        out_specs=[VMEM] * 2,
        scratch_shapes=[
            pltpu.VMEM((table.size, 2, heads, page_len, head_dim), BF16),
            pltpu.SemaphoreType.DMA((table.size,)),
            pltpu.VMEM(flat, F32),
            pltpu.VMEM(flat, F32),
            pltpu.VMEM((rows, head_dim), I32),
        ],
        compiler_params=PARAMS,
        cost_estimate=pl.CostEstimate(flops=800_000_000, bytes_accessed=12_000_000, transcendentals=400_000),
        name="local_attention",
    )(
        *[in_hbm(x) for x in (table, context, fills)],
        queries,
        new_kv.reshape(steps, rows, 2 * heads * head_dim),
        *[in_hbm(x) for x in (freq, sign, cache_kv)],
    )


def pieces(x):
    high = x.astype(BF16).astype(F32)
    middle = (x - high).astype(BF16).astype(F32)
    return [high, middle, x - high - middle]


def arrived_kernel(npool, pair, me_ref, own_ref, *refs):
    blocks = refs[:npool]
    keys_ref, prompt_ref, out_ref, queries, values, sem = refs[npool:]
    items = npool * pair
    _, heads, page_len, head_dim = keys_ref.shape
    rows, block = blocks[0].shape[0] - 1, blocks[0].shape[1]
    group = block // heads
    together = LANES // block
    me = me_ref[0]
    owners = [owner_of(me, npool, apart, flip) for apart, flip in block_order(npool)]
    page_values = pltpu.make_async_copy(prompt_ref.at[:, 1], values, sem)
    page_values.start()
    line = lax.broadcasted_iota(I32, (STAT_ROWS, LANES), 0)
    lane = lax.broadcasted_iota(I32, (STAT_ROWS, LANES), 1)
    number, seen, request = [], [], []
    for x in range(items):
        at = owners[x // pair] * pair + x % pair
        slot = own_ref[2 * items + at]
        side = blocks[x // pair][rows, :STAT_ROWS, :].astype(F32)
        reader = read_scalar(side, (lane == slot) & (line == 0))
        left = read_scalar(side, (lane == slot) & (line == 1))
        queries[x * block : (x + 1) * block, :] = blocks[x // pair][jnp.maximum(reader, 0)]
        number.append(own_ref[at])
        seen.append(jnp.minimum(left, own_ref[items + at]))
        request.append(jnp.where(slot >= 0, reader, -1))
    page_values.wait()
    token = lax.broadcasted_iota(I32, (page_len, LANES), 0)
    for i in range(items // together):
        own = range(i * together, (i + 1) * together)
        keys = [keys_ref[number[x], k] for x in own for k in range(heads)]
        scores = transposed_scores(queries[i * LANES : (i + 1) * LANES, :], keys, group)
        limit = lane_values([seen[x] for x in own], block, (1, LANES))
        scores = jnp.where(token < limit, scores, -jnp.inf)
        top = jnp.max(scores, axis=0, keepdims=True)
        top = jnp.where(top > -jnp.inf, top, 0.0)
        weights = jnp.exp(scores - top)
        stats = pieces(top) + pieces(jnp.sum(weights, axis=0, keepdims=True))
        stats.append(lane_values([request[x] for x in own], block, (1, LANES)).astype(F32))
        stats = jnp.concatenate(stats + [jnp.zeros((STAT_ROWS - len(stats), LANES), F32)], axis=0).astype(BF16)
        weights = jnp.transpose(weights, (1, 0)).astype(BF16)
        for c, x in enumerate(own):
            both = [values[number[x], k] for k in range(heads)]
            both = weighted_values(weights[c * block : (c + 1) * block, :], both)
            at = (x % pair) * block
            out_ref[owners[x // pair], at : at + block, :] = both.astype(BF16)
        for place in sorted({x // pair for x in own}):
            out_ref[owners[place], pair * block : pair * block + STAT_ROWS, :] = stats


def arrived_attention(me, own, blocks, keys, prompt_kv):
    npool = len(blocks)
    pages, _, heads, page_len, head_dim = prompt_kv.shape
    block = blocks[0].shape[1]
    items = own.shape[0] // 3
    pair = items // npool
    return pl.pallas_call(
        functools.partial(arrived_kernel, npool, pair),
        out_shape=jax.ShapeDtypeStruct((npool, pair * block + STAT_ROWS, head_dim), BF16),
        in_specs=[SMEM] * 2 + [VMEM] * (npool + 1) + [ANY],
        out_specs=VMEM,
        scratch_shapes=[
            pltpu.VMEM((items * block, head_dim), BF16),
            pltpu.VMEM((pages, heads, page_len, head_dim), BF16),
            pltpu.SemaphoreType.DMA,
        ],
        compiler_params=PARAMS,
        cost_estimate=pl.CostEstimate(flops=200_000_000, bytes_accessed=4_000_000, transcendentals=70_000),
        name="arrived_attention",
    )(me, own, *blocks, keys, in_hbm(prompt_kv))


def merge_kernel(pair, heads, me_ref, parts_ref, o_ref, stat_ref, out_ref, mixed, top, total, turned):
    npool = parts_ref.shape[0]
    steps, rows, width = out_ref.shape
    head_dim = o_ref.shape[1]
    per = width // head_dim // heads
    group = steps * per
    block = heads * group
    me = me_ref[0]
    shape = top.shape
    mixed[...] = o_ref[...]
    top[...] = jnp.broadcast_to(stat_ref[:, group : group + 1], shape)
    total[...] = jnp.broadcast_to(stat_ref[:, group + 8 : group + 9], shape)
    tops, totals, readers = [], [], []
    chain = lax.broadcasted_iota(I32, (1, LANES), 1) // block
    for d in range(npool):
        x = parts_ref[d, pair * block : pair * block + STAT_ROWS, :].astype(F32)
        tops.append(x[0:1] + x[1:2] + x[2:3])
        totals.append(x[3:4] + x[4:5] + x[5:6])
        readers.append(x[6:7])
    empty = [jnp.zeros((LANES // 2 - npool, LANES), F32)]
    turned[...] = jnp.transpose(jnp.concatenate(tops + empty + totals + empty, axis=0), (1, 0))
    for d in range(npool):
        for p in range(pair):
            part = lax.rem(place_of(me, npool, d) * pair + p, LANES // block)
            r = read_scalar(readers[d], chain == part)
            there = r >= 0
            at = pl.ds(pl.multiple_of(jnp.maximum(r, 0) * block, block), block)
            lane = pl.ds(pl.multiple_of(part * block, block), block)
            m = jnp.broadcast_to(turned[lane, d : d + 1], (block, head_dim))
            l = jnp.broadcast_to(turned[lane, LANES // 2 + d : LANES // 2 + d + 1], (block, head_dim))
            seen = (l > 0.0) & there
            o = parts_ref[d, p * block : (p + 1) * block, :].astype(F32)
            old = top[at, :]
            new = jnp.where(seen, jnp.maximum(old, m), old)
            a = jnp.exp(old - new)
            b = jnp.where(seen, jnp.exp(m - new), 0.0)
            top[at, :] = new
            total[at, :] = total[at, :] * a + l * b
            mixed[at, :] = mixed[at, :] * a + o * b
    for s in range(steps):
        for h in range(heads * per):
            k, g = divmod(h, per)
            at = pl.ds(k * group + s * per + g, rows, stride=block)
            out_ref[s, :, h * head_dim : (h + 1) * head_dim] = (mixed[at, :] / total[at, :]).astype(BF16)


def merged(me, parts, local, shape, heads, pair):
    flat = local[0].shape
    return pl.pallas_call(
        functools.partial(merge_kernel, pair, heads),
        out_shape=jax.ShapeDtypeStruct(shape, BF16),
        in_specs=[SMEM] + [VMEM] * 3,
        out_specs=VMEM,
        scratch_shapes=[pltpu.VMEM(flat, F32)] * 3 + [pltpu.VMEM((LANES, LANES), F32)],
        compiler_params=PARAMS,
        cost_estimate=pl.CostEstimate(flops=2_000_000, bytes_accessed=1_500_000, transcendentals=100_000),
        name="merge",
    )(me, parts, *local)


def project_kernel(npool, chunk, place_ref, *refs):
    blocks = refs[:npool]
    weight_ref, mine_ref, other_ref, lhs, weight, total, sems, weight_sems = refs[npool:]
    steps, rows, _ = blocks[0].shape
    depth, columns = weight.shape
    half = columns // 2
    every = npool * rows
    me, core = place_ref[0], place_ref[1]
    fetch = []
    for i in range(depth // chunk):
        at = pl.ds(i * chunk, chunk)
        fetch.append(pltpu.make_async_copy(weight_ref.at[at], weight.at[at], weight_sems.at[i]))
        if i == 0:
            fetch[i].start()
    copies = []
    for x, (apart, flip) in enumerate(block_order(npool)):
        owner = owner_of(me, npool, apart, flip)
        for s in range(steps):
            at = pl.ds(pl.multiple_of(s * every + owner * rows, rows), rows)
            copies.append(pltpu.make_async_copy(blocks[x].at[s], lhs.at[at], sems.at[x * steps + s]))
            copies[-1].start()
    for x in fetch[1:]:
        x.start()
    for x in copies:
        x.wait()
    for i in range(depth // chunk):
        fetch[i].wait()
        at = slice(i * chunk, (i + 1) * chunk)
        terms = jnp.dot(lhs[:, at], weight[at, :], preferred_element_type=F32)
        total[...] = terms if i == 0 else total[...] + terms
    for s in range(steps):
        at = slice(s * every, (s + 1) * every)
        mine = pl.ds(pl.multiple_of(core * half, LANES), half)
        other = pl.ds(pl.multiple_of((1 - core) * half, LANES), half)
        mine_ref[s] = total[at, mine]
        other_ref[s] = total[at, other]


def projection(me, core, blocks, weight):
    npool = len(blocks)
    steps, rows, width = blocks[0].shape
    columns = weight.shape[1]
    every = steps * npool * rows
    chunk = 512
    return pl.pallas_call(
        functools.partial(project_kernel, npool, chunk),
        out_shape=[jax.ShapeDtypeStruct((steps, npool * rows, columns // 2), F32)] * 2,
        in_specs=[SMEM] + [ANY] * (npool + 1),
        out_specs=[VMEM] * 2,
        scratch_shapes=[
            pltpu.VMEM((every, width), BF16),
            pltpu.VMEM(weight.shape, BF16),
            pltpu.VMEM((every, columns), F32),
            pltpu.SemaphoreType.DMA((npool * steps,)),
            pltpu.SemaphoreType.DMA((width // chunk,)),
        ],
        compiler_params=PARAMS,
        cost_estimate=pl.CostEstimate(
            flops=2 * every * width * columns, bytes_accessed=6_000_000, transcendentals=0
        ),
        name="project",
    )(jnp.stack([me, core]), *blocks, in_hbm(weight))


def block_order(npool):
    return [(apart, flip) for flip in (0, 1) for apart in range(npool // 2)]


def owner_of(me, npool, apart, flip):
    half = npool // 2
    pair, side = me // 2, me % 2
    side = 1 - side if flip else side
    return lax.rem(pair + half - apart, half) * 2 + side


def place_of(me, npool, holder):
    half = npool // 2
    apart = lax.rem(holder // 2 - me // 2 + half, half)
    flip = lax.rem(me + holder, 2)
    return flip * half + apart


def in_hbm(x):
    return pltpu.with_memory_space_constraint(x, pltpu.HBM)


def gathered(x, npool):
    ahead = lambda x, by: lax.ppermute(x, "pool", [(i, (i + 2 * by) % npool) for i in range(npool)])
    across = lambda x: lax.ppermute(x, "pool", [(i, i ^ 1) for i in range(npool)])
    straight = [x] + [ahead(x, by) for by in range(1, npool // 2)]
    return straight + [across(y) for y in straight]


def swap_halves(x):
    return lax.ppermute(x, "tp", [(0, 1), (1, 0)])


def shards(
    prompt_kv,
    prompt_lengths,
    page_slot,
    cache_kv,
    cache_fill,
    page_table,
    context_lengths,
    queries,
    new_kv,
    out_weight,
):
    npool = lax.axis_size("pool")
    me = lax.axis_index("pool").astype(I32)
    pages, _, heads, page_len, head_dim = prompt_kv.shape
    cache_pages = cache_kv.shape[0]
    pair = (pages + npool - 1) // npool
    tabs = tables(page_len, head_dim, pages)
    me1 = me[None]
    table = page_table.T

    asked = asked_queries(table, context_lengths, queries, page_len, heads, head_dim)
    asked_all = gathered(asked, npool)
    keys, own = rotated_keys(prompt_kv, page_slot, prompt_lengths, tabs, npool, pair, cache_pages)
    local = local_attention(table, context_lengths, cache_fill, asked, new_kv, cache_kv, tabs)
    parts = arrived_attention(me1, own, asked_all, keys, prompt_kv)
    parts = lax.all_to_all(parts, "pool", split_axis=0, concat_axis=0, tiled=True)
    attention = merged(me1, parts, local, queries.shape, heads, pair)
    blocks = gathered(attention, npool)
    core = lax.axis_index("tp").astype(I32)
    terms, other_terms = projection(me, core, blocks, out_weight)
    other_terms = swap_halves(other_terms)
    return (terms + other_terms).astype(BF16)


def solution(mesh):
    return jax.shard_map(
        shards,
        mesh=mesh,
        in_specs=(
            P(("group", "pool"), None, "tp", None, None),
            P(("group", "pool"), None),
            P(("group", "pool")),
            P(("group", "pool"), None, "tp", None, None),
            P(("group", "pool")),
            P(("group", "pool"), None),
            P(("group", "pool")),
            P(None, ("group", "pool"), "tp"),
            P(None, ("group", "pool"), None, "tp", None),
            P("tp", "pool"),
        ),
        out_specs=P(None, "group", ("pool", "tp")),
        check_vma=False,
    )
```

```python
import functools

import jax
import jax.numpy as jnp
import numpy as np
from jax import lax
from jax.experimental import pallas as pl
from jax.experimental.pallas import tpu as pltpu
from jax.sharding import PartitionSpec as P

ROPE_BASE = 500000.0
BF16, F32, I32 = jnp.bfloat16, jnp.float32, jnp.int32
SMEM = pl.BlockSpec(memory_space=pltpu.SMEM)
VMEM = pl.BlockSpec(memory_space=pltpu.VMEM)
ANY = pl.BlockSpec(memory_space=pl.ANY)
PARAMS = pltpu.CompilerParams(vmem_limit_bytes=24 * 2**20)
LANES = 128
STAT_ROWS = 16
CODE = 256


def tables(page_len, head_dim, pages):
    half = head_dim // 2
    freq = ROPE_BASE ** (-(np.arange(half) * 2.0) / head_dim)
    freq = np.concatenate([freq, freq])[None, :]
    sign = np.concatenate([-np.ones(half), np.ones(half)])[None, :]
    token = np.arange(page_len)[:, None] * freq
    first = np.arange(pages)[:, None] * page_len * freq
    out = (np.cos(token), sign * np.sin(token), np.cos(first), sign * np.sin(first), freq, sign)
    return [jnp.asarray(x, F32) for x in out]


def rope_kernel(
    npool, cache_pages, per, slot_ref, len_ref, pages_ref, ct_ref, st_ref, cp_ref, sp_ref, out_ref, own_ref, count
):
    _, _, heads, page_len, head_dim = pages_ref.shape

    @pl.when(pl.program_id(0) == 0)
    def _():
        items = own_ref.shape[0] // 3
        for e in range(npool):
            count[e] = 0
        for i in range(items):
            own_ref[i] = 0
            own_ref[items + i] = 0
            own_ref[2 * items + i] = -1
        for n in range(slot_ref.shape[0]):
            slot = slot_ref[n]
            target = slot // cache_pages
            at = target * (items // npool) + count[target]
            count[target] = count[target] + 1
            own_ref[at] = n
            own_ref[items + at] = page_place(len_ref, page_len, n)[1]
            own_ref[2 * items + at] = slot - target * cache_pages

    for i in range(per):
        number, _ = page_place(len_ref, page_len, pl.program_id(0) * per + i)
        c0, s0 = cp_ref[pl.ds(number, 1), :], sp_ref[pl.ds(number, 1), :]
        ct, st = ct_ref[...], st_ref[...]
        cos = c0 * ct - s0 * st
        sin = s0 * ct + c0 * st
        for k in range(heads):
            x = pages_ref[i, 0, k].astype(F32)
            out_ref[i, 0, k] = (x * cos + pltpu.roll(x, head_dim // 2, 1) * sin).astype(BF16)
            out_ref[i, 1, k] = pages_ref[i, 1, k]


def page_place(len_ref, page_len, n):
    begin = jnp.int32(0)
    number, fill = jnp.int32(0), jnp.int32(0)
    for q in range(len_ref.shape[1]):
        length = len_ref[0, q]
        count = (length + page_len - 1) // page_len
        here = (n >= begin) & (n < begin + count)
        number = jnp.where(here, n - begin, number)
        fill = jnp.where(here, jnp.clip(length - (n - begin) * page_len, 0, page_len), fill)
        begin = begin + count
    return number, fill


def rotated_pages(prompt_kv, page_slot, prompt_lengths, tabs, npool, pair, cache_pages):
    pages, _, heads, page_len, head_dim = prompt_kv.shape
    per = pages // 2
    ct, st, cp, sp, _, _ = tabs
    whole = lambda x: pl.BlockSpec(x.shape, lambda i: (0, 0))
    return pl.pallas_call(
        functools.partial(rope_kernel, npool, cache_pages, per),
        grid=(pages // per,),
        out_shape=[
            jax.ShapeDtypeStruct(prompt_kv.shape, BF16),
            jax.ShapeDtypeStruct((3 * npool * pair,), I32),
        ],
        in_specs=[
            SMEM,
            SMEM,
            pl.BlockSpec((per,) + prompt_kv.shape[1:], lambda i: (i, 0, 0, 0, 0)),
            whole(ct),
            whole(st),
            whole(cp),
            whole(sp),
        ],
        out_specs=[pl.BlockSpec((per,) + prompt_kv.shape[1:], lambda i: (i, 0, 0, 0, 0)), SMEM],
        scratch_shapes=[pltpu.SMEM((npool,), I32)],
        compiler_params=PARAMS,
        cost_estimate=pl.CostEstimate(flops=6_000_000, bytes_accessed=2_000_000, transcendentals=0),
        name="rope_pages",
    )(*[in_hbm(x) for x in (page_slot, prompt_lengths, prompt_kv, ct, st, cp, sp)])


def asked_kernel(page_len, heads, table_ref, context_ref, q_ref, out_ref, spread):
    most, rows = table_ref.shape
    steps, _, width = q_ref.shape
    block, head_dim = out_ref.shape[1:]
    per = width // head_dim // heads
    for s in range(steps):
        for h in range(heads * per):
            k, g = divmod(h, per)
            at = pl.ds(k * steps * per + s * per + g, rows, stride=block)
            spread[at, :] = q_ref[s, :, h * head_dim : (h + 1) * head_dim].astype(F32)
    for r in range(rows):
        out_ref[r] = spread[r * block : (r + 1) * block, :].astype(BF16)
    lane = lax.broadcasted_iota(I32, (block, LANES), 1)
    line = lax.broadcasted_iota(I32, (block, LANES), 0)
    request = jnp.zeros((block, LANES), I32)
    left = jnp.zeros((block, LANES), I32)
    for r in range(rows):
        context = context_ref[r]
        for j in range(most):
            here = lane == table_ref[j, r]
            request = jnp.where(here, r, request)
            left = jnp.where(here, jnp.clip(context - j * page_len, 0, page_len), left)
    out_ref[rows] = jnp.where(line == 0, request, left).astype(F32).astype(BF16)


def asked_queries(table, context, queries, page_len, heads, head_dim):
    steps, rows, width = queries.shape
    block = steps * width // head_dim
    return pl.pallas_call(
        functools.partial(asked_kernel, page_len, heads),
        out_shape=jax.ShapeDtypeStruct((rows + 1, block, head_dim), BF16),
        in_specs=[SMEM, SMEM, VMEM],
        out_specs=VMEM,
        scratch_shapes=[pltpu.VMEM((rows * block, head_dim), F32)],
        compiler_params=PARAMS,
        cost_estimate=pl.CostEstimate(flops=100_000, bytes_accessed=300_000, transcendentals=0),
        name="asked_queries",
    )(in_hbm(table), in_hbm(context), in_hbm(queries))


def read_scalar(x, pick):
    return jnp.max(jnp.where(pick, x, -2.0)).astype(I32)


def transposed_scores(queries, keys, group):
    turned = jnp.transpose(queries.astype(F32), (1, 0)).astype(BF16)
    chain = lax.broadcasted_iota(I32, (1, turned.shape[1]), 1) // group
    spread = [turned * jnp.where(chain == c, 1.0, 0.0).astype(BF16) for c in range(len(keys))]
    scores = jnp.dot(
        jnp.concatenate(keys, axis=1), jnp.concatenate(spread, axis=0), preferred_element_type=F32
    )
    return scores * (queries.shape[1] ** -0.5)


def weighted_values(weights, values):
    heads, head_dim = len(values), values[0].shape[1]
    group = weights.shape[0] // heads
    out = jnp.dot(weights, jnp.concatenate(values, axis=1), preferred_element_type=F32)
    parts = [out[k * group : (k + 1) * group, k * head_dim : (k + 1) * head_dim] for k in range(heads)]
    return jnp.concatenate(parts, axis=0)


def lane_values(scalars, lanes_each, shape):
    chain = lax.broadcasted_iota(I32, shape, 1) // lanes_each
    out = jnp.zeros(shape, I32)
    for i, x in enumerate(scalars):
        out = jnp.where(chain == i, x, out)
    return out


def local_kernel(
    page_len,
    heads,
    table_ref,
    context_ref,
    fill_ref,
    q_ref,
    new_ref,
    freq_ref,
    sign_ref,
    cache_ref,
    o_ref,
    stat_ref,
    kv,
    sems,
    kf,
    vf,
    position,
):
    rows, block, head_dim = q_ref.shape
    rows = rows - 1
    steps = new_ref.shape[0]
    most = table_ref.shape[0]
    group = block // heads
    per = group // steps
    together = LANES // block

    def copy(r, j):
        n = r * most + j
        return pltpu.make_async_copy(cache_ref.at[table_ref[j, r]], kv.at[n], sems.at[n])

    for r in range(rows):
        for j in range(most):
            copy(r, j).start()
    kf[...] = jnp.zeros_like(kf)
    vf[...] = jnp.zeros_like(vf)
    for r in range(rows):
        position[r : r + 1, :] = jnp.full((1, head_dim), context_ref[r], I32)
    for u in range(steps):
        angle = (position[...] + u).astype(F32) * freq_ref[...]
        cos, sin = jnp.cos(angle), jnp.sin(angle) * sign_ref[...]
        for k in range(heads):
            x = new_ref[u, :, k * head_dim : (k + 1) * head_dim].astype(F32)
            at = k * group + u
            kf[pl.ds(at, rows, stride=block), :] = x * cos + pltpu.roll(x, head_dim // 2, 1) * sin
            x = new_ref[u, :, (heads + k) * head_dim : (heads + k + 1) * head_dim].astype(F32)
            vf[pl.ds(at, rows, stride=block), :] = x
    token = lax.broadcasted_iota(I32, (page_len, LANES), 0)
    fresh = lax.broadcasted_iota(I32, (group, LANES), 0)
    step = lax.broadcasted_iota(I32, (group, LANES), 1) % group // per
    fresh_mask = (fresh <= step) & (fresh < steps)

    for i in range(rows // together):
        requests = range(i * together, (i + 1) * together)
        chains = [(r, k) for r in requests for k in range(heads)]
        if i % 2 == 0:
            for r in range(i * together, min(rows, (i + 2) * together)):
                for j in range(most):
                    copy(r, j).wait()
        queries = q_ref[i * together : (i + 1) * together].reshape(LANES, head_dim)
        keys, values = [], []
        for r, k in chains:
            at = r * block + k * group
            page = lambda what: [kv[r * most + j, what, k] for j in range(most)]
            keys.append(jnp.concatenate(page(0) + [kf[at : at + group, :].astype(BF16)], axis=0))
            values.append(page(1) + [vf[at : at + group, :].astype(BF16)])
        scores = transposed_scores(queries, keys, group)
        mask = []
        for j in range(most):
            seen = [jnp.minimum(fill_ref[table_ref[j, r]], context_ref[r] - j * page_len) for r in requests]
            mask.append(token < lane_values(seen, block, (1, LANES)))
        parts = [
            jnp.where(m, scores[n * page_len : n * page_len + m.shape[0]], -jnp.inf)
            for n, m in enumerate(mask + [fresh_mask])
        ]
        top = functools.reduce(jnp.maximum, [jnp.max(x, axis=0, keepdims=True) for x in parts])
        parts = [jnp.exp(x - top) for x in parts]
        total = functools.reduce(jnp.add, [jnp.sum(x, axis=0, keepdims=True) for x in parts])
        stats = jnp.concatenate(
            [parts[most], jnp.broadcast_to(top, (8, LANES)), jnp.broadcast_to(total, (8, LANES))]
            + [jnp.zeros((LANES - group - 16, LANES), F32)],
            axis=0,
        )
        stats = jnp.transpose(stats, (1, 0))
        weights = [jnp.transpose(x, (1, 0)).astype(BF16) for x in parts[:most]]
        weights.append(stats[:, :group].astype(BF16))
        weights = jnp.concatenate(weights, axis=1)
        for x in range(together):
            both = [jnp.concatenate(values[x * heads + k], axis=0) for k in range(heads)]
            both = weighted_values(weights[x * block : (x + 1) * block, :], both)
            o_ref[i * LANES + x * block : i * LANES + (x + 1) * block, :] = both
        stat_ref[i * LANES : (i + 1) * LANES, :] = stats


def local_attention(table, context, fills, queries, new_kv, cache_kv, tabs):
    rows, block, _ = queries.shape
    rows = rows - 1
    steps = new_kv.shape[0]
    slots, _, heads, page_len, head_dim = cache_kv.shape
    flat = (rows * block, head_dim)
    freq, sign = tabs[4:]
    return pl.pallas_call(
        functools.partial(local_kernel, page_len, heads),
        out_shape=[jax.ShapeDtypeStruct(flat, F32)] * 2,
        in_specs=[SMEM] * 3 + [VMEM] * 4 + [ANY],
        out_specs=[VMEM] * 2,
        scratch_shapes=[
            pltpu.VMEM((table.size, 2, heads, page_len, head_dim), BF16),
            pltpu.SemaphoreType.DMA((table.size,)),
            pltpu.VMEM(flat, F32),
            pltpu.VMEM(flat, F32),
            pltpu.VMEM((rows, head_dim), I32),
        ],
        compiler_params=PARAMS,
        cost_estimate=pl.CostEstimate(flops=800_000_000, bytes_accessed=12_000_000, transcendentals=400_000),
        name="local_attention",
    )(
        *[in_hbm(x) for x in (table, context, fills)],
        queries,
        new_kv.reshape(steps, rows, 2 * heads * head_dim),
        *[in_hbm(x) for x in (freq, sign, cache_kv)],
    )


def pieces(x):
    high = x.astype(BF16).astype(F32)
    middle = (x - high).astype(BF16).astype(F32)
    return [high, middle, x - high - middle]


def arrived_kernel(npool, pair, me_ref, own_ref, *refs):
    blocks = refs[:npool]
    pages_ref, out_ref, queries = refs[npool:]
    items = npool * pair
    _, _, heads, page_len, head_dim = pages_ref.shape
    rows, block = blocks[0].shape[0] - 1, blocks[0].shape[1]
    group = block // heads
    together = LANES // block
    me = me_ref[0]
    owners = [owner_of(me, npool, apart, flip) for apart, flip in block_order(npool)]
    lane = lax.broadcasted_iota(I32, (1, LANES), 1)
    codes = [x[rows, :STAT_ROWS, :].astype(F32) for x in blocks]
    codes = [x[0:1] * CODE + x[1:2] for x in codes]
    number, seen, request = [], [], []
    for x in range(items):
        at = owners[x // pair] * pair + x % pair
        slot = own_ref[2 * items + at]
        code = jnp.maximum(read_scalar(codes[x // pair], lane == slot), 0)
        reader, left = code // CODE, code % CODE
        queries[x * block : (x + 1) * block, :] = blocks[x // pair][reader]
        number.append(own_ref[at])
        seen.append(jnp.minimum(left, own_ref[items + at]))
        request.append(jnp.where(slot >= 0, reader, -1))
    token = lax.broadcasted_iota(I32, (page_len, LANES), 0)
    for i in range(items // together):
        own = range(i * together, (i + 1) * together)
        keys = [pages_ref[number[x], 0, k] for x in own for k in range(heads)]
        scores = transposed_scores(queries[i * LANES : (i + 1) * LANES, :], keys, group)
        limit = lane_values([seen[x] for x in own], block, (1, LANES))
        scores = jnp.where(token < limit, scores, -jnp.inf)
        top = jnp.max(scores, axis=0, keepdims=True)
        top = jnp.where(top > -jnp.inf, top, 0.0)
        weights = jnp.exp(scores - top)
        stats = pieces(top) + pieces(jnp.sum(weights, axis=0, keepdims=True))
        stats.append(lane_values([request[x] for x in own], block, (1, LANES)).astype(F32))
        stats = jnp.concatenate(stats + [jnp.zeros((STAT_ROWS - len(stats), LANES), F32)], axis=0).astype(BF16)
        weights = jnp.transpose(weights, (1, 0)).astype(BF16)
        for c, x in enumerate(own):
            both = [pages_ref[number[x], 1, k] for k in range(heads)]
            both = weighted_values(weights[c * block : (c + 1) * block, :], both)
            at = (x % pair) * block
            out_ref[owners[x // pair], at : at + block, :] = both.astype(BF16)
        for place in sorted({x // pair for x in own}):
            out_ref[owners[place], pair * block : pair * block + STAT_ROWS, :] = stats


def arrived_attention(me, own, blocks, arrived):
    npool = len(blocks)
    head_dim = arrived.shape[4]
    block = blocks[0].shape[1]
    items = own.shape[0] // 3
    pair = items // npool
    return pl.pallas_call(
        functools.partial(arrived_kernel, npool, pair),
        out_shape=jax.ShapeDtypeStruct((npool, pair * block + STAT_ROWS, head_dim), BF16),
        in_specs=[SMEM] * 2 + [VMEM] * (npool + 1),
        out_specs=VMEM,
        scratch_shapes=[pltpu.VMEM((items * block, head_dim), BF16)],
        compiler_params=PARAMS,
        cost_estimate=pl.CostEstimate(flops=200_000_000, bytes_accessed=4_000_000, transcendentals=70_000),
        name="arrived_attention",
    )(me, own, *blocks, arrived)


def merge_kernel(pair, heads, me_ref, parts_ref, o_ref, stat_ref, out_ref, mixed, top, total, turned):
    npool = parts_ref.shape[0]
    steps, rows, width = out_ref.shape
    head_dim = o_ref.shape[1]
    per = width // head_dim // heads
    group = steps * per
    block = heads * group
    me = me_ref[0]
    shape = top.shape
    mixed[...] = o_ref[...]
    top[...] = jnp.broadcast_to(stat_ref[:, group : group + 1], shape)
    total[...] = jnp.broadcast_to(stat_ref[:, group + 8 : group + 9], shape)
    tops, totals, readers = [], [], []
    chain = lax.broadcasted_iota(I32, (1, LANES), 1) // block
    for d in range(npool):
        x = parts_ref[d, pair * block : pair * block + STAT_ROWS, :].astype(F32)
        tops.append(x[0:1] + x[1:2] + x[2:3])
        totals.append(x[3:4] + x[4:5] + x[5:6])
        readers.append(x[6:7])
    empty = [jnp.zeros((LANES // 2 - npool, LANES), F32)]
    turned[...] = jnp.transpose(jnp.concatenate(tops + empty + totals + empty, axis=0), (1, 0))
    for d in range(npool):
        for p in range(pair):
            part = lax.rem(place_of(me, npool, d) * pair + p, LANES // block)
            r = read_scalar(readers[d], chain == part)
            there = r >= 0
            at = pl.ds(pl.multiple_of(jnp.maximum(r, 0) * block, block), block)
            lane = pl.ds(pl.multiple_of(part * block, block), block)
            m = jnp.broadcast_to(turned[lane, d : d + 1], (block, head_dim))
            l = jnp.broadcast_to(turned[lane, LANES // 2 + d : LANES // 2 + d + 1], (block, head_dim))
            seen = (l > 0.0) & there
            o = parts_ref[d, p * block : (p + 1) * block, :].astype(F32)
            old = top[at, :]
            new = jnp.where(seen, jnp.maximum(old, m), old)
            a = jnp.exp(old - new)
            b = jnp.where(seen, jnp.exp(m - new), 0.0)
            top[at, :] = new
            total[at, :] = total[at, :] * a + l * b
            mixed[at, :] = mixed[at, :] * a + o * b
    for s in range(steps):
        for h in range(heads * per):
            k, g = divmod(h, per)
            at = pl.ds(k * group + s * per + g, rows, stride=block)
            out_ref[s, :, h * head_dim : (h + 1) * head_dim] = (mixed[at, :] / total[at, :]).astype(BF16)


def merged(me, parts, local, shape, heads, pair):
    flat = local[0].shape
    return pl.pallas_call(
        functools.partial(merge_kernel, pair, heads),
        out_shape=jax.ShapeDtypeStruct(shape, BF16),
        in_specs=[SMEM] + [VMEM] * 3,
        out_specs=VMEM,
        scratch_shapes=[pltpu.VMEM(flat, F32)] * 3 + [pltpu.VMEM((LANES, LANES), F32)],
        compiler_params=PARAMS,
        cost_estimate=pl.CostEstimate(flops=2_000_000, bytes_accessed=1_500_000, transcendentals=100_000),
        name="merge",
    )(me, parts, *local)


def fetch_kernel(weight_ref, after_ref, out_ref, sem):
    del after_ref
    copy = pltpu.make_async_copy(weight_ref, out_ref, sem)
    copy.start()
    copy.wait()


def fetched(weight, after):
    return pl.pallas_call(
        fetch_kernel,
        out_shape=pltpu.VMEM(weight.shape, weight.dtype),
        in_specs=[ANY, ANY],
        out_specs=ANY,
        scratch_shapes=[pltpu.SemaphoreType.DMA],
        compiler_params=PARAMS,
        cost_estimate=pl.CostEstimate(flops=0, bytes_accessed=2 * weight.size * 2, transcendentals=0),
        name="fetch_weight",
    )(in_hbm(weight), after)


def project_kernel(npool, place_ref, *refs):
    blocks = refs[:npool]
    weight_ref, mine_ref, other_ref, lhs, sems = refs[npool:]
    steps, rows, _ = blocks[0].shape
    half = weight_ref.shape[1] // 2
    tile = min(half, 256)
    every = npool * rows
    me, core = place_ref[0], place_ref[1]
    copies = []
    for x, (apart, flip) in enumerate(block_order(npool)):
        owner = owner_of(me, npool, apart, flip)
        for s in range(steps):
            at = pl.ds(pl.multiple_of(s * every + owner * rows, rows), rows)
            copies.append(pltpu.make_async_copy(blocks[x].at[s], lhs.at[at], sems.at[x * steps + s]))
            copies[-1].start()
    for x in copies:
        x.wait()
    for out_ref, first in ((mine_ref, core * half), (other_ref, (1 - core) * half)):
        for i in range(half // tile):
            at = pl.ds(pl.multiple_of(first + i * tile, LANES), tile)
            terms = jnp.dot(lhs[...], weight_ref[:, at], preferred_element_type=F32)
            for s in range(steps):
                out_ref[s, :, i * tile : (i + 1) * tile] = terms[s * every : (s + 1) * every]


def projection(place, blocks, weight):
    npool = len(blocks)
    steps, rows, width = blocks[0].shape
    columns = weight.shape[1]
    every = steps * npool * rows
    return pl.pallas_call(
        functools.partial(project_kernel, npool),
        out_shape=[jax.ShapeDtypeStruct((steps, npool * rows, columns // 2), F32)] * 2,
        in_specs=[SMEM] + [ANY] * npool + [VMEM],
        out_specs=[VMEM] * 2,
        scratch_shapes=[pltpu.VMEM((every, width), BF16), pltpu.SemaphoreType.DMA((npool * steps,))],
        compiler_params=PARAMS,
        cost_estimate=pl.CostEstimate(
            flops=2 * every * width * columns, bytes_accessed=6_000_000, transcendentals=0
        ),
        name="project",
    )(place, *blocks, weight)


def block_order(npool):
    return [(apart, flip) for flip in (0, 1) for apart in range(npool // 2)]


def owner_of(me, npool, apart, flip):
    half = npool // 2
    pair, side = me // 2, me % 2
    side = 1 - side if flip else side
    return lax.rem(pair + half - apart, half) * 2 + side


def place_of(me, npool, holder):
    half = npool // 2
    apart = lax.rem(holder // 2 - me // 2 + half, half)
    flip = lax.rem(me + holder, 2)
    return flip * half + apart


def in_hbm(x):
    return pltpu.with_memory_space_constraint(x, pltpu.HBM)


def gathered(x, npool):
    ahead = lambda x, by: lax.ppermute(x, "pool", [(i, (i + 2 * by) % npool) for i in range(npool)])
    across = lambda x: lax.ppermute(x, "pool", [(i, i ^ 1) for i in range(npool)])
    straight = [x] + [ahead(x, by) for by in range(1, npool // 2)]
    return straight + [across(y) for y in straight]


def swap_halves(x):
    return lax.ppermute(x, "tp", [(0, 1), (1, 0)])


def shards(
    prompt_kv,
    prompt_lengths,
    page_slot,
    cache_kv,
    cache_fill,
    page_table,
    context_lengths,
    queries,
    new_kv,
    out_weight,
):
    npool = lax.axis_size("pool")
    me = lax.axis_index("pool").astype(I32)
    pages, _, heads, page_len, head_dim = prompt_kv.shape
    cache_pages = cache_kv.shape[0]
    pair = (pages + npool - 1) // npool
    tabs = tables(page_len, head_dim, pages)
    place = jnp.stack([me, lax.axis_index("tp").astype(I32)])
    table = page_table.T

    asked = asked_queries(table, context_lengths, queries, page_len, heads, head_dim)
    asked_all = gathered(asked, npool)
    arrived, own = rotated_pages(prompt_kv, page_slot, prompt_lengths, tabs, npool, pair, cache_pages)
    local = local_attention(table, context_lengths, cache_fill, asked, new_kv, cache_kv, tabs)
    parts = arrived_attention(place, own, asked_all, arrived)
    parts = lax.all_to_all(parts, "pool", split_axis=0, concat_axis=0, tiled=True)
    attention = merged(place, parts, local, queries.shape, heads, pair)
    blocks = gathered(attention, npool)
    weight = fetched(out_weight, attention)
    terms, other_terms = projection(place, blocks, weight)
    other_terms = swap_halves(other_terms)
    return (terms + other_terms).astype(BF16)


def solution(mesh):
    return jax.shard_map(
        shards,
        mesh=mesh,
        in_specs=(
            P(("group", "pool"), None, "tp", None, None),
            P(("group", "pool"), None),
            P(("group", "pool")),
            P(("group", "pool"), None, "tp", None, None),
            P(("group", "pool")),
            P(("group", "pool"), None),
            P(("group", "pool")),
            P(None, ("group", "pool"), "tp"),
            P(None, ("group", "pool"), None, "tp", None),
            P("tp", "pool"),
        ),
        out_specs=P(None, "group", ("pool", "tp")),
        check_vma=False,
    )
```

```python
import functools

import jax
import jax.numpy as jnp
import numpy as np
from jax import lax
from jax.experimental import pallas as pl
from jax.experimental.pallas import tpu as pltpu
from jax.sharding import PartitionSpec as P

ROPE_BASE = 500000.0
BF16, F32, I32 = jnp.bfloat16, jnp.float32, jnp.int32
SMEM = pl.BlockSpec(memory_space=pltpu.SMEM)
VMEM = pl.BlockSpec(memory_space=pltpu.VMEM)
ANY = pl.BlockSpec(memory_space=pl.ANY)
PARAMS = pltpu.CompilerParams(vmem_limit_bytes=24 * 2**20)
LANES = 128
STAT_ROWS = 16
CODE = 256


def tables(page_len, head_dim, pages):
    half = head_dim // 2
    freq = ROPE_BASE ** (-(np.arange(half) * 2.0) / head_dim)
    freq = np.concatenate([freq, freq])[None, :]
    sign = np.concatenate([-np.ones(half), np.ones(half)])[None, :]
    token = np.arange(page_len)[:, None] * freq
    first = np.arange(pages)[:, None] * page_len * freq
    out = (np.cos(token), sign * np.sin(token), np.cos(first), sign * np.sin(first), freq, sign)
    return [jnp.asarray(x, F32) for x in out]


def rope_kernel(
    npool, cache_pages, per, slot_ref, len_ref, pages_ref, ct_ref, st_ref, cp_ref, sp_ref, out_ref, own_ref, count
):
    _, _, heads, page_len, head_dim = pages_ref.shape

    @pl.when(pl.program_id(0) == 0)
    def _():
        items = own_ref.shape[0] // 3
        for e in range(npool):
            count[e] = 0
        for i in range(items):
            own_ref[i] = 0
            own_ref[items + i] = 0
            own_ref[2 * items + i] = -1
        for n in range(slot_ref.shape[0]):
            slot = slot_ref[n]
            target = slot // cache_pages
            at = target * (items // npool) + count[target]
            count[target] = count[target] + 1
            own_ref[at] = n
            own_ref[items + at] = page_place(len_ref, page_len, n)[1]
            own_ref[2 * items + at] = slot - target * cache_pages

    for i in range(per):
        number, _ = page_place(len_ref, page_len, pl.program_id(0) * per + i)
        c0, s0 = cp_ref[pl.ds(number, 1), :], sp_ref[pl.ds(number, 1), :]
        ct, st = ct_ref[...], st_ref[...]
        cos = c0 * ct - s0 * st
        sin = s0 * ct + c0 * st
        for k in range(heads):
            x = pages_ref[i, 0, k].astype(F32)
            out_ref[i, 0, k] = (x * cos + pltpu.roll(x, head_dim // 2, 1) * sin).astype(BF16)
            out_ref[i, 1, k] = pages_ref[i, 1, k]


def page_place(len_ref, page_len, n):
    begin = jnp.int32(0)
    number, fill = jnp.int32(0), jnp.int32(0)
    for q in range(len_ref.shape[1]):
        length = len_ref[0, q]
        count = (length + page_len - 1) // page_len
        here = (n >= begin) & (n < begin + count)
        number = jnp.where(here, n - begin, number)
        fill = jnp.where(here, jnp.clip(length - (n - begin) * page_len, 0, page_len), fill)
        begin = begin + count
    return number, fill


def rotated_pages(prompt_kv, page_slot, prompt_lengths, tabs, npool, pair, cache_pages):
    pages, _, heads, page_len, head_dim = prompt_kv.shape
    per = pages // 2
    ct, st, cp, sp, _, _ = tabs
    whole = lambda x: pl.BlockSpec(x.shape, lambda i: (0, 0))
    return pl.pallas_call(
        functools.partial(rope_kernel, npool, cache_pages, per),
        grid=(pages // per,),
        out_shape=[
            jax.ShapeDtypeStruct(prompt_kv.shape, BF16),
            jax.ShapeDtypeStruct((3 * npool * pair,), I32),
        ],
        in_specs=[
            SMEM,
            SMEM,
            pl.BlockSpec((per,) + prompt_kv.shape[1:], lambda i: (i, 0, 0, 0, 0)),
            whole(ct),
            whole(st),
            whole(cp),
            whole(sp),
        ],
        out_specs=[pl.BlockSpec((per,) + prompt_kv.shape[1:], lambda i: (i, 0, 0, 0, 0)), SMEM],
        scratch_shapes=[pltpu.SMEM((npool,), I32)],
        compiler_params=PARAMS,
        cost_estimate=pl.CostEstimate(flops=6_000_000, bytes_accessed=2_000_000, transcendentals=0),
        name="rope_pages",
    )(*[in_hbm(x) for x in (page_slot, prompt_lengths, prompt_kv, ct, st, cp, sp)])


def asked_kernel(page_len, heads, table_ref, context_ref, q_ref, out_ref, spread):
    most, rows = table_ref.shape
    steps, _, width = q_ref.shape
    block, head_dim = out_ref.shape[1:]
    per = width // head_dim // heads
    for s in range(steps):
        for h in range(heads * per):
            k, g = divmod(h, per)
            at = pl.ds(k * steps * per + s * per + g, rows, stride=block)
            spread[at, :] = q_ref[s, :, h * head_dim : (h + 1) * head_dim].astype(F32)
    for r in range(rows):
        out_ref[r] = spread[r * block : (r + 1) * block, :].astype(BF16)
    lane = lax.broadcasted_iota(I32, (block, LANES), 1)
    line = lax.broadcasted_iota(I32, (block, LANES), 0)
    request = jnp.zeros((block, LANES), I32)
    left = jnp.zeros((block, LANES), I32)
    for r in range(rows):
        context = context_ref[r]
        for j in range(most):
            here = lane == table_ref[j, r]
            request = jnp.where(here, r, request)
            left = jnp.where(here, jnp.clip(context - j * page_len, 0, page_len), left)
    out_ref[rows] = jnp.where(line == 0, request, left).astype(F32).astype(BF16)


def asked_queries(table, context, queries, page_len, heads, head_dim):
    steps, rows, width = queries.shape
    block = steps * width // head_dim
    return pl.pallas_call(
        functools.partial(asked_kernel, page_len, heads),
        out_shape=jax.ShapeDtypeStruct((rows + 1, block, head_dim), BF16),
        in_specs=[SMEM, SMEM, VMEM],
        out_specs=VMEM,
        scratch_shapes=[pltpu.VMEM((rows * block, head_dim), F32)],
        compiler_params=PARAMS,
        cost_estimate=pl.CostEstimate(flops=100_000, bytes_accessed=300_000, transcendentals=0),
        name="asked_queries",
    )(in_hbm(table), in_hbm(context), in_hbm(queries))


def read_scalar(x, pick):
    return jnp.max(jnp.where(pick, x, -2.0)).astype(I32)


def transposed_scores(queries, keys, group):
    turned = jnp.transpose(queries.astype(F32), (1, 0)).astype(BF16)
    chain = lax.broadcasted_iota(I32, (1, turned.shape[1]), 1) // group
    spread = [turned * jnp.where(chain == c, 1.0, 0.0).astype(BF16) for c in range(len(keys))]
    scores = jnp.dot(
        jnp.concatenate(keys, axis=1), jnp.concatenate(spread, axis=0), preferred_element_type=F32
    )
    return scores * (queries.shape[1] ** -0.5)


def weighted_values(weights, values):
    heads, head_dim = len(values), values[0].shape[1]
    group = weights.shape[0] // heads
    out = jnp.dot(weights, jnp.concatenate(values, axis=1), preferred_element_type=F32)
    parts = [out[k * group : (k + 1) * group, k * head_dim : (k + 1) * head_dim] for k in range(heads)]
    return jnp.concatenate(parts, axis=0)


def lane_values(scalars, lanes_each, shape):
    chain = lax.broadcasted_iota(I32, shape, 1) // lanes_each
    out = jnp.zeros(shape, I32)
    for i, x in enumerate(scalars):
        out = jnp.where(chain == i, x, out)
    return out


def local_kernel(
    page_len,
    heads,
    table_ref,
    context_ref,
    fill_ref,
    q_ref,
    new_ref,
    freq_ref,
    sign_ref,
    cache_ref,
    o_ref,
    stat_ref,
    kv,
    sems,
    kf,
    vf,
    position,
):
    rows, block, head_dim = q_ref.shape
    rows = rows - 1
    steps = new_ref.shape[0]
    most = table_ref.shape[0]
    group = block // heads
    per = group // steps
    together = LANES // block

    def copy(r, j):
        n = r * most + j
        return pltpu.make_async_copy(cache_ref.at[table_ref[j, r]], kv.at[n], sems.at[n])

    for r in range(rows):
        for j in range(most):
            copy(r, j).start()
    kf[...] = jnp.zeros_like(kf)
    vf[...] = jnp.zeros_like(vf)
    for r in range(rows):
        position[r : r + 1, :] = jnp.full((1, head_dim), context_ref[r], I32)
    for u in range(steps):
        angle = (position[...] + u).astype(F32) * freq_ref[...]
        cos, sin = jnp.cos(angle), jnp.sin(angle) * sign_ref[...]
        for k in range(heads):
            x = new_ref[u, :, k * head_dim : (k + 1) * head_dim].astype(F32)
            at = k * group + u
            kf[pl.ds(at, rows, stride=block), :] = x * cos + pltpu.roll(x, head_dim // 2, 1) * sin
            x = new_ref[u, :, (heads + k) * head_dim : (heads + k + 1) * head_dim].astype(F32)
            vf[pl.ds(at, rows, stride=block), :] = x
    token = lax.broadcasted_iota(I32, (page_len, LANES), 0)
    fresh = lax.broadcasted_iota(I32, (group, LANES), 0)
    step = lax.broadcasted_iota(I32, (group, LANES), 1) % group // per
    fresh_mask = (fresh <= step) & (fresh < steps)

    for i in range(rows // together):
        requests = range(i * together, (i + 1) * together)
        chains = [(r, k) for r in requests for k in range(heads)]
        if i % 2 == 0:
            for r in range(i * together, min(rows, (i + 2) * together)):
                for j in range(most):
                    copy(r, j).wait()
        queries = q_ref[i * together : (i + 1) * together].reshape(LANES, head_dim)
        keys, values = [], []
        for r, k in chains:
            at = r * block + k * group
            page = lambda what: [kv[r * most + j, what, k] for j in range(most)]
            keys.append(jnp.concatenate(page(0) + [kf[at : at + group, :].astype(BF16)], axis=0))
            values.append(page(1) + [vf[at : at + group, :].astype(BF16)])
        scores = transposed_scores(queries, keys, group)
        mask = []
        for j in range(most):
            seen = [jnp.minimum(fill_ref[table_ref[j, r]], context_ref[r] - j * page_len) for r in requests]
            mask.append(token < lane_values(seen, block, (1, LANES)))
        parts = [
            jnp.where(m, scores[n * page_len : n * page_len + m.shape[0]], -jnp.inf)
            for n, m in enumerate(mask + [fresh_mask])
        ]
        top = functools.reduce(jnp.maximum, [jnp.max(x, axis=0, keepdims=True) for x in parts])
        parts = [jnp.exp(x - top) for x in parts]
        total = functools.reduce(jnp.add, [jnp.sum(x, axis=0, keepdims=True) for x in parts])
        stats = jnp.concatenate(
            [parts[most], jnp.broadcast_to(top, (8, LANES)), jnp.broadcast_to(total, (8, LANES))]
            + [jnp.zeros((LANES - group - 16, LANES), F32)],
            axis=0,
        )
        stats = jnp.transpose(stats, (1, 0))
        weights = [jnp.transpose(x, (1, 0)).astype(BF16) for x in parts[:most]]
        weights.append(stats[:, :group].astype(BF16))
        weights = jnp.concatenate(weights, axis=1)
        for x in range(together):
            both = [jnp.concatenate(values[x * heads + k], axis=0) for k in range(heads)]
            both = weighted_values(weights[x * block : (x + 1) * block, :], both)
            o_ref[i * LANES + x * block : i * LANES + (x + 1) * block, :] = both
        stat_ref[i * LANES : (i + 1) * LANES, :] = stats


def local_attention(table, context, fills, queries, new_kv, cache_kv, tabs):
    rows, block, _ = queries.shape
    rows = rows - 1
    steps = new_kv.shape[0]
    slots, _, heads, page_len, head_dim = cache_kv.shape
    flat = (rows * block, head_dim)
    freq, sign = tabs[4:]
    return pl.pallas_call(
        functools.partial(local_kernel, page_len, heads),
        out_shape=[jax.ShapeDtypeStruct(flat, F32)] * 2,
        in_specs=[SMEM] * 3 + [VMEM] * 4 + [ANY],
        out_specs=[VMEM] * 2,
        scratch_shapes=[
            pltpu.VMEM((table.size, 2, heads, page_len, head_dim), BF16),
            pltpu.SemaphoreType.DMA((table.size,)),
            pltpu.VMEM(flat, F32),
            pltpu.VMEM(flat, F32),
            pltpu.VMEM((rows, head_dim), I32),
        ],
        compiler_params=PARAMS,
        cost_estimate=pl.CostEstimate(flops=800_000_000, bytes_accessed=12_000_000, transcendentals=400_000),
        name="local_attention",
    )(
        *[in_hbm(x) for x in (table, context, fills)],
        queries,
        new_kv.reshape(steps, rows, 2 * heads * head_dim),
        *[in_hbm(x) for x in (freq, sign, cache_kv)],
    )


def pieces(x):
    high = x.astype(BF16).astype(F32)
    middle = (x - high).astype(BF16).astype(F32)
    return [high, middle, x - high - middle]


def arrived_kernel(npool, pair, me_ref, own_ref, *refs):
    blocks = refs[:npool]
    pages_ref, out_ref, queries = refs[npool:]
    items = npool * pair
    _, _, heads, page_len, head_dim = pages_ref.shape
    rows, block = blocks[0].shape[0] - 1, blocks[0].shape[1]
    group = block // heads
    together = LANES // block
    me = me_ref[0]
    owners = [owner_of(me, npool, apart, flip) for apart, flip in block_order(npool)]
    lane = lax.broadcasted_iota(I32, (1, LANES), 1)
    codes = [x[rows, :STAT_ROWS, :].astype(F32) for x in blocks]
    codes = [x[0:1] * CODE + x[1:2] for x in codes]
    number, seen, request = [], [], []
    for x in range(items):
        at = owners[x // pair] * pair + x % pair
        slot = own_ref[2 * items + at]
        code = jnp.maximum(read_scalar(codes[x // pair], lane == slot), 0)
        reader, left = code // CODE, code % CODE
        queries[x * block : (x + 1) * block, :] = blocks[x // pair][reader]
        number.append(own_ref[at])
        seen.append(jnp.minimum(left, own_ref[items + at]))
        request.append(jnp.where(slot >= 0, reader, -1))
    token = lax.broadcasted_iota(I32, (page_len, LANES), 0)
    for i in range(items // together):
        own = range(i * together, (i + 1) * together)
        keys = [pages_ref[number[x], 0, k] for x in own for k in range(heads)]
        scores = transposed_scores(queries[i * LANES : (i + 1) * LANES, :], keys, group)
        limit = lane_values([seen[x] for x in own], block, (1, LANES))
        scores = jnp.where(token < limit, scores, -jnp.inf)
        top = jnp.max(scores, axis=0, keepdims=True)
        top = jnp.where(top > -jnp.inf, top, 0.0)
        weights = jnp.exp(scores - top)
        stats = pieces(top) + pieces(jnp.sum(weights, axis=0, keepdims=True))
        stats.append(lane_values([request[x] for x in own], block, (1, LANES)).astype(F32))
        stats = jnp.concatenate(stats + [jnp.zeros((STAT_ROWS - len(stats), LANES), F32)], axis=0).astype(BF16)
        weights = jnp.transpose(weights, (1, 0)).astype(BF16)
        for c, x in enumerate(own):
            both = [pages_ref[number[x], 1, k] for k in range(heads)]
            both = weighted_values(weights[c * block : (c + 1) * block, :], both)
            at = (x % pair) * block
            out_ref[owners[x // pair], at : at + block, :] = both.astype(BF16)
        for place in sorted({x // pair for x in own}):
            out_ref[owners[place], pair * block : pair * block + STAT_ROWS, :] = stats


def arrived_attention(me, own, blocks, arrived):
    npool = len(blocks)
    head_dim = arrived.shape[4]
    block = blocks[0].shape[1]
    items = own.shape[0] // 3
    pair = items // npool
    return pl.pallas_call(
        functools.partial(arrived_kernel, npool, pair),
        out_shape=jax.ShapeDtypeStruct((npool, pair * block + STAT_ROWS, head_dim), BF16),
        in_specs=[SMEM] * 2 + [VMEM] * (npool + 1),
        out_specs=VMEM,
        scratch_shapes=[pltpu.VMEM((items * block, head_dim), BF16)],
        compiler_params=PARAMS,
        cost_estimate=pl.CostEstimate(flops=200_000_000, bytes_accessed=4_000_000, transcendentals=70_000),
        name="arrived_attention",
    )(me, own, *blocks, arrived)


def merge_kernel(pair, heads, me_ref, parts_ref, o_ref, stat_ref, out_ref, mixed, top, total, turned):
    npool = parts_ref.shape[0]
    steps, rows, width = out_ref.shape
    head_dim = o_ref.shape[1]
    per = width // head_dim // heads
    group = steps * per
    block = heads * group
    me = me_ref[0]
    shape = top.shape
    mixed[...] = o_ref[...]
    top[...] = jnp.broadcast_to(stat_ref[:, group : group + 1], shape)
    total[...] = jnp.broadcast_to(stat_ref[:, group + 8 : group + 9], shape)
    tops, totals, readers = [], [], []
    chain = lax.broadcasted_iota(I32, (1, LANES), 1) // block
    for d in range(npool):
        x = parts_ref[d, pair * block : pair * block + STAT_ROWS, :].astype(F32)
        tops.append(x[0:1] + x[1:2] + x[2:3])
        totals.append(x[3:4] + x[4:5] + x[5:6])
        readers.append(x[6:7])
    empty = [jnp.zeros((LANES // 2 - npool, LANES), F32)]
    turned[...] = jnp.transpose(jnp.concatenate(tops + empty + totals + empty, axis=0), (1, 0))
    for d in range(npool):
        for p in range(pair):
            part = lax.rem(place_of(me, npool, d) * pair + p, LANES // block)
            r = read_scalar(readers[d], chain == part)
            there = r >= 0
            at = pl.ds(pl.multiple_of(jnp.maximum(r, 0) * block, block), block)
            lane = pl.ds(pl.multiple_of(part * block, block), block)
            m = jnp.broadcast_to(turned[lane, d : d + 1], (block, head_dim))
            l = jnp.broadcast_to(turned[lane, LANES // 2 + d : LANES // 2 + d + 1], (block, head_dim))
            seen = (l > 0.0) & there
            o = parts_ref[d, p * block : (p + 1) * block, :].astype(F32)
            old = top[at, :]
            new = jnp.where(seen, jnp.maximum(old, m), old)
            a = jnp.exp(old - new)
            b = jnp.where(seen, jnp.exp(m - new), 0.0)
            top[at, :] = new
            total[at, :] = total[at, :] * a + l * b
            mixed[at, :] = mixed[at, :] * a + o * b
    for s in range(steps):
        for h in range(heads * per):
            k, g = divmod(h, per)
            at = pl.ds(k * group + s * per + g, rows, stride=block)
            out_ref[s, :, h * head_dim : (h + 1) * head_dim] = (mixed[at, :] / total[at, :]).astype(BF16)


def merged(me, parts, local, shape, heads, pair):
    flat = local[0].shape
    return pl.pallas_call(
        functools.partial(merge_kernel, pair, heads),
        out_shape=jax.ShapeDtypeStruct(shape, BF16),
        in_specs=[SMEM] + [VMEM] * 3,
        out_specs=VMEM,
        scratch_shapes=[pltpu.VMEM(flat, F32)] * 3 + [pltpu.VMEM((LANES, LANES), F32)],
        compiler_params=PARAMS,
        cost_estimate=pl.CostEstimate(flops=2_000_000, bytes_accessed=1_500_000, transcendentals=100_000),
        name="merge",
    )(me, parts, *local)


def fetch_kernel(weight_ref, x_ref, weight_out, x_out, sems):
    copies = [
        pltpu.make_async_copy(weight_ref, weight_out, sems.at[0]),
        pltpu.make_async_copy(x_ref, x_out, sems.at[1]),
    ]
    for copy in copies:
        copy.start()
    for copy in copies:
        copy.wait()


def fetched(weight, x):
    return pl.pallas_call(
        fetch_kernel,
        out_shape=[pltpu.VMEM(weight.shape, weight.dtype), pltpu.VMEM(x.shape, x.dtype)],
        in_specs=[ANY, ANY],
        out_specs=[ANY, ANY],
        scratch_shapes=[pltpu.SemaphoreType.DMA((2,))],
        compiler_params=PARAMS,
        cost_estimate=pl.CostEstimate(flops=0, bytes_accessed=2 * weight.size * 2, transcendentals=0),
        name="fetch_weight",
    )(in_hbm(weight), x)


def project_kernel(npool, place_ref, *refs):
    blocks = refs[:npool]
    weight_ref, mine_ref, other_ref, lhs = refs[npool:]
    steps, rows, _ = blocks[0].shape
    half = weight_ref.shape[1] // 2
    tile = min(half, 256)
    every = npool * rows
    me, core = place_ref[0], place_ref[1]
    for x, (apart, flip) in enumerate(block_order(npool)):
        owner = owner_of(me, npool, apart, flip)
        for s in range(steps):
            lhs[pl.ds(pl.multiple_of(s * every + owner * rows, rows), rows), :] = blocks[x][s]
    for out_ref, first in ((mine_ref, core * half), (other_ref, (1 - core) * half)):
        for i in range(half // tile):
            at = pl.ds(pl.multiple_of(first + i * tile, LANES), tile)
            terms = jnp.dot(lhs[...], weight_ref[:, at], preferred_element_type=F32)
            for s in range(steps):
                out_ref[s, :, i * tile : (i + 1) * tile] = terms[s * every : (s + 1) * every]


def projection(place, blocks, weight):
    npool = len(blocks)
    steps, rows, width = blocks[0].shape
    columns = weight.shape[1]
    every = steps * npool * rows
    return pl.pallas_call(
        functools.partial(project_kernel, npool),
        out_shape=[jax.ShapeDtypeStruct((steps, npool * rows, columns // 2), F32)] * 2,
        in_specs=[SMEM] + [VMEM] * (npool + 1),
        out_specs=[VMEM] * 2,
        scratch_shapes=[pltpu.VMEM((every, width), BF16)],
        compiler_params=PARAMS,
        cost_estimate=pl.CostEstimate(
            flops=2 * every * width * columns, bytes_accessed=6_000_000, transcendentals=0
        ),
        name="project",
    )(place, *blocks, weight)


def block_order(npool):
    return [(apart, flip) for flip in (0, 1) for apart in range(npool // 2)]


def owner_of(me, npool, apart, flip):
    half = npool // 2
    pair, side = me // 2, me % 2
    side = 1 - side if flip else side
    return lax.rem(pair + half - apart, half) * 2 + side


def place_of(me, npool, holder):
    half = npool // 2
    apart = lax.rem(holder // 2 - me // 2 + half, half)
    flip = lax.rem(me + holder, 2)
    return flip * half + apart


def in_hbm(x):
    return pltpu.with_memory_space_constraint(x, pltpu.HBM)


def gathered(x, npool, later=None):
    half = npool // 2
    later = x if later is None else later
    ahead = lambda x, by: lax.ppermute(x, "pool", [(i, (i + 2 * by) % npool) for i in range(npool)])
    across = lambda x: lax.ppermute(x, "pool", [(i, i ^ 1) for i in range(npool)])
    straight = [x] + [ahead(x if by == half // 2 else later, by) for by in range(1, half)]
    return straight + [across(y) for y in straight]


def swap_halves(x):
    return lax.ppermute(x, "tp", [(0, 1), (1, 0)])


def shards(
    prompt_kv,
    prompt_lengths,
    page_slot,
    cache_kv,
    cache_fill,
    page_table,
    context_lengths,
    queries,
    new_kv,
    out_weight,
):
    npool = lax.axis_size("pool")
    me = lax.axis_index("pool").astype(I32)
    pages, _, heads, page_len, head_dim = prompt_kv.shape
    cache_pages = cache_kv.shape[0]
    pair = (pages + npool - 1) // npool
    tabs = tables(page_len, head_dim, pages)
    place = jnp.stack([me, lax.axis_index("tp").astype(I32)])
    table = page_table.T

    asked = asked_queries(table, context_lengths, queries, page_len, heads, head_dim)
    asked_all = gathered(asked, npool)
    arrived, own = rotated_pages(prompt_kv, page_slot, prompt_lengths, tabs, npool, pair, cache_pages)
    local = local_attention(table, context_lengths, cache_fill, asked, new_kv, cache_kv, tabs)
    parts = arrived_attention(place, own, asked_all, arrived)
    parts = lax.all_to_all(parts, "pool", split_axis=0, concat_axis=0, tiled=True)
    attention = merged(place, parts, local, queries.shape, heads, pair)
    weight, again = fetched(out_weight, attention)
    blocks = gathered(attention, npool, again)
    terms, other_terms = projection(place, blocks, weight)
    other_terms = swap_halves(other_terms)
    return (terms + other_terms).astype(BF16)


def solution(mesh):
    return jax.shard_map(
        shards,
        mesh=mesh,
        in_specs=(
            P(("group", "pool"), None, "tp", None, None),
            P(("group", "pool"), None),
            P(("group", "pool")),
            P(("group", "pool"), None, "tp", None, None),
            P(("group", "pool")),
            P(("group", "pool"), None),
            P(("group", "pool")),
            P(None, ("group", "pool"), "tp"),
            P(None, ("group", "pool"), None, "tp", None),
            P("tp", "pool"),
        ),
        out_specs=P(None, "group", ("pool", "tp")),
        check_vma=False,
    )
```

```python
import functools

import jax
import jax.numpy as jnp
import numpy as np
from jax import lax
from jax.experimental import pallas as pl
from jax.experimental.pallas import tpu as pltpu
from jax.sharding import PartitionSpec as P

ROPE_BASE = 500000.0
BF16, F32, I32 = jnp.bfloat16, jnp.float32, jnp.int32
SMEM = pl.BlockSpec(memory_space=pltpu.SMEM)
VMEM = pl.BlockSpec(memory_space=pltpu.VMEM)
ANY = pl.BlockSpec(memory_space=pl.ANY)
PARAMS = pltpu.CompilerParams(vmem_limit_bytes=24 * 2**20)
LANES = 128
STAT_ROWS = 16
CODE = 256


def tables(page_len, head_dim, pages):
    half = head_dim // 2
    freq = ROPE_BASE ** (-(np.arange(half) * 2.0) / head_dim)
    freq = np.concatenate([freq, freq])[None, :]
    sign = np.concatenate([-np.ones(half), np.ones(half)])[None, :]
    token = np.arange(page_len)[:, None] * freq
    first = np.arange(pages)[:, None] * page_len * freq
    out = (np.cos(token), sign * np.sin(token), np.cos(first), sign * np.sin(first), freq, sign)
    return [jnp.asarray(x, F32) for x in out]


def rope_kernel(
    npool, cache_pages, per, slot_ref, len_ref, x_ref, pages_ref, ct_ref, st_ref, cp_ref, sp_ref, out_ref, own_ref, x_out, count
):
    _, _, heads, page_len, head_dim = pages_ref.shape

    @pl.when(pl.program_id(0) == 0)
    def _():
        x_out[...] = x_ref[...]
        items = own_ref.shape[0] // 3
        for e in range(npool):
            count[e] = 0
        for i in range(items):
            own_ref[i] = 0
            own_ref[items + i] = 0
            own_ref[2 * items + i] = -1
        for n in range(slot_ref.shape[0]):
            slot = slot_ref[n]
            target = slot // cache_pages
            at = target * (items // npool) + count[target]
            count[target] = count[target] + 1
            own_ref[at] = n
            own_ref[items + at] = page_place(len_ref, page_len, n)[1]
            own_ref[2 * items + at] = slot - target * cache_pages

    for i in range(per):
        number, _ = page_place(len_ref, page_len, pl.program_id(0) * per + i)
        c0, s0 = cp_ref[pl.ds(number, 1), :], sp_ref[pl.ds(number, 1), :]
        ct, st = ct_ref[...], st_ref[...]
        cos = c0 * ct - s0 * st
        sin = s0 * ct + c0 * st
        for k in range(heads):
            x = pages_ref[i, 0, k].astype(F32)
            out_ref[i, 0, k] = (x * cos + pltpu.roll(x, head_dim // 2, 1) * sin).astype(BF16)
            out_ref[i, 1, k] = pages_ref[i, 1, k]


def page_place(len_ref, page_len, n):
    begin = jnp.int32(0)
    number, fill = jnp.int32(0), jnp.int32(0)
    for q in range(len_ref.shape[1]):
        length = len_ref[0, q]
        count = (length + page_len - 1) // page_len
        here = (n >= begin) & (n < begin + count)
        number = jnp.where(here, n - begin, number)
        fill = jnp.where(here, jnp.clip(length - (n - begin) * page_len, 0, page_len), fill)
        begin = begin + count
    return number, fill


def rotated_pages(prompt_kv, page_slot, prompt_lengths, x, tabs, npool, pair, cache_pages):
    pages, _, heads, page_len, head_dim = prompt_kv.shape
    per = pages // 2
    ct, st, cp, sp, _, _ = tabs
    whole = lambda x: pl.BlockSpec(x.shape, lambda i: (0,) * x.ndim)
    return pl.pallas_call(
        functools.partial(rope_kernel, npool, cache_pages, per),
        grid=(pages // per,),
        out_shape=[
            jax.ShapeDtypeStruct(prompt_kv.shape, BF16),
            jax.ShapeDtypeStruct((3 * npool * pair,), I32),
            jax.ShapeDtypeStruct(x.shape, x.dtype),
        ],
        in_specs=[
            SMEM,
            SMEM,
            whole(x),
            pl.BlockSpec((per,) + prompt_kv.shape[1:], lambda i: (i, 0, 0, 0, 0)),
            whole(ct),
            whole(st),
            whole(cp),
            whole(sp),
        ],
        out_specs=[pl.BlockSpec((per,) + prompt_kv.shape[1:], lambda i: (i, 0, 0, 0, 0)), SMEM, whole(x)],
        scratch_shapes=[pltpu.SMEM((npool,), I32)],
        compiler_params=PARAMS,
        cost_estimate=pl.CostEstimate(flops=6_000_000, bytes_accessed=2_000_000, transcendentals=0),
        name="rope_pages",
    )(in_hbm(page_slot), in_hbm(prompt_lengths), x, *[in_hbm(y) for y in (prompt_kv, ct, st, cp, sp)])


def asked_kernel(page_len, heads, table_ref, context_ref, q_ref, out_ref, spread):
    most, rows = table_ref.shape
    steps, _, width = q_ref.shape
    block, head_dim = out_ref.shape[1:]
    per = width // head_dim // heads
    for s in range(steps):
        for h in range(heads * per):
            k, g = divmod(h, per)
            at = pl.ds(k * steps * per + s * per + g, rows, stride=block)
            spread[at, :] = q_ref[s, :, h * head_dim : (h + 1) * head_dim].astype(F32)
    for r in range(rows):
        out_ref[r] = spread[r * block : (r + 1) * block, :].astype(BF16)
    lane = lax.broadcasted_iota(I32, (block, LANES), 1)
    line = lax.broadcasted_iota(I32, (block, LANES), 0)
    request = jnp.zeros((block, LANES), I32)
    left = jnp.zeros((block, LANES), I32)
    for r in range(rows):
        context = context_ref[r]
        for j in range(most):
            here = lane == table_ref[j, r]
            request = jnp.where(here, r, request)
            left = jnp.where(here, jnp.clip(context - j * page_len, 0, page_len), left)
    out_ref[rows] = jnp.where(line == 0, request, left).astype(F32).astype(BF16)


def asked_queries(table, context, queries, page_len, heads, head_dim):
    steps, rows, width = queries.shape
    block = steps * width // head_dim
    return pl.pallas_call(
        functools.partial(asked_kernel, page_len, heads),
        out_shape=jax.ShapeDtypeStruct((rows + 1, block, head_dim), BF16),
        in_specs=[SMEM, SMEM, VMEM],
        out_specs=VMEM,
        scratch_shapes=[pltpu.VMEM((rows * block, head_dim), F32)],
        compiler_params=PARAMS,
        cost_estimate=pl.CostEstimate(flops=100_000, bytes_accessed=300_000, transcendentals=0),
        name="asked_queries",
    )(in_hbm(table), in_hbm(context), in_hbm(queries))


def read_scalar(x, pick):
    return jnp.max(jnp.where(pick, x, -2.0)).astype(I32)


def transposed_scores(queries, keys, group):
    turned = jnp.transpose(queries.astype(F32), (1, 0)).astype(BF16)
    chain = lax.broadcasted_iota(I32, (1, turned.shape[1]), 1) // group
    spread = [turned * jnp.where(chain == c, 1.0, 0.0).astype(BF16) for c in range(len(keys))]
    scores = jnp.dot(
        jnp.concatenate(keys, axis=1), jnp.concatenate(spread, axis=0), preferred_element_type=F32
    )
    return scores * (queries.shape[1] ** -0.5)


def weighted_values(weights, values):
    heads, head_dim = len(values), values[0].shape[1]
    group = weights.shape[0] // heads
    out = jnp.dot(weights, jnp.concatenate(values, axis=1), preferred_element_type=F32)
    parts = [out[k * group : (k + 1) * group, k * head_dim : (k + 1) * head_dim] for k in range(heads)]
    return jnp.concatenate(parts, axis=0)


def lane_values(scalars, lanes_each, shape):
    chain = lax.broadcasted_iota(I32, shape, 1) // lanes_each
    out = jnp.zeros(shape, I32)
    for i, x in enumerate(scalars):
        out = jnp.where(chain == i, x, out)
    return out


def local_kernel(
    page_len,
    heads,
    table_ref,
    context_ref,
    fill_ref,
    q_ref,
    new_ref,
    freq_ref,
    sign_ref,
    cache_ref,
    o_ref,
    stat_ref,
    kv,
    sems,
    kf,
    vf,
    position,
):
    rows, block, head_dim = q_ref.shape
    rows = rows - 1
    steps = new_ref.shape[0]
    most = table_ref.shape[0]
    group = block // heads
    per = group // steps
    together = LANES // block

    def copy(r, j):
        n = r * most + j
        return pltpu.make_async_copy(cache_ref.at[table_ref[j, r]], kv.at[n], sems.at[n])

    for r in range(rows):
        for j in range(most):
            copy(r, j).start()
    kf[...] = jnp.zeros_like(kf)
    vf[...] = jnp.zeros_like(vf)
    for r in range(rows):
        position[r : r + 1, :] = jnp.full((1, head_dim), context_ref[r], I32)
    for u in range(steps):
        angle = (position[...] + u).astype(F32) * freq_ref[...]
        cos, sin = jnp.cos(angle), jnp.sin(angle) * sign_ref[...]
        for k in range(heads):
            x = new_ref[u, :, k * head_dim : (k + 1) * head_dim].astype(F32)
            at = k * group + u
            kf[pl.ds(at, rows, stride=block), :] = x * cos + pltpu.roll(x, head_dim // 2, 1) * sin
            x = new_ref[u, :, (heads + k) * head_dim : (heads + k + 1) * head_dim].astype(F32)
            vf[pl.ds(at, rows, stride=block), :] = x
    token = lax.broadcasted_iota(I32, (page_len, LANES), 0)
    fresh = lax.broadcasted_iota(I32, (group, LANES), 0)
    step = lax.broadcasted_iota(I32, (group, LANES), 1) % group // per
    fresh_mask = (fresh <= step) & (fresh < steps)

    for i in range(rows // together):
        requests = range(i * together, (i + 1) * together)
        chains = [(r, k) for r in requests for k in range(heads)]
        if i % 2 == 0:
            for r in range(i * together, min(rows, (i + 2) * together)):
                for j in range(most):
                    copy(r, j).wait()
        queries = q_ref[i * together : (i + 1) * together].reshape(LANES, head_dim)
        keys, values = [], []
        for r, k in chains:
            at = r * block + k * group
            page = lambda what: [kv[r * most + j, what, k] for j in range(most)]
            keys.append(jnp.concatenate(page(0) + [kf[at : at + group, :].astype(BF16)], axis=0))
            values.append(page(1) + [vf[at : at + group, :].astype(BF16)])
        scores = transposed_scores(queries, keys, group)
        mask = []
        for j in range(most):
            seen = [jnp.minimum(fill_ref[table_ref[j, r]], context_ref[r] - j * page_len) for r in requests]
            mask.append(token < lane_values(seen, block, (1, LANES)))
        parts = [
            jnp.where(m, scores[n * page_len : n * page_len + m.shape[0]], -jnp.inf)
            for n, m in enumerate(mask + [fresh_mask])
        ]
        top = functools.reduce(jnp.maximum, [jnp.max(x, axis=0, keepdims=True) for x in parts])
        parts = [jnp.exp(x - top) for x in parts]
        total = functools.reduce(jnp.add, [jnp.sum(x, axis=0, keepdims=True) for x in parts])
        stats = jnp.concatenate(
            [parts[most], jnp.broadcast_to(top, (8, LANES)), jnp.broadcast_to(total, (8, LANES))]
            + [jnp.zeros((LANES - group - 16, LANES), F32)],
            axis=0,
        )
        stats = jnp.transpose(stats, (1, 0))
        weights = [jnp.transpose(x, (1, 0)).astype(BF16) for x in parts[:most]]
        weights.append(stats[:, :group].astype(BF16))
        weights = jnp.concatenate(weights, axis=1)
        for x in range(together):
            both = [jnp.concatenate(values[x * heads + k], axis=0) for k in range(heads)]
            both = weighted_values(weights[x * block : (x + 1) * block, :], both)
            o_ref[i * LANES + x * block : i * LANES + (x + 1) * block, :] = both
        stat_ref[i * LANES : (i + 1) * LANES, :] = stats


def local_attention(table, context, fills, queries, new_kv, cache_kv, tabs):
    rows, block, _ = queries.shape
    rows = rows - 1
    steps = new_kv.shape[0]
    slots, _, heads, page_len, head_dim = cache_kv.shape
    flat = (rows * block, head_dim)
    freq, sign = tabs[4:]
    return pl.pallas_call(
        functools.partial(local_kernel, page_len, heads),
        out_shape=[jax.ShapeDtypeStruct(flat, F32)] * 2,
        in_specs=[SMEM] * 3 + [VMEM] * 4 + [ANY],
        out_specs=[VMEM] * 2,
        scratch_shapes=[
            pltpu.VMEM((table.size, 2, heads, page_len, head_dim), BF16),
            pltpu.SemaphoreType.DMA((table.size,)),
            pltpu.VMEM(flat, F32),
            pltpu.VMEM(flat, F32),
            pltpu.VMEM((rows, head_dim), I32),
        ],
        compiler_params=PARAMS,
        cost_estimate=pl.CostEstimate(flops=800_000_000, bytes_accessed=12_000_000, transcendentals=400_000),
        name="local_attention",
    )(
        *[in_hbm(x) for x in (table, context, fills)],
        queries,
        new_kv.reshape(steps, rows, 2 * heads * head_dim),
        *[in_hbm(x) for x in (freq, sign, cache_kv)],
    )


def pieces(x):
    high = x.astype(BF16).astype(F32)
    middle = (x - high).astype(BF16).astype(F32)
    return [high, middle, x - high - middle]


def arrived_kernel(npool, pair, me_ref, own_ref, *refs):
    blocks = refs[:npool]
    pages_ref, out_ref, queries = refs[npool:]
    items = npool * pair
    _, _, heads, page_len, head_dim = pages_ref.shape
    rows, block = blocks[0].shape[0] - 1, blocks[0].shape[1]
    group = block // heads
    together = LANES // block
    me = me_ref[0]
    owners = [owner_of(me, which) for which in block_order(npool)]
    lane = lax.broadcasted_iota(I32, (1, LANES), 1)
    codes = [x[rows, :STAT_ROWS, :].astype(F32) for x in blocks]
    codes = [x[0:1] * CODE + x[1:2] for x in codes]
    number, seen, request = [], [], []
    for x in range(items):
        at = owners[x // pair] * pair + x % pair
        slot = own_ref[2 * items + at]
        code = jnp.maximum(read_scalar(codes[x // pair], lane == slot), 0)
        reader, left = code // CODE, code % CODE
        queries[x * block : (x + 1) * block, :] = blocks[x // pair][reader]
        number.append(own_ref[at])
        seen.append(jnp.minimum(left, own_ref[items + at]))
        request.append(jnp.where(slot >= 0, reader, -1))
    token = lax.broadcasted_iota(I32, (page_len, LANES), 0)
    for i in range(items // together):
        own = range(i * together, (i + 1) * together)
        keys = [pages_ref[number[x], 0, k] for x in own for k in range(heads)]
        scores = transposed_scores(queries[i * LANES : (i + 1) * LANES, :], keys, group)
        limit = lane_values([seen[x] for x in own], block, (1, LANES))
        scores = jnp.where(token < limit, scores, -jnp.inf)
        top = jnp.max(scores, axis=0, keepdims=True)
        top = jnp.where(top > -jnp.inf, top, 0.0)
        weights = jnp.exp(scores - top)
        stats = pieces(top) + pieces(jnp.sum(weights, axis=0, keepdims=True))
        stats.append(lane_values([request[x] for x in own], block, (1, LANES)).astype(F32))
        stats = jnp.concatenate(stats + [jnp.zeros((STAT_ROWS - len(stats), LANES), F32)], axis=0).astype(BF16)
        weights = jnp.transpose(weights, (1, 0)).astype(BF16)
        for c, x in enumerate(own):
            both = [pages_ref[number[x], 1, k] for k in range(heads)]
            both = weighted_values(weights[c * block : (c + 1) * block, :], both)
            at = (x % pair) * block
            out_ref[owners[x // pair], at : at + block, :] = both.astype(BF16)
        for place in sorted({x // pair for x in own}):
            out_ref[owners[place], pair * block : pair * block + STAT_ROWS, :] = stats


def arrived_attention(me, own, blocks, arrived):
    npool = len(blocks)
    head_dim = arrived.shape[4]
    block = blocks[0].shape[1]
    items = own.shape[0] // 3
    pair = items // npool
    return pl.pallas_call(
        functools.partial(arrived_kernel, npool, pair),
        out_shape=jax.ShapeDtypeStruct((npool, pair * block + STAT_ROWS, head_dim), BF16),
        in_specs=[SMEM] * 2 + [VMEM] * (npool + 1),
        out_specs=VMEM,
        scratch_shapes=[pltpu.VMEM((items * block, head_dim), BF16)],
        compiler_params=PARAMS,
        cost_estimate=pl.CostEstimate(flops=200_000_000, bytes_accessed=4_000_000, transcendentals=70_000),
        name="arrived_attention",
    )(me, own, *blocks, arrived)


def merge_kernel(pair, heads, me_ref, parts_ref, o_ref, stat_ref, out_ref, mixed, top, total, turned):
    npool = parts_ref.shape[0]
    steps, rows, width = out_ref.shape
    head_dim = o_ref.shape[1]
    per = width // head_dim // heads
    group = steps * per
    block = heads * group
    me = me_ref[0]
    shape = top.shape
    mixed[...] = o_ref[...]
    top[...] = jnp.broadcast_to(stat_ref[:, group : group + 1], shape)
    total[...] = jnp.broadcast_to(stat_ref[:, group + 8 : group + 9], shape)
    tops, totals, readers = [], [], []
    chain = lax.broadcasted_iota(I32, (1, LANES), 1) // block
    for d in range(npool):
        x = parts_ref[d, pair * block : pair * block + STAT_ROWS, :].astype(F32)
        tops.append(x[0:1] + x[1:2] + x[2:3])
        totals.append(x[3:4] + x[4:5] + x[5:6])
        readers.append(x[6:7])
    empty = [jnp.zeros((LANES // 2 - npool, LANES), F32)]
    turned[...] = jnp.transpose(jnp.concatenate(tops + empty + totals + empty, axis=0), (1, 0))
    for d in range(npool):
        for p in range(pair):
            part = lax.rem(place_of(me, npool, d) * pair + p, LANES // block)
            r = read_scalar(readers[d], chain == part)
            there = r >= 0
            at = pl.ds(pl.multiple_of(jnp.maximum(r, 0) * block, block), block)
            lane = pl.ds(pl.multiple_of(part * block, block), block)
            m = jnp.broadcast_to(turned[lane, d : d + 1], (block, head_dim))
            l = jnp.broadcast_to(turned[lane, LANES // 2 + d : LANES // 2 + d + 1], (block, head_dim))
            seen = (l > 0.0) & there
            o = parts_ref[d, p * block : (p + 1) * block, :].astype(F32)
            old = top[at, :]
            new = jnp.where(seen, jnp.maximum(old, m), old)
            a = jnp.exp(old - new)
            b = jnp.where(seen, jnp.exp(m - new), 0.0)
            top[at, :] = new
            total[at, :] = total[at, :] * a + l * b
            mixed[at, :] = mixed[at, :] * a + o * b
    for s in range(steps):
        for h in range(heads * per):
            k, g = divmod(h, per)
            at = pl.ds(k * group + s * per + g, rows, stride=block)
            out_ref[s, :, h * head_dim : (h + 1) * head_dim] = (mixed[at, :] / total[at, :]).astype(BF16)


def merged(me, parts, local, shape, heads, pair):
    flat = local[0].shape
    return pl.pallas_call(
        functools.partial(merge_kernel, pair, heads),
        out_shape=jax.ShapeDtypeStruct(shape, BF16),
        in_specs=[SMEM] + [VMEM] * 3,
        out_specs=VMEM,
        scratch_shapes=[pltpu.VMEM(flat, F32)] * 3 + [pltpu.VMEM((LANES, LANES), F32)],
        compiler_params=PARAMS,
        cost_estimate=pl.CostEstimate(flops=2_000_000, bytes_accessed=1_500_000, transcendentals=100_000),
        name="merge",
    )(me, parts, *local)


def fetch_kernel(weight_ref, x_ref, weight_out, x_out, sems):
    copies = [
        pltpu.make_async_copy(weight_ref, weight_out, sems.at[0]),
        pltpu.make_async_copy(x_ref, x_out, sems.at[1]),
    ]
    for copy in copies:
        copy.start()
    for copy in copies:
        copy.wait()


def fetched(weight, x):
    return pl.pallas_call(
        fetch_kernel,
        out_shape=[pltpu.VMEM(weight.shape, weight.dtype), pltpu.VMEM(x.shape, x.dtype)],
        in_specs=[ANY, ANY],
        out_specs=[ANY, ANY],
        scratch_shapes=[pltpu.SemaphoreType.DMA((2,))],
        compiler_params=PARAMS,
        cost_estimate=pl.CostEstimate(flops=0, bytes_accessed=2 * weight.size * 2, transcendentals=0),
        name="fetch_weight",
    )(in_hbm(weight), x)


def rows_kernel(npool, place_ref, *refs):
    blocks = refs[:npool]
    weight_ref, out_ref, lhs = refs[npool:]
    steps, rows, _ = blocks[0].shape
    every = npool * rows
    for x, which in enumerate(block_order(npool)):
        owner = owner_of(place_ref[0], which)
        for s in range(steps):
            lhs[pl.ds(pl.multiple_of(s * every + owner * rows, rows), rows), :] = blocks[x][s]
    multiply(lhs, weight_ref, out_ref, 1 - place_ref[1])


def multiply(lhs, weight_ref, out_ref, which):
    steps, every, half = out_ref.shape
    tile = min(half, 256)
    for i in range(half // tile):
        at = pl.ds(pl.multiple_of(which * half + i * tile, LANES), tile)
        terms = jnp.dot(lhs[...], weight_ref[:, at], preferred_element_type=F32)
        for s in range(steps):
            out_ref[s, :, i * tile : (i + 1) * tile] = terms[s * every : (s + 1) * every]


def other_projection(place, blocks, weight):
    npool = len(blocks)
    steps, rows, width = blocks[0].shape
    half = weight.shape[1] // 2
    every = steps * npool * rows
    return pl.pallas_call(
        functools.partial(rows_kernel, npool),
        out_shape=[
            jax.ShapeDtypeStruct((steps, npool * rows, half), F32),
            jax.ShapeDtypeStruct((every, width), BF16),
        ],
        in_specs=[SMEM] + [VMEM] * (npool + 1),
        out_specs=[VMEM] * 2,
        compiler_params=PARAMS,
        cost_estimate=pl.CostEstimate(flops=2 * every * width * half, bytes_accessed=4_000_000, transcendentals=0),
        name="project_other",
    )(place, *blocks, weight)


def own_kernel(place_ref, lhs, weight_ref, out_ref):
    multiply(lhs, weight_ref, out_ref, place_ref[1])


def own_projection(place, lhs, weight, steps):
    every, width = lhs.shape
    half = weight.shape[1] // 2
    return pl.pallas_call(
        own_kernel,
        out_shape=jax.ShapeDtypeStruct((steps, every // steps, half), F32),
        in_specs=[SMEM] + [VMEM] * 2,
        out_specs=VMEM,
        compiler_params=PARAMS,
        cost_estimate=pl.CostEstimate(flops=2 * every * width * half, bytes_accessed=4_000_000, transcendentals=0),
        name="project_own",
    )(place, lhs, weight)


def block_order(npool):
    return [2 * apart + flip for flip in (0, 1) for apart in range(npool // 2)]


def owner_of(me, which):
    return jnp.bitwise_xor(me, which)


def place_of(me, npool, holder):
    which = jnp.bitwise_xor(me, holder)
    return (which % 2) * (npool // 2) + which // 2


def in_hbm(x):
    return pltpu.with_memory_space_constraint(x, pltpu.HBM)


def gathered(x, npool, later):
    swap = lambda x, by: lax.ppermute(x, "pool", [(i, i ^ by) for i in range(npool)])
    straight = {0: later}
    apart = npool // 4
    while apart:
        for i in list(straight):
            own = x if i == 0 and apart == npool // 4 else straight[i]
            straight[i + apart] = swap(own, 2 * apart)
        apart //= 2
    straight = [straight[i] for i in range(npool // 2)]
    return straight + [swap(y, 1) for y in straight]


def swap_halves(x):
    return lax.ppermute(x, "tp", [(0, 1), (1, 0)])


def shards(
    prompt_kv,
    prompt_lengths,
    page_slot,
    cache_kv,
    cache_fill,
    page_table,
    context_lengths,
    queries,
    new_kv,
    out_weight,
):
    npool = lax.axis_size("pool")
    me = lax.axis_index("pool").astype(I32)
    pages, _, heads, page_len, head_dim = prompt_kv.shape
    cache_pages = cache_kv.shape[0]
    pair = (pages + npool - 1) // npool
    tabs = tables(page_len, head_dim, pages)
    place = jnp.stack([me, lax.axis_index("tp").astype(I32)])
    table = page_table.T

    asked = asked_queries(table, context_lengths, queries, page_len, heads, head_dim)
    arrived, own, again = rotated_pages(
        prompt_kv, page_slot, prompt_lengths, asked, tabs, npool, pair, cache_pages
    )
    asked_all = gathered(asked, npool, again)
    local = local_attention(table, context_lengths, cache_fill, asked, new_kv, cache_kv, tabs)
    parts = arrived_attention(place, own, asked_all, arrived)
    parts = lax.all_to_all(parts, "pool", split_axis=0, concat_axis=0, tiled=True)
    attention = merged(place, parts, local, queries.shape, heads, pair)
    weight, again = fetched(out_weight, attention)
    blocks = gathered(attention, npool, again)
    other_terms, lhs = other_projection(place, blocks, weight)
    other_terms = swap_halves(other_terms)
    terms = own_projection(place, lhs, weight, queries.shape[0])
    return (terms + other_terms).astype(BF16)


def solution(mesh):
    return jax.shard_map(
        shards,
        mesh=mesh,
        in_specs=(
            P(("group", "pool"), None, "tp", None, None),
            P(("group", "pool"), None),
            P(("group", "pool")),
            P(("group", "pool"), None, "tp", None, None),
            P(("group", "pool")),
            P(("group", "pool"), None),
            P(("group", "pool")),
            P(None, ("group", "pool"), "tp"),
            P(None, ("group", "pool"), None, "tp", None),
            P("tp", "pool"),
        ),
        out_specs=P(None, "group", ("pool", "tp")),
        check_vma=False,
    )
```

```python
import functools

import jax
import jax.numpy as jnp
import numpy as np
from jax import lax
from jax.experimental import pallas as pl
from jax.experimental.pallas import tpu as pltpu
from jax.sharding import PartitionSpec as P

ROPE_BASE = 500000.0
BF16, F32, I32 = jnp.bfloat16, jnp.float32, jnp.int32
SMEM = pl.BlockSpec(memory_space=pltpu.SMEM)
VMEM = pl.BlockSpec(memory_space=pltpu.VMEM)
ANY = pl.BlockSpec(memory_space=pl.ANY)
PARAMS = pltpu.CompilerParams(vmem_limit_bytes=24 * 2**20)
LANES = 128
STAT_ROWS = 16
CODE = 256


def tables(page_len, head_dim, pages):
    half = head_dim // 2
    freq = ROPE_BASE ** (-(np.arange(half) * 2.0) / head_dim)
    freq = np.concatenate([freq, freq])[None, :]
    sign = np.concatenate([-np.ones(half), np.ones(half)])[None, :]
    token = np.arange(page_len)[:, None] * freq
    first = np.arange(pages)[:, None] * page_len * freq
    out = (np.cos(token), sign * np.sin(token), np.cos(first), sign * np.sin(first), freq, sign)
    return [jnp.asarray(x, F32) for x in out]


def rope_kernel(
    npool, cache_pages, per, slot_ref, len_ref, x_ref, pages_ref, ct_ref, st_ref, cp_ref, sp_ref, out_ref, own_ref, x_out, count
):
    _, _, heads, page_len, head_dim = pages_ref.shape

    @pl.when(pl.program_id(0) == 0)
    def _():
        x_out[...] = x_ref[...]
        items = own_ref.shape[0] // 3
        for e in range(npool):
            count[e] = 0
        for i in range(items):
            own_ref[i] = 0
            own_ref[items + i] = 0
            own_ref[2 * items + i] = -1
        for n in range(slot_ref.shape[0]):
            slot = slot_ref[n]
            target = slot // cache_pages
            at = target * (items // npool) + count[target]
            count[target] = count[target] + 1
            own_ref[at] = n
            own_ref[items + at] = page_place(len_ref, page_len, n)[1]
            own_ref[2 * items + at] = slot - target * cache_pages

    for i in range(per):
        number, _ = page_place(len_ref, page_len, pl.program_id(0) * per + i)
        c0, s0 = cp_ref[pl.ds(number, 1), :], sp_ref[pl.ds(number, 1), :]
        ct, st = ct_ref[...], st_ref[...]
        cos = c0 * ct - s0 * st
        sin = s0 * ct + c0 * st
        for k in range(heads):
            x = pages_ref[i, 0, k].astype(F32)
            out_ref[i, 0, k] = (x * cos + pltpu.roll(x, head_dim // 2, 1) * sin).astype(BF16)
            out_ref[i, 1, k] = pages_ref[i, 1, k]


def page_place(len_ref, page_len, n):
    begin = jnp.int32(0)
    number, fill = jnp.int32(0), jnp.int32(0)
    for q in range(len_ref.shape[1]):
        length = len_ref[0, q]
        count = (length + page_len - 1) // page_len
        here = (n >= begin) & (n < begin + count)
        number = jnp.where(here, n - begin, number)
        fill = jnp.where(here, jnp.clip(length - (n - begin) * page_len, 0, page_len), fill)
        begin = begin + count
    return number, fill


def rotated_pages(prompt_kv, page_slot, prompt_lengths, x, tabs, npool, pair, cache_pages):
    pages, _, heads, page_len, head_dim = prompt_kv.shape
    per = pages // 2
    ct, st, cp, sp, _, _ = tabs
    whole = lambda x: pl.BlockSpec(x.shape, lambda i: (0,) * x.ndim)
    return pl.pallas_call(
        functools.partial(rope_kernel, npool, cache_pages, per),
        grid=(pages // per,),
        out_shape=[
            jax.ShapeDtypeStruct(prompt_kv.shape, BF16),
            jax.ShapeDtypeStruct((3 * npool * pair,), I32),
            jax.ShapeDtypeStruct(x.shape, x.dtype),
        ],
        in_specs=[
            SMEM,
            SMEM,
            whole(x),
            pl.BlockSpec((per,) + prompt_kv.shape[1:], lambda i: (i, 0, 0, 0, 0)),
            whole(ct),
            whole(st),
            whole(cp),
            whole(sp),
        ],
        out_specs=[pl.BlockSpec((per,) + prompt_kv.shape[1:], lambda i: (i, 0, 0, 0, 0)), SMEM, whole(x)],
        scratch_shapes=[pltpu.SMEM((npool,), I32)],
        compiler_params=PARAMS,
        cost_estimate=pl.CostEstimate(flops=6_000_000, bytes_accessed=2_000_000, transcendentals=0),
        name="rope_pages",
    )(in_hbm(page_slot), in_hbm(prompt_lengths), x, *[in_hbm(y) for y in (prompt_kv, ct, st, cp, sp)])


def asked_kernel(page_len, heads, table_ref, context_ref, q_ref, out_ref, spread):
    most, rows = table_ref.shape
    steps, _, width = q_ref.shape
    block, head_dim = out_ref.shape[1:]
    per = width // head_dim // heads
    for s in range(steps):
        for h in range(heads * per):
            k, g = divmod(h, per)
            at = pl.ds(k * steps * per + s * per + g, rows, stride=block)
            spread[at, :] = q_ref[s, :, h * head_dim : (h + 1) * head_dim].astype(F32)
    for r in range(rows):
        out_ref[r] = spread[r * block : (r + 1) * block, :].astype(BF16)
    lane = lax.broadcasted_iota(I32, (block, LANES), 1)
    line = lax.broadcasted_iota(I32, (block, LANES), 0)
    request = jnp.zeros((block, LANES), I32)
    left = jnp.zeros((block, LANES), I32)
    for r in range(rows):
        context = context_ref[r]
        for j in range(most):
            here = lane == table_ref[j, r]
            request = jnp.where(here, r, request)
            left = jnp.where(here, jnp.clip(context - j * page_len, 0, page_len), left)
    out_ref[rows] = jnp.where(line == 0, request, left).astype(F32).astype(BF16)


def asked_queries(table, context, queries, page_len, heads, head_dim):
    steps, rows, width = queries.shape
    block = steps * width // head_dim
    return pl.pallas_call(
        functools.partial(asked_kernel, page_len, heads),
        out_shape=jax.ShapeDtypeStruct((rows + 1, block, head_dim), BF16),
        in_specs=[SMEM, SMEM, VMEM],
        out_specs=VMEM,
        scratch_shapes=[pltpu.VMEM((rows * block, head_dim), F32)],
        compiler_params=PARAMS,
        cost_estimate=pl.CostEstimate(flops=100_000, bytes_accessed=300_000, transcendentals=0),
        name="asked_queries",
    )(in_hbm(table), in_hbm(context), in_hbm(queries))


def read_scalar(x, pick):
    return jnp.max(jnp.where(pick, x, -2.0)).astype(I32)


def transposed_scores(queries, keys, group):
    turned = jnp.transpose(queries.astype(F32), (1, 0)).astype(BF16)
    chain = lax.broadcasted_iota(I32, (1, turned.shape[1]), 1) // group
    spread = [turned * jnp.where(chain == c, 1.0, 0.0).astype(BF16) for c in range(len(keys))]
    scores = jnp.dot(
        jnp.concatenate(keys, axis=1), jnp.concatenate(spread, axis=0), preferred_element_type=F32
    )
    return scores * (queries.shape[1] ** -0.5)


def weighted_values(weights, values):
    heads, head_dim = len(values), values[0].shape[1]
    group = weights.shape[0] // heads
    out = jnp.dot(weights, jnp.concatenate(values, axis=1), preferred_element_type=F32)
    parts = [out[k * group : (k + 1) * group, k * head_dim : (k + 1) * head_dim] for k in range(heads)]
    return jnp.concatenate(parts, axis=0)


def lane_values(scalars, lanes_each, shape):
    chain = lax.broadcasted_iota(I32, shape, 1) // lanes_each
    out = jnp.zeros(shape, I32)
    for i, x in enumerate(scalars):
        out = jnp.where(chain == i, x, out)
    return out


def local_kernel(
    page_len,
    heads,
    table_ref,
    context_ref,
    fill_ref,
    q_ref,
    new_ref,
    freq_ref,
    sign_ref,
    cache_ref,
    o_ref,
    stat_ref,
    kv,
    sems,
    kf,
    vf,
    position,
):
    rows, block, head_dim = q_ref.shape
    rows = rows - 1
    steps = new_ref.shape[0]
    most = table_ref.shape[0]
    group = block // heads
    per = group // steps
    together = LANES // block

    def copy(r, j):
        n = r * most + j
        return pltpu.make_async_copy(cache_ref.at[table_ref[j, r]], kv.at[n], sems.at[n])

    for r in range(rows):
        for j in range(most):
            copy(r, j).start()
    kf[...] = jnp.zeros_like(kf)
    vf[...] = jnp.zeros_like(vf)
    for r in range(rows):
        position[r : r + 1, :] = jnp.full((1, head_dim), context_ref[r], I32)
    for u in range(steps):
        angle = (position[...] + u).astype(F32) * freq_ref[...]
        cos, sin = jnp.cos(angle), jnp.sin(angle) * sign_ref[...]
        for k in range(heads):
            x = new_ref[u, :, k * head_dim : (k + 1) * head_dim].astype(F32)
            at = k * group + u
            kf[pl.ds(at, rows, stride=block), :] = x * cos + pltpu.roll(x, head_dim // 2, 1) * sin
            x = new_ref[u, :, (heads + k) * head_dim : (heads + k + 1) * head_dim].astype(F32)
            vf[pl.ds(at, rows, stride=block), :] = x
    token = lax.broadcasted_iota(I32, (page_len, LANES), 0)
    fresh = lax.broadcasted_iota(I32, (group, LANES), 0)
    step = lax.broadcasted_iota(I32, (group, LANES), 1) % group // per
    fresh_mask = (fresh <= step) & (fresh < steps)

    for i in range(rows // together):
        requests = range(i * together, (i + 1) * together)
        chains = [(r, k) for r in requests for k in range(heads)]
        if i % 2 == 0:
            for r in range(i * together, min(rows, (i + 2) * together)):
                for j in range(most):
                    copy(r, j).wait()
        queries = q_ref[i * together : (i + 1) * together].reshape(LANES, head_dim)
        keys, values = [], []
        for r, k in chains:
            at = r * block + k * group
            page = lambda what: [kv[r * most + j, what, k] for j in range(most)]
            keys.append(jnp.concatenate(page(0) + [kf[at : at + group, :].astype(BF16)], axis=0))
            values.append(page(1) + [vf[at : at + group, :].astype(BF16)])
        scores = transposed_scores(queries, keys, group)
        mask = []
        for j in range(most):
            seen = [jnp.minimum(fill_ref[table_ref[j, r]], context_ref[r] - j * page_len) for r in requests]
            mask.append(token < lane_values(seen, block, (1, LANES)))
        parts = [
            jnp.where(m, scores[n * page_len : n * page_len + m.shape[0]], -jnp.inf)
            for n, m in enumerate(mask + [fresh_mask])
        ]
        top = functools.reduce(jnp.maximum, [jnp.max(x, axis=0, keepdims=True) for x in parts])
        parts = [jnp.exp(x - top) for x in parts]
        total = functools.reduce(jnp.add, [jnp.sum(x, axis=0, keepdims=True) for x in parts])
        stats = jnp.concatenate(
            [parts[most], jnp.broadcast_to(top, (8, LANES)), jnp.broadcast_to(total, (8, LANES))]
            + [jnp.zeros((LANES - group - 16, LANES), F32)],
            axis=0,
        )
        stats = jnp.transpose(stats, (1, 0))
        weights = [jnp.transpose(x, (1, 0)).astype(BF16) for x in parts[:most]]
        weights.append(stats[:, :group].astype(BF16))
        weights = jnp.concatenate(weights, axis=1)
        for x in range(together):
            both = [jnp.concatenate(values[x * heads + k], axis=0) for k in range(heads)]
            both = weighted_values(weights[x * block : (x + 1) * block, :], both)
            o_ref[i * LANES + x * block : i * LANES + (x + 1) * block, :] = both
        stat_ref[i * LANES : (i + 1) * LANES, :] = stats


def local_attention(table, context, fills, queries, new_kv, cache_kv, tabs):
    rows, block, _ = queries.shape
    rows = rows - 1
    steps = new_kv.shape[0]
    slots, _, heads, page_len, head_dim = cache_kv.shape
    flat = (rows * block, head_dim)
    freq, sign = tabs[4:]
    return pl.pallas_call(
        functools.partial(local_kernel, page_len, heads),
        out_shape=[jax.ShapeDtypeStruct(flat, F32)] * 2,
        in_specs=[SMEM] * 3 + [VMEM] * 4 + [ANY],
        out_specs=[VMEM] * 2,
        scratch_shapes=[
            pltpu.VMEM((table.size, 2, heads, page_len, head_dim), BF16),
            pltpu.SemaphoreType.DMA((table.size,)),
            pltpu.VMEM(flat, F32),
            pltpu.VMEM(flat, F32),
            pltpu.VMEM((rows, head_dim), I32),
        ],
        compiler_params=PARAMS,
        cost_estimate=pl.CostEstimate(flops=800_000_000, bytes_accessed=12_000_000, transcendentals=400_000),
        name="local_attention",
    )(
        *[in_hbm(x) for x in (table, context, fills)],
        queries,
        new_kv.reshape(steps, rows, 2 * heads * head_dim),
        *[in_hbm(x) for x in (freq, sign, cache_kv)],
    )


def pieces(x):
    high = x.astype(BF16).astype(F32)
    middle = (x - high).astype(BF16).astype(F32)
    return [high, middle, x - high - middle]


def arrived_kernel(npool, pair, flip, me_ref, own_ref, pages_ref, *refs):
    half = npool // 2
    blocks = refs[:half]
    before_ref, out_ref, queries = (None,) * (1 - flip) + refs[half:]
    every, items = npool * pair, half * pair
    _, _, heads, page_len, head_dim = pages_ref.shape
    rows, block = blocks[0].shape[0] - 1, blocks[0].shape[1]
    group = block // heads
    together = LANES // block
    me = me_ref[0]
    owners = [owner_of(me, npool, apart, flip) for apart in range(half)]
    if flip:
        for apart in range(half):
            out_ref[owner_of(me, npool, apart, 0)] = before_ref[apart]
        where = owners
    else:
        where = range(half)
    lane = lax.broadcasted_iota(I32, (1, LANES), 1)
    codes = [x[rows, :STAT_ROWS, :].astype(F32) for x in blocks]
    codes = [x[0:1] * CODE + x[1:2] for x in codes]
    number, seen, request = [], [], []
    for x in range(items):
        at = owners[x // pair] * pair + x % pair
        slot = own_ref[2 * every + at]
        code = jnp.maximum(read_scalar(codes[x // pair], lane == slot), 0)
        reader, left = code // CODE, code % CODE
        queries[x * block : (x + 1) * block, :] = blocks[x // pair][reader]
        number.append(own_ref[at])
        seen.append(jnp.minimum(left, own_ref[every + at]))
        request.append(jnp.where(slot >= 0, reader, -1))
    token = lax.broadcasted_iota(I32, (page_len, LANES), 0)
    for i in range(items // together):
        own = range(i * together, (i + 1) * together)
        keys = [pages_ref[number[x], 0, k] for x in own for k in range(heads)]
        scores = transposed_scores(queries[i * LANES : (i + 1) * LANES, :], keys, group)
        limit = lane_values([seen[x] for x in own], block, (1, LANES))
        scores = jnp.where(token < limit, scores, -jnp.inf)
        top = jnp.max(scores, axis=0, keepdims=True)
        top = jnp.where(top > -jnp.inf, top, 0.0)
        weights = jnp.exp(scores - top)
        stats = pieces(top) + pieces(jnp.sum(weights, axis=0, keepdims=True))
        stats.append(lane_values([request[x] for x in own], block, (1, LANES)).astype(F32))
        stats = jnp.concatenate(stats + [jnp.zeros((STAT_ROWS - len(stats), LANES), F32)], axis=0).astype(BF16)
        weights = jnp.transpose(weights, (1, 0)).astype(BF16)
        for c, x in enumerate(own):
            both = [pages_ref[number[x], 1, k] for k in range(heads)]
            both = weighted_values(weights[c * block : (c + 1) * block, :], both)
            at = (x % pair) * block
            out_ref[where[x // pair], at : at + block, :] = both.astype(BF16)
        for place in sorted({x // pair for x in own}):
            out_ref[where[place], pair * block : pair * block + STAT_ROWS, :] = stats


def arrived_attention(me, own, blocks, arrived, before=None):
    flip = 0 if before is None else 1
    half = len(blocks)
    npool = 2 * half
    head_dim = arrived.shape[4]
    block = blocks[0].shape[1]
    pair = own.shape[0] // 3 // npool
    earlier = [before] if flip else []
    return pl.pallas_call(
        functools.partial(arrived_kernel, npool, pair, flip),
        out_shape=jax.ShapeDtypeStruct((half * (1 + flip), pair * block + STAT_ROWS, head_dim), BF16),
        in_specs=[SMEM] * 2 + [VMEM] * (1 + half + flip),
        out_specs=VMEM,
        scratch_shapes=[pltpu.VMEM((half * pair * block, head_dim), BF16)],
        compiler_params=PARAMS,
        cost_estimate=pl.CostEstimate(flops=100_000_000, bytes_accessed=2_000_000, transcendentals=35_000),
        name="arrived_attention",
    )(me, own, arrived, *blocks, *earlier)


def merge_kernel(pair, heads, me_ref, parts_ref, o_ref, stat_ref, out_ref, mixed, top, total, turned):
    npool = parts_ref.shape[0]
    steps, rows, width = out_ref.shape
    head_dim = o_ref.shape[1]
    per = width // head_dim // heads
    group = steps * per
    block = heads * group
    me = me_ref[0]
    shape = top.shape
    mixed[...] = o_ref[...]
    top[...] = jnp.broadcast_to(stat_ref[:, group : group + 1], shape)
    total[...] = jnp.broadcast_to(stat_ref[:, group + 8 : group + 9], shape)
    tops, totals, readers = [], [], []
    chain = lax.broadcasted_iota(I32, (1, LANES), 1) // block
    for d in range(npool):
        x = parts_ref[d, pair * block : pair * block + STAT_ROWS, :].astype(F32)
        tops.append(x[0:1] + x[1:2] + x[2:3])
        totals.append(x[3:4] + x[4:5] + x[5:6])
        readers.append(x[6:7])
    empty = [jnp.zeros((LANES // 2 - npool, LANES), F32)]
    turned[...] = jnp.transpose(jnp.concatenate(tops + empty + totals + empty, axis=0), (1, 0))
    for d in range(npool):
        for p in range(pair):
            part = lax.rem(place_of(me, npool, d) * pair + p, LANES // block)
            r = read_scalar(readers[d], chain == part)
            there = r >= 0
            at = pl.ds(pl.multiple_of(jnp.maximum(r, 0) * block, block), block)
            lane = pl.ds(pl.multiple_of(part * block, block), block)
            m = jnp.broadcast_to(turned[lane, d : d + 1], (block, head_dim))
            l = jnp.broadcast_to(turned[lane, LANES // 2 + d : LANES // 2 + d + 1], (block, head_dim))
            seen = (l > 0.0) & there
            o = parts_ref[d, p * block : (p + 1) * block, :].astype(F32)
            old = top[at, :]
            new = jnp.where(seen, jnp.maximum(old, m), old)
            a = jnp.exp(old - new)
            b = jnp.where(seen, jnp.exp(m - new), 0.0)
            top[at, :] = new
            total[at, :] = total[at, :] * a + l * b
            mixed[at, :] = mixed[at, :] * a + o * b
    for s in range(steps):
        for h in range(heads * per):
            k, g = divmod(h, per)
            at = pl.ds(k * group + s * per + g, rows, stride=block)
            out_ref[s, :, h * head_dim : (h + 1) * head_dim] = (mixed[at, :] / total[at, :]).astype(BF16)


def merged(me, parts, local, shape, heads, pair):
    flat = local[0].shape
    return pl.pallas_call(
        functools.partial(merge_kernel, pair, heads),
        out_shape=jax.ShapeDtypeStruct(shape, BF16),
        in_specs=[SMEM] + [VMEM] * 3,
        out_specs=VMEM,
        scratch_shapes=[pltpu.VMEM(flat, F32)] * 3 + [pltpu.VMEM((LANES, LANES), F32)],
        compiler_params=PARAMS,
        cost_estimate=pl.CostEstimate(flops=2_000_000, bytes_accessed=1_500_000, transcendentals=100_000),
        name="merge",
    )(me, parts, *local)


def fetch_kernel(weight_ref, x_ref, weight_out, x_out, sems):
    copies = [
        pltpu.make_async_copy(weight_ref, weight_out, sems.at[0]),
        pltpu.make_async_copy(x_ref, x_out, sems.at[1]),
    ]
    for copy in copies:
        copy.start()
    for copy in copies:
        copy.wait()


def fetched(weight, x):
    return pl.pallas_call(
        fetch_kernel,
        out_shape=[pltpu.VMEM(weight.shape, weight.dtype), pltpu.VMEM(x.shape, x.dtype)],
        in_specs=[ANY, ANY],
        out_specs=[ANY, ANY],
        scratch_shapes=[pltpu.SemaphoreType.DMA((2,))],
        compiler_params=PARAMS,
        cost_estimate=pl.CostEstimate(flops=0, bytes_accessed=2 * weight.size * 2, transcendentals=0),
        name="fetch_weight",
    )(in_hbm(weight), x)


def rows_kernel(npool, place_ref, *refs):
    blocks = refs[:npool]
    weight_ref, out_ref, lhs = refs[npool:]
    steps, rows, _ = blocks[0].shape
    every = npool * rows
    for x, (apart, flip) in enumerate(block_order(npool)):
        owner = owner_of(place_ref[0], npool, apart, flip)
        for s in range(steps):
            lhs[pl.ds(pl.multiple_of(s * every + owner * rows, rows), rows), :] = blocks[x][s]
    multiply(lhs, weight_ref, out_ref, 1 - place_ref[1])


def multiply(lhs, weight_ref, out_ref, which):
    steps, every, half = out_ref.shape
    tile = min(half, 256)
    for i in range(half // tile):
        at = pl.ds(pl.multiple_of(which * half + i * tile, LANES), tile)
        terms = jnp.dot(lhs[...], weight_ref[:, at], preferred_element_type=F32)
        for s in range(steps):
            out_ref[s, :, i * tile : (i + 1) * tile] = terms[s * every : (s + 1) * every]


def other_projection(place, blocks, weight):
    npool = len(blocks)
    steps, rows, width = blocks[0].shape
    half = weight.shape[1] // 2
    every = steps * npool * rows
    return pl.pallas_call(
        functools.partial(rows_kernel, npool),
        out_shape=[
            jax.ShapeDtypeStruct((steps, npool * rows, half), F32),
            jax.ShapeDtypeStruct((every, width), BF16),
        ],
        in_specs=[SMEM] + [VMEM] * (npool + 1),
        out_specs=[VMEM] * 2,
        compiler_params=PARAMS,
        cost_estimate=pl.CostEstimate(flops=2 * every * width * half, bytes_accessed=4_000_000, transcendentals=0),
        name="project_other",
    )(place, *blocks, weight)


def own_kernel(place_ref, lhs, weight_ref, out_ref):
    multiply(lhs, weight_ref, out_ref, place_ref[1])


def own_projection(place, lhs, weight, steps):
    every, width = lhs.shape
    half = weight.shape[1] // 2
    return pl.pallas_call(
        own_kernel,
        out_shape=jax.ShapeDtypeStruct((steps, every // steps, half), F32),
        in_specs=[SMEM] + [VMEM] * 2,
        out_specs=VMEM,
        compiler_params=PARAMS,
        cost_estimate=pl.CostEstimate(flops=2 * every * width * half, bytes_accessed=4_000_000, transcendentals=0),
        name="project_own",
    )(place, lhs, weight)


def block_order(npool):
    return [(apart, flip) for flip in (0, 1) for apart in range(npool // 2)]


def owner_of(me, npool, apart, flip):
    half = npool // 2
    pair, side = me // 2, me % 2
    side = 1 - side if flip else side
    return lax.rem(pair + half - apart, half) * 2 + side


def place_of(me, npool, holder):
    half = npool // 2
    apart = lax.rem(holder // 2 - me // 2 + half, half)
    flip = lax.rem(me + holder, 2)
    return flip * half + apart


def in_hbm(x):
    return pltpu.with_memory_space_constraint(x, pltpu.HBM)


def gathered(x, npool, later=None):
    half = npool // 2
    later = x if later is None else later
    ahead = lambda x, by: lax.ppermute(x, "pool", [(i, (i + 2 * by) % npool) for i in range(npool)])
    across = lambda x: lax.ppermute(x, "pool", [(i, i ^ 1) for i in range(npool)])
    straight = [x] + [ahead(x if by == half // 2 else later, by) for by in range(1, half)]
    return straight + [across(y) for y in straight]


def swap_halves(x):
    return lax.ppermute(x, "tp", [(0, 1), (1, 0)])


def shards(
    prompt_kv,
    prompt_lengths,
    page_slot,
    cache_kv,
    cache_fill,
    page_table,
    context_lengths,
    queries,
    new_kv,
    out_weight,
):
    npool = lax.axis_size("pool")
    me = lax.axis_index("pool").astype(I32)
    pages, _, heads, page_len, head_dim = prompt_kv.shape
    cache_pages = cache_kv.shape[0]
    pair = (pages + npool - 1) // npool
    tabs = tables(page_len, head_dim, pages)
    place = jnp.stack([me, lax.axis_index("tp").astype(I32)])
    table = page_table.T

    asked = asked_queries(table, context_lengths, queries, page_len, heads, head_dim)
    arrived, own, again = rotated_pages(
        prompt_kv, page_slot, prompt_lengths, asked, tabs, npool, pair, cache_pages
    )
    asked_all = gathered(asked, npool, again)
    local = local_attention(table, context_lengths, cache_fill, asked, new_kv, cache_kv, tabs)
    half = npool // 2
    parts = arrived_attention(place, own, asked_all[:half], arrived)
    parts = arrived_attention(place, own, asked_all[half:], arrived, parts)
    parts = lax.all_to_all(parts, "pool", split_axis=0, concat_axis=0, tiled=True)
    attention = merged(place, parts, local, queries.shape, heads, pair)
    weight, again = fetched(out_weight, attention)
    blocks = gathered(attention, npool, again)
    other_terms, lhs = other_projection(place, blocks, weight)
    other_terms = swap_halves(other_terms)
    terms = own_projection(place, lhs, weight, queries.shape[0])
    return (terms + other_terms).astype(BF16)


def solution(mesh):
    return jax.shard_map(
        shards,
        mesh=mesh,
        in_specs=(
            P(("group", "pool"), None, "tp", None, None),
            P(("group", "pool"), None),
            P(("group", "pool")),
            P(("group", "pool"), None, "tp", None, None),
            P(("group", "pool")),
            P(("group", "pool"), None),
            P(("group", "pool")),
            P(None, ("group", "pool"), "tp"),
            P(None, ("group", "pool"), None, "tp", None),
            P("tp", "pool"),
        ),
        out_specs=P(None, "group", ("pool", "tp")),
        check_vma=False,
    )
```

```python
import functools

import jax
import jax.numpy as jnp
import numpy as np
from jax import lax
from jax.experimental import pallas as pl
from jax.experimental.pallas import tpu as pltpu
from jax.sharding import PartitionSpec as P

ROPE_BASE = 500000.0
BF16, F32, I32 = jnp.bfloat16, jnp.float32, jnp.int32
SMEM = pl.BlockSpec(memory_space=pltpu.SMEM)
VMEM = pl.BlockSpec(memory_space=pltpu.VMEM)
ANY = pl.BlockSpec(memory_space=pl.ANY)
PARAMS = pltpu.CompilerParams(vmem_limit_bytes=24 * 2**20)
LANES = 128
STAT_ROWS = 16
CODE = 256


def tables(page_len, head_dim, pages):
    half = head_dim // 2
    freq = ROPE_BASE ** (-(np.arange(half) * 2.0) / head_dim)
    freq = np.concatenate([freq, freq])[None, :]
    sign = np.concatenate([-np.ones(half), np.ones(half)])[None, :]
    token = np.arange(page_len)[:, None] * freq
    first = np.arange(pages)[:, None] * page_len * freq
    out = (np.cos(token), sign * np.sin(token), np.cos(first), sign * np.sin(first), freq, sign)
    return [jnp.asarray(x, F32) for x in out]


def rope_kernel(
    npool, cache_pages, per, slot_ref, len_ref, pages_ref, ct_ref, st_ref, cp_ref, sp_ref, out_ref, own_ref, count
):
    _, _, heads, page_len, head_dim = pages_ref.shape

    @pl.when(pl.program_id(0) == 0)
    def _():
        items = own_ref.shape[0] // 3
        for e in range(npool):
            count[e] = 0
        for i in range(items):
            own_ref[i] = 0
            own_ref[items + i] = 0
            own_ref[2 * items + i] = -1
        for n in range(slot_ref.shape[0]):
            slot = slot_ref[n]
            target = slot // cache_pages
            at = target * (items // npool) + count[target]
            count[target] = count[target] + 1
            own_ref[at] = n
            own_ref[items + at] = page_place(len_ref, page_len, n)[1]
            own_ref[2 * items + at] = slot - target * cache_pages

    for i in range(per):
        number, _ = page_place(len_ref, page_len, pl.program_id(0) * per + i)
        c0, s0 = cp_ref[pl.ds(number, 1), :], sp_ref[pl.ds(number, 1), :]
        ct, st = ct_ref[...], st_ref[...]
        cos = c0 * ct - s0 * st
        sin = s0 * ct + c0 * st
        for k in range(heads):
            x = pages_ref[i, 0, k].astype(F32)
            out_ref[i, 0, k] = (x * cos + pltpu.roll(x, head_dim // 2, 1) * sin).astype(BF16)
            out_ref[i, 1, k] = pages_ref[i, 1, k]


def page_place(len_ref, page_len, n):
    begin = jnp.int32(0)
    number, fill = jnp.int32(0), jnp.int32(0)
    for q in range(len_ref.shape[1]):
        length = len_ref[0, q]
        count = (length + page_len - 1) // page_len
        here = (n >= begin) & (n < begin + count)
        number = jnp.where(here, n - begin, number)
        fill = jnp.where(here, jnp.clip(length - (n - begin) * page_len, 0, page_len), fill)
        begin = begin + count
    return number, fill


def rotated_pages(prompt_kv, page_slot, prompt_lengths, tabs, npool, pair, cache_pages):
    pages, _, heads, page_len, head_dim = prompt_kv.shape
    per = pages // 2
    ct, st, cp, sp, _, _ = tabs
    whole = lambda x: pl.BlockSpec(x.shape, lambda i: (0, 0))
    return pl.pallas_call(
        functools.partial(rope_kernel, npool, cache_pages, per),
        grid=(pages // per,),
        out_shape=[
            jax.ShapeDtypeStruct(prompt_kv.shape, BF16),
            jax.ShapeDtypeStruct((3 * npool * pair,), I32),
        ],
        in_specs=[
            SMEM,
            SMEM,
            pl.BlockSpec((per,) + prompt_kv.shape[1:], lambda i: (i, 0, 0, 0, 0)),
            whole(ct),
            whole(st),
            whole(cp),
            whole(sp),
        ],
        out_specs=[pl.BlockSpec((per,) + prompt_kv.shape[1:], lambda i: (i, 0, 0, 0, 0)), SMEM],
        scratch_shapes=[pltpu.SMEM((npool,), I32)],
        compiler_params=PARAMS,
        cost_estimate=pl.CostEstimate(flops=6_000_000, bytes_accessed=2_000_000, transcendentals=0),
        name="rope_pages",
    )(*[in_hbm(x) for x in (page_slot, prompt_lengths, prompt_kv, ct, st, cp, sp)])


def asked_kernel(page_len, heads, table_ref, context_ref, q_ref, out_ref, spread):
    most, rows = table_ref.shape
    steps, _, width = q_ref.shape
    block, head_dim = out_ref.shape[1:]
    per = width // head_dim // heads
    for s in range(steps):
        for h in range(heads * per):
            k, g = divmod(h, per)
            at = pl.ds(k * steps * per + s * per + g, rows, stride=block)
            spread[at, :] = q_ref[s, :, h * head_dim : (h + 1) * head_dim].astype(F32)
    for r in range(rows):
        out_ref[r] = spread[r * block : (r + 1) * block, :].astype(BF16)
    lane = lax.broadcasted_iota(I32, (block, LANES), 1)
    line = lax.broadcasted_iota(I32, (block, LANES), 0)
    request = jnp.zeros((block, LANES), I32)
    left = jnp.zeros((block, LANES), I32)
    for r in range(rows):
        context = context_ref[r]
        for j in range(most):
            here = lane == table_ref[j, r]
            request = jnp.where(here, r, request)
            left = jnp.where(here, jnp.clip(context - j * page_len, 0, page_len), left)
    out_ref[rows] = jnp.where(line == 0, request, left).astype(F32).astype(BF16)


def asked_queries(table, context, queries, page_len, heads, head_dim):
    steps, rows, width = queries.shape
    block = steps * width // head_dim
    return pl.pallas_call(
        functools.partial(asked_kernel, page_len, heads),
        out_shape=jax.ShapeDtypeStruct((rows + 1, block, head_dim), BF16),
        in_specs=[SMEM, SMEM, VMEM],
        out_specs=VMEM,
        scratch_shapes=[pltpu.VMEM((rows * block, head_dim), F32)],
        compiler_params=PARAMS,
        cost_estimate=pl.CostEstimate(flops=100_000, bytes_accessed=300_000, transcendentals=0),
        name="asked_queries",
    )(in_hbm(table), in_hbm(context), in_hbm(queries))


def read_scalar(x, pick):
    return jnp.max(jnp.where(pick, x, -2.0)).astype(I32)


def transposed_scores(queries, keys, group):
    turned = jnp.transpose(queries.astype(F32), (1, 0)).astype(BF16)
    chain = lax.broadcasted_iota(I32, (1, turned.shape[1]), 1) // group
    spread = [turned * jnp.where(chain == c, 1.0, 0.0).astype(BF16) for c in range(len(keys))]
    scores = jnp.dot(
        jnp.concatenate(keys, axis=1), jnp.concatenate(spread, axis=0), preferred_element_type=F32
    )
    return scores * (queries.shape[1] ** -0.5)


def weighted_values(weights, values):
    heads, head_dim = len(values), values[0].shape[1]
    group = weights.shape[0] // heads
    out = jnp.dot(weights, jnp.concatenate(values, axis=1), preferred_element_type=F32)
    parts = [out[k * group : (k + 1) * group, k * head_dim : (k + 1) * head_dim] for k in range(heads)]
    return jnp.concatenate(parts, axis=0)


def lane_values(scalars, lanes_each, shape):
    chain = lax.broadcasted_iota(I32, shape, 1) // lanes_each
    out = jnp.zeros(shape, I32)
    for i, x in enumerate(scalars):
        out = jnp.where(chain == i, x, out)
    return out


def local_kernel(
    page_len,
    heads,
    table_ref,
    context_ref,
    fill_ref,
    q_ref,
    new_ref,
    freq_ref,
    sign_ref,
    cache_ref,
    o_ref,
    stat_ref,
    kv,
    sems,
    kf,
    vf,
    position,
):
    rows, block, head_dim = q_ref.shape
    rows = rows - 1
    steps = new_ref.shape[0]
    most = table_ref.shape[0]
    group = block // heads
    per = group // steps
    together = LANES // block

    def copy(r, j):
        n = r * most + j
        return pltpu.make_async_copy(cache_ref.at[table_ref[j, r]], kv.at[n], sems.at[n])

    for r in range(rows):
        for j in range(most):
            copy(r, j).start()
    kf[...] = jnp.zeros_like(kf)
    vf[...] = jnp.zeros_like(vf)
    for r in range(rows):
        position[r : r + 1, :] = jnp.full((1, head_dim), context_ref[r], I32)
    for u in range(steps):
        angle = (position[...] + u).astype(F32) * freq_ref[...]
        cos, sin = jnp.cos(angle), jnp.sin(angle) * sign_ref[...]
        for k in range(heads):
            x = new_ref[u, :, k * head_dim : (k + 1) * head_dim].astype(F32)
            at = k * group + u
            kf[pl.ds(at, rows, stride=block), :] = x * cos + pltpu.roll(x, head_dim // 2, 1) * sin
            x = new_ref[u, :, (heads + k) * head_dim : (heads + k + 1) * head_dim].astype(F32)
            vf[pl.ds(at, rows, stride=block), :] = x
    token = lax.broadcasted_iota(I32, (page_len, LANES), 0)
    fresh = lax.broadcasted_iota(I32, (group, LANES), 0)
    step = lax.broadcasted_iota(I32, (group, LANES), 1) % group // per
    fresh_mask = (fresh <= step) & (fresh < steps)

    for i in range(rows // together):
        requests = range(i * together, (i + 1) * together)
        chains = [(r, k) for r in requests for k in range(heads)]
        if i % 2 == 0:
            for r in range(i * together, min(rows, (i + 2) * together)):
                for j in range(most):
                    copy(r, j).wait()
        queries = q_ref[i * together : (i + 1) * together].reshape(LANES, head_dim)
        keys, values = [], []
        for r, k in chains:
            at = r * block + k * group
            page = lambda what: [kv[r * most + j, what, k] for j in range(most)]
            keys.append(jnp.concatenate(page(0) + [kf[at : at + group, :].astype(BF16)], axis=0))
            values.append(page(1) + [vf[at : at + group, :].astype(BF16)])
        scores = transposed_scores(queries, keys, group)
        mask = []
        for j in range(most):
            seen = [jnp.minimum(fill_ref[table_ref[j, r]], context_ref[r] - j * page_len) for r in requests]
            mask.append(token < lane_values(seen, block, (1, LANES)))
        parts = [
            jnp.where(m, scores[n * page_len : n * page_len + m.shape[0]], -jnp.inf)
            for n, m in enumerate(mask + [fresh_mask])
        ]
        top = functools.reduce(jnp.maximum, [jnp.max(x, axis=0, keepdims=True) for x in parts])
        parts = [jnp.exp(x - top) for x in parts]
        total = functools.reduce(jnp.add, [jnp.sum(x, axis=0, keepdims=True) for x in parts])
        stats = jnp.concatenate(
            [parts[most], jnp.broadcast_to(top, (8, LANES)), jnp.broadcast_to(total, (8, LANES))]
            + [jnp.zeros((LANES - group - 16, LANES), F32)],
            axis=0,
        )
        stats = jnp.transpose(stats, (1, 0))
        weights = [jnp.transpose(x, (1, 0)).astype(BF16) for x in parts[:most]]
        weights.append(stats[:, :group].astype(BF16))
        weights = jnp.concatenate(weights, axis=1)
        for x in range(together):
            both = [jnp.concatenate(values[x * heads + k], axis=0) for k in range(heads)]
            both = weighted_values(weights[x * block : (x + 1) * block, :], both)
            o_ref[i * LANES + x * block : i * LANES + (x + 1) * block, :] = both
        stat_ref[i * LANES : (i + 1) * LANES, :] = stats


def local_attention(table, context, fills, queries, new_kv, cache_kv, tabs):
    rows, block, _ = queries.shape
    rows = rows - 1
    steps = new_kv.shape[0]
    slots, _, heads, page_len, head_dim = cache_kv.shape
    flat = (rows * block, head_dim)
    freq, sign = tabs[4:]
    return pl.pallas_call(
        functools.partial(local_kernel, page_len, heads),
        out_shape=[jax.ShapeDtypeStruct(flat, F32)] * 2,
        in_specs=[SMEM] * 3 + [VMEM] * 4 + [ANY],
        out_specs=[VMEM] * 2,
        scratch_shapes=[
            pltpu.VMEM((table.size, 2, heads, page_len, head_dim), BF16),
            pltpu.SemaphoreType.DMA((table.size,)),
            pltpu.VMEM(flat, F32),
            pltpu.VMEM(flat, F32),
            pltpu.VMEM((rows, head_dim), I32),
        ],
        compiler_params=PARAMS,
        cost_estimate=pl.CostEstimate(flops=800_000_000, bytes_accessed=12_000_000, transcendentals=400_000),
        name="local_attention",
    )(
        *[in_hbm(x) for x in (table, context, fills)],
        queries,
        new_kv.reshape(steps, rows, 2 * heads * head_dim),
        *[in_hbm(x) for x in (freq, sign, cache_kv)],
    )


def pieces(x):
    high = x.astype(BF16).astype(F32)
    middle = (x - high).astype(BF16).astype(F32)
    return [high, middle, x - high - middle]


def arrived_kernel(npool, pair, me_ref, own_ref, *refs):
    blocks = refs[:npool]
    pages_ref, out_ref, queries = refs[npool:]
    items = npool * pair
    _, _, heads, page_len, head_dim = pages_ref.shape
    rows, block = blocks[0].shape[0] - 1, blocks[0].shape[1]
    group = block // heads
    together = LANES // block
    me = me_ref[0]
    owners = [owner_of(me, npool, apart, flip) for apart, flip in block_order(npool)]
    lane = lax.broadcasted_iota(I32, (1, LANES), 1)
    codes = [x[rows, :STAT_ROWS, :].astype(F32) for x in blocks]
    codes = [x[0:1] * CODE + x[1:2] for x in codes]
    number, seen, request = [], [], []
    for x in range(items):
        at = owners[x // pair] * pair + x % pair
        slot = own_ref[2 * items + at]
        code = jnp.maximum(read_scalar(codes[x // pair], lane == slot), 0)
        reader, left = code // CODE, code % CODE
        queries[x * block : (x + 1) * block, :] = blocks[x // pair][reader]
        number.append(own_ref[at])
        seen.append(jnp.minimum(left, own_ref[items + at]))
        request.append(jnp.where(slot >= 0, reader, -1))
    token = lax.broadcasted_iota(I32, (page_len, LANES), 0)
    for i in range(items // together):
        own = range(i * together, (i + 1) * together)
        keys = [pages_ref[number[x], 0, k] for x in own for k in range(heads)]
        scores = transposed_scores(queries[i * LANES : (i + 1) * LANES, :], keys, group)
        limit = lane_values([seen[x] for x in own], block, (1, LANES))
        scores = jnp.where(token < limit, scores, -jnp.inf)
        top = jnp.max(scores, axis=0, keepdims=True)
        top = jnp.where(top > -jnp.inf, top, 0.0)
        weights = jnp.exp(scores - top)
        stats = pieces(top) + pieces(jnp.sum(weights, axis=0, keepdims=True))
        stats.append(lane_values([request[x] for x in own], block, (1, LANES)).astype(F32))
        stats = jnp.concatenate(stats + [jnp.zeros((STAT_ROWS - len(stats), LANES), F32)], axis=0).astype(BF16)
        weights = jnp.transpose(weights, (1, 0)).astype(BF16)
        for c, x in enumerate(own):
            both = [pages_ref[number[x], 1, k] for k in range(heads)]
            both = weighted_values(weights[c * block : (c + 1) * block, :], both)
            at = (x % pair) * block
            out_ref[owners[x // pair], at : at + block, :] = both.astype(BF16)
        for place in sorted({x // pair for x in own}):
            out_ref[owners[place], pair * block : pair * block + STAT_ROWS, :] = stats


def arrived_attention(me, own, blocks, arrived):
    npool = len(blocks)
    head_dim = arrived.shape[4]
    block = blocks[0].shape[1]
    items = own.shape[0] // 3
    pair = items // npool
    return pl.pallas_call(
        functools.partial(arrived_kernel, npool, pair),
        out_shape=jax.ShapeDtypeStruct((npool, pair * block + STAT_ROWS, head_dim), BF16),
        in_specs=[SMEM] * 2 + [VMEM] * (npool + 1),
        out_specs=VMEM,
        scratch_shapes=[pltpu.VMEM((items * block, head_dim), BF16)],
        compiler_params=PARAMS,
        cost_estimate=pl.CostEstimate(flops=200_000_000, bytes_accessed=4_000_000, transcendentals=70_000),
        name="arrived_attention",
    )(me, own, *blocks, arrived)


def merge_kernel(pair, heads, me_ref, parts_ref, o_ref, stat_ref, out_ref, mixed, top, total, turned):
    npool = parts_ref.shape[0]
    steps, rows, width = out_ref.shape
    head_dim = o_ref.shape[1]
    per = width // head_dim // heads
    group = steps * per
    block = heads * group
    me = me_ref[0]
    shape = top.shape
    mixed[...] = o_ref[...]
    top[...] = jnp.broadcast_to(stat_ref[:, group : group + 1], shape)
    total[...] = jnp.broadcast_to(stat_ref[:, group + 8 : group + 9], shape)
    tops, totals, readers = [], [], []
    chain = lax.broadcasted_iota(I32, (1, LANES), 1) // block
    for d in range(npool):
        x = parts_ref[d, pair * block : pair * block + STAT_ROWS, :].astype(F32)
        tops.append(x[0:1] + x[1:2] + x[2:3])
        totals.append(x[3:4] + x[4:5] + x[5:6])
        readers.append(x[6:7])
    empty = [jnp.zeros((LANES // 2 - npool, LANES), F32)]
    turned[...] = jnp.transpose(jnp.concatenate(tops + empty + totals + empty, axis=0), (1, 0))
    for d in range(npool):
        for p in range(pair):
            part = lax.rem(place_of(me, npool, d) * pair + p, LANES // block)
            r = read_scalar(readers[d], chain == part)
            there = r >= 0
            at = pl.ds(pl.multiple_of(jnp.maximum(r, 0) * block, block), block)
            lane = pl.ds(pl.multiple_of(part * block, block), block)
            m = jnp.broadcast_to(turned[lane, d : d + 1], (block, head_dim))
            l = jnp.broadcast_to(turned[lane, LANES // 2 + d : LANES // 2 + d + 1], (block, head_dim))
            seen = (l > 0.0) & there
            o = parts_ref[d, p * block : (p + 1) * block, :].astype(F32)
            old = top[at, :]
            new = jnp.where(seen, jnp.maximum(old, m), old)
            a = jnp.exp(old - new)
            b = jnp.where(seen, jnp.exp(m - new), 0.0)
            top[at, :] = new
            total[at, :] = total[at, :] * a + l * b
            mixed[at, :] = mixed[at, :] * a + o * b
    for s in range(steps):
        for h in range(heads * per):
            k, g = divmod(h, per)
            at = pl.ds(k * group + s * per + g, rows, stride=block)
            out_ref[s, :, h * head_dim : (h + 1) * head_dim] = (mixed[at, :] / total[at, :]).astype(BF16)


def merged(me, parts, local, shape, heads, pair):
    flat = local[0].shape
    return pl.pallas_call(
        functools.partial(merge_kernel, pair, heads),
        out_shape=jax.ShapeDtypeStruct(shape, BF16),
        in_specs=[SMEM] + [VMEM] * 3,
        out_specs=VMEM,
        scratch_shapes=[pltpu.VMEM(flat, F32)] * 3 + [pltpu.VMEM((LANES, LANES), F32)],
        compiler_params=PARAMS,
        cost_estimate=pl.CostEstimate(flops=2_000_000, bytes_accessed=1_500_000, transcendentals=100_000),
        name="merge",
    )(me, parts, *local)


def fetch_kernel(weight_ref, x_ref, weight_out, x_out, sems):
    copies = [
        pltpu.make_async_copy(weight_ref, weight_out, sems.at[0]),
        pltpu.make_async_copy(x_ref, x_out, sems.at[1]),
    ]
    for copy in copies:
        copy.start()
    for copy in copies:
        copy.wait()


def fetched(weight, x):
    return pl.pallas_call(
        fetch_kernel,
        out_shape=[pltpu.VMEM(weight.shape, weight.dtype), pltpu.VMEM(x.shape, x.dtype)],
        in_specs=[ANY, ANY],
        out_specs=[ANY, ANY],
        scratch_shapes=[pltpu.SemaphoreType.DMA((2,))],
        compiler_params=PARAMS,
        cost_estimate=pl.CostEstimate(flops=0, bytes_accessed=2 * weight.size * 2, transcendentals=0),
        name="fetch_weight",
    )(in_hbm(weight), x)


def rows_kernel(npool, place_ref, *refs):
    blocks = refs[:npool]
    weight_ref, out_ref, lhs = refs[npool:]
    steps, rows, _ = blocks[0].shape
    every = npool * rows
    for x, (apart, flip) in enumerate(block_order(npool)):
        owner = owner_of(place_ref[0], npool, apart, flip)
        for s in range(steps):
            lhs[pl.ds(pl.multiple_of(s * every + owner * rows, rows), rows), :] = blocks[x][s]
    multiply(lhs, weight_ref, out_ref, 1 - place_ref[1])


def multiply(lhs, weight_ref, out_ref, which):
    steps, every, half = out_ref.shape
    tile = min(half, 256)
    for i in range(half // tile):
        at = pl.ds(pl.multiple_of(which * half + i * tile, LANES), tile)
        terms = jnp.dot(lhs[...], weight_ref[:, at], preferred_element_type=F32)
        for s in range(steps):
            out_ref[s, :, i * tile : (i + 1) * tile] = terms[s * every : (s + 1) * every]


def other_projection(place, blocks, weight):
    npool = len(blocks)
    steps, rows, width = blocks[0].shape
    half = weight.shape[1] // 2
    every = steps * npool * rows
    return pl.pallas_call(
        functools.partial(rows_kernel, npool),
        out_shape=[
            jax.ShapeDtypeStruct((steps, npool * rows, half), F32),
            jax.ShapeDtypeStruct((every, width), BF16),
        ],
        in_specs=[SMEM] + [VMEM] * (npool + 1),
        out_specs=[VMEM] * 2,
        compiler_params=PARAMS,
        cost_estimate=pl.CostEstimate(flops=2 * every * width * half, bytes_accessed=4_000_000, transcendentals=0),
        name="project_other",
    )(place, *blocks, weight)


def own_kernel(place_ref, lhs, weight_ref, out_ref):
    multiply(lhs, weight_ref, out_ref, place_ref[1])


def own_projection(place, lhs, weight, steps):
    every, width = lhs.shape
    half = weight.shape[1] // 2
    return pl.pallas_call(
        own_kernel,
        out_shape=jax.ShapeDtypeStruct((steps, every // steps, half), F32),
        in_specs=[SMEM] + [VMEM] * 2,
        out_specs=VMEM,
        compiler_params=PARAMS,
        cost_estimate=pl.CostEstimate(flops=2 * every * width * half, bytes_accessed=4_000_000, transcendentals=0),
        name="project_own",
    )(place, lhs, weight)


def distances(npool):
    half = npool // 2
    return sorted(range(half), key=lambda apart: -abs(apart - half // 2))


def block_order(npool):
    return [(apart, flip) for flip in (0, 1) for apart in distances(npool)]


def owner_of(me, npool, apart, flip):
    half = npool // 2
    pair, side = me // 2, me % 2
    side = 1 - side if flip else side
    return lax.rem(pair + half - apart, half) * 2 + side


def place_of(me, npool, holder):
    half = npool // 2
    apart = lax.rem(holder // 2 - me // 2 + half, half)
    flip = lax.rem(me + holder, 2)
    return flip * half + sum(jnp.where(apart == x, i, 0) for i, x in enumerate(distances(npool)))


def in_hbm(x):
    return pltpu.with_memory_space_constraint(x, pltpu.HBM)


def gathered(x, npool, later=None):
    half = npool // 2
    later = x if later is None else later
    ahead = lambda x, by: lax.ppermute(x, "pool", [(i, (i + 2 * by) % npool) for i in range(npool)])
    across = lambda x: lax.ppermute(x, "pool", [(i, i ^ 1) for i in range(npool)])
    straight = {0: x}
    for by in distances(npool)[1:]:
        straight[by] = ahead(x if by == half // 2 else later, by)
    return list(straight.values()) + [across(y) for y in straight.values()]


def swap_halves(x):
    return lax.ppermute(x, "tp", [(0, 1), (1, 0)])


def shards(
    prompt_kv,
    prompt_lengths,
    page_slot,
    cache_kv,
    cache_fill,
    page_table,
    context_lengths,
    queries,
    new_kv,
    out_weight,
):
    npool = lax.axis_size("pool")
    me = lax.axis_index("pool").astype(I32)
    pages, _, heads, page_len, head_dim = prompt_kv.shape
    cache_pages = cache_kv.shape[0]
    pair = (pages + npool - 1) // npool
    tabs = tables(page_len, head_dim, pages)
    place = jnp.stack([me, lax.axis_index("tp").astype(I32)])
    table = page_table.T

    asked = asked_queries(table, context_lengths, queries, page_len, heads, head_dim)
    asked_all = gathered(asked, npool)
    arrived, own = rotated_pages(prompt_kv, page_slot, prompt_lengths, tabs, npool, pair, cache_pages)
    local = local_attention(table, context_lengths, cache_fill, asked, new_kv, cache_kv, tabs)
    parts = arrived_attention(place, own, asked_all, arrived)
    parts = lax.all_to_all(parts, "pool", split_axis=0, concat_axis=0, tiled=True)
    attention = merged(place, parts, local, queries.shape, heads, pair)
    weight, again = fetched(out_weight, attention)
    blocks = gathered(attention, npool, again)
    other_terms, lhs = other_projection(place, blocks, weight)
    other_terms = swap_halves(other_terms)
    terms = own_projection(place, lhs, weight, queries.shape[0])
    return (terms + other_terms).astype(BF16)


def solution(mesh):
    return jax.shard_map(
        shards,
        mesh=mesh,
        in_specs=(
            P(("group", "pool"), None, "tp", None, None),
            P(("group", "pool"), None),
            P(("group", "pool")),
            P(("group", "pool"), None, "tp", None, None),
            P(("group", "pool")),
            P(("group", "pool"), None),
            P(("group", "pool")),
            P(None, ("group", "pool"), "tp"),
            P(None, ("group", "pool"), None, "tp", None),
            P("tp", "pool"),
        ),
        out_specs=P(None, "group", ("pool", "tp")),
        check_vma=False,
    )
```

```python
import functools

import jax
import jax.numpy as jnp
import numpy as np
from jax import lax
from jax.experimental import pallas as pl
from jax.experimental.pallas import tpu as pltpu
from jax.sharding import PartitionSpec as P

ROPE_BASE = 500000.0
BF16, F32, I32 = jnp.bfloat16, jnp.float32, jnp.int32
SMEM = pl.BlockSpec(memory_space=pltpu.SMEM)
VMEM = pl.BlockSpec(memory_space=pltpu.VMEM)
ANY = pl.BlockSpec(memory_space=pl.ANY)
PARAMS = pltpu.CompilerParams(vmem_limit_bytes=24 * 2**20)
LANES = 128
STAT_ROWS = 16
CODE = 256


def tables(page_len, head_dim, pages):
    half = head_dim // 2
    freq = ROPE_BASE ** (-(np.arange(half) * 2.0) / head_dim)
    freq = np.concatenate([freq, freq])[None, :]
    sign = np.concatenate([-np.ones(half), np.ones(half)])[None, :]
    token = np.arange(page_len)[:, None] * freq
    first = np.arange(pages)[:, None] * page_len * freq
    out = (np.cos(token), sign * np.sin(token), np.cos(first), sign * np.sin(first), freq, sign)
    return [jnp.asarray(x, F32) for x in out]


def rope_kernel(
    npool, cache_pages, per, slot_ref, len_ref, pages_ref, ct_ref, st_ref, cp_ref, sp_ref, out_ref, own_ref, count
):
    _, _, heads, page_len, head_dim = pages_ref.shape

    @pl.when(pl.program_id(0) == 0)
    def _():
        items = own_ref.shape[0] // 3
        for e in range(npool):
            count[e] = 0
        for i in range(items):
            own_ref[i] = 0
            own_ref[items + i] = 0
            own_ref[2 * items + i] = -1
        for n in range(slot_ref.shape[0]):
            slot = slot_ref[n]
            target = slot // cache_pages
            at = target * (items // npool) + count[target]
            count[target] = count[target] + 1
            own_ref[at] = n
            own_ref[items + at] = page_place(len_ref, page_len, n)[1]
            own_ref[2 * items + at] = slot - target * cache_pages

    for i in range(per):
        number, _ = page_place(len_ref, page_len, pl.program_id(0) * per + i)
        c0, s0 = cp_ref[pl.ds(number, 1), :], sp_ref[pl.ds(number, 1), :]
        ct, st = ct_ref[...], st_ref[...]
        cos = c0 * ct - s0 * st
        sin = s0 * ct + c0 * st
        for k in range(heads):
            x = pages_ref[i, 0, k].astype(F32)
            out_ref[i, 0, k] = (x * cos + pltpu.roll(x, head_dim // 2, 1) * sin).astype(BF16)
            out_ref[i, 1, k] = pages_ref[i, 1, k]


def page_place(len_ref, page_len, n):
    begin = jnp.int32(0)
    number, fill = jnp.int32(0), jnp.int32(0)
    for q in range(len_ref.shape[1]):
        length = len_ref[0, q]
        count = (length + page_len - 1) // page_len
        here = (n >= begin) & (n < begin + count)
        number = jnp.where(here, n - begin, number)
        fill = jnp.where(here, jnp.clip(length - (n - begin) * page_len, 0, page_len), fill)
        begin = begin + count
    return number, fill


def rotated_pages(prompt_kv, page_slot, prompt_lengths, tabs, npool, pair, cache_pages):
    pages, _, heads, page_len, head_dim = prompt_kv.shape
    per = pages // 2
    ct, st, cp, sp, _, _ = tabs
    whole = lambda x: pl.BlockSpec(x.shape, lambda i: (0, 0))
    return pl.pallas_call(
        functools.partial(rope_kernel, npool, cache_pages, per),
        grid=(pages // per,),
        out_shape=[
            jax.ShapeDtypeStruct(prompt_kv.shape, BF16),
            jax.ShapeDtypeStruct((3 * npool * pair,), I32),
        ],
        in_specs=[
            SMEM,
            SMEM,
            pl.BlockSpec((per,) + prompt_kv.shape[1:], lambda i: (i, 0, 0, 0, 0)),
            whole(ct),
            whole(st),
            whole(cp),
            whole(sp),
        ],
        out_specs=[pl.BlockSpec((per,) + prompt_kv.shape[1:], lambda i: (i, 0, 0, 0, 0)), SMEM],
        scratch_shapes=[pltpu.SMEM((npool,), I32)],
        compiler_params=PARAMS,
        cost_estimate=pl.CostEstimate(flops=6_000_000, bytes_accessed=2_000_000, transcendentals=0),
        name="rope_pages",
    )(*[in_hbm(x) for x in (page_slot, prompt_lengths, prompt_kv, ct, st, cp, sp)])


def asked_kernel(page_len, heads, table_ref, context_ref, q_ref, out_ref, spread):
    most, rows = table_ref.shape
    steps, _, width = q_ref.shape
    block, head_dim = out_ref.shape[1:]
    per = width // head_dim // heads
    for s in range(steps):
        for h in range(heads * per):
            k, g = divmod(h, per)
            at = pl.ds(k * steps * per + s * per + g, rows, stride=block)
            spread[at, :] = q_ref[s, :, h * head_dim : (h + 1) * head_dim].astype(F32)
    for r in range(rows):
        out_ref[r] = spread[r * block : (r + 1) * block, :].astype(BF16)
    lane = lax.broadcasted_iota(I32, (block, LANES), 1)
    line = lax.broadcasted_iota(I32, (block, LANES), 0)
    request = jnp.zeros((block, LANES), I32)
    left = jnp.zeros((block, LANES), I32)
    for r in range(rows):
        context = context_ref[r]
        for j in range(most):
            here = lane == table_ref[j, r]
            request = jnp.where(here, r, request)
            left = jnp.where(here, jnp.clip(context - j * page_len, 0, page_len), left)
    out_ref[rows] = jnp.where(line == 0, request, left).astype(F32).astype(BF16)


def asked_queries(table, context, queries, page_len, heads, head_dim):
    steps, rows, width = queries.shape
    block = steps * width // head_dim
    return pl.pallas_call(
        functools.partial(asked_kernel, page_len, heads),
        out_shape=jax.ShapeDtypeStruct((rows + 1, block, head_dim), BF16),
        in_specs=[SMEM, SMEM, VMEM],
        out_specs=VMEM,
        scratch_shapes=[pltpu.VMEM((rows * block, head_dim), F32)],
        compiler_params=PARAMS,
        cost_estimate=pl.CostEstimate(flops=100_000, bytes_accessed=300_000, transcendentals=0),
        name="asked_queries",
    )(in_hbm(table), in_hbm(context), in_hbm(queries))


def read_scalar(x, pick):
    return jnp.max(jnp.where(pick, x, -2.0)).astype(I32)


def transposed_scores(queries, keys, group):
    turned = jnp.transpose(queries.astype(F32), (1, 0)).astype(BF16)
    chain = lax.broadcasted_iota(I32, (1, turned.shape[1]), 1) // group
    spread = [turned * jnp.where(chain == c, 1.0, 0.0).astype(BF16) for c in range(len(keys))]
    scores = jnp.dot(
        jnp.concatenate(keys, axis=1), jnp.concatenate(spread, axis=0), preferred_element_type=F32
    )
    return scores * (queries.shape[1] ** -0.5)


def weighted_values(weights, values):
    heads, head_dim = len(values), values[0].shape[1]
    group = weights.shape[0] // heads
    out = jnp.dot(weights, jnp.concatenate(values, axis=1), preferred_element_type=F32)
    parts = [out[k * group : (k + 1) * group, k * head_dim : (k + 1) * head_dim] for k in range(heads)]
    return jnp.concatenate(parts, axis=0)


def lane_values(scalars, lanes_each, shape):
    chain = lax.broadcasted_iota(I32, shape, 1) // lanes_each
    out = jnp.zeros(shape, I32)
    for i, x in enumerate(scalars):
        out = jnp.where(chain == i, x, out)
    return out


def local_kernel(
    page_len,
    heads,
    table_ref,
    context_ref,
    fill_ref,
    q_ref,
    new_ref,
    freq_ref,
    sign_ref,
    cache_ref,
    o_ref,
    stat_ref,
    kv,
    sems,
    kf,
    vf,
    position,
    where,
):
    rows, block, head_dim = q_ref.shape
    rows = rows - 1
    steps = new_ref.shape[0]
    most = table_ref.shape[0]
    group = block // heads
    per = group // steps
    together = LANES // block

    zeros = rows * most

    def copy(r, j):
        n = r * most + j
        return pltpu.make_async_copy(cache_ref.at[table_ref[j, r]], kv.at[n], sems.at[n])

    def seen_tokens(r, j):
        return jnp.minimum(fill_ref[table_ref[j, r]], context_ref[r] - j * page_len)

    for r in range(rows):
        for j in range(most):
            needed = seen_tokens(r, j) > 0
            where[r * most + j] = jnp.where(needed, r * most + j, zeros)
            pl.when(needed)(copy(r, j).start)
    kv[zeros] = jnp.zeros(kv.shape[1:], BF16)
    kf[...] = jnp.zeros_like(kf)
    vf[...] = jnp.zeros_like(vf)
    for r in range(rows):
        position[r : r + 1, :] = jnp.full((1, head_dim), context_ref[r], I32)
    for u in range(steps):
        angle = (position[...] + u).astype(F32) * freq_ref[...]
        cos, sin = jnp.cos(angle), jnp.sin(angle) * sign_ref[...]
        for k in range(heads):
            x = new_ref[u, :, k * head_dim : (k + 1) * head_dim].astype(F32)
            at = k * group + u
            kf[pl.ds(at, rows, stride=block), :] = x * cos + pltpu.roll(x, head_dim // 2, 1) * sin
            x = new_ref[u, :, (heads + k) * head_dim : (heads + k + 1) * head_dim].astype(F32)
            vf[pl.ds(at, rows, stride=block), :] = x
    token = lax.broadcasted_iota(I32, (page_len, LANES), 0)
    fresh = lax.broadcasted_iota(I32, (group, LANES), 0)
    step = lax.broadcasted_iota(I32, (group, LANES), 1) % group // per
    fresh_mask = (fresh <= step) & (fresh < steps)

    for i in range(rows // together):
        requests = range(i * together, (i + 1) * together)
        chains = [(r, k) for r in requests for k in range(heads)]
        if i % 2 == 0:
            for r in range(i * together, min(rows, (i + 2) * together)):
                for j in range(most):
                    pl.when(where[r * most + j] < zeros)(copy(r, j).wait)
        queries = q_ref[i * together : (i + 1) * together].reshape(LANES, head_dim)
        keys, values = [], []
        for r, k in chains:
            at = r * block + k * group
            page = lambda what: [kv[where[r * most + j], what, k] for j in range(most)]
            keys.append(jnp.concatenate(page(0) + [kf[at : at + group, :].astype(BF16)], axis=0))
            values.append(page(1) + [vf[at : at + group, :].astype(BF16)])
        scores = transposed_scores(queries, keys, group)
        mask = []
        for j in range(most):
            seen = [seen_tokens(r, j) for r in requests]
            mask.append(token < lane_values(seen, block, (1, LANES)))
        parts = [
            jnp.where(m, scores[n * page_len : n * page_len + m.shape[0]], -jnp.inf)
            for n, m in enumerate(mask + [fresh_mask])
        ]
        top = functools.reduce(jnp.maximum, [jnp.max(x, axis=0, keepdims=True) for x in parts])
        parts = [jnp.exp(x - top) for x in parts]
        total = functools.reduce(jnp.add, [jnp.sum(x, axis=0, keepdims=True) for x in parts])
        stats = jnp.concatenate(
            [parts[most], jnp.broadcast_to(top, (8, LANES)), jnp.broadcast_to(total, (8, LANES))]
            + [jnp.zeros((LANES - group - 16, LANES), F32)],
            axis=0,
        )
        stats = jnp.transpose(stats, (1, 0))
        weights = [jnp.transpose(x, (1, 0)).astype(BF16) for x in parts[:most]]
        weights.append(stats[:, :group].astype(BF16))
        weights = jnp.concatenate(weights, axis=1)
        for x in range(together):
            both = [jnp.concatenate(values[x * heads + k], axis=0) for k in range(heads)]
            both = weighted_values(weights[x * block : (x + 1) * block, :], both)
            o_ref[i * LANES + x * block : i * LANES + (x + 1) * block, :] = both
        stat_ref[i * LANES : (i + 1) * LANES, :] = stats


def local_attention(table, context, fills, queries, new_kv, cache_kv, tabs):
    rows, block, _ = queries.shape
    rows = rows - 1
    steps = new_kv.shape[0]
    slots, _, heads, page_len, head_dim = cache_kv.shape
    flat = (rows * block, head_dim)
    freq, sign = tabs[4:]
    return pl.pallas_call(
        functools.partial(local_kernel, page_len, heads),
        out_shape=[jax.ShapeDtypeStruct(flat, F32)] * 2,
        in_specs=[SMEM] * 3 + [VMEM] * 4 + [ANY],
        out_specs=[VMEM] * 2,
        scratch_shapes=[
            pltpu.VMEM((table.size + 1, 2, heads, page_len, head_dim), BF16),
            pltpu.SemaphoreType.DMA((table.size,)),
            pltpu.VMEM(flat, F32),
            pltpu.VMEM(flat, F32),
            pltpu.VMEM((rows, head_dim), I32),
            pltpu.SMEM((table.size,), I32),
        ],
        compiler_params=PARAMS,
        cost_estimate=pl.CostEstimate(flops=800_000_000, bytes_accessed=12_000_000, transcendentals=400_000),
        name="local_attention",
    )(
        *[in_hbm(x) for x in (table, context, fills)],
        queries,
        new_kv.reshape(steps, rows, 2 * heads * head_dim),
        *[in_hbm(x) for x in (freq, sign, cache_kv)],
    )


def pieces(x):
    high = x.astype(BF16).astype(F32)
    middle = (x - high).astype(BF16).astype(F32)
    return [high, middle, x - high - middle]


def arrived_kernel(npool, pair, me_ref, own_ref, *refs):
    blocks = refs[:npool]
    pages_ref, out_ref, queries = refs[npool:]
    items = npool * pair
    _, _, heads, page_len, head_dim = pages_ref.shape
    rows, block = blocks[0].shape[0] - 1, blocks[0].shape[1]
    group = block // heads
    together = LANES // block
    me = me_ref[0]
    owners = [owner_of(me, npool, apart, flip) for apart, flip in block_order(npool)]
    lane = lax.broadcasted_iota(I32, (1, LANES), 1)
    codes = [x[rows, :STAT_ROWS, :].astype(F32) for x in blocks]
    codes = [x[0:1] * CODE + x[1:2] for x in codes]
    number, seen, request = [], [], []
    for x in range(items):
        at = owners[x // pair] * pair + x % pair
        slot = own_ref[2 * items + at]
        code = jnp.maximum(read_scalar(codes[x // pair], lane == slot), 0)
        reader, left = code // CODE, code % CODE
        queries[x * block : (x + 1) * block, :] = blocks[x // pair][reader]
        number.append(own_ref[at])
        seen.append(jnp.minimum(left, own_ref[items + at]))
        request.append(jnp.where(slot >= 0, reader, -1))
    token = lax.broadcasted_iota(I32, (page_len, LANES), 0)
    for i in range(items // together):
        own = range(i * together, (i + 1) * together)
        keys = [pages_ref[number[x], 0, k] for x in own for k in range(heads)]
        scores = transposed_scores(queries[i * LANES : (i + 1) * LANES, :], keys, group)
        limit = lane_values([seen[x] for x in own], block, (1, LANES))
        scores = jnp.where(token < limit, scores, -jnp.inf)
        top = jnp.max(scores, axis=0, keepdims=True)
        top = jnp.where(top > -jnp.inf, top, 0.0)
        weights = jnp.exp(scores - top)
        stats = pieces(top) + pieces(jnp.sum(weights, axis=0, keepdims=True))
        stats.append(lane_values([request[x] for x in own], block, (1, LANES)).astype(F32))
        stats = jnp.concatenate(stats + [jnp.zeros((STAT_ROWS - len(stats), LANES), F32)], axis=0).astype(BF16)
        weights = jnp.transpose(weights, (1, 0)).astype(BF16)
        for c, x in enumerate(own):
            both = [pages_ref[number[x], 1, k] for k in range(heads)]
            both = weighted_values(weights[c * block : (c + 1) * block, :], both)
            at = (x % pair) * block
            out_ref[owners[x // pair], at : at + block, :] = both.astype(BF16)
        for place in sorted({x // pair for x in own}):
            out_ref[owners[place], pair * block : pair * block + STAT_ROWS, :] = stats


def arrived_attention(me, own, blocks, arrived):
    npool = len(blocks)
    head_dim = arrived.shape[4]
    block = blocks[0].shape[1]
    items = own.shape[0] // 3
    pair = items // npool
    return pl.pallas_call(
        functools.partial(arrived_kernel, npool, pair),
        out_shape=jax.ShapeDtypeStruct((npool, pair * block + STAT_ROWS, head_dim), BF16),
        in_specs=[SMEM] * 2 + [VMEM] * (npool + 1),
        out_specs=VMEM,
        scratch_shapes=[pltpu.VMEM((items * block, head_dim), BF16)],
        compiler_params=PARAMS,
        cost_estimate=pl.CostEstimate(flops=200_000_000, bytes_accessed=4_000_000, transcendentals=70_000),
        name="arrived_attention",
    )(me, own, *blocks, arrived)


def merge_kernel(pair, heads, me_ref, parts_ref, o_ref, stat_ref, out_ref, mixed, top, total, turned):
    npool = parts_ref.shape[0]
    steps, rows, width = out_ref.shape
    head_dim = o_ref.shape[1]
    per = width // head_dim // heads
    group = steps * per
    block = heads * group
    me = me_ref[0]
    shape = top.shape
    mixed[...] = o_ref[...]
    top[...] = jnp.broadcast_to(stat_ref[:, group : group + 1], shape)
    total[...] = jnp.broadcast_to(stat_ref[:, group + 8 : group + 9], shape)
    tops, totals, readers = [], [], []
    chain = lax.broadcasted_iota(I32, (1, LANES), 1) // block
    for d in range(npool):
        x = parts_ref[d, pair * block : pair * block + STAT_ROWS, :].astype(F32)
        tops.append(x[0:1] + x[1:2] + x[2:3])
        totals.append(x[3:4] + x[4:5] + x[5:6])
        readers.append(x[6:7])
    empty = [jnp.zeros((LANES // 2 - npool, LANES), F32)]
    turned[...] = jnp.transpose(jnp.concatenate(tops + empty + totals + empty, axis=0), (1, 0))
    for d in range(npool):
        for p in range(pair):
            part = lax.rem(place_of(me, npool, d) * pair + p, LANES // block)
            r = read_scalar(readers[d], chain == part)
            there = r >= 0
            at = pl.ds(pl.multiple_of(jnp.maximum(r, 0) * block, block), block)
            lane = pl.ds(pl.multiple_of(part * block, block), block)
            m = jnp.broadcast_to(turned[lane, d : d + 1], (block, head_dim))
            l = jnp.broadcast_to(turned[lane, LANES // 2 + d : LANES // 2 + d + 1], (block, head_dim))
            seen = (l > 0.0) & there
            o = parts_ref[d, p * block : (p + 1) * block, :].astype(F32)
            old = top[at, :]
            new = jnp.where(seen, jnp.maximum(old, m), old)
            a = jnp.exp(old - new)
            b = jnp.where(seen, jnp.exp(m - new), 0.0)
            top[at, :] = new
            total[at, :] = total[at, :] * a + l * b
            mixed[at, :] = mixed[at, :] * a + o * b
    for s in range(steps):
        for h in range(heads * per):
            k, g = divmod(h, per)
            at = pl.ds(k * group + s * per + g, rows, stride=block)
            out_ref[s, :, h * head_dim : (h + 1) * head_dim] = (mixed[at, :] / total[at, :]).astype(BF16)


def merged(me, parts, local, shape, heads, pair):
    flat = local[0].shape
    return pl.pallas_call(
        functools.partial(merge_kernel, pair, heads),
        out_shape=jax.ShapeDtypeStruct(shape, BF16),
        in_specs=[SMEM] + [VMEM] * 3,
        out_specs=VMEM,
        scratch_shapes=[pltpu.VMEM(flat, F32)] * 3 + [pltpu.VMEM((LANES, LANES), F32)],
        compiler_params=PARAMS,
        cost_estimate=pl.CostEstimate(flops=2_000_000, bytes_accessed=1_500_000, transcendentals=100_000),
        name="merge",
    )(me, parts, *local)


def fetch_kernel(weight_ref, x_ref, weight_out, x_out, sems):
    copies = [
        pltpu.make_async_copy(weight_ref, weight_out, sems.at[0]),
        pltpu.make_async_copy(x_ref, x_out, sems.at[1]),
    ]
    for copy in copies:
        copy.start()
    for copy in copies:
        copy.wait()


def fetched(weight, x):
    return pl.pallas_call(
        fetch_kernel,
        out_shape=[pltpu.VMEM(weight.shape, weight.dtype), pltpu.VMEM(x.shape, x.dtype)],
        in_specs=[ANY, ANY],
        out_specs=[ANY, ANY],
        scratch_shapes=[pltpu.SemaphoreType.DMA((2,))],
        compiler_params=PARAMS,
        cost_estimate=pl.CostEstimate(flops=0, bytes_accessed=2 * weight.size * 2, transcendentals=0),
        name="fetch_weight",
    )(in_hbm(weight), x)


def rows_kernel(npool, place_ref, *refs):
    blocks = refs[:npool]
    weight_ref, out_ref, lhs = refs[npool:]
    steps, rows, _ = blocks[0].shape
    every = npool * rows
    for x, (apart, flip) in enumerate(block_order(npool)):
        owner = owner_of(place_ref[0], npool, apart, flip)
        for s in range(steps):
            lhs[pl.ds(pl.multiple_of(s * every + owner * rows, rows), rows), :] = blocks[x][s]
    multiply(lhs, weight_ref, out_ref, 1 - place_ref[1])


def multiply(lhs, weight_ref, out_ref, which):
    steps, every, half = out_ref.shape
    tile = min(half, 256)
    for i in range(half // tile):
        at = pl.ds(pl.multiple_of(which * half + i * tile, LANES), tile)
        terms = jnp.dot(lhs[...], weight_ref[:, at], preferred_element_type=F32)
        for s in range(steps):
            out_ref[s, :, i * tile : (i + 1) * tile] = terms[s * every : (s + 1) * every]


def other_projection(place, blocks, weight):
    npool = len(blocks)
    steps, rows, width = blocks[0].shape
    half = weight.shape[1] // 2
    every = steps * npool * rows
    return pl.pallas_call(
        functools.partial(rows_kernel, npool),
        out_shape=[
            jax.ShapeDtypeStruct((steps, npool * rows, half), F32),
            jax.ShapeDtypeStruct((every, width), BF16),
        ],
        in_specs=[SMEM] + [VMEM] * (npool + 1),
        out_specs=[VMEM] * 2,
        compiler_params=PARAMS,
        cost_estimate=pl.CostEstimate(flops=2 * every * width * half, bytes_accessed=4_000_000, transcendentals=0),
        name="project_other",
    )(place, *blocks, weight)


def own_kernel(place_ref, lhs, weight_ref, out_ref):
    multiply(lhs, weight_ref, out_ref, place_ref[1])


def own_projection(place, lhs, weight, steps):
    every, width = lhs.shape
    half = weight.shape[1] // 2
    return pl.pallas_call(
        own_kernel,
        out_shape=jax.ShapeDtypeStruct((steps, every // steps, half), F32),
        in_specs=[SMEM] + [VMEM] * 2,
        out_specs=VMEM,
        compiler_params=PARAMS,
        cost_estimate=pl.CostEstimate(flops=2 * every * width * half, bytes_accessed=4_000_000, transcendentals=0),
        name="project_own",
    )(place, lhs, weight)


def block_order(npool):
    return [(apart, flip) for flip in (0, 1) for apart in range(npool // 2)]


def owner_of(me, npool, apart, flip):
    half = npool // 2
    pair, side = me // 2, me % 2
    side = 1 - side if flip else side
    return lax.rem(pair + half - apart, half) * 2 + side


def place_of(me, npool, holder):
    half = npool // 2
    apart = lax.rem(holder // 2 - me // 2 + half, half)
    flip = lax.rem(me + holder, 2)
    return flip * half + apart


def in_hbm(x):
    return pltpu.with_memory_space_constraint(x, pltpu.HBM)


def gathered(x, npool, later=None):
    half = npool // 2
    later = x if later is None else later
    ahead = lambda x, by: lax.ppermute(x, "pool", [(i, (i + 2 * by) % npool) for i in range(npool)])
    across = lambda x: lax.ppermute(x, "pool", [(i, i ^ 1) for i in range(npool)])
    straight = [x] + [ahead(x if by == half // 2 else later, by) for by in range(1, half)]
    return straight + [across(y) for y in straight]


def swap_halves(x):
    return lax.ppermute(x, "tp", [(0, 1), (1, 0)])


def shards(
    prompt_kv,
    prompt_lengths,
    page_slot,
    cache_kv,
    cache_fill,
    page_table,
    context_lengths,
    queries,
    new_kv,
    out_weight,
):
    npool = lax.axis_size("pool")
    me = lax.axis_index("pool").astype(I32)
    pages, _, heads, page_len, head_dim = prompt_kv.shape
    cache_pages = cache_kv.shape[0]
    pair = (pages + npool - 1) // npool
    tabs = tables(page_len, head_dim, pages)
    place = jnp.stack([me, lax.axis_index("tp").astype(I32)])
    table = page_table.T

    asked = asked_queries(table, context_lengths, queries, page_len, heads, head_dim)
    asked_all = gathered(asked, npool)
    arrived, own = rotated_pages(prompt_kv, page_slot, prompt_lengths, tabs, npool, pair, cache_pages)
    local = local_attention(table, context_lengths, cache_fill, asked, new_kv, cache_kv, tabs)
    parts = arrived_attention(place, own, asked_all, arrived)
    parts = lax.all_to_all(parts, "pool", split_axis=0, concat_axis=0, tiled=True)
    attention = merged(place, parts, local, queries.shape, heads, pair)
    weight, again = fetched(out_weight, attention)
    blocks = gathered(attention, npool, again)
    other_terms, lhs = other_projection(place, blocks, weight)
    other_terms = swap_halves(other_terms)
    terms = own_projection(place, lhs, weight, queries.shape[0])
    return (terms + other_terms).astype(BF16)


def solution(mesh):
    return jax.shard_map(
        shards,
        mesh=mesh,
        in_specs=(
            P(("group", "pool"), None, "tp", None, None),
            P(("group", "pool"), None),
            P(("group", "pool")),
            P(("group", "pool"), None, "tp", None, None),
            P(("group", "pool")),
            P(("group", "pool"), None),
            P(("group", "pool")),
            P(None, ("group", "pool"), "tp"),
            P(None, ("group", "pool"), None, "tp", None),
            P("tp", "pool"),
        ),
        out_specs=P(None, "group", ("pool", "tp")),
        check_vma=False,
    )
```

```python
import functools

import jax
import jax.numpy as jnp
import numpy as np
from jax import lax
from jax.experimental import pallas as pl
from jax.experimental.pallas import tpu as pltpu
from jax.sharding import PartitionSpec as P

ROPE_BASE = 500000.0
BF16, F32, I32 = jnp.bfloat16, jnp.float32, jnp.int32
SMEM = pl.BlockSpec(memory_space=pltpu.SMEM)
VMEM = pl.BlockSpec(memory_space=pltpu.VMEM)
ANY = pl.BlockSpec(memory_space=pl.ANY)
PARAMS = pltpu.CompilerParams(vmem_limit_bytes=24 * 2**20)
LANES = 128
STAT_ROWS = 16
CODE = 256


def tables(page_len, head_dim, pages):
    half = head_dim // 2
    freq = ROPE_BASE ** (-(np.arange(half) * 2.0) / head_dim)
    freq = np.concatenate([freq, freq])[None, :]
    sign = np.concatenate([-np.ones(half), np.ones(half)])[None, :]
    token = np.arange(page_len)[:, None] * freq
    first = np.arange(pages)[:, None] * page_len * freq
    out = (np.cos(token), sign * np.sin(token), np.cos(first), sign * np.sin(first), freq, sign)
    return [jnp.asarray(x, F32) for x in out]


def rope_kernel(
    npool, cache_pages, per, slot_ref, len_ref, pages_ref, ct_ref, st_ref, cp_ref, sp_ref, out_ref, own_ref, count
):
    _, _, heads, page_len, head_dim = pages_ref.shape

    @pl.when(pl.program_id(0) == 0)
    def _():
        items = own_ref.shape[0] // 3
        for e in range(npool):
            count[e] = 0
        for i in range(items):
            own_ref[i] = 0
            own_ref[items + i] = 0
            own_ref[2 * items + i] = -1
        for n in range(slot_ref.shape[0]):
            slot = slot_ref[n]
            target = slot // cache_pages
            at = target * (items // npool) + count[target]
            count[target] = count[target] + 1
            own_ref[at] = n
            own_ref[items + at] = page_place(len_ref, page_len, n)[1]
            own_ref[2 * items + at] = slot - target * cache_pages

    for i in range(per):
        number, _ = page_place(len_ref, page_len, pl.program_id(0) * per + i)
        c0, s0 = cp_ref[pl.ds(number, 1), :], sp_ref[pl.ds(number, 1), :]
        ct, st = ct_ref[...], st_ref[...]
        cos = c0 * ct - s0 * st
        sin = s0 * ct + c0 * st
        for k in range(heads):
            x = pages_ref[i, 0, k].astype(F32)
            out_ref[i, 0, k] = (x * cos + pltpu.roll(x, head_dim // 2, 1) * sin).astype(BF16)
            out_ref[i, 1, k] = pages_ref[i, 1, k]


def page_place(len_ref, page_len, n):
    begin = jnp.int32(0)
    number, fill = jnp.int32(0), jnp.int32(0)
    for q in range(len_ref.shape[1]):
        length = len_ref[0, q]
        count = (length + page_len - 1) // page_len
        here = (n >= begin) & (n < begin + count)
        number = jnp.where(here, n - begin, number)
        fill = jnp.where(here, jnp.clip(length - (n - begin) * page_len, 0, page_len), fill)
        begin = begin + count
    return number, fill


def rotated_pages(prompt_kv, page_slot, prompt_lengths, tabs, npool, pair, cache_pages):
    pages, _, heads, page_len, head_dim = prompt_kv.shape
    per = pages // 2
    ct, st, cp, sp, _, _ = tabs
    whole = lambda x: pl.BlockSpec(x.shape, lambda i: (0, 0))
    return pl.pallas_call(
        functools.partial(rope_kernel, npool, cache_pages, per),
        grid=(pages // per,),
        out_shape=[
            jax.ShapeDtypeStruct(prompt_kv.shape, BF16),
            jax.ShapeDtypeStruct((3 * npool * pair,), I32),
        ],
        in_specs=[
            SMEM,
            SMEM,
            pl.BlockSpec((per,) + prompt_kv.shape[1:], lambda i: (i, 0, 0, 0, 0)),
            whole(ct),
            whole(st),
            whole(cp),
            whole(sp),
        ],
        out_specs=[pl.BlockSpec((per,) + prompt_kv.shape[1:], lambda i: (i, 0, 0, 0, 0)), SMEM],
        scratch_shapes=[pltpu.SMEM((npool,), I32)],
        compiler_params=PARAMS,
        cost_estimate=pl.CostEstimate(flops=6_000_000, bytes_accessed=2_000_000, transcendentals=0),
        name="rope_pages",
    )(*[in_hbm(x) for x in (page_slot, prompt_lengths, prompt_kv, ct, st, cp, sp)])


def asked_kernel(page_len, heads, table_ref, context_ref, q_ref, out_ref, spread):
    most, rows = table_ref.shape
    steps, _, width = q_ref.shape
    block, head_dim = out_ref.shape[1:]
    per = width // head_dim // heads
    for s in range(steps):
        for h in range(heads * per):
            k, g = divmod(h, per)
            at = pl.ds(k * steps * per + s * per + g, rows, stride=block)
            spread[at, :] = q_ref[s, :, h * head_dim : (h + 1) * head_dim].astype(F32)
    for r in range(rows):
        out_ref[r] = spread[r * block : (r + 1) * block, :].astype(BF16)
    lane = lax.broadcasted_iota(I32, (block, LANES), 1)
    line = lax.broadcasted_iota(I32, (block, LANES), 0)
    request = jnp.zeros((block, LANES), I32)
    left = jnp.zeros((block, LANES), I32)
    for r in range(rows):
        context = context_ref[r]
        for j in range(most):
            here = lane == table_ref[j, r]
            request = jnp.where(here, r, request)
            left = jnp.where(here, jnp.clip(context - j * page_len, 0, page_len), left)
    out_ref[rows] = jnp.where(line == 0, request, left).astype(F32).astype(BF16)


def asked_queries(table, context, queries, page_len, heads, head_dim):
    steps, rows, width = queries.shape
    block = steps * width // head_dim
    return pl.pallas_call(
        functools.partial(asked_kernel, page_len, heads),
        out_shape=jax.ShapeDtypeStruct((rows + 1, block, head_dim), BF16),
        in_specs=[SMEM, SMEM, VMEM],
        out_specs=VMEM,
        scratch_shapes=[pltpu.VMEM((rows * block, head_dim), F32)],
        compiler_params=PARAMS,
        cost_estimate=pl.CostEstimate(flops=100_000, bytes_accessed=300_000, transcendentals=0),
        name="asked_queries",
    )(in_hbm(table), in_hbm(context), in_hbm(queries))


def read_scalar(x, pick):
    return jnp.max(jnp.where(pick, x, -2.0)).astype(I32)


def transposed_scores(queries, keys, group):
    turned = jnp.transpose(queries, (1, 0))
    chain = lax.broadcasted_iota(I32, (1, turned.shape[1]), 1) // group
    spread = [turned * jnp.where(chain == c, 1.0, 0.0).astype(BF16) for c in range(len(keys))]
    scores = jnp.dot(
        jnp.concatenate(keys, axis=1), jnp.concatenate(spread, axis=0), preferred_element_type=F32
    )
    return scores * (queries.shape[1] ** -0.5)


def weighted_values(weights, values):
    heads, head_dim = len(values), values[0].shape[1]
    group = weights.shape[0] // heads
    out = jnp.dot(weights, jnp.concatenate(values, axis=1), preferred_element_type=F32)
    parts = [out[k * group : (k + 1) * group, k * head_dim : (k + 1) * head_dim] for k in range(heads)]
    return jnp.concatenate(parts, axis=0)


def lane_values(scalars, lanes_each, shape):
    chain = lax.broadcasted_iota(I32, shape, 1) // lanes_each
    out = jnp.zeros(shape, I32)
    for i, x in enumerate(scalars):
        out = jnp.where(chain == i, x, out)
    return out


def local_kernel(
    page_len,
    heads,
    table_ref,
    context_ref,
    fill_ref,
    q_ref,
    new_ref,
    freq_ref,
    sign_ref,
    cache_ref,
    o_ref,
    stat_ref,
    kv,
    sems,
    kf,
    vf,
    position,
    where,
):
    rows, block, head_dim = q_ref.shape
    rows = rows - 1
    steps = new_ref.shape[0]
    most = table_ref.shape[0]
    group = block // heads
    per = group // steps
    together = LANES // block

    zeros = rows * most

    def copy(r, j):
        n = r * most + j
        return pltpu.make_async_copy(cache_ref.at[table_ref[j, r]], kv.at[n], sems.at[n])

    def seen_tokens(r, j):
        return jnp.minimum(fill_ref[table_ref[j, r]], context_ref[r] - j * page_len)

    for r in range(rows):
        for j in range(most):
            needed = seen_tokens(r, j) > 0
            where[r * most + j] = jnp.where(needed, r * most + j, zeros)
            pl.when(needed)(copy(r, j).start)
    kv[zeros] = jnp.zeros(kv.shape[1:], BF16)
    kf[...] = jnp.zeros_like(kf)
    vf[...] = jnp.zeros_like(vf)
    for r in range(rows):
        position[r : r + 1, :] = jnp.full((1, head_dim), context_ref[r], I32)
    for u in range(steps):
        angle = (position[...] + u).astype(F32) * freq_ref[...]
        cos, sin = jnp.cos(angle), jnp.sin(angle) * sign_ref[...]
        for k in range(heads):
            x = new_ref[u, :, k * head_dim : (k + 1) * head_dim].astype(F32)
            at = k * group + u
            kf[pl.ds(at, rows, stride=block), :] = x * cos + pltpu.roll(x, head_dim // 2, 1) * sin
            x = new_ref[u, :, (heads + k) * head_dim : (heads + k + 1) * head_dim].astype(F32)
            vf[pl.ds(at, rows, stride=block), :] = x
    token = lax.broadcasted_iota(I32, (page_len, LANES), 0)
    fresh = lax.broadcasted_iota(I32, (group, LANES), 0)
    step = lax.broadcasted_iota(I32, (group, LANES), 1) % group // per
    fresh_mask = (fresh <= step) & (fresh < steps)

    for i in range(rows // together):
        requests = range(i * together, (i + 1) * together)
        chains = [(r, k) for r in requests for k in range(heads)]
        if i % 2 == 0:
            for r in range(i * together, min(rows, (i + 2) * together)):
                for j in range(most):
                    pl.when(where[r * most + j] < zeros)(copy(r, j).wait)
        queries = q_ref[i * together : (i + 1) * together].reshape(LANES, head_dim)
        keys, values = [], []
        for r, k in chains:
            at = r * block + k * group
            page = lambda what: [kv[where[r * most + j], what, k] for j in range(most)]
            keys.append(jnp.concatenate(page(0) + [kf[at : at + group, :].astype(BF16)], axis=0))
            values.append(page(1) + [vf[at : at + group, :].astype(BF16)])
        scores = transposed_scores(queries, keys, group)
        mask = []
        for j in range(most):
            seen = [seen_tokens(r, j) for r in requests]
            mask.append(token < lane_values(seen, block, (1, LANES)))
        parts = [
            jnp.where(m, scores[n * page_len : n * page_len + m.shape[0]], -jnp.inf)
            for n, m in enumerate(mask + [fresh_mask])
        ]
        top = functools.reduce(jnp.maximum, [jnp.max(x, axis=0, keepdims=True) for x in parts])
        parts = [jnp.exp(x - top) for x in parts]
        total = functools.reduce(jnp.add, [jnp.sum(x, axis=0, keepdims=True) for x in parts])
        stats = jnp.concatenate(
            [parts[most], jnp.broadcast_to(top, (8, LANES)), jnp.broadcast_to(total, (8, LANES))], axis=0
        )
        stats = jnp.transpose(stats, (1, 0))
        weights = [jnp.transpose(x.astype(BF16), (1, 0)) for x in parts[:most]]
        weights.append(stats[:, :group].astype(BF16))
        weights = jnp.concatenate(weights, axis=1)
        for x in range(together):
            both = [jnp.concatenate(values[x * heads + k], axis=0) for k in range(heads)]
            both = weighted_values(weights[x * block : (x + 1) * block, :], both)
            o_ref[i * LANES + x * block : i * LANES + (x + 1) * block, :] = both
        stat_ref[i * LANES : (i + 1) * LANES, : stats.shape[1]] = stats


def local_attention(table, context, fills, queries, new_kv, cache_kv, tabs):
    rows, block, _ = queries.shape
    rows = rows - 1
    steps = new_kv.shape[0]
    slots, _, heads, page_len, head_dim = cache_kv.shape
    flat = (rows * block, head_dim)
    freq, sign = tabs[4:]
    return pl.pallas_call(
        functools.partial(local_kernel, page_len, heads),
        out_shape=[jax.ShapeDtypeStruct(flat, F32)] * 2,
        in_specs=[SMEM] * 3 + [VMEM] * 4 + [ANY],
        out_specs=[VMEM] * 2,
        scratch_shapes=[
            pltpu.VMEM((table.size + 1, 2, heads, page_len, head_dim), BF16),
            pltpu.SemaphoreType.DMA((table.size,)),
            pltpu.VMEM(flat, F32),
            pltpu.VMEM(flat, F32),
            pltpu.VMEM((rows, head_dim), I32),
            pltpu.SMEM((table.size,), I32),
        ],
        compiler_params=PARAMS,
        cost_estimate=pl.CostEstimate(flops=800_000_000, bytes_accessed=12_000_000, transcendentals=400_000),
        name="local_attention",
    )(
        *[in_hbm(x) for x in (table, context, fills)],
        queries,
        new_kv.reshape(steps, rows, 2 * heads * head_dim),
        *[in_hbm(x) for x in (freq, sign, cache_kv)],
    )


def pieces(x):
    high = x.astype(BF16).astype(F32)
    middle = (x - high).astype(BF16).astype(F32)
    return [high, middle, x - high - middle]


def arrived_kernel(npool, pair, me_ref, own_ref, *refs):
    blocks = refs[:npool]
    pages_ref, out_ref, queries = refs[npool:]
    items = npool * pair
    _, _, heads, page_len, head_dim = pages_ref.shape
    rows, block = blocks[0].shape[0] - 1, blocks[0].shape[1]
    group = block // heads
    together = LANES // block
    me = me_ref[0]
    owners = [owner_of(me, npool, apart, flip) for apart, flip in block_order(npool)]
    lane = lax.broadcasted_iota(I32, (1, LANES), 1)
    codes = [x[rows, :STAT_ROWS, :].astype(F32) for x in blocks]
    codes = [x[0:1] * CODE + x[1:2] for x in codes]
    number, seen, request = [], [], []
    for x in range(items):
        at = owners[x // pair] * pair + x % pair
        slot = own_ref[2 * items + at]
        code = jnp.maximum(read_scalar(codes[x // pair], lane == slot), 0)
        reader, left = code // CODE, code % CODE
        queries[x * block : (x + 1) * block, :] = blocks[x // pair][reader]
        number.append(own_ref[at])
        seen.append(jnp.minimum(left, own_ref[items + at]))
        request.append(jnp.where(slot >= 0, reader, -1))
    token = lax.broadcasted_iota(I32, (page_len, LANES), 0)
    for i in range(items // together):
        own = range(i * together, (i + 1) * together)
        keys = [pages_ref[number[x], 0, k] for x in own for k in range(heads)]
        scores = transposed_scores(queries[i * LANES : (i + 1) * LANES, :], keys, group)
        limit = lane_values([seen[x] for x in own], block, (1, LANES))
        scores = jnp.where(token < limit, scores, -jnp.inf)
        top = jnp.max(scores, axis=0, keepdims=True)
        top = jnp.where(top > -jnp.inf, top, 0.0)
        weights = jnp.exp(scores - top)
        stats = pieces(top) + pieces(jnp.sum(weights, axis=0, keepdims=True))
        stats.append(lane_values([request[x] for x in own], block, (1, LANES)).astype(F32))
        stats = jnp.concatenate(stats + [jnp.zeros((STAT_ROWS - len(stats), LANES), F32)], axis=0).astype(BF16)
        weights = jnp.transpose(weights.astype(BF16), (1, 0))
        for c, x in enumerate(own):
            both = [pages_ref[number[x], 1, k] for k in range(heads)]
            both = weighted_values(weights[c * block : (c + 1) * block, :], both)
            at = (x % pair) * block
            out_ref[owners[x // pair], at : at + block, :] = both.astype(BF16)
        for place in sorted({x // pair for x in own}):
            out_ref[owners[place], pair * block : pair * block + STAT_ROWS, :] = stats


def arrived_attention(me, own, blocks, arrived):
    npool = len(blocks)
    head_dim = arrived.shape[4]
    block = blocks[0].shape[1]
    items = own.shape[0] // 3
    pair = items // npool
    return pl.pallas_call(
        functools.partial(arrived_kernel, npool, pair),
        out_shape=jax.ShapeDtypeStruct((npool, pair * block + STAT_ROWS, head_dim), BF16),
        in_specs=[SMEM] * 2 + [VMEM] * (npool + 1),
        out_specs=VMEM,
        scratch_shapes=[pltpu.VMEM((items * block, head_dim), BF16)],
        compiler_params=PARAMS,
        cost_estimate=pl.CostEstimate(flops=200_000_000, bytes_accessed=4_000_000, transcendentals=70_000),
        name="arrived_attention",
    )(me, own, *blocks, arrived)


def merge_kernel(pair, heads, me_ref, parts_ref, o_ref, stat_ref, out_ref, mixed, top, total, turned):
    npool = parts_ref.shape[0]
    steps, rows, width = out_ref.shape
    head_dim = o_ref.shape[1]
    per = width // head_dim // heads
    group = steps * per
    block = heads * group
    me = me_ref[0]
    shape = top.shape
    mixed[...] = o_ref[...]
    top[...] = jnp.broadcast_to(stat_ref[:, group : group + 1], shape)
    total[...] = jnp.broadcast_to(stat_ref[:, group + 8 : group + 9], shape)
    tops, totals, readers = [], [], []
    chain = lax.broadcasted_iota(I32, (1, LANES), 1) // block
    for d in range(npool):
        x = parts_ref[d, pair * block : pair * block + STAT_ROWS, :].astype(F32)
        tops.append(x[0:1] + x[1:2] + x[2:3])
        totals.append(x[3:4] + x[4:5] + x[5:6])
        readers.append(x[6:7])
    empty = [jnp.zeros((LANES // 2 - npool, LANES), F32)]
    turned[...] = jnp.transpose(jnp.concatenate(tops + empty + totals + empty, axis=0), (1, 0))
    for d in range(npool):
        for p in range(pair):
            part = lax.rem(place_of(me, npool, d) * pair + p, LANES // block)
            r = read_scalar(readers[d], chain == part)
            there = r >= 0
            at = pl.ds(pl.multiple_of(jnp.maximum(r, 0) * block, block), block)
            lane = pl.ds(pl.multiple_of(part * block, block), block)
            m = jnp.broadcast_to(turned[lane, d : d + 1], (block, head_dim))
            l = jnp.broadcast_to(turned[lane, LANES // 2 + d : LANES // 2 + d + 1], (block, head_dim))
            seen = (l > 0.0) & there
            o = parts_ref[d, p * block : (p + 1) * block, :].astype(F32)
            old = top[at, :]
            new = jnp.where(seen, jnp.maximum(old, m), old)
            a = jnp.exp(old - new)
            b = jnp.where(seen, jnp.exp(m - new), 0.0)
            top[at, :] = new
            total[at, :] = total[at, :] * a + l * b
            mixed[at, :] = mixed[at, :] * a + o * b
    for s in range(steps):
        for h in range(heads * per):
            k, g = divmod(h, per)
            at = pl.ds(k * group + s * per + g, rows, stride=block)
            out_ref[s, :, h * head_dim : (h + 1) * head_dim] = (mixed[at, :] / total[at, :]).astype(BF16)


def merged(me, parts, local, shape, heads, pair):
    flat = local[0].shape
    return pl.pallas_call(
        functools.partial(merge_kernel, pair, heads),
        out_shape=jax.ShapeDtypeStruct(shape, BF16),
        in_specs=[SMEM] + [VMEM] * 3,
        out_specs=VMEM,
        scratch_shapes=[pltpu.VMEM(flat, F32)] * 3 + [pltpu.VMEM((LANES, LANES), F32)],
        compiler_params=PARAMS,
        cost_estimate=pl.CostEstimate(flops=2_000_000, bytes_accessed=1_500_000, transcendentals=100_000),
        name="merge",
    )(me, parts, *local)


def fetch_kernel(weight_ref, x_ref, weight_out, x_out, sems):
    chunks = sems.shape[0] - 1
    rows = weight_ref.shape[0] // chunks
    copies = []
    for i in range(chunks):
        at = pl.ds(i * rows, rows)
        copies.append(pltpu.make_async_copy(weight_ref.at[at], weight_out.at[at], sems.at[i]))
    copies.append(pltpu.make_async_copy(x_ref, x_out, sems.at[chunks]))
    for copy in copies:
        copy.start()
    for copy in copies:
        copy.wait()


def fetched(weight, x):
    return pl.pallas_call(
        fetch_kernel,
        out_shape=[pltpu.VMEM(weight.shape, weight.dtype), pltpu.VMEM(x.shape, x.dtype)],
        in_specs=[ANY, ANY],
        out_specs=[ANY, ANY],
        scratch_shapes=[pltpu.SemaphoreType.DMA((9,))],
        compiler_params=PARAMS,
        cost_estimate=pl.CostEstimate(flops=0, bytes_accessed=2 * weight.size * 2, transcendentals=0),
        name="fetch_weight",
    )(in_hbm(weight), x)


def rows_kernel(npool, place_ref, *refs):
    blocks = refs[:npool]
    weight_ref, out_ref, lhs = refs[npool:]
    steps, rows, _ = blocks[0].shape
    every = npool * rows
    for x, (apart, flip) in enumerate(block_order(npool)):
        owner = owner_of(place_ref[0], npool, apart, flip)
        for s in range(steps):
            lhs[pl.ds(pl.multiple_of(s * every + owner * rows, rows), rows), :] = blocks[x][s]
    multiply(lhs, weight_ref, out_ref, 1 - place_ref[1])


def multiply(lhs, weight_ref, out_ref, which):
    steps, every, half = out_ref.shape
    tile = min(half, 256)
    for i in range(half // tile):
        at = pl.ds(pl.multiple_of(which * half + i * tile, LANES), tile)
        terms = jnp.dot(lhs[...], weight_ref[:, at], preferred_element_type=F32)
        for s in range(steps):
            out_ref[s, :, i * tile : (i + 1) * tile] = terms[s * every : (s + 1) * every]


def other_projection(place, blocks, weight):
    npool = len(blocks)
    steps, rows, width = blocks[0].shape
    half = weight.shape[1] // 2
    every = steps * npool * rows
    return pl.pallas_call(
        functools.partial(rows_kernel, npool),
        out_shape=[
            jax.ShapeDtypeStruct((steps, npool * rows, half), F32),
            jax.ShapeDtypeStruct((every, width), BF16),
        ],
        in_specs=[SMEM] + [VMEM] * (npool + 1),
        out_specs=[VMEM] * 2,
        compiler_params=PARAMS,
        cost_estimate=pl.CostEstimate(flops=2 * every * width * half, bytes_accessed=4_000_000, transcendentals=0),
        name="project_other",
    )(place, *blocks, weight)


def own_kernel(place_ref, lhs, weight_ref, out_ref):
    multiply(lhs, weight_ref, out_ref, place_ref[1])


def own_projection(place, lhs, weight, steps):
    every, width = lhs.shape
    half = weight.shape[1] // 2
    return pl.pallas_call(
        own_kernel,
        out_shape=jax.ShapeDtypeStruct((steps, every // steps, half), F32),
        in_specs=[SMEM] + [VMEM] * 2,
        out_specs=VMEM,
        compiler_params=PARAMS,
        cost_estimate=pl.CostEstimate(flops=2 * every * width * half, bytes_accessed=4_000_000, transcendentals=0),
        name="project_own",
    )(place, lhs, weight)


def block_order(npool):
    return [(apart, flip) for flip in (0, 1) for apart in range(npool // 2)]


def owner_of(me, npool, apart, flip):
    half = npool // 2
    pair, side = me // 2, me % 2
    side = 1 - side if flip else side
    return lax.rem(pair + half - apart, half) * 2 + side


def place_of(me, npool, holder):
    half = npool // 2
    apart = lax.rem(holder // 2 - me // 2 + half, half)
    flip = lax.rem(me + holder, 2)
    return flip * half + apart


def in_hbm(x):
    return pltpu.with_memory_space_constraint(x, pltpu.HBM)


def gathered(x, npool, later=None):
    half = npool // 2
    later = x if later is None else later
    ahead = lambda x, by: lax.ppermute(x, "pool", [(i, (i + 2 * by) % npool) for i in range(npool)])
    across = lambda x: lax.ppermute(x, "pool", [(i, i ^ 1) for i in range(npool)])
    straight = [x] + [ahead(x if by == half // 2 else later, by) for by in range(1, half)]
    return straight + [across(y) for y in straight]


def swap_halves(x):
    return lax.ppermute(x, "tp", [(0, 1), (1, 0)])


def shards(
    prompt_kv,
    prompt_lengths,
    page_slot,
    cache_kv,
    cache_fill,
    page_table,
    context_lengths,
    queries,
    new_kv,
    out_weight,
):
    npool = lax.axis_size("pool")
    me = lax.axis_index("pool").astype(I32)
    pages, _, heads, page_len, head_dim = prompt_kv.shape
    cache_pages = cache_kv.shape[0]
    pair = (pages + npool - 1) // npool
    tabs = tables(page_len, head_dim, pages)
    place = jnp.stack([me, lax.axis_index("tp").astype(I32)])
    table = page_table.T

    asked = asked_queries(table, context_lengths, queries, page_len, heads, head_dim)
    asked_all = gathered(asked, npool)
    arrived, own = rotated_pages(prompt_kv, page_slot, prompt_lengths, tabs, npool, pair, cache_pages)
    local = local_attention(table, context_lengths, cache_fill, asked, new_kv, cache_kv, tabs)
    parts = arrived_attention(place, own, asked_all, arrived)
    parts = lax.all_to_all(parts, "pool", split_axis=0, concat_axis=0, tiled=True)
    attention = merged(place, parts, local, queries.shape, heads, pair)
    weight, again = fetched(out_weight, attention)
    blocks = gathered(attention, npool, again)
    other_terms, lhs = other_projection(place, blocks, weight)
    other_terms = swap_halves(other_terms)
    terms = own_projection(place, lhs, weight, queries.shape[0])
    return (terms + other_terms).astype(BF16)


def solution(mesh):
    return jax.shard_map(
        shards,
        mesh=mesh,
        in_specs=(
            P(("group", "pool"), None, "tp", None, None),
            P(("group", "pool"), None),
            P(("group", "pool")),
            P(("group", "pool"), None, "tp", None, None),
            P(("group", "pool")),
            P(("group", "pool"), None),
            P(("group", "pool")),
            P(None, ("group", "pool"), "tp"),
            P(None, ("group", "pool"), None, "tp", None),
            P("tp", "pool"),
        ),
        out_specs=P(None, "group", ("pool", "tp")),
        check_vma=False,
    )
```

```python
import functools

import jax
import jax.numpy as jnp
import numpy as np
from jax import lax
from jax.experimental import pallas as pl
from jax.experimental.pallas import tpu as pltpu
from jax.sharding import PartitionSpec as P

ROPE_BASE = 500000.0
BF16, F32, I32 = jnp.bfloat16, jnp.float32, jnp.int32
SMEM = pl.BlockSpec(memory_space=pltpu.SMEM)
VMEM = pl.BlockSpec(memory_space=pltpu.VMEM)
ANY = pl.BlockSpec(memory_space=pl.ANY)
PARAMS = pltpu.CompilerParams(vmem_limit_bytes=24 * 2**20)
LANES = 128
STAT_ROWS = 16
CODE = 256


def tables(page_len, head_dim, pages):
    half = head_dim // 2
    freq = ROPE_BASE ** (-(np.arange(half) * 2.0) / head_dim)
    freq = np.concatenate([freq, freq])[None, :]
    sign = np.concatenate([-np.ones(half), np.ones(half)])[None, :]
    token = np.arange(page_len)[:, None] * freq
    first = np.arange(pages)[:, None] * page_len * freq
    out = (np.cos(token), sign * np.sin(token), np.cos(first), sign * np.sin(first), freq, sign)
    return [jnp.asarray(x, F32) for x in out]


def rope_kernel(
    npool, cache_pages, per, slot_ref, len_ref, pages_ref, ct_ref, st_ref, cp_ref, sp_ref, out_ref, own_ref, count
):
    _, _, heads, page_len, head_dim = pages_ref.shape

    @pl.when(pl.program_id(0) == 0)
    def _():
        items = own_ref.shape[0] // 3
        for e in range(npool):
            count[e] = 0
        for i in range(items):
            own_ref[i] = 0
            own_ref[items + i] = 0
            own_ref[2 * items + i] = -1
        for n in range(slot_ref.shape[0]):
            slot = slot_ref[n]
            target = slot // cache_pages
            at = target * (items // npool) + count[target]
            count[target] = count[target] + 1
            own_ref[at] = n
            own_ref[items + at] = page_place(len_ref, page_len, n)[1]
            own_ref[2 * items + at] = slot - target * cache_pages

    for i in range(per):
        number, _ = page_place(len_ref, page_len, pl.program_id(0) * per + i)
        c0, s0 = cp_ref[pl.ds(number, 1), :], sp_ref[pl.ds(number, 1), :]
        ct, st = ct_ref[...], st_ref[...]
        cos = c0 * ct - s0 * st
        sin = s0 * ct + c0 * st
        for k in range(heads):
            x = pages_ref[i, 0, k].astype(F32)
            out_ref[i, 0, k] = (x * cos + pltpu.roll(x, head_dim // 2, 1) * sin).astype(BF16)
            out_ref[i, 1, k] = pages_ref[i, 1, k]


def page_place(len_ref, page_len, n):
    begin = jnp.int32(0)
    number, fill = jnp.int32(0), jnp.int32(0)
    for q in range(len_ref.shape[1]):
        length = len_ref[0, q]
        count = (length + page_len - 1) // page_len
        here = (n >= begin) & (n < begin + count)
        number = jnp.where(here, n - begin, number)
        fill = jnp.where(here, jnp.clip(length - (n - begin) * page_len, 0, page_len), fill)
        begin = begin + count
    return number, fill


def rotated_pages(prompt_kv, page_slot, prompt_lengths, tabs, npool, pair, cache_pages):
    pages, _, heads, page_len, head_dim = prompt_kv.shape
    per = pages // 2
    ct, st, cp, sp, _, _ = tabs
    whole = lambda x: pl.BlockSpec(x.shape, lambda i: (0, 0))
    return pl.pallas_call(
        functools.partial(rope_kernel, npool, cache_pages, per),
        grid=(pages // per,),
        out_shape=[
            jax.ShapeDtypeStruct(prompt_kv.shape, BF16),
            jax.ShapeDtypeStruct((3 * npool * pair,), I32),
        ],
        in_specs=[
            SMEM,
            SMEM,
            pl.BlockSpec((per,) + prompt_kv.shape[1:], lambda i: (i, 0, 0, 0, 0)),
            whole(ct),
            whole(st),
            whole(cp),
            whole(sp),
        ],
        out_specs=[pl.BlockSpec((per,) + prompt_kv.shape[1:], lambda i: (i, 0, 0, 0, 0)), SMEM],
        scratch_shapes=[pltpu.SMEM((npool,), I32)],
        compiler_params=PARAMS,
        cost_estimate=pl.CostEstimate(flops=6_000_000, bytes_accessed=2_000_000, transcendentals=0),
        name="rope_pages",
    )(*[in_hbm(x) for x in (page_slot, prompt_lengths, prompt_kv, ct, st, cp, sp)])


def asked_kernel(page_len, heads, table_ref, context_ref, q_ref, out_ref, spread):
    most, rows = table_ref.shape
    steps, _, width = q_ref.shape
    block, head_dim = out_ref.shape[1:]
    per = width // head_dim // heads
    for s in range(steps):
        for h in range(heads * per):
            k, g = divmod(h, per)
            at = pl.ds(k * steps * per + s * per + g, rows, stride=block)
            spread[at, :] = q_ref[s, :, h * head_dim : (h + 1) * head_dim].astype(F32)
    for r in range(rows):
        out_ref[r] = spread[r * block : (r + 1) * block, :].astype(BF16)
    lane = lax.broadcasted_iota(I32, (block, LANES), 1)
    line = lax.broadcasted_iota(I32, (block, LANES), 0)
    request = jnp.zeros((block, LANES), I32)
    left = jnp.zeros((block, LANES), I32)
    for r in range(rows):
        context = context_ref[r]
        for j in range(most):
            here = lane == table_ref[j, r]
            request = jnp.where(here, r, request)
            left = jnp.where(here, jnp.clip(context - j * page_len, 0, page_len), left)
    out_ref[rows] = jnp.where(line == 0, request, left).astype(F32).astype(BF16)


def asked_queries(table, context, queries, page_len, heads, head_dim):
    steps, rows, width = queries.shape
    block = steps * width // head_dim
    return pl.pallas_call(
        functools.partial(asked_kernel, page_len, heads),
        out_shape=jax.ShapeDtypeStruct((rows + 1, block, head_dim), BF16),
        in_specs=[SMEM, SMEM, VMEM],
        out_specs=VMEM,
        scratch_shapes=[pltpu.VMEM((rows * block, head_dim), F32)],
        compiler_params=PARAMS,
        cost_estimate=pl.CostEstimate(flops=100_000, bytes_accessed=300_000, transcendentals=0),
        name="asked_queries",
    )(in_hbm(table), in_hbm(context), in_hbm(queries))


def read_scalar(x, pick):
    return jnp.max(jnp.where(pick, x, -2.0)).astype(I32)


def transposed_scores(queries, keys, group):
    turned = jnp.transpose(queries, (1, 0))
    chain = lax.broadcasted_iota(I32, (1, turned.shape[1]), 1) // group
    spread = [turned * jnp.where(chain == c, 1.0, 0.0).astype(BF16) for c in range(len(keys))]
    scores = jnp.dot(
        jnp.concatenate(keys, axis=1), jnp.concatenate(spread, axis=0), preferred_element_type=F32
    )
    return scores * (queries.shape[1] ** -0.5)


def weighted_values(weights, values):
    heads, head_dim = len(values), values[0].shape[1]
    group = weights.shape[0] // heads
    out = jnp.dot(weights, jnp.concatenate(values, axis=1), preferred_element_type=F32)
    parts = [out[k * group : (k + 1) * group, k * head_dim : (k + 1) * head_dim] for k in range(heads)]
    return jnp.concatenate(parts, axis=0)


def lane_values(scalars, lanes_each, shape):
    chain = lax.broadcasted_iota(I32, shape, 1) // lanes_each
    out = jnp.zeros(shape, I32)
    for i, x in enumerate(scalars):
        out = jnp.where(chain == i, x, out)
    return out


def local_kernel(
    page_len,
    heads,
    table_ref,
    context_ref,
    fill_ref,
    q_ref,
    new_ref,
    freq_ref,
    sign_ref,
    cache_ref,
    o_ref,
    stat_ref,
    kv,
    sems,
    kf,
    vf,
    position,
    where,
):
    rows, block, head_dim = q_ref.shape
    rows = rows - 1
    steps = new_ref.shape[0]
    most = table_ref.shape[0]
    group = block // heads
    per = group // steps
    together = LANES // block

    zeros = rows * most

    def copy(r, j):
        n = r * most + j
        return pltpu.make_async_copy(cache_ref.at[table_ref[j, r]], kv.at[n], sems.at[n])

    def seen_tokens(r, j):
        return jnp.minimum(fill_ref[table_ref[j, r]], context_ref[r] - j * page_len)

    for r in range(rows):
        for j in range(most):
            needed = seen_tokens(r, j) > 0
            where[r * most + j] = jnp.where(needed, r * most + j, zeros)
            pl.when(needed)(copy(r, j).start)
    kv[zeros] = jnp.zeros(kv.shape[1:], BF16)
    kf[...] = jnp.zeros_like(kf)
    vf[...] = jnp.zeros_like(vf)
    for r in range(rows):
        position[r : r + 1, :] = jnp.full((1, head_dim), context_ref[r], I32)
    for u in range(steps):
        angle = (position[...] + u).astype(F32) * freq_ref[...]
        cos, sin = jnp.cos(angle), jnp.sin(angle) * sign_ref[...]
        for k in range(heads):
            x = new_ref[u, :, k * head_dim : (k + 1) * head_dim].astype(F32)
            at = k * group + u
            kf[pl.ds(at, rows, stride=block), :] = x * cos + pltpu.roll(x, head_dim // 2, 1) * sin
            x = new_ref[u, :, (heads + k) * head_dim : (heads + k + 1) * head_dim].astype(F32)
            vf[pl.ds(at, rows, stride=block), :] = x
    token = lax.broadcasted_iota(I32, (page_len, LANES), 0)
    fresh = lax.broadcasted_iota(I32, (group, LANES), 0)
    step = lax.broadcasted_iota(I32, (group, LANES), 1) % group // per
    fresh_mask = (fresh <= step) & (fresh < steps)

    groups = [range(i * together, (i + 1) * together) for i in range(rows // together)]
    all_scores, all_weights = [], []
    for i, requests in enumerate(groups):
        if i % 2 == 0:
            for r in range(i * together, min(rows, (i + 2) * together)):
                for j in range(most):
                    pl.when(where[r * most + j] < zeros)(copy(r, j).wait)
        keys = []
        for r in requests:
            for k in range(heads):
                at = r * block + k * group
                pages = [kv[where[r * most + j], 0, k] for j in range(most)]
                keys.append(jnp.concatenate(pages + [kf[at : at + group, :].astype(BF16)], axis=0))
        queries = q_ref[i * together : (i + 1) * together].reshape(LANES, head_dim)
        all_scores.append(transposed_scores(queries, keys, group))
    for i, requests in enumerate(groups):
        mask = []
        for j in range(most):
            seen = [seen_tokens(r, j) for r in requests]
            mask.append(token < lane_values(seen, block, (1, LANES)))
        parts = [
            jnp.where(m, all_scores[i][n * page_len : n * page_len + m.shape[0]], -jnp.inf)
            for n, m in enumerate(mask + [fresh_mask])
        ]
        top = functools.reduce(jnp.maximum, [jnp.max(x, axis=0, keepdims=True) for x in parts])
        parts = [jnp.exp(x - top) for x in parts]
        total = functools.reduce(jnp.add, [jnp.sum(x, axis=0, keepdims=True) for x in parts])
        stats = jnp.concatenate(
            [parts[most], jnp.broadcast_to(top, (8, LANES)), jnp.broadcast_to(total, (8, LANES))], axis=0
        )
        stats = jnp.transpose(stats, (1, 0))
        stat_ref[i * LANES : (i + 1) * LANES, : stats.shape[1]] = stats
        weights = [jnp.transpose(x.astype(BF16), (1, 0)) for x in parts[:most]]
        weights.append(stats[:, :group].astype(BF16))
        all_weights.append(jnp.concatenate(weights, axis=1))
    for i, requests in enumerate(groups):
        for x, r in enumerate(requests):
            both = []
            for k in range(heads):
                at = r * block + k * group
                pages = [kv[where[r * most + j], 1, k] for j in range(most)]
                both.append(jnp.concatenate(pages + [vf[at : at + group, :].astype(BF16)], axis=0))
            both = weighted_values(all_weights[i][x * block : (x + 1) * block, :], both)
            o_ref[r * block : (r + 1) * block, :] = both


def local_attention(table, context, fills, queries, new_kv, cache_kv, tabs):
    rows, block, _ = queries.shape
    rows = rows - 1
    steps = new_kv.shape[0]
    slots, _, heads, page_len, head_dim = cache_kv.shape
    flat = (rows * block, head_dim)
    freq, sign = tabs[4:]
    return pl.pallas_call(
        functools.partial(local_kernel, page_len, heads),
        out_shape=[jax.ShapeDtypeStruct(flat, F32)] * 2,
        in_specs=[SMEM] * 3 + [VMEM] * 4 + [ANY],
        out_specs=[VMEM] * 2,
        scratch_shapes=[
            pltpu.VMEM((table.size + 1, 2, heads, page_len, head_dim), BF16),
            pltpu.SemaphoreType.DMA((table.size,)),
            pltpu.VMEM(flat, F32),
            pltpu.VMEM(flat, F32),
            pltpu.VMEM((rows, head_dim), I32),
            pltpu.SMEM((table.size,), I32),
        ],
        compiler_params=PARAMS,
        cost_estimate=pl.CostEstimate(flops=800_000_000, bytes_accessed=12_000_000, transcendentals=400_000),
        name="local_attention",
    )(
        *[in_hbm(x) for x in (table, context, fills)],
        queries,
        new_kv.reshape(steps, rows, 2 * heads * head_dim),
        *[in_hbm(x) for x in (freq, sign, cache_kv)],
    )


def pieces(x):
    high = x.astype(BF16).astype(F32)
    middle = (x - high).astype(BF16).astype(F32)
    return [high, middle, x - high - middle]


def arrived_kernel(npool, pair, me_ref, own_ref, *refs):
    blocks = refs[:npool]
    pages_ref, out_ref, queries = refs[npool:]
    items = npool * pair
    _, _, heads, page_len, head_dim = pages_ref.shape
    rows, block = blocks[0].shape[0] - 1, blocks[0].shape[1]
    group = block // heads
    together = LANES // block
    me = me_ref[0]
    owners = [owner_of(me, npool, apart, flip) for apart, flip in block_order(npool)]
    lane = lax.broadcasted_iota(I32, (1, LANES), 1)
    codes = [x[rows, :STAT_ROWS, :].astype(F32) for x in blocks]
    codes = [x[0:1] * CODE + x[1:2] for x in codes]
    number, seen, request = [], [], []
    for x in range(items):
        at = owners[x // pair] * pair + x % pair
        slot = own_ref[2 * items + at]
        code = jnp.maximum(read_scalar(codes[x // pair], lane == slot), 0)
        reader, left = code // CODE, code % CODE
        queries[x * block : (x + 1) * block, :] = blocks[x // pair][reader]
        number.append(own_ref[at])
        seen.append(jnp.minimum(left, own_ref[items + at]))
        request.append(jnp.where(slot >= 0, reader, -1))
    token = lax.broadcasted_iota(I32, (page_len, LANES), 0)
    groups = [range(i * together, (i + 1) * together) for i in range(items // together)]
    all_scores, all_weights = [], []
    for i, own in enumerate(groups):
        keys = [pages_ref[number[x], 0, k] for x in own for k in range(heads)]
        all_scores.append(transposed_scores(queries[i * LANES : (i + 1) * LANES, :], keys, group))
    for i, own in enumerate(groups):
        limit = lane_values([seen[x] for x in own], block, (1, LANES))
        scores = jnp.where(token < limit, all_scores[i], -jnp.inf)
        top = jnp.max(scores, axis=0, keepdims=True)
        top = jnp.where(top > -jnp.inf, top, 0.0)
        weights = jnp.exp(scores - top)
        stats = pieces(top) + pieces(jnp.sum(weights, axis=0, keepdims=True))
        stats.append(lane_values([request[x] for x in own], block, (1, LANES)).astype(F32))
        stats = jnp.concatenate(stats + [jnp.zeros((STAT_ROWS - len(stats), LANES), F32)], axis=0).astype(BF16)
        for place in sorted({x // pair for x in own}):
            out_ref[owners[place], pair * block : pair * block + STAT_ROWS, :] = stats
        all_weights.append(jnp.transpose(weights.astype(BF16), (1, 0)))
    for i, own in enumerate(groups):
        for c, x in enumerate(own):
            both = [pages_ref[number[x], 1, k] for k in range(heads)]
            both = weighted_values(all_weights[i][c * block : (c + 1) * block, :], both)
            at = (x % pair) * block
            out_ref[owners[x // pair], at : at + block, :] = both.astype(BF16)


def arrived_attention(me, own, blocks, arrived):
    npool = len(blocks)
    head_dim = arrived.shape[4]
    block = blocks[0].shape[1]
    items = own.shape[0] // 3
    pair = items // npool
    return pl.pallas_call(
        functools.partial(arrived_kernel, npool, pair),
        out_shape=jax.ShapeDtypeStruct((npool, pair * block + STAT_ROWS, head_dim), BF16),
        in_specs=[SMEM] * 2 + [VMEM] * (npool + 1),
        out_specs=VMEM,
        scratch_shapes=[pltpu.VMEM((items * block, head_dim), BF16)],
        compiler_params=PARAMS,
        cost_estimate=pl.CostEstimate(flops=200_000_000, bytes_accessed=4_000_000, transcendentals=70_000),
        name="arrived_attention",
    )(me, own, *blocks, arrived)


def merge_kernel(pair, heads, me_ref, parts_ref, o_ref, stat_ref, out_ref, mixed, top, total, turned):
    npool = parts_ref.shape[0]
    steps, rows, width = out_ref.shape
    head_dim = o_ref.shape[1]
    per = width // head_dim // heads
    group = steps * per
    block = heads * group
    me = me_ref[0]
    shape = top.shape
    mixed[...] = o_ref[...]
    top[...] = jnp.broadcast_to(stat_ref[:, group : group + 1], shape)
    total[...] = jnp.broadcast_to(stat_ref[:, group + 8 : group + 9], shape)
    tops, totals, readers = [], [], []
    chain = lax.broadcasted_iota(I32, (1, LANES), 1) // block
    for d in range(npool):
        x = parts_ref[d, pair * block : pair * block + STAT_ROWS, :].astype(F32)
        tops.append(x[0:1] + x[1:2] + x[2:3])
        totals.append(x[3:4] + x[4:5] + x[5:6])
        readers.append(x[6:7])
    empty = [jnp.zeros((LANES // 2 - npool, LANES), F32)]
    turned[...] = jnp.transpose(jnp.concatenate(tops + empty + totals + empty, axis=0), (1, 0))
    for d in range(npool):
        for p in range(pair):
            part = lax.rem(place_of(me, npool, d) * pair + p, LANES // block)
            r = read_scalar(readers[d], chain == part)
            there = r >= 0
            at = pl.ds(pl.multiple_of(jnp.maximum(r, 0) * block, block), block)
            lane = pl.ds(pl.multiple_of(part * block, block), block)
            m = jnp.broadcast_to(turned[lane, d : d + 1], (block, head_dim))
            l = jnp.broadcast_to(turned[lane, LANES // 2 + d : LANES // 2 + d + 1], (block, head_dim))
            seen = (l > 0.0) & there
            o = parts_ref[d, p * block : (p + 1) * block, :].astype(F32)
            old = top[at, :]
            new = jnp.where(seen, jnp.maximum(old, m), old)
            a = jnp.exp(old - new)
            b = jnp.where(seen, jnp.exp(m - new), 0.0)
            top[at, :] = new
            total[at, :] = total[at, :] * a + l * b
            mixed[at, :] = mixed[at, :] * a + o * b
    for s in range(steps):
        for h in range(heads * per):
            k, g = divmod(h, per)
            at = pl.ds(k * group + s * per + g, rows, stride=block)
            out_ref[s, :, h * head_dim : (h + 1) * head_dim] = (mixed[at, :] / total[at, :]).astype(BF16)


def merged(me, parts, local, shape, heads, pair):
    flat = local[0].shape
    return pl.pallas_call(
        functools.partial(merge_kernel, pair, heads),
        out_shape=jax.ShapeDtypeStruct(shape, BF16),
        in_specs=[SMEM] + [VMEM] * 3,
        out_specs=VMEM,
        scratch_shapes=[pltpu.VMEM(flat, F32)] * 3 + [pltpu.VMEM((LANES, LANES), F32)],
        compiler_params=PARAMS,
        cost_estimate=pl.CostEstimate(flops=2_000_000, bytes_accessed=1_500_000, transcendentals=100_000),
        name="merge",
    )(me, parts, *local)


def fetch_kernel(weight_ref, x_ref, weight_out, x_out, sems):
    chunks = sems.shape[0] - 1
    rows = weight_ref.shape[0] // chunks
    copies = []
    for i in range(chunks):
        at = pl.ds(i * rows, rows)
        copies.append(pltpu.make_async_copy(weight_ref.at[at], weight_out.at[at], sems.at[i]))
    copies.append(pltpu.make_async_copy(x_ref, x_out, sems.at[chunks]))
    for copy in copies:
        copy.start()
    for copy in copies:
        copy.wait()


def fetched(weight, x):
    return pl.pallas_call(
        fetch_kernel,
        out_shape=[pltpu.VMEM(weight.shape, weight.dtype), pltpu.VMEM(x.shape, x.dtype)],
        in_specs=[ANY, ANY],
        out_specs=[ANY, ANY],
        scratch_shapes=[pltpu.SemaphoreType.DMA((9,))],
        compiler_params=PARAMS,
        cost_estimate=pl.CostEstimate(flops=0, bytes_accessed=2 * weight.size * 2, transcendentals=0),
        name="fetch_weight",
    )(in_hbm(weight), x)


def rows_kernel(npool, place_ref, *refs):
    blocks = refs[:npool]
    weight_ref, out_ref, lhs = refs[npool:]
    steps, rows, _ = blocks[0].shape
    every = npool * rows
    for x, (apart, flip) in enumerate(block_order(npool)):
        owner = owner_of(place_ref[0], npool, apart, flip)
        for s in range(steps):
            lhs[pl.ds(pl.multiple_of(s * every + owner * rows, rows), rows), :] = blocks[x][s]
    multiply(lhs, weight_ref, out_ref, 1 - place_ref[1])


def multiply(lhs, weight_ref, out_ref, which):
    steps, every, half = out_ref.shape
    tile = min(half, 256)
    for i in range(half // tile):
        at = pl.ds(pl.multiple_of(which * half + i * tile, LANES), tile)
        terms = jnp.dot(lhs[...], weight_ref[:, at], preferred_element_type=F32)
        for s in range(steps):
            out_ref[s, :, i * tile : (i + 1) * tile] = terms[s * every : (s + 1) * every]


def other_projection(place, blocks, weight):
    npool = len(blocks)
    steps, rows, width = blocks[0].shape
    half = weight.shape[1] // 2
    every = steps * npool * rows
    return pl.pallas_call(
        functools.partial(rows_kernel, npool),
        out_shape=[
            jax.ShapeDtypeStruct((steps, npool * rows, half), F32),
            jax.ShapeDtypeStruct((every, width), BF16),
        ],
        in_specs=[SMEM] + [VMEM] * (npool + 1),
        out_specs=[VMEM] * 2,
        compiler_params=PARAMS,
        cost_estimate=pl.CostEstimate(flops=2 * every * width * half, bytes_accessed=4_000_000, transcendentals=0),
        name="project_other",
    )(place, *blocks, weight)


def own_kernel(place_ref, lhs, weight_ref, out_ref):
    multiply(lhs, weight_ref, out_ref, place_ref[1])


def own_projection(place, lhs, weight, steps):
    every, width = lhs.shape
    half = weight.shape[1] // 2
    return pl.pallas_call(
        own_kernel,
        out_shape=jax.ShapeDtypeStruct((steps, every // steps, half), F32),
        in_specs=[SMEM] + [VMEM] * 2,
        out_specs=VMEM,
        compiler_params=PARAMS,
        cost_estimate=pl.CostEstimate(flops=2 * every * width * half, bytes_accessed=4_000_000, transcendentals=0),
        name="project_own",
    )(place, lhs, weight)


def block_order(npool):
    return [(apart, flip) for flip in (0, 1) for apart in range(npool // 2)]


def owner_of(me, npool, apart, flip):
    half = npool // 2
    pair, side = me // 2, me % 2
    side = 1 - side if flip else side
    return lax.rem(pair + half - apart, half) * 2 + side


def place_of(me, npool, holder):
    half = npool // 2
    apart = lax.rem(holder // 2 - me // 2 + half, half)
    flip = lax.rem(me + holder, 2)
    return flip * half + apart


def in_hbm(x):
    return pltpu.with_memory_space_constraint(x, pltpu.HBM)


def gathered(x, npool, later=None):
    half = npool // 2
    later = x if later is None else later
    ahead = lambda x, by: lax.ppermute(x, "pool", [(i, (i + 2 * by) % npool) for i in range(npool)])
    across = lambda x: lax.ppermute(x, "pool", [(i, i ^ 1) for i in range(npool)])
    straight = [x] + [ahead(x if by == half // 2 else later, by) for by in range(1, half)]
    return straight + [across(y) for y in straight]


def swap_halves(x):
    return lax.ppermute(x, "tp", [(0, 1), (1, 0)])


def shards(
    prompt_kv,
    prompt_lengths,
    page_slot,
    cache_kv,
    cache_fill,
    page_table,
    context_lengths,
    queries,
    new_kv,
    out_weight,
):
    npool = lax.axis_size("pool")
    me = lax.axis_index("pool").astype(I32)
    pages, _, heads, page_len, head_dim = prompt_kv.shape
    cache_pages = cache_kv.shape[0]
    pair = (pages + npool - 1) // npool
    tabs = tables(page_len, head_dim, pages)
    place = jnp.stack([me, lax.axis_index("tp").astype(I32)])
    table = page_table.T

    asked = asked_queries(table, context_lengths, queries, page_len, heads, head_dim)
    asked_all = gathered(asked, npool)
    arrived, own = rotated_pages(prompt_kv, page_slot, prompt_lengths, tabs, npool, pair, cache_pages)
    local = local_attention(table, context_lengths, cache_fill, asked, new_kv, cache_kv, tabs)
    parts = arrived_attention(place, own, asked_all, arrived)
    parts = lax.all_to_all(parts, "pool", split_axis=0, concat_axis=0, tiled=True)
    attention = merged(place, parts, local, queries.shape, heads, pair)
    weight, again = fetched(out_weight, attention)
    blocks = gathered(attention, npool, again)
    other_terms, lhs = other_projection(place, blocks, weight)
    other_terms = swap_halves(other_terms)
    terms = own_projection(place, lhs, weight, queries.shape[0])
    return (terms + other_terms).astype(BF16)


def solution(mesh):
    return jax.shard_map(
        shards,
        mesh=mesh,
        in_specs=(
            P(("group", "pool"), None, "tp", None, None),
            P(("group", "pool"), None),
            P(("group", "pool")),
            P(("group", "pool"), None, "tp", None, None),
            P(("group", "pool")),
            P(("group", "pool"), None),
            P(("group", "pool")),
            P(None, ("group", "pool"), "tp"),
            P(None, ("group", "pool"), None, "tp", None),
            P("tp", "pool"),
        ),
        out_specs=P(None, "group", ("pool", "tp")),
        check_vma=False,
    )
```

```python
import functools

import jax
import jax.numpy as jnp
import numpy as np
from jax import lax
from jax.experimental import pallas as pl
from jax.experimental.pallas import tpu as pltpu
from jax.sharding import PartitionSpec as P

ROPE_BASE = 500000.0
BF16, F32, I32 = jnp.bfloat16, jnp.float32, jnp.int32
SMEM = pl.BlockSpec(memory_space=pltpu.SMEM)
VMEM = pl.BlockSpec(memory_space=pltpu.VMEM)
ANY = pl.BlockSpec(memory_space=pl.ANY)
PARAMS = pltpu.CompilerParams(vmem_limit_bytes=24 * 2**20)
LANES = 128
STAT_ROWS = 16
CODE = 256


def tables(page_len, head_dim, pages):
    half = head_dim // 2
    freq = ROPE_BASE ** (-(np.arange(half) * 2.0) / head_dim)
    freq = np.concatenate([freq, freq])[None, :]
    sign = np.concatenate([-np.ones(half), np.ones(half)])[None, :]
    token = np.arange(page_len)[:, None] * freq
    first = np.arange(pages)[:, None] * page_len * freq
    out = (np.cos(token), sign * np.sin(token), np.cos(first), sign * np.sin(first), freq, sign)
    return [jnp.asarray(x, F32) for x in out]


def rope_kernel(
    npool, cache_pages, per, slot_ref, len_ref, pages_ref, ct_ref, st_ref, cp_ref, sp_ref, out_ref, own_ref, count
):
    _, _, heads, page_len, head_dim = pages_ref.shape

    @pl.when(pl.program_id(0) == 0)
    def _():
        items = own_ref.shape[0] // 3
        for e in range(npool):
            count[e] = 0
        for i in range(items):
            own_ref[i] = 0
            own_ref[items + i] = 0
            own_ref[2 * items + i] = -1
        for n in range(slot_ref.shape[0]):
            slot = slot_ref[n]
            target = slot // cache_pages
            at = target * (items // npool) + count[target]
            count[target] = count[target] + 1
            own_ref[at] = n
            own_ref[items + at] = page_place(len_ref, page_len, n)[1]
            own_ref[2 * items + at] = slot - target * cache_pages

    for i in range(per):
        number, _ = page_place(len_ref, page_len, pl.program_id(0) * per + i)
        c0, s0 = cp_ref[pl.ds(number, 1), :], sp_ref[pl.ds(number, 1), :]
        ct, st = ct_ref[...], st_ref[...]
        cos = c0 * ct - s0 * st
        sin = s0 * ct + c0 * st
        for k in range(heads):
            x = pages_ref[i, 0, k].astype(F32)
            out_ref[i, 0, k] = (x * cos + pltpu.roll(x, head_dim // 2, 1) * sin).astype(BF16)
            out_ref[i, 1, k] = pages_ref[i, 1, k]


def page_place(len_ref, page_len, n):
    begin = jnp.int32(0)
    number, fill = jnp.int32(0), jnp.int32(0)
    for q in range(len_ref.shape[1]):
        length = len_ref[0, q]
        count = (length + page_len - 1) // page_len
        here = (n >= begin) & (n < begin + count)
        number = jnp.where(here, n - begin, number)
        fill = jnp.where(here, jnp.clip(length - (n - begin) * page_len, 0, page_len), fill)
        begin = begin + count
    return number, fill


def rotated_pages(prompt_kv, page_slot, prompt_lengths, tabs, npool, pair, cache_pages):
    pages, _, heads, page_len, head_dim = prompt_kv.shape
    per = pages // 2
    ct, st, cp, sp, _, _ = tabs
    whole = lambda x: pl.BlockSpec(x.shape, lambda i: (0, 0))
    return pl.pallas_call(
        functools.partial(rope_kernel, npool, cache_pages, per),
        grid=(pages // per,),
        out_shape=[
            jax.ShapeDtypeStruct(prompt_kv.shape, BF16),
            jax.ShapeDtypeStruct((3 * npool * pair,), I32),
        ],
        in_specs=[
            SMEM,
            SMEM,
            pl.BlockSpec((per,) + prompt_kv.shape[1:], lambda i: (i, 0, 0, 0, 0)),
            whole(ct),
            whole(st),
            whole(cp),
            whole(sp),
        ],
        out_specs=[pl.BlockSpec((per,) + prompt_kv.shape[1:], lambda i: (i, 0, 0, 0, 0)), SMEM],
        scratch_shapes=[pltpu.SMEM((npool,), I32)],
        compiler_params=PARAMS,
        cost_estimate=pl.CostEstimate(flops=6_000_000, bytes_accessed=2_000_000, transcendentals=0),
        name="rope_pages",
    )(*[in_hbm(x) for x in (page_slot, prompt_lengths, prompt_kv, ct, st, cp, sp)])


def asked_kernel(page_len, heads, table_ref, context_ref, q_ref, out_ref, spread):
    most, rows = table_ref.shape
    steps, _, width = q_ref.shape
    block, head_dim = out_ref.shape[1:]
    per = width // head_dim // heads
    for s in range(steps):
        for h in range(heads * per):
            k, g = divmod(h, per)
            at = pl.ds(k * steps * per + s * per + g, rows, stride=block)
            spread[at, :] = q_ref[s, :, h * head_dim : (h + 1) * head_dim].astype(F32)
    for r in range(rows):
        out_ref[r] = spread[r * block : (r + 1) * block, :].astype(BF16)
    lane = lax.broadcasted_iota(I32, (block, LANES), 1)
    line = lax.broadcasted_iota(I32, (block, LANES), 0)
    request = jnp.zeros((block, LANES), I32)
    left = jnp.zeros((block, LANES), I32)
    for r in range(rows):
        context = context_ref[r]
        for j in range(most):
            here = lane == table_ref[j, r]
            request = jnp.where(here, r, request)
            left = jnp.where(here, jnp.clip(context - j * page_len, 0, page_len), left)
    out_ref[rows] = jnp.where(line == 0, request, left).astype(F32).astype(BF16)


def asked_queries(table, context, queries, page_len, heads, head_dim):
    steps, rows, width = queries.shape
    block = steps * width // head_dim
    return pl.pallas_call(
        functools.partial(asked_kernel, page_len, heads),
        out_shape=jax.ShapeDtypeStruct((rows + 1, block, head_dim), BF16),
        in_specs=[SMEM, SMEM, VMEM],
        out_specs=VMEM,
        scratch_shapes=[pltpu.VMEM((rows * block, head_dim), F32)],
        compiler_params=PARAMS,
        cost_estimate=pl.CostEstimate(flops=100_000, bytes_accessed=300_000, transcendentals=0),
        name="asked_queries",
    )(in_hbm(table), in_hbm(context), in_hbm(queries))


def read_scalar(x, pick):
    return jnp.max(jnp.where(pick, x, -2.0)).astype(I32)


def transposed_scores(queries, keys, group):
    turned = jnp.transpose(queries, (1, 0))
    chain = lax.broadcasted_iota(I32, (1, turned.shape[1]), 1) // group
    spread = [turned * jnp.where(chain == c, 1.0, 0.0).astype(BF16) for c in range(len(keys))]
    scores = jnp.dot(
        jnp.concatenate(keys, axis=1), jnp.concatenate(spread, axis=0), preferred_element_type=F32
    )
    return scores * (queries.shape[1] ** -0.5)


def weighted_values(weights, values):
    heads, head_dim = len(values), values[0].shape[1]
    group = weights.shape[0] // heads
    out = jnp.dot(weights, jnp.concatenate(values, axis=1), preferred_element_type=F32)
    parts = [out[k * group : (k + 1) * group, k * head_dim : (k + 1) * head_dim] for k in range(heads)]
    return jnp.concatenate(parts, axis=0)


def lane_values(scalars, lanes_each, shape):
    chain = lax.broadcasted_iota(I32, shape, 1) // lanes_each
    out = jnp.zeros(shape, I32)
    for i, x in enumerate(scalars):
        out = jnp.where(chain == i, x, out)
    return out


def local_kernel(
    page_len,
    heads,
    table_ref,
    context_ref,
    fill_ref,
    q_ref,
    new_ref,
    freq_ref,
    sign_ref,
    cache_ref,
    o_ref,
    stat_ref,
    kv,
    sems,
    kf,
    vf,
    position,
    where,
):
    rows, block, head_dim = q_ref.shape
    rows = rows - 1
    steps = new_ref.shape[0]
    most = table_ref.shape[0]
    group = block // heads
    per = group // steps
    together = LANES // block

    zeros = rows * most

    def copy(r, j):
        n = r * most + j
        return pltpu.make_async_copy(cache_ref.at[table_ref[j, r]], kv.at[n], sems.at[n])

    def seen_tokens(r, j):
        return jnp.minimum(fill_ref[table_ref[j, r]], context_ref[r] - j * page_len)

    for r in range(rows):
        for j in range(most):
            needed = seen_tokens(r, j) > 0
            where[r * most + j] = jnp.where(needed, r * most + j, zeros)
            pl.when(needed)(copy(r, j).start)
    kv[zeros] = jnp.zeros(kv.shape[1:], BF16)
    kf[...] = jnp.zeros_like(kf)
    vf[...] = jnp.zeros_like(vf)
    for r in range(rows):
        position[r : r + 1, :] = jnp.full((1, head_dim), context_ref[r], I32)
    for u in range(steps):
        angle = (position[...] + u).astype(F32) * freq_ref[...]
        cos, sin = jnp.cos(angle), jnp.sin(angle) * sign_ref[...]
        for k in range(heads):
            x = new_ref[u, :, k * head_dim : (k + 1) * head_dim].astype(F32)
            at = k * group + u
            kf[pl.ds(at, rows, stride=block), :] = x * cos + pltpu.roll(x, head_dim // 2, 1) * sin
            x = new_ref[u, :, (heads + k) * head_dim : (heads + k + 1) * head_dim].astype(F32)
            vf[pl.ds(at, rows, stride=block), :] = x
    token = lax.broadcasted_iota(I32, (page_len, LANES), 0)
    fresh = lax.broadcasted_iota(I32, (group, LANES), 0)
    step = lax.broadcasted_iota(I32, (group, LANES), 1) % group // per
    fresh_mask = (fresh <= step) & (fresh < steps)

    groups = [range(i * together, (i + 1) * together) for i in range(rows // together)]
    all_scores, all_weights = [], []
    for i, requests in enumerate(groups):
        if i % 2 == 0:
            for r in range(i * together, min(rows, (i + 2) * together)):
                for j in range(most):
                    pl.when(where[r * most + j] < zeros)(copy(r, j).wait)
        keys = []
        for r in requests:
            for k in range(heads):
                at = r * block + k * group
                pages = [kv[where[r * most + j], 0, k] for j in range(most)]
                keys.append(jnp.concatenate(pages + [kf[at : at + group, :].astype(BF16)], axis=0))
        queries = q_ref[i * together : (i + 1) * together].reshape(LANES, head_dim)
        all_scores.append(transposed_scores(queries, keys, group))
    for i, requests in enumerate(groups):
        mask = []
        for j in range(most):
            seen = [seen_tokens(r, j) for r in requests]
            mask.append(token < lane_values(seen, block, (1, LANES)))
        parts = [
            jnp.where(m, all_scores[i][n * page_len : n * page_len + m.shape[0]], -jnp.inf)
            for n, m in enumerate(mask + [fresh_mask])
        ]
        top = functools.reduce(jnp.maximum, [jnp.max(x, axis=0, keepdims=True) for x in parts])
        parts = [jnp.exp(x - top) for x in parts]
        total = functools.reduce(jnp.add, [jnp.sum(x, axis=0, keepdims=True) for x in parts])
        stats = jnp.concatenate(
            [parts[most], jnp.broadcast_to(top, (8, LANES)), jnp.broadcast_to(total, (8, LANES))], axis=0
        )
        stats = jnp.transpose(stats, (1, 0))
        stat_ref[i * LANES : (i + 1) * LANES, : stats.shape[1]] = stats
        weights = [jnp.transpose(x.astype(BF16), (1, 0)) for x in parts[:most]]
        weights.append(stats[:, :group].astype(BF16))
        all_weights.append(jnp.concatenate(weights, axis=1))
    for i, requests in enumerate(groups):
        for x, r in enumerate(requests):
            both = []
            for k in range(heads):
                at = r * block + k * group
                pages = [kv[where[r * most + j], 1, k] for j in range(most)]
                both.append(jnp.concatenate(pages + [vf[at : at + group, :].astype(BF16)], axis=0))
            both = weighted_values(all_weights[i][x * block : (x + 1) * block, :], both)
            o_ref[r * block : (r + 1) * block, :] = both


def local_attention(table, context, fills, queries, new_kv, cache_kv, tabs):
    rows, block, _ = queries.shape
    rows = rows - 1
    steps = new_kv.shape[0]
    slots, _, heads, page_len, head_dim = cache_kv.shape
    flat = (rows * block, head_dim)
    freq, sign = tabs[4:]
    return pl.pallas_call(
        functools.partial(local_kernel, page_len, heads),
        out_shape=[jax.ShapeDtypeStruct(flat, F32)] * 2,
        in_specs=[SMEM] * 3 + [VMEM] * 4 + [ANY],
        out_specs=[VMEM] * 2,
        scratch_shapes=[
            pltpu.VMEM((table.size + 1, 2, heads, page_len, head_dim), BF16),
            pltpu.SemaphoreType.DMA((table.size,)),
            pltpu.VMEM(flat, F32),
            pltpu.VMEM(flat, F32),
            pltpu.VMEM((rows, head_dim), I32),
            pltpu.SMEM((table.size,), I32),
        ],
        compiler_params=PARAMS,
        cost_estimate=pl.CostEstimate(flops=800_000_000, bytes_accessed=12_000_000, transcendentals=400_000),
        name="local_attention",
    )(
        *[in_hbm(x) for x in (table, context, fills)],
        queries,
        new_kv.reshape(steps, rows, 2 * heads * head_dim),
        *[in_hbm(x) for x in (freq, sign, cache_kv)],
    )


def pieces(x):
    high = x.astype(BF16).astype(F32)
    middle = (x - high).astype(BF16).astype(F32)
    return [high, middle, x - high - middle]


def arrived_kernel(npool, pair, me_ref, own_ref, *refs):
    blocks = refs[:npool]
    pages_ref, out_ref, queries = refs[npool:]
    items = npool * pair
    _, _, heads, page_len, head_dim = pages_ref.shape
    rows, block = blocks[0].shape[0] - 1, blocks[0].shape[1]
    group = block // heads
    together = LANES // block
    me = me_ref[0]
    owners = [owner_of(me, npool, apart, flip) for apart, flip in block_order(npool)]
    lane = lax.broadcasted_iota(I32, (1, LANES), 1)
    codes = [x[rows, :STAT_ROWS, :].astype(F32) for x in blocks]
    codes = [x[0:1] * CODE + x[1:2] for x in codes]
    number, seen, request = [], [], []
    for x in range(items):
        at = owners[x // pair] * pair + x % pair
        slot = own_ref[2 * items + at]
        code = jnp.maximum(read_scalar(codes[x // pair], lane == slot), 0)
        reader, left = code // CODE, code % CODE
        queries[x * block : (x + 1) * block, :] = blocks[x // pair][reader]
        number.append(own_ref[at])
        seen.append(jnp.minimum(left, own_ref[items + at]))
        request.append(jnp.where(slot >= 0, reader, -1))
    token = lax.broadcasted_iota(I32, (page_len, LANES), 0)
    groups = [range(i * together, (i + 1) * together) for i in range(items // together)]
    all_scores, all_weights = [], []
    for i, own in enumerate(groups):
        keys = [pages_ref[number[x], 0, k] for x in own for k in range(heads)]
        all_scores.append(transposed_scores(queries[i * LANES : (i + 1) * LANES, :], keys, group))
    for i, own in enumerate(groups):
        limit = lane_values([seen[x] for x in own], block, (1, LANES))
        scores = jnp.where(token < limit, all_scores[i], -jnp.inf)
        top = jnp.max(scores, axis=0, keepdims=True)
        top = jnp.where(top > -jnp.inf, top, 0.0)
        weights = jnp.exp(scores - top)
        stats = pieces(top) + pieces(jnp.sum(weights, axis=0, keepdims=True))
        stats.append(lane_values([request[x] for x in own], block, (1, LANES)).astype(F32))
        stats = jnp.concatenate(stats + [jnp.zeros((STAT_ROWS - len(stats), LANES), F32)], axis=0).astype(BF16)
        for place in sorted({x // pair for x in own}):
            out_ref[owners[place], pair * block : pair * block + STAT_ROWS, :] = stats
        all_weights.append(jnp.transpose(weights.astype(BF16), (1, 0)))
    for i, own in enumerate(groups):
        for c, x in enumerate(own):
            both = [pages_ref[number[x], 1, k] for k in range(heads)]
            both = weighted_values(all_weights[i][c * block : (c + 1) * block, :], both)
            at = (x % pair) * block
            out_ref[owners[x // pair], at : at + block, :] = both.astype(BF16)


def arrived_attention(me, own, blocks, arrived):
    npool = len(blocks)
    head_dim = arrived.shape[4]
    block = blocks[0].shape[1]
    items = own.shape[0] // 3
    pair = items // npool
    return pl.pallas_call(
        functools.partial(arrived_kernel, npool, pair),
        out_shape=jax.ShapeDtypeStruct((npool, pair * block + STAT_ROWS, head_dim), BF16),
        in_specs=[SMEM] * 2 + [VMEM] * (npool + 1),
        out_specs=VMEM,
        scratch_shapes=[pltpu.VMEM((items * block, head_dim), BF16)],
        compiler_params=PARAMS,
        cost_estimate=pl.CostEstimate(flops=200_000_000, bytes_accessed=4_000_000, transcendentals=70_000),
        name="arrived_attention",
    )(me, own, *blocks, arrived)


def merge_kernel(pair, heads, me_ref, parts_ref, o_ref, stat_ref, out_ref, mixed, top, total, turned):
    npool = parts_ref.shape[0]
    steps, rows, width = out_ref.shape
    head_dim = o_ref.shape[1]
    per = width // head_dim // heads
    group = steps * per
    block = heads * group
    me = me_ref[0]
    shape = top.shape
    mixed[...] = o_ref[...]
    top[...] = jnp.broadcast_to(stat_ref[:, group : group + 1], shape)
    total[...] = jnp.broadcast_to(stat_ref[:, group + 8 : group + 9], shape)
    tops, totals, readers = [], [], []
    chain = lax.broadcasted_iota(I32, (1, LANES), 1) // block
    for d in range(npool):
        x = parts_ref[d, pair * block : pair * block + STAT_ROWS, :].astype(F32)
        tops.append(x[0:1] + x[1:2] + x[2:3])
        totals.append(x[3:4] + x[4:5] + x[5:6])
        readers.append(x[6:7])
    empty = [jnp.zeros((LANES // 2 - npool, LANES), F32)]
    turned[...] = jnp.transpose(jnp.concatenate(tops + empty + totals + empty, axis=0), (1, 0))
    items = []
    for d in range(npool):
        for p in range(pair):
            part = lax.rem(place_of(me, npool, d) * pair + p, LANES // block)
            r = read_scalar(readers[d], chain == part)
            at = pl.ds(pl.multiple_of(jnp.maximum(r, 0) * block, block), block)
            lane = pl.ds(pl.multiple_of(part * block, block), block)
            m = jnp.broadcast_to(turned[lane, d : d + 1], (block, head_dim))
            l = jnp.broadcast_to(turned[lane, LANES // 2 + d : LANES // 2 + d + 1], (block, head_dim))
            items.append((d, p, at, m, l, (l > 0.0) & (r >= 0)))
    for d, p, at, m, l, seen in items:
        top[at, :] = jnp.where(seen, jnp.maximum(top[at, :], m), top[at, :])
    scale = jnp.exp(jnp.broadcast_to(stat_ref[:, group : group + 1], shape) - top[...])
    total[...] = total[...] * scale
    mixed[...] = mixed[...] * scale
    shares = [jnp.where(seen, jnp.exp(m - top[at, :]), 0.0) for _, _, at, m, _, seen in items]
    for (d, p, at, m, l, seen), share in zip(items, shares):
        o = parts_ref[d, p * block : (p + 1) * block, :].astype(F32)
        total[at, :] = total[at, :] + l * share
        mixed[at, :] = mixed[at, :] + o * share
    for s in range(steps):
        for h in range(heads * per):
            k, g = divmod(h, per)
            at = pl.ds(k * group + s * per + g, rows, stride=block)
            out_ref[s, :, h * head_dim : (h + 1) * head_dim] = (mixed[at, :] / total[at, :]).astype(BF16)


def merged(me, parts, local, shape, heads, pair):
    flat = local[0].shape
    return pl.pallas_call(
        functools.partial(merge_kernel, pair, heads),
        out_shape=jax.ShapeDtypeStruct(shape, BF16),
        in_specs=[SMEM] + [VMEM] * 3,
        out_specs=VMEM,
        scratch_shapes=[pltpu.VMEM(flat, F32)] * 3 + [pltpu.VMEM((LANES, LANES), F32)],
        compiler_params=PARAMS,
        cost_estimate=pl.CostEstimate(flops=2_000_000, bytes_accessed=1_500_000, transcendentals=100_000),
        name="merge",
    )(me, parts, *local)


def fetch_kernel(weight_ref, x_ref, weight_out, x_out, sems):
    chunks = sems.shape[0] - 1
    rows = weight_ref.shape[0] // chunks
    copies = []
    for i in range(chunks):
        at = pl.ds(i * rows, rows)
        copies.append(pltpu.make_async_copy(weight_ref.at[at], weight_out.at[at], sems.at[i]))
    copies.append(pltpu.make_async_copy(x_ref, x_out, sems.at[chunks]))
    for copy in copies:
        copy.start()
    for copy in copies:
        copy.wait()


def fetched(weight, x):
    return pl.pallas_call(
        fetch_kernel,
        out_shape=[pltpu.VMEM(weight.shape, weight.dtype), pltpu.VMEM(x.shape, x.dtype)],
        in_specs=[ANY, ANY],
        out_specs=[ANY, ANY],
        scratch_shapes=[pltpu.SemaphoreType.DMA((9,))],
        compiler_params=PARAMS,
        cost_estimate=pl.CostEstimate(flops=0, bytes_accessed=2 * weight.size * 2, transcendentals=0),
        name="fetch_weight",
    )(in_hbm(weight), x)


def rows_kernel(npool, place_ref, *refs):
    blocks = refs[:npool]
    weight_ref, out_ref, lhs = refs[npool:]
    steps, rows, _ = blocks[0].shape
    every = npool * rows
    for x, (apart, flip) in enumerate(block_order(npool)):
        owner = owner_of(place_ref[0], npool, apart, flip)
        for s in range(steps):
            lhs[pl.ds(pl.multiple_of(s * every + owner * rows, rows), rows), :] = blocks[x][s]
    multiply(lhs, weight_ref, out_ref, 1 - place_ref[1])


def multiply(lhs, weight_ref, out_ref, which):
    steps, every, half = out_ref.shape
    tile = min(half, 256)
    for i in range(half // tile):
        at = pl.ds(pl.multiple_of(which * half + i * tile, LANES), tile)
        terms = jnp.dot(lhs[...], weight_ref[:, at], preferred_element_type=F32)
        for s in range(steps):
            out_ref[s, :, i * tile : (i + 1) * tile] = terms[s * every : (s + 1) * every].astype(out_ref.dtype)


def other_projection(place, blocks, weight):
    npool = len(blocks)
    steps, rows, width = blocks[0].shape
    half = weight.shape[1] // 2
    every = steps * npool * rows
    return pl.pallas_call(
        functools.partial(rows_kernel, npool),
        out_shape=[
            jax.ShapeDtypeStruct((steps, npool * rows, half), BF16),
            jax.ShapeDtypeStruct((every, width), BF16),
        ],
        in_specs=[SMEM] + [VMEM] * (npool + 1),
        out_specs=[VMEM] * 2,
        compiler_params=PARAMS,
        cost_estimate=pl.CostEstimate(flops=2 * every * width * half, bytes_accessed=4_000_000, transcendentals=0),
        name="project_other",
    )(place, *blocks, weight)


def own_kernel(place_ref, lhs, weight_ref, out_ref):
    multiply(lhs, weight_ref, out_ref, place_ref[1])


def own_projection(place, lhs, weight, steps):
    every, width = lhs.shape
    half = weight.shape[1] // 2
    return pl.pallas_call(
        own_kernel,
        out_shape=jax.ShapeDtypeStruct((steps, every // steps, half), F32),
        in_specs=[SMEM] + [VMEM] * 2,
        out_specs=VMEM,
        compiler_params=PARAMS,
        cost_estimate=pl.CostEstimate(flops=2 * every * width * half, bytes_accessed=4_000_000, transcendentals=0),
        name="project_own",
    )(place, lhs, weight)


def block_order(npool):
    return [(apart, flip) for flip in (0, 1) for apart in range(npool // 2)]


def owner_of(me, npool, apart, flip):
    half = npool // 2
    pair, side = me // 2, me % 2
    side = 1 - side if flip else side
    return lax.rem(pair + half - apart, half) * 2 + side


def place_of(me, npool, holder):
    half = npool // 2
    apart = lax.rem(holder // 2 - me // 2 + half, half)
    flip = lax.rem(me + holder, 2)
    return flip * half + apart


def in_hbm(x):
    return pltpu.with_memory_space_constraint(x, pltpu.HBM)


def gathered(x, npool, later=None):
    half = npool // 2
    later = x if later is None else later
    ahead = lambda x, by: lax.ppermute(x, "pool", [(i, (i + 2 * by) % npool) for i in range(npool)])
    across = lambda x: lax.ppermute(x, "pool", [(i, i ^ 1) for i in range(npool)])
    straight = [x] + [ahead(x if by == half // 2 else later, by) for by in range(1, half)]
    partners = {by: across(straight[by]) for by in range(half) if by != 1}
    partners[1] = ahead(partners[0], 1)
    return straight + [partners[by] for by in range(half)]


def swap_halves(x):
    return lax.ppermute(x, "tp", [(0, 1), (1, 0)])


def shards(
    prompt_kv,
    prompt_lengths,
    page_slot,
    cache_kv,
    cache_fill,
    page_table,
    context_lengths,
    queries,
    new_kv,
    out_weight,
):
    npool = lax.axis_size("pool")
    me = lax.axis_index("pool").astype(I32)
    pages, _, heads, page_len, head_dim = prompt_kv.shape
    cache_pages = cache_kv.shape[0]
    pair = (pages + npool - 1) // npool
    tabs = tables(page_len, head_dim, pages)
    place = jnp.stack([me, lax.axis_index("tp").astype(I32)])
    table = page_table.T

    asked = asked_queries(table, context_lengths, queries, page_len, heads, head_dim)
    asked_all = gathered(asked, npool)
    arrived, own = rotated_pages(prompt_kv, page_slot, prompt_lengths, tabs, npool, pair, cache_pages)
    local = local_attention(table, context_lengths, cache_fill, asked, new_kv, cache_kv, tabs)
    parts = arrived_attention(place, own, asked_all, arrived)
    parts = lax.all_to_all(parts, "pool", split_axis=0, concat_axis=0, tiled=True)
    attention = merged(place, parts, local, queries.shape, heads, pair)
    weight, again = fetched(out_weight, attention)
    blocks = gathered(attention, npool, again)
    other_terms, lhs = other_projection(place, blocks, weight)
    other_terms = swap_halves(other_terms)
    terms = own_projection(place, lhs, weight, queries.shape[0])
    return (terms + other_terms.astype(F32)).astype(BF16)


def solution(mesh):
    return jax.shard_map(
        shards,
        mesh=mesh,
        in_specs=(
            P(("group", "pool"), None, "tp", None, None),
            P(("group", "pool"), None),
            P(("group", "pool")),
            P(("group", "pool"), None, "tp", None, None),
            P(("group", "pool")),
            P(("group", "pool"), None),
            P(("group", "pool")),
            P(None, ("group", "pool"), "tp"),
            P(None, ("group", "pool"), None, "tp", None),
            P("tp", "pool"),
        ),
        out_specs=P(None, "group", ("pool", "tp")),
        check_vma=False,
    )
```

```python
import functools

import jax
import jax.numpy as jnp
import numpy as np
from jax import lax
from jax.experimental import pallas as pl
from jax.experimental.pallas import tpu as pltpu
from jax.sharding import PartitionSpec as P

ROPE_BASE = 500000.0
BF16, F32, I32 = jnp.bfloat16, jnp.float32, jnp.int32
SMEM = pl.BlockSpec(memory_space=pltpu.SMEM)
VMEM = pl.BlockSpec(memory_space=pltpu.VMEM)
ANY = pl.BlockSpec(memory_space=pl.ANY)
PARAMS = pltpu.CompilerParams(vmem_limit_bytes=24 * 2**20)
LANES = 128
STAT_ROWS = 16
CODE = 256


def tables(page_len, head_dim, pages):
    half = head_dim // 2
    freq = ROPE_BASE ** (-(np.arange(half) * 2.0) / head_dim)
    freq = np.concatenate([freq, freq])[None, :]
    sign = np.concatenate([-np.ones(half), np.ones(half)])[None, :]
    token = np.arange(page_len)[:, None] * freq
    first = np.arange(pages)[:, None] * page_len * freq
    out = (np.cos(token), sign * np.sin(token), np.cos(first), sign * np.sin(first), freq, sign)
    return [jnp.asarray(x, F32) for x in out]


def rope_kernel(
    npool, cache_pages, per, slot_ref, len_ref, pages_ref, ct_ref, st_ref, cp_ref, sp_ref, out_ref, own_ref, count
):
    _, _, heads, page_len, head_dim = pages_ref.shape

    @pl.when(pl.program_id(0) == 0)
    def _():
        items = own_ref.shape[0] // 3
        for e in range(npool):
            count[e] = 0
        for i in range(items):
            own_ref[i] = 0
            own_ref[items + i] = 0
            own_ref[2 * items + i] = -1
        for n in range(slot_ref.shape[0]):
            slot = slot_ref[n]
            target = slot // cache_pages
            at = target * (items // npool) + count[target]
            count[target] = count[target] + 1
            own_ref[at] = n
            own_ref[items + at] = page_place(len_ref, page_len, n)[1]
            own_ref[2 * items + at] = slot - target * cache_pages

    for i in range(per):
        number, _ = page_place(len_ref, page_len, pl.program_id(0) * per + i)
        c0, s0 = cp_ref[pl.ds(number, 1), :], sp_ref[pl.ds(number, 1), :]
        ct, st = ct_ref[...], st_ref[...]
        cos = c0 * ct - s0 * st
        sin = s0 * ct + c0 * st
        for k in range(heads):
            x = pages_ref[i, 0, k].astype(F32)
            out_ref[i, 0, k] = (x * cos + pltpu.roll(x, head_dim // 2, 1) * sin).astype(BF16)
            out_ref[i, 1, k] = pages_ref[i, 1, k]


def page_place(len_ref, page_len, n):
    begin = jnp.int32(0)
    number, fill = jnp.int32(0), jnp.int32(0)
    for q in range(len_ref.shape[1]):
        length = len_ref[0, q]
        count = (length + page_len - 1) // page_len
        here = (n >= begin) & (n < begin + count)
        number = jnp.where(here, n - begin, number)
        fill = jnp.where(here, jnp.clip(length - (n - begin) * page_len, 0, page_len), fill)
        begin = begin + count
    return number, fill


def rotated_pages(prompt_kv, page_slot, prompt_lengths, tabs, npool, pair, cache_pages):
    pages, _, heads, page_len, head_dim = prompt_kv.shape
    per = pages // 2
    ct, st, cp, sp, _, _ = tabs
    whole = lambda x: pl.BlockSpec(x.shape, lambda i: (0, 0))
    return pl.pallas_call(
        functools.partial(rope_kernel, npool, cache_pages, per),
        grid=(pages // per,),
        out_shape=[
            jax.ShapeDtypeStruct(prompt_kv.shape, BF16),
            jax.ShapeDtypeStruct((3 * npool * pair,), I32),
        ],
        in_specs=[
            SMEM,
            SMEM,
            pl.BlockSpec((per,) + prompt_kv.shape[1:], lambda i: (i, 0, 0, 0, 0)),
            whole(ct),
            whole(st),
            whole(cp),
            whole(sp),
        ],
        out_specs=[pl.BlockSpec((per,) + prompt_kv.shape[1:], lambda i: (i, 0, 0, 0, 0)), SMEM],
        scratch_shapes=[pltpu.SMEM((npool,), I32)],
        compiler_params=PARAMS,
        cost_estimate=pl.CostEstimate(flops=6_000_000, bytes_accessed=2_000_000, transcendentals=0),
        name="rope_pages",
    )(*[in_hbm(x) for x in (page_slot, prompt_lengths, prompt_kv, ct, st, cp, sp)])


def asked_kernel(page_len, heads, table_ref, context_ref, q_ref, out_ref, spread):
    most, rows = table_ref.shape
    steps, _, width = q_ref.shape
    block, head_dim = out_ref.shape[1:]
    per = width // head_dim // heads
    for s in range(steps):
        for h in range(heads * per):
            k, g = divmod(h, per)
            at = pl.ds(k * steps * per + s * per + g, rows, stride=block)
            spread[at, :] = q_ref[s, :, h * head_dim : (h + 1) * head_dim].astype(F32)
    for r in range(rows):
        out_ref[r] = spread[r * block : (r + 1) * block, :].astype(BF16)
    lane = lax.broadcasted_iota(I32, (block, LANES), 1)
    line = lax.broadcasted_iota(I32, (block, LANES), 0)
    request = jnp.zeros((block, LANES), I32)
    left = jnp.zeros((block, LANES), I32)
    for r in range(rows):
        context = context_ref[r]
        for j in range(most):
            here = lane == table_ref[j, r]
            request = jnp.where(here, r, request)
            left = jnp.where(here, jnp.clip(context - j * page_len, 0, page_len), left)
    out_ref[rows] = jnp.where(line == 0, request, left).astype(F32).astype(BF16)


def asked_queries(table, context, queries, page_len, heads, head_dim):
    steps, rows, width = queries.shape
    block = steps * width // head_dim
    return pl.pallas_call(
        functools.partial(asked_kernel, page_len, heads),
        out_shape=jax.ShapeDtypeStruct((rows + 1, block, head_dim), BF16),
        in_specs=[SMEM, SMEM, VMEM],
        out_specs=VMEM,
        scratch_shapes=[pltpu.VMEM((rows * block, head_dim), F32)],
        compiler_params=PARAMS,
        cost_estimate=pl.CostEstimate(flops=100_000, bytes_accessed=300_000, transcendentals=0),
        name="asked_queries",
    )(in_hbm(table), in_hbm(context), in_hbm(queries))


def read_scalar(x, pick):
    return jnp.max(jnp.where(pick, x, -2.0)).astype(I32)


def transposed_scores(queries, keys, group):
    turned = jnp.transpose(queries, (1, 0))
    chain = lax.broadcasted_iota(I32, (1, turned.shape[1]), 1) // group
    spread = [turned * jnp.where(chain == c, 1.0, 0.0).astype(BF16) for c in range(len(keys))]
    scores = jnp.dot(
        jnp.concatenate(keys, axis=1), jnp.concatenate(spread, axis=0), preferred_element_type=F32
    )
    return scores * (queries.shape[1] ** -0.5)


def weighted_values(weights, values):
    heads, head_dim = len(values), values[0].shape[1]
    group = weights.shape[0] // heads
    out = jnp.dot(weights, jnp.concatenate(values, axis=1), preferred_element_type=F32)
    parts = [out[k * group : (k + 1) * group, k * head_dim : (k + 1) * head_dim] for k in range(heads)]
    return jnp.concatenate(parts, axis=0)


def lane_values(scalars, lanes_each, shape):
    chain = lax.broadcasted_iota(I32, shape, 1) // lanes_each
    out = jnp.zeros(shape, I32)
    for i, x in enumerate(scalars):
        out = jnp.where(chain == i, x, out)
    return out


def local_kernel(
    page_len,
    heads,
    table_ref,
    context_ref,
    fill_ref,
    q_ref,
    new_ref,
    freq_ref,
    sign_ref,
    cache_ref,
    o_ref,
    stat_ref,
    kv,
    sems,
    kf,
    vf,
    position,
    where,
):
    rows, block, head_dim = q_ref.shape
    rows = rows - 1
    steps = new_ref.shape[0]
    most = table_ref.shape[0]
    group = block // heads
    per = group // steps
    together = LANES // block

    zeros = rows * most

    def copy(r, j):
        n = r * most + j
        return pltpu.make_async_copy(cache_ref.at[table_ref[j, r]], kv.at[n], sems.at[n])

    def seen_tokens(r, j):
        return jnp.minimum(fill_ref[table_ref[j, r]], context_ref[r] - j * page_len)

    for r in range(rows):
        for j in range(most):
            needed = seen_tokens(r, j) > 0
            where[r * most + j] = jnp.where(needed, r * most + j, zeros)
            pl.when(needed)(copy(r, j).start)
    kv[zeros] = jnp.zeros(kv.shape[1:], BF16)
    kf[...] = jnp.zeros_like(kf)
    vf[...] = jnp.zeros_like(vf)
    for r in range(rows):
        position[r : r + 1, :] = jnp.full((1, head_dim), context_ref[r], I32)
    for u in range(steps):
        angle = (position[...] + u).astype(F32) * freq_ref[...]
        cos, sin = jnp.cos(angle), jnp.sin(angle) * sign_ref[...]
        for k in range(heads):
            x = new_ref[u, :, k * head_dim : (k + 1) * head_dim].astype(F32)
            at = k * group + u
            kf[pl.ds(at, rows, stride=block), :] = x * cos + pltpu.roll(x, head_dim // 2, 1) * sin
            x = new_ref[u, :, (heads + k) * head_dim : (heads + k + 1) * head_dim].astype(F32)
            vf[pl.ds(at, rows, stride=block), :] = x
    token = lax.broadcasted_iota(I32, (page_len, LANES), 0)
    fresh = lax.broadcasted_iota(I32, (group, LANES), 0)
    step = lax.broadcasted_iota(I32, (group, LANES), 1) % group // per
    fresh_mask = (fresh <= step) & (fresh < steps)

    groups = [range(i * together, (i + 1) * together) for i in range(rows // together)]
    all_scores, all_weights = [], []
    for i, requests in enumerate(groups):
        if i % 2 == 0:
            for r in range(i * together, min(rows, (i + 2) * together)):
                for j in range(most):
                    pl.when(where[r * most + j] < zeros)(copy(r, j).wait)
        keys = []
        for r in requests:
            for k in range(heads):
                at = r * block + k * group
                pages = [kv[where[r * most + j], 0, k] for j in range(most)]
                keys.append(jnp.concatenate(pages + [kf[at : at + group, :].astype(BF16)], axis=0))
        queries = q_ref[i * together : (i + 1) * together].reshape(LANES, head_dim)
        all_scores.append(transposed_scores(queries, keys, group))
    for i, requests in enumerate(groups):
        mask = []
        for j in range(most):
            seen = [seen_tokens(r, j) for r in requests]
            mask.append(token < lane_values(seen, block, (1, LANES)))
        parts = [
            jnp.where(m, all_scores[i][n * page_len : n * page_len + m.shape[0]], -jnp.inf)
            for n, m in enumerate(mask + [fresh_mask])
        ]
        top = functools.reduce(jnp.maximum, [jnp.max(x, axis=0, keepdims=True) for x in parts])
        parts = [jnp.exp(x - top) for x in parts]
        total = functools.reduce(jnp.add, [jnp.sum(x, axis=0, keepdims=True) for x in parts])
        stats = jnp.concatenate(
            [parts[most], jnp.broadcast_to(top, (8, LANES)), jnp.broadcast_to(total, (8, LANES))], axis=0
        )
        stats = jnp.transpose(stats, (1, 0))
        stat_ref[i * LANES : (i + 1) * LANES, : stats.shape[1]] = stats
        weights = [jnp.transpose(x.astype(BF16), (1, 0)) for x in parts[:most]]
        weights.append(stats[:, :group].astype(BF16))
        all_weights.append(jnp.concatenate(weights, axis=1))
    for i, requests in enumerate(groups):
        for x, r in enumerate(requests):
            both = []
            for k in range(heads):
                at = r * block + k * group
                pages = [kv[where[r * most + j], 1, k] for j in range(most)]
                both.append(jnp.concatenate(pages + [vf[at : at + group, :].astype(BF16)], axis=0))
            both = weighted_values(all_weights[i][x * block : (x + 1) * block, :], both)
            o_ref[r * block : (r + 1) * block, :] = both


def local_attention(table, context, fills, queries, new_kv, cache_kv, tabs):
    rows, block, _ = queries.shape
    rows = rows - 1
    steps = new_kv.shape[0]
    slots, _, heads, page_len, head_dim = cache_kv.shape
    flat = (rows * block, head_dim)
    freq, sign = tabs[4:]
    return pl.pallas_call(
        functools.partial(local_kernel, page_len, heads),
        out_shape=[jax.ShapeDtypeStruct(flat, F32)] * 2,
        in_specs=[SMEM] * 3 + [VMEM] * 4 + [ANY],
        out_specs=[VMEM] * 2,
        scratch_shapes=[
            pltpu.VMEM((table.size + 1, 2, heads, page_len, head_dim), BF16),
            pltpu.SemaphoreType.DMA((table.size,)),
            pltpu.VMEM(flat, F32),
            pltpu.VMEM(flat, F32),
            pltpu.VMEM((rows, head_dim), I32),
            pltpu.SMEM((table.size,), I32),
        ],
        compiler_params=PARAMS,
        cost_estimate=pl.CostEstimate(flops=800_000_000, bytes_accessed=12_000_000, transcendentals=400_000),
        name="local_attention",
    )(
        *[in_hbm(x) for x in (table, context, fills)],
        queries,
        new_kv.reshape(steps, rows, 2 * heads * head_dim),
        *[in_hbm(x) for x in (freq, sign, cache_kv)],
    )


def pieces(x):
    high = x.astype(BF16).astype(F32)
    middle = (x - high).astype(BF16).astype(F32)
    return [high, middle, x - high - middle]


def arrived_kernel(npool, pair, me_ref, own_ref, *refs):
    blocks = refs[:npool]
    pages_ref, out_ref, queries = refs[npool:]
    items = npool * pair
    _, _, heads, page_len, head_dim = pages_ref.shape
    rows, block = blocks[0].shape[0] - 1, blocks[0].shape[1]
    group = block // heads
    together = LANES // block
    me = me_ref[0]
    owners = [owner_of(me, npool, apart, flip) for apart, flip in block_order(npool)]
    lane = lax.broadcasted_iota(I32, (1, LANES), 1)
    codes = [x[rows, :STAT_ROWS, :].astype(F32) for x in blocks]
    codes = [x[0:1] * CODE + x[1:2] for x in codes]
    number, seen, request = [], [], []
    for x in range(items):
        at = owners[x // pair] * pair + x % pair
        slot = own_ref[2 * items + at]
        code = jnp.maximum(read_scalar(codes[x // pair], lane == slot), 0)
        reader, left = code // CODE, code % CODE
        queries[x * block : (x + 1) * block, :] = blocks[x // pair][reader]
        number.append(own_ref[at])
        seen.append(jnp.minimum(left, own_ref[items + at]))
        request.append(jnp.where(slot >= 0, reader, -1))
    token = lax.broadcasted_iota(I32, (page_len, LANES), 0)
    groups = [range(i * together, (i + 1) * together) for i in range(items // together)]
    all_scores, all_weights = [], []
    for i, own in enumerate(groups):
        keys = [pages_ref[number[x], 0, k] for x in own for k in range(heads)]
        all_scores.append(transposed_scores(queries[i * LANES : (i + 1) * LANES, :], keys, group))
    for i, own in enumerate(groups):
        limit = lane_values([seen[x] for x in own], block, (1, LANES))
        scores = jnp.where(token < limit, all_scores[i], -jnp.inf)
        top = jnp.max(scores, axis=0, keepdims=True)
        top = jnp.where(top > -jnp.inf, top, 0.0)
        weights = jnp.exp(scores - top)
        stats = pieces(top) + pieces(jnp.sum(weights, axis=0, keepdims=True))
        stats.append(lane_values([request[x] for x in own], block, (1, LANES)).astype(F32))
        stats = jnp.concatenate(stats + [jnp.zeros((STAT_ROWS - len(stats), LANES), F32)], axis=0).astype(BF16)
        for place in sorted({x // pair for x in own}):
            out_ref[owners[place], pair * block : pair * block + STAT_ROWS, :] = stats
        all_weights.append(jnp.transpose(weights.astype(BF16), (1, 0)))
    for i, own in enumerate(groups):
        for c, x in enumerate(own):
            both = [pages_ref[number[x], 1, k] for k in range(heads)]
            both = weighted_values(all_weights[i][c * block : (c + 1) * block, :], both)
            at = (x % pair) * block
            out_ref[owners[x // pair], at : at + block, :] = both.astype(BF16)


def arrived_attention(me, own, blocks, arrived):
    npool = len(blocks)
    head_dim = arrived.shape[4]
    block = blocks[0].shape[1]
    items = own.shape[0] // 3
    pair = items // npool
    return pl.pallas_call(
        functools.partial(arrived_kernel, npool, pair),
        out_shape=jax.ShapeDtypeStruct((npool, pair * block + STAT_ROWS, head_dim), BF16),
        in_specs=[SMEM] * 2 + [VMEM] * (npool + 1),
        out_specs=VMEM,
        scratch_shapes=[pltpu.VMEM((items * block, head_dim), BF16)],
        compiler_params=PARAMS,
        cost_estimate=pl.CostEstimate(flops=200_000_000, bytes_accessed=4_000_000, transcendentals=70_000),
        name="arrived_attention",
    )(me, own, *blocks, arrived)


def merge_kernel(pair, heads, me_ref, parts_ref, o_ref, stat_ref, out_ref, mixed, top, total, turned):
    npool = parts_ref.shape[0]
    steps, rows, width = out_ref.shape
    head_dim = o_ref.shape[1]
    per = width // head_dim // heads
    group = steps * per
    block = heads * group
    me = me_ref[0]
    shape = top.shape
    mixed[...] = o_ref[...]
    top[...] = jnp.broadcast_to(stat_ref[:, group : group + 1], shape)
    total[...] = jnp.broadcast_to(stat_ref[:, group + 8 : group + 9], shape)
    tops, totals, readers = [], [], []
    chain = lax.broadcasted_iota(I32, (1, LANES), 1) // block
    for d in range(npool):
        x = parts_ref[d, pair * block : pair * block + STAT_ROWS, :].astype(F32)
        tops.append(x[0:1] + x[1:2] + x[2:3])
        totals.append(x[3:4] + x[4:5] + x[5:6])
        readers.append(x[6:7])
    empty = [jnp.zeros((LANES // 2 - npool, LANES), F32)]
    turned[...] = jnp.transpose(jnp.concatenate(tops + empty + totals + empty, axis=0), (1, 0))
    for d in range(npool):
        for p in range(pair):
            part = lax.rem(place_of(me, npool, d) * pair + p, LANES // block)
            r = read_scalar(readers[d], chain == part)
            there = r >= 0
            at = pl.ds(pl.multiple_of(jnp.maximum(r, 0) * block, block), block)
            lane = pl.ds(pl.multiple_of(part * block, block), block)
            m = jnp.broadcast_to(turned[lane, d : d + 1], (block, head_dim))
            l = jnp.broadcast_to(turned[lane, LANES // 2 + d : LANES // 2 + d + 1], (block, head_dim))
            seen = (l > 0.0) & there
            o = parts_ref[d, p * block : (p + 1) * block, :].astype(F32)
            old = top[at, :]
            new = jnp.where(seen, jnp.maximum(old, m), old)
            a = jnp.exp(old - new)
            b = jnp.where(seen, jnp.exp(m - new), 0.0)
            top[at, :] = new
            total[at, :] = total[at, :] * a + l * b
            mixed[at, :] = mixed[at, :] * a + o * b
    for s in range(steps):
        for h in range(heads * per):
            k, g = divmod(h, per)
            at = pl.ds(k * group + s * per + g, rows, stride=block)
            out_ref[s, :, h * head_dim : (h + 1) * head_dim] = (mixed[at, :] / total[at, :]).astype(BF16)


def merged(me, parts, local, shape, heads, pair):
    flat = local[0].shape
    return pl.pallas_call(
        functools.partial(merge_kernel, pair, heads),
        out_shape=jax.ShapeDtypeStruct(shape, BF16),
        in_specs=[SMEM] + [VMEM] * 3,
        out_specs=VMEM,
        scratch_shapes=[pltpu.VMEM(flat, F32)] * 3 + [pltpu.VMEM((LANES, LANES), F32)],
        compiler_params=PARAMS,
        cost_estimate=pl.CostEstimate(flops=2_000_000, bytes_accessed=1_500_000, transcendentals=100_000),
        name="merge",
    )(me, parts, *local)


def fetch_kernel(weight_ref, x_ref, weight_out, x_out, sems):
    chunks = sems.shape[0] - 1
    rows = weight_ref.shape[0] // chunks
    copies = []
    for i in range(chunks):
        at = pl.ds(i * rows, rows)
        copies.append(pltpu.make_async_copy(weight_ref.at[at], weight_out.at[at], sems.at[i]))
    copies.append(pltpu.make_async_copy(x_ref, x_out, sems.at[chunks]))
    for copy in copies:
        copy.start()
    for copy in copies:
        copy.wait()


def fetched(weight, x):
    return pl.pallas_call(
        fetch_kernel,
        out_shape=[pltpu.VMEM(weight.shape, weight.dtype), pltpu.VMEM(x.shape, x.dtype)],
        in_specs=[ANY, ANY],
        out_specs=[ANY, ANY],
        scratch_shapes=[pltpu.SemaphoreType.DMA((9,))],
        compiler_params=PARAMS,
        cost_estimate=pl.CostEstimate(flops=0, bytes_accessed=2 * weight.size * 2, transcendentals=0),
        name="fetch_weight",
    )(in_hbm(weight), x)


def rows_kernel(npool, place_ref, *refs):
    blocks = refs[:npool]
    weight_ref, out_ref, lhs = refs[npool:]
    steps, rows, _ = blocks[0].shape
    every = npool * rows
    for x, (apart, flip) in enumerate(block_order(npool)):
        owner = owner_of(place_ref[0], npool, apart, flip)
        for s in range(steps):
            lhs[pl.ds(pl.multiple_of(s * every + owner * rows, rows), rows), :] = blocks[x][s]
    multiply(lhs, weight_ref, out_ref, 1 - place_ref[1])


def multiply(lhs, weight_ref, out_ref, which):
    steps, every, half = out_ref.shape
    tile = min(half, 256)
    for i in range(half // tile):
        at = pl.ds(pl.multiple_of(which * half + i * tile, LANES), tile)
        terms = jnp.dot(lhs[...], weight_ref[:, at], preferred_element_type=F32)
        for s in range(steps):
            out_ref[s, :, i * tile : (i + 1) * tile] = terms[s * every : (s + 1) * every].astype(out_ref.dtype)


def other_projection(place, blocks, weight):
    npool = len(blocks)
    steps, rows, width = blocks[0].shape
    half = weight.shape[1] // 2
    every = steps * npool * rows
    return pl.pallas_call(
        functools.partial(rows_kernel, npool),
        out_shape=[
            jax.ShapeDtypeStruct((steps, npool * rows, half), BF16),
            jax.ShapeDtypeStruct((every, width), BF16),
        ],
        in_specs=[SMEM] + [VMEM] * (npool + 1),
        out_specs=[VMEM] * 2,
        compiler_params=PARAMS,
        cost_estimate=pl.CostEstimate(flops=2 * every * width * half, bytes_accessed=4_000_000, transcendentals=0),
        name="project_other",
    )(place, *blocks, weight)


def own_kernel(place_ref, lhs, weight_ref, out_ref):
    multiply(lhs, weight_ref, out_ref, place_ref[1])


def own_projection(place, lhs, weight, steps):
    every, width = lhs.shape
    half = weight.shape[1] // 2
    return pl.pallas_call(
        own_kernel,
        out_shape=jax.ShapeDtypeStruct((steps, every // steps, half), F32),
        in_specs=[SMEM] + [VMEM] * 2,
        out_specs=VMEM,
        compiler_params=PARAMS,
        cost_estimate=pl.CostEstimate(flops=2 * every * width * half, bytes_accessed=4_000_000, transcendentals=0),
        name="project_own",
    )(place, lhs, weight)


def block_order(npool):
    return [(apart, flip) for flip in (0, 1) for apart in range(npool // 2)]


def owner_of(me, npool, apart, flip):
    half = npool // 2
    pair, side = me // 2, me % 2
    side = 1 - side if flip else side
    return lax.rem(pair + half - apart, half) * 2 + side


def place_of(me, npool, holder):
    half = npool // 2
    apart = lax.rem(holder // 2 - me // 2 + half, half)
    flip = lax.rem(me + holder, 2)
    return flip * half + apart


def in_hbm(x):
    return pltpu.with_memory_space_constraint(x, pltpu.HBM)


def gathered(x, npool, later=None):
    half = npool // 2
    later = x if later is None else later
    ahead = lambda x, by: lax.ppermute(x, "pool", [(i, (i + 2 * by) % npool) for i in range(npool)])
    across = lambda x: lax.ppermute(x, "pool", [(i, i ^ 1) for i in range(npool)])
    partner = across(x)
    last = x
    if later is not x:
        last, partner = lax.optimization_barrier((later, partner))
    sent = {half // 2: x, 1: last}
    straight = [x] + [ahead(sent.get(by, later), by) for by in range(1, half)]
    return straight + [partner] + [across(y) for y in straight[1:]]


def swap_halves(x):
    return lax.ppermute(x, "tp", [(0, 1), (1, 0)])


def shards(
    prompt_kv,
    prompt_lengths,
    page_slot,
    cache_kv,
    cache_fill,
    page_table,
    context_lengths,
    queries,
    new_kv,
    out_weight,
):
    npool = lax.axis_size("pool")
    me = lax.axis_index("pool").astype(I32)
    pages, _, heads, page_len, head_dim = prompt_kv.shape
    cache_pages = cache_kv.shape[0]
    pair = (pages + npool - 1) // npool
    tabs = tables(page_len, head_dim, pages)
    place = jnp.stack([me, lax.axis_index("tp").astype(I32)])
    table = page_table.T

    asked = asked_queries(table, context_lengths, queries, page_len, heads, head_dim)
    asked_all = gathered(asked, npool)
    arrived, own = rotated_pages(prompt_kv, page_slot, prompt_lengths, tabs, npool, pair, cache_pages)
    local = local_attention(table, context_lengths, cache_fill, asked, new_kv, cache_kv, tabs)
    parts = arrived_attention(place, own, asked_all, arrived)
    parts = lax.all_to_all(parts, "pool", split_axis=0, concat_axis=0, tiled=True)
    attention = merged(place, parts, local, queries.shape, heads, pair)
    weight, again = fetched(out_weight, attention)
    blocks = gathered(attention, npool, again)
    other_terms, lhs = other_projection(place, blocks, weight)
    other_terms = swap_halves(other_terms)
    terms = own_projection(place, lhs, weight, queries.shape[0])
    return (terms + other_terms.astype(F32)).astype(BF16)


def solution(mesh):
    return jax.shard_map(
        shards,
        mesh=mesh,
        in_specs=(
            P(("group", "pool"), None, "tp", None, None),
            P(("group", "pool"), None),
            P(("group", "pool")),
            P(("group", "pool"), None, "tp", None, None),
            P(("group", "pool")),
            P(("group", "pool"), None),
            P(("group", "pool")),
            P(None, ("group", "pool"), "tp"),
            P(None, ("group", "pool"), None, "tp", None),
            P("tp", "pool"),
        ),
        out_specs=P(None, "group", ("pool", "tp")),
        check_vma=False,
    )
```

```python
import functools

import jax
import jax.numpy as jnp
import numpy as np
from jax import lax
from jax.experimental import pallas as pl
from jax.experimental.pallas import tpu as pltpu
from jax.sharding import PartitionSpec as P

ROPE_BASE = 500000.0
BF16, F32, I32 = jnp.bfloat16, jnp.float32, jnp.int32
SMEM = pl.BlockSpec(memory_space=pltpu.SMEM)
VMEM = pl.BlockSpec(memory_space=pltpu.VMEM)
ANY = pl.BlockSpec(memory_space=pl.ANY)
PARAMS = pltpu.CompilerParams(vmem_limit_bytes=24 * 2**20)
LANES = 128
STAT_ROWS = 16
CODE = 256


def tables(page_len, head_dim, pages):
    half = head_dim // 2
    freq = ROPE_BASE ** (-(np.arange(half) * 2.0) / head_dim)
    freq = np.concatenate([freq, freq])[None, :]
    sign = np.concatenate([-np.ones(half), np.ones(half)])[None, :]
    token = np.arange(page_len)[:, None] * freq
    first = np.arange(pages)[:, None] * page_len * freq
    out = (np.cos(token), sign * np.sin(token), np.cos(first), sign * np.sin(first), freq, sign)
    return [jnp.asarray(x, F32) for x in out]


def rope_kernel(
    npool, cache_pages, per, slot_ref, len_ref, pages_ref, ct_ref, st_ref, cp_ref, sp_ref, out_ref, own_ref, count
):
    _, _, heads, page_len, head_dim = pages_ref.shape

    @pl.when(pl.program_id(0) == 0)
    def _():
        items = own_ref.shape[0] // 3
        for e in range(npool):
            count[e] = 0
        for i in range(items):
            own_ref[i] = 0
            own_ref[items + i] = 0
            own_ref[2 * items + i] = -1
        for n in range(slot_ref.shape[0]):
            slot = slot_ref[n]
            target = slot // cache_pages
            at = target * (items // npool) + count[target]
            count[target] = count[target] + 1
            own_ref[at] = n
            own_ref[items + at] = page_place(len_ref, page_len, n)[1]
            own_ref[2 * items + at] = slot - target * cache_pages

    for i in range(per):
        number, _ = page_place(len_ref, page_len, pl.program_id(0) * per + i)
        c0, s0 = cp_ref[pl.ds(number, 1), :], sp_ref[pl.ds(number, 1), :]
        ct, st = ct_ref[...], st_ref[...]
        cos = c0 * ct - s0 * st
        sin = s0 * ct + c0 * st
        for k in range(heads):
            x = pages_ref[i, 0, k].astype(F32)
            out_ref[i, 0, k] = (x * cos + pltpu.roll(x, head_dim // 2, 1) * sin).astype(BF16)
            out_ref[i, 1, k] = pages_ref[i, 1, k]


def page_place(len_ref, page_len, n):
    begin = jnp.int32(0)
    number, fill = jnp.int32(0), jnp.int32(0)
    for q in range(len_ref.shape[1]):
        length = len_ref[0, q]
        count = (length + page_len - 1) // page_len
        here = (n >= begin) & (n < begin + count)
        number = jnp.where(here, n - begin, number)
        fill = jnp.where(here, jnp.clip(length - (n - begin) * page_len, 0, page_len), fill)
        begin = begin + count
    return number, fill


def rotated_pages(prompt_kv, page_slot, prompt_lengths, tabs, npool, pair, cache_pages):
    pages, _, heads, page_len, head_dim = prompt_kv.shape
    per = pages // 2
    ct, st, cp, sp, _, _ = tabs
    whole = lambda x: pl.BlockSpec(x.shape, lambda i: (0, 0))
    return pl.pallas_call(
        functools.partial(rope_kernel, npool, cache_pages, per),
        grid=(pages // per,),
        out_shape=[
            jax.ShapeDtypeStruct(prompt_kv.shape, BF16),
            jax.ShapeDtypeStruct((3 * npool * pair,), I32),
        ],
        in_specs=[
            SMEM,
            SMEM,
            pl.BlockSpec((per,) + prompt_kv.shape[1:], lambda i: (i, 0, 0, 0, 0)),
            whole(ct),
            whole(st),
            whole(cp),
            whole(sp),
        ],
        out_specs=[pl.BlockSpec((per,) + prompt_kv.shape[1:], lambda i: (i, 0, 0, 0, 0)), SMEM],
        scratch_shapes=[pltpu.SMEM((npool,), I32)],
        compiler_params=PARAMS,
        cost_estimate=pl.CostEstimate(flops=6_000_000, bytes_accessed=2_000_000, transcendentals=0),
        name="rope_pages",
    )(*[in_hbm(x) for x in (page_slot, prompt_lengths, prompt_kv, ct, st, cp, sp)])


def asked_kernel(page_len, heads, table_ref, context_ref, q_ref, out_ref, spread):
    most, rows = table_ref.shape
    steps, _, width = q_ref.shape
    block, head_dim = out_ref.shape[1:]
    per = width // head_dim // heads
    for s in range(steps):
        for h in range(heads * per):
            k, g = divmod(h, per)
            at = pl.ds(k * steps * per + s * per + g, rows, stride=block)
            spread[at, :] = q_ref[s, :, h * head_dim : (h + 1) * head_dim].astype(F32)
    for r in range(rows):
        out_ref[r] = spread[r * block : (r + 1) * block, :].astype(BF16)
    lane = lax.broadcasted_iota(I32, (block, LANES), 1)
    line = lax.broadcasted_iota(I32, (block, LANES), 0)
    request = jnp.zeros((block, LANES), I32)
    left = jnp.zeros((block, LANES), I32)
    for r in range(rows):
        context = context_ref[r]
        for j in range(most):
            here = lane == table_ref[j, r]
            request = jnp.where(here, r, request)
            left = jnp.where(here, jnp.clip(context - j * page_len, 0, page_len), left)
    out_ref[rows] = jnp.where(line == 0, request, left).astype(F32).astype(BF16)


def asked_queries(table, context, queries, page_len, heads, head_dim):
    steps, rows, width = queries.shape
    block = steps * width // head_dim
    return pl.pallas_call(
        functools.partial(asked_kernel, page_len, heads),
        out_shape=jax.ShapeDtypeStruct((rows + 1, block, head_dim), BF16),
        in_specs=[SMEM, SMEM, VMEM],
        out_specs=VMEM,
        scratch_shapes=[pltpu.VMEM((rows * block, head_dim), F32)],
        compiler_params=PARAMS,
        cost_estimate=pl.CostEstimate(flops=100_000, bytes_accessed=300_000, transcendentals=0),
        name="asked_queries",
    )(in_hbm(table), in_hbm(context), in_hbm(queries))


def read_scalar(x, pick):
    return jnp.max(jnp.where(pick, x, -2.0)).astype(I32)


def transposed_scores(queries, keys, group):
    turned = jnp.transpose(queries, (1, 0))
    chain = lax.broadcasted_iota(I32, (1, turned.shape[1]), 1) // group
    spread = [turned * jnp.where(chain == c, 1.0, 0.0).astype(BF16) for c in range(len(keys))]
    scores = jnp.dot(
        jnp.concatenate(keys, axis=1), jnp.concatenate(spread, axis=0), preferred_element_type=F32
    )
    return scores * (queries.shape[1] ** -0.5)


def weighted_values(weights, values):
    heads, head_dim = len(values), values[0].shape[1]
    group = weights.shape[0] // heads
    out = jnp.dot(weights, jnp.concatenate(values, axis=1), preferred_element_type=F32)
    parts = [out[k * group : (k + 1) * group, k * head_dim : (k + 1) * head_dim] for k in range(heads)]
    return jnp.concatenate(parts, axis=0)


def lane_values(scalars, lanes_each, shape):
    chain = lax.broadcasted_iota(I32, shape, 1) // lanes_each
    out = jnp.zeros(shape, I32)
    for i, x in enumerate(scalars):
        out = jnp.where(chain == i, x, out)
    return out


def local_kernel(
    page_len,
    heads,
    table_ref,
    context_ref,
    fill_ref,
    q_ref,
    new_ref,
    freq_ref,
    sign_ref,
    cache_ref,
    o_ref,
    stat_ref,
    kv,
    sems,
    kf,
    vf,
    position,
    where,
):
    rows, block, head_dim = q_ref.shape
    rows = rows - 1
    steps = new_ref.shape[0]
    most = table_ref.shape[0]
    group = block // heads
    per = group // steps
    together = LANES // block

    zeros = rows * most

    def copy(r, j):
        n = r * most + j
        return pltpu.make_async_copy(cache_ref.at[table_ref[j, r]], kv.at[n], sems.at[n])

    def seen_tokens(r, j):
        return jnp.minimum(fill_ref[table_ref[j, r]], context_ref[r] - j * page_len)

    for r in range(rows):
        for j in range(most):
            needed = seen_tokens(r, j) > 0
            where[r * most + j] = jnp.where(needed, r * most + j, zeros)
            pl.when(needed)(copy(r, j).start)
    kv[zeros] = jnp.zeros(kv.shape[1:], BF16)
    kf[...] = jnp.zeros_like(kf)
    vf[...] = jnp.zeros_like(vf)
    for r in range(rows):
        position[r : r + 1, :] = jnp.full((1, head_dim), context_ref[r], I32)
    for u in range(steps):
        angle = (position[...] + u).astype(F32) * freq_ref[...]
        cos, sin = jnp.cos(angle), jnp.sin(angle) * sign_ref[...]
        for k in range(heads):
            x = new_ref[u, :, k * head_dim : (k + 1) * head_dim].astype(F32)
            at = k * group + u
            kf[pl.ds(at, rows, stride=block), :] = x * cos + pltpu.roll(x, head_dim // 2, 1) * sin
            x = new_ref[u, :, (heads + k) * head_dim : (heads + k + 1) * head_dim].astype(F32)
            vf[pl.ds(at, rows, stride=block), :] = x
    token = lax.broadcasted_iota(I32, (page_len, LANES), 0)
    fresh = lax.broadcasted_iota(I32, (group, LANES), 0)
    step = lax.broadcasted_iota(I32, (group, LANES), 1) % group // per
    fresh_mask = (fresh <= step) & (fresh < steps)

    groups = [range(i * together, (i + 1) * together) for i in range(rows // together)]
    all_scores, all_weights = [], []
    for i, requests in enumerate(groups):
        if i % 2 == 0:
            for r in range(i * together, min(rows, (i + 2) * together)):
                for j in range(most):
                    pl.when(where[r * most + j] < zeros)(copy(r, j).wait)
        keys = []
        for r in requests:
            for k in range(heads):
                at = r * block + k * group
                pages = [kv[where[r * most + j], 0, k] for j in range(most)]
                keys.append(jnp.concatenate(pages + [kf[at : at + group, :].astype(BF16)], axis=0))
        queries = q_ref[i * together : (i + 1) * together].reshape(LANES, head_dim)
        all_scores.append(transposed_scores(queries, keys, group))
    for i, requests in enumerate(groups):
        mask = []
        for j in range(most):
            seen = [seen_tokens(r, j) for r in requests]
            mask.append(token < lane_values(seen, block, (1, LANES)))
        parts = [
            jnp.where(m, all_scores[i][n * page_len : n * page_len + m.shape[0]], -jnp.inf)
            for n, m in enumerate(mask + [fresh_mask])
        ]
        top = functools.reduce(jnp.maximum, [jnp.max(x, axis=0, keepdims=True) for x in parts])
        parts = [jnp.exp(x - top) for x in parts]
        total = functools.reduce(jnp.add, [jnp.sum(x, axis=0, keepdims=True) for x in parts])
        stats = jnp.concatenate(
            [parts[most], jnp.broadcast_to(top, (8, LANES)), jnp.broadcast_to(total, (8, LANES))], axis=0
        )
        stats = jnp.transpose(stats, (1, 0))
        stat_ref[i * LANES : (i + 1) * LANES, : stats.shape[1]] = stats
        weights = [jnp.transpose(x.astype(BF16), (1, 0)) for x in parts[:most]]
        weights.append(stats[:, :group].astype(BF16))
        all_weights.append(jnp.concatenate(weights, axis=1))
    for i, requests in enumerate(groups):
        for x, r in enumerate(requests):
            both = []
            for k in range(heads):
                at = r * block + k * group
                pages = [kv[where[r * most + j], 1, k] for j in range(most)]
                both.append(jnp.concatenate(pages + [vf[at : at + group, :].astype(BF16)], axis=0))
            both = weighted_values(all_weights[i][x * block : (x + 1) * block, :], both)
            o_ref[r * block : (r + 1) * block, :] = both


def local_attention(table, context, fills, queries, new_kv, cache_kv, tabs):
    rows, block, _ = queries.shape
    rows = rows - 1
    steps = new_kv.shape[0]
    slots, _, heads, page_len, head_dim = cache_kv.shape
    flat = (rows * block, head_dim)
    freq, sign = tabs[4:]
    return pl.pallas_call(
        functools.partial(local_kernel, page_len, heads),
        out_shape=[jax.ShapeDtypeStruct(flat, F32)] * 2,
        in_specs=[SMEM] * 3 + [VMEM] * 4 + [ANY],
        out_specs=[VMEM] * 2,
        scratch_shapes=[
            pltpu.VMEM((table.size + 1, 2, heads, page_len, head_dim), BF16),
            pltpu.SemaphoreType.DMA((table.size,)),
            pltpu.VMEM(flat, F32),
            pltpu.VMEM(flat, F32),
            pltpu.VMEM((rows, head_dim), I32),
            pltpu.SMEM((table.size,), I32),
        ],
        compiler_params=PARAMS,
        cost_estimate=pl.CostEstimate(flops=800_000_000, bytes_accessed=12_000_000, transcendentals=400_000),
        name="local_attention",
    )(
        *[in_hbm(x) for x in (table, context, fills)],
        queries,
        new_kv.reshape(steps, rows, 2 * heads * head_dim),
        *[in_hbm(x) for x in (freq, sign, cache_kv)],
    )


def pieces(x):
    high = x.astype(BF16).astype(F32)
    middle = (x - high).astype(BF16).astype(F32)
    return [high, middle, x - high - middle]


def arrived_kernel(npool, pair, me_ref, own_ref, *refs):
    blocks = refs[:npool]
    pages_ref, out_ref, queries = refs[npool:]
    items = npool * pair
    _, _, heads, page_len, head_dim = pages_ref.shape
    rows, block = blocks[0].shape[0] - 1, blocks[0].shape[1]
    group = block // heads
    together = LANES // block
    me = me_ref[0]
    owners = [owner_of(me, npool, apart, flip) for apart, flip in block_order(npool)]
    lane = lax.broadcasted_iota(I32, (1, LANES), 1)
    codes = [x[rows, :STAT_ROWS, :].astype(F32) for x in blocks]
    codes = [x[0:1] * CODE + x[1:2] for x in codes]
    places = [owners[x // pair] * pair + x % pair for x in range(items)]
    slots = [own_ref[2 * items + at] for at in places]
    read = [jnp.maximum(read_scalar(codes[x // pair], lane == slots[x]), 0) for x in range(items)]
    number = [own_ref[at] for at in places]
    seen = [jnp.minimum(code % CODE, own_ref[items + at]) for code, at in zip(read, places)]
    request = [jnp.where(slot >= 0, code // CODE, -1) for slot, code in zip(slots, read)]
    for x in range(items):
        queries[x * block : (x + 1) * block, :] = blocks[x // pair][read[x] // CODE]
    token = lax.broadcasted_iota(I32, (page_len, LANES), 0)
    groups = [range(i * together, (i + 1) * together) for i in range(items // together)]
    all_scores, all_weights = [], []
    for i, own in enumerate(groups):
        keys = [pages_ref[number[x], 0, k] for x in own for k in range(heads)]
        all_scores.append(transposed_scores(queries[i * LANES : (i + 1) * LANES, :], keys, group))
    for i, own in enumerate(groups):
        limit = lane_values([seen[x] for x in own], block, (1, LANES))
        scores = jnp.where(token < limit, all_scores[i], -jnp.inf)
        top = jnp.max(scores, axis=0, keepdims=True)
        top = jnp.where(top > -jnp.inf, top, 0.0)
        weights = jnp.exp(scores - top)
        stats = pieces(top) + pieces(jnp.sum(weights, axis=0, keepdims=True))
        stats.append(lane_values([request[x] for x in own], block, (1, LANES)).astype(F32))
        stats = jnp.concatenate(stats + [jnp.zeros((STAT_ROWS - len(stats), LANES), F32)], axis=0).astype(BF16)
        for place in sorted({x // pair for x in own}):
            out_ref[owners[place], pair * block : pair * block + STAT_ROWS, :] = stats
        all_weights.append(jnp.transpose(weights.astype(BF16), (1, 0)))
    for i, own in enumerate(groups):
        for c, x in enumerate(own):
            both = [pages_ref[number[x], 1, k] for k in range(heads)]
            both = weighted_values(all_weights[i][c * block : (c + 1) * block, :], both)
            at = (x % pair) * block
            out_ref[owners[x // pair], at : at + block, :] = both.astype(BF16)


def arrived_attention(me, own, blocks, arrived):
    npool = len(blocks)
    head_dim = arrived.shape[4]
    block = blocks[0].shape[1]
    items = own.shape[0] // 3
    pair = items // npool
    return pl.pallas_call(
        functools.partial(arrived_kernel, npool, pair),
        out_shape=jax.ShapeDtypeStruct((npool, pair * block + STAT_ROWS, head_dim), BF16),
        in_specs=[SMEM] * 2 + [VMEM] * (npool + 1),
        out_specs=VMEM,
        scratch_shapes=[pltpu.VMEM((items * block, head_dim), BF16)],
        compiler_params=PARAMS,
        cost_estimate=pl.CostEstimate(flops=200_000_000, bytes_accessed=4_000_000, transcendentals=70_000),
        name="arrived_attention",
    )(me, own, *blocks, arrived)


def merge_kernel(pair, heads, me_ref, parts_ref, o_ref, stat_ref, out_ref, mixed, top, total, turned):
    npool = parts_ref.shape[0]
    steps, rows, width = out_ref.shape
    head_dim = o_ref.shape[1]
    per = width // head_dim // heads
    group = steps * per
    block = heads * group
    me = me_ref[0]
    shape = top.shape
    mixed[...] = o_ref[...]
    top[...] = jnp.broadcast_to(stat_ref[:, group : group + 1], shape)
    total[...] = jnp.broadcast_to(stat_ref[:, group + 8 : group + 9], shape)
    tops, totals, readers = [], [], []
    chain = lax.broadcasted_iota(I32, (1, LANES), 1) // block
    for d in range(npool):
        x = parts_ref[d, pair * block : pair * block + STAT_ROWS, :].astype(F32)
        tops.append(x[0:1] + x[1:2] + x[2:3])
        totals.append(x[3:4] + x[4:5] + x[5:6])
        readers.append(x[6:7])
    empty = [jnp.zeros((LANES // 2 - npool, LANES), F32)]
    turned[...] = jnp.transpose(jnp.concatenate(tops + empty + totals + empty, axis=0), (1, 0))
    for d in range(npool):
        for p in range(pair):
            part = lax.rem(place_of(me, npool, d) * pair + p, LANES // block)
            r = read_scalar(readers[d], chain == part)
            there = r >= 0
            at = pl.ds(pl.multiple_of(jnp.maximum(r, 0) * block, block), block)
            lane = pl.ds(pl.multiple_of(part * block, block), block)
            m = jnp.broadcast_to(turned[lane, d : d + 1], (block, head_dim))
            l = jnp.broadcast_to(turned[lane, LANES // 2 + d : LANES // 2 + d + 1], (block, head_dim))
            seen = (l > 0.0) & there
            o = parts_ref[d, p * block : (p + 1) * block, :].astype(F32)
            old = top[at, :]
            new = jnp.where(seen, jnp.maximum(old, m), old)
            a = jnp.exp(old - new)
            b = jnp.where(seen, jnp.exp(m - new), 0.0)
            top[at, :] = new
            total[at, :] = total[at, :] * a + l * b
            mixed[at, :] = mixed[at, :] * a + o * b
    for s in range(steps):
        for h in range(heads * per):
            k, g = divmod(h, per)
            at = pl.ds(k * group + s * per + g, rows, stride=block)
            out_ref[s, :, h * head_dim : (h + 1) * head_dim] = (mixed[at, :] / total[at, :]).astype(BF16)


def merged(me, parts, local, shape, heads, pair):
    flat = local[0].shape
    return pl.pallas_call(
        functools.partial(merge_kernel, pair, heads),
        out_shape=jax.ShapeDtypeStruct(shape, BF16),
        in_specs=[SMEM] + [VMEM] * 3,
        out_specs=VMEM,
        scratch_shapes=[pltpu.VMEM(flat, F32)] * 3 + [pltpu.VMEM((LANES, LANES), F32)],
        compiler_params=PARAMS,
        cost_estimate=pl.CostEstimate(flops=2_000_000, bytes_accessed=1_500_000, transcendentals=100_000),
        name="merge",
    )(me, parts, *local)


def fetch_kernel(weight_ref, x_ref, weight_out, x_out, sems):
    chunks = sems.shape[0] - 1
    rows = weight_ref.shape[0] // chunks
    copies = []
    for i in range(chunks):
        at = pl.ds(i * rows, rows)
        copies.append(pltpu.make_async_copy(weight_ref.at[at], weight_out.at[at], sems.at[i]))
    copies.append(pltpu.make_async_copy(x_ref, x_out, sems.at[chunks]))
    for copy in copies:
        copy.start()
    for copy in copies:
        copy.wait()


def fetched(weight, x):
    return pl.pallas_call(
        fetch_kernel,
        out_shape=[pltpu.VMEM(weight.shape, weight.dtype), pltpu.VMEM(x.shape, x.dtype)],
        in_specs=[ANY, ANY],
        out_specs=[ANY, ANY],
        scratch_shapes=[pltpu.SemaphoreType.DMA((9,))],
        compiler_params=PARAMS,
        cost_estimate=pl.CostEstimate(flops=0, bytes_accessed=2 * weight.size * 2, transcendentals=0),
        name="fetch_weight",
    )(in_hbm(weight), x)


def rows_kernel(npool, me_ref, core_ref, *refs):
    blocks = refs[:npool]
    weight_ref, out_ref, lhs = refs[npool:]
    steps, rows, _ = blocks[0].shape
    every = npool * rows
    for x, (apart, flip) in enumerate(block_order(npool)):
        owner = owner_of(me_ref[0], npool, apart, flip)
        for s in range(steps):
            lhs[pl.ds(pl.multiple_of(s * every + owner * rows, rows), rows), :] = blocks[x][s]
    multiply(lhs, weight_ref, out_ref, 1 - core_ref[0])


def multiply(lhs, weight_ref, out_ref, which):
    steps, every, half = out_ref.shape
    tile = min(half, 256)
    for i in range(half // tile):
        at = pl.ds(pl.multiple_of(which * half + i * tile, LANES), tile)
        terms = jnp.dot(lhs[...], weight_ref[:, at], preferred_element_type=F32)
        for s in range(steps):
            out_ref[s, :, i * tile : (i + 1) * tile] = terms[s * every : (s + 1) * every].astype(out_ref.dtype)


def other_projection(me, core, blocks, weight):
    npool = len(blocks)
    steps, rows, width = blocks[0].shape
    half = weight.shape[1] // 2
    every = steps * npool * rows
    return pl.pallas_call(
        functools.partial(rows_kernel, npool),
        out_shape=[
            jax.ShapeDtypeStruct((steps, npool * rows, half), BF16),
            jax.ShapeDtypeStruct((every, width), BF16),
        ],
        in_specs=[SMEM] * 2 + [VMEM] * (npool + 1),
        out_specs=[VMEM] * 2,
        compiler_params=PARAMS,
        cost_estimate=pl.CostEstimate(flops=2 * every * width * half, bytes_accessed=4_000_000, transcendentals=0),
        name="project_other",
    )(me, core, *blocks, weight)


def own_kernel(core_ref, lhs, weight_ref, out_ref):
    multiply(lhs, weight_ref, out_ref, core_ref[0])


def own_projection(core, lhs, weight, steps):
    every, width = lhs.shape
    half = weight.shape[1] // 2
    return pl.pallas_call(
        own_kernel,
        out_shape=jax.ShapeDtypeStruct((steps, every // steps, half), F32),
        in_specs=[SMEM] + [VMEM] * 2,
        out_specs=VMEM,
        compiler_params=PARAMS,
        cost_estimate=pl.CostEstimate(flops=2 * every * width * half, bytes_accessed=4_000_000, transcendentals=0),
        name="project_own",
    )(core, lhs, weight)


def block_order(npool):
    return [(apart, flip) for flip in (0, 1) for apart in range(npool // 2)]


def owner_of(me, npool, apart, flip):
    half = npool // 2
    pair, side = me // 2, me % 2
    side = 1 - side if flip else side
    return lax.rem(pair + half - apart, half) * 2 + side


def place_of(me, npool, holder):
    half = npool // 2
    apart = lax.rem(holder // 2 - me // 2 + half, half)
    flip = lax.rem(me + holder, 2)
    return flip * half + apart


def in_hbm(x):
    return pltpu.with_memory_space_constraint(x, pltpu.HBM)


def gathered(x, npool, later=None):
    half = npool // 2
    later = x if later is None else later
    ahead = lambda x, by: lax.ppermute(x, "pool", [(i, (i + 2 * by) % npool) for i in range(npool)])
    across = lambda x: lax.ppermute(x, "pool", [(i, i ^ 1) for i in range(npool)])
    straight = [x] + [ahead(x if by == half // 2 else later, by) for by in range(1, half)]
    return straight + [across(y) for y in straight]


def swap_halves(x):
    return lax.ppermute(x, "tp", [(0, 1), (1, 0)])


def shards(
    prompt_kv,
    prompt_lengths,
    page_slot,
    cache_kv,
    cache_fill,
    page_table,
    context_lengths,
    queries,
    new_kv,
    out_weight,
):
    npool = lax.axis_size("pool")
    me = lax.axis_index("pool").astype(I32)
    pages, _, heads, page_len, head_dim = prompt_kv.shape
    cache_pages = cache_kv.shape[0]
    pair = (pages + npool - 1) // npool
    tabs = tables(page_len, head_dim, pages)
    me1, core1 = me[None], lax.axis_index("tp").astype(I32)[None]
    table = page_table.T

    asked = asked_queries(table, context_lengths, queries, page_len, heads, head_dim)
    asked_all = gathered(asked, npool)
    arrived, own = rotated_pages(prompt_kv, page_slot, prompt_lengths, tabs, npool, pair, cache_pages)
    local = local_attention(table, context_lengths, cache_fill, asked, new_kv, cache_kv, tabs)
    parts = arrived_attention(me1, own, asked_all, arrived)
    parts = lax.all_to_all(parts, "pool", split_axis=0, concat_axis=0, tiled=True)
    attention = merged(me1, parts, local, queries.shape, heads, pair)
    weight, again = fetched(out_weight, attention)
    blocks = gathered(attention, npool, again)
    other_terms, lhs = other_projection(me1, core1, blocks, weight)
    other_terms = swap_halves(other_terms)
    terms = own_projection(core1, lhs, weight, queries.shape[0])
    return (terms + other_terms.astype(F32)).astype(BF16)


def solution(mesh):
    return jax.shard_map(
        shards,
        mesh=mesh,
        in_specs=(
            P(("group", "pool"), None, "tp", None, None),
            P(("group", "pool"), None),
            P(("group", "pool")),
            P(("group", "pool"), None, "tp", None, None),
            P(("group", "pool")),
            P(("group", "pool"), None),
            P(("group", "pool")),
            P(None, ("group", "pool"), "tp"),
            P(None, ("group", "pool"), None, "tp", None),
            P("tp", "pool"),
        ),
        out_specs=P(None, "group", ("pool", "tp")),
        check_vma=False,
    )
```

```python
import functools

import jax
import jax.numpy as jnp
import numpy as np
from jax import lax
from jax.experimental import pallas as pl
from jax.experimental.pallas import tpu as pltpu
from jax.sharding import PartitionSpec as P

ROPE_BASE = 500000.0
BF16, F32, I32 = jnp.bfloat16, jnp.float32, jnp.int32
SMEM = pl.BlockSpec(memory_space=pltpu.SMEM)
VMEM = pl.BlockSpec(memory_space=pltpu.VMEM)
ANY = pl.BlockSpec(memory_space=pl.ANY)
PARAMS = pltpu.CompilerParams(vmem_limit_bytes=24 * 2**20)
LANES = 128
STAT_ROWS = 16
CODE = 256


def tables(page_len, head_dim, pages):
    half = head_dim // 2
    freq = ROPE_BASE ** (-(np.arange(half) * 2.0) / head_dim)
    freq = np.concatenate([freq, freq])[None, :]
    sign = np.concatenate([-np.ones(half), np.ones(half)])[None, :]
    token = np.arange(page_len)[:, None] * freq
    first = np.arange(pages)[:, None] * page_len * freq
    out = (np.cos(token), sign * np.sin(token), np.cos(first), sign * np.sin(first), freq, sign)
    return [jnp.asarray(x, F32) for x in out]


def rope_kernel(
    npool, cache_pages, per, slot_ref, len_ref, pages_ref, ct_ref, st_ref, cp_ref, sp_ref, out_ref, own_ref, count
):
    _, _, heads, page_len, head_dim = pages_ref.shape

    @pl.when(pl.program_id(0) == 0)
    def _():
        items = own_ref.shape[0] // 3
        for e in range(npool):
            count[e] = 0
        for i in range(items):
            own_ref[i] = 0
            own_ref[items + i] = 0
            own_ref[2 * items + i] = -1
        for n in range(slot_ref.shape[0]):
            slot = slot_ref[n]
            target = slot // cache_pages
            at = target * (items // npool) + count[target]
            count[target] = count[target] + 1
            own_ref[at] = n
            own_ref[items + at] = page_place(len_ref, page_len, n)[1]
            own_ref[2 * items + at] = slot - target * cache_pages

    for i in range(per):
        number, _ = page_place(len_ref, page_len, pl.program_id(0) * per + i)
        c0, s0 = cp_ref[pl.ds(number, 1), :], sp_ref[pl.ds(number, 1), :]
        ct, st = ct_ref[...], st_ref[...]
        cos = c0 * ct - s0 * st
        sin = s0 * ct + c0 * st
        for k in range(heads):
            x = pages_ref[i, 0, k].astype(F32)
            out_ref[i, 0, k] = (x * cos + pltpu.roll(x, head_dim // 2, 1) * sin).astype(BF16)
            out_ref[i, 1, k] = pages_ref[i, 1, k]


def page_place(len_ref, page_len, n):
    begin = jnp.int32(0)
    number, fill = jnp.int32(0), jnp.int32(0)
    for q in range(len_ref.shape[1]):
        length = len_ref[0, q]
        count = (length + page_len - 1) // page_len
        here = (n >= begin) & (n < begin + count)
        number = jnp.where(here, n - begin, number)
        fill = jnp.where(here, jnp.clip(length - (n - begin) * page_len, 0, page_len), fill)
        begin = begin + count
    return number, fill


def rotated_pages(prompt_kv, page_slot, prompt_lengths, tabs, npool, pair, cache_pages):
    pages, _, heads, page_len, head_dim = prompt_kv.shape
    per = pages // 2
    ct, st, cp, sp, _, _ = tabs
    whole = lambda x: pl.BlockSpec(x.shape, lambda i: (0, 0))
    return pl.pallas_call(
        functools.partial(rope_kernel, npool, cache_pages, per),
        grid=(pages // per,),
        out_shape=[
            jax.ShapeDtypeStruct(prompt_kv.shape, BF16),
            jax.ShapeDtypeStruct((3 * npool * pair,), I32),
        ],
        in_specs=[
            SMEM,
            SMEM,
            pl.BlockSpec((per,) + prompt_kv.shape[1:], lambda i: (i, 0, 0, 0, 0)),
            whole(ct),
            whole(st),
            whole(cp),
            whole(sp),
        ],
        out_specs=[pl.BlockSpec((per,) + prompt_kv.shape[1:], lambda i: (i, 0, 0, 0, 0)), SMEM],
        scratch_shapes=[pltpu.SMEM((npool,), I32)],
        compiler_params=PARAMS,
        cost_estimate=pl.CostEstimate(flops=6_000_000, bytes_accessed=2_000_000, transcendentals=0),
        name="rope_pages",
    )(*[in_hbm(x) for x in (page_slot, prompt_lengths, prompt_kv, ct, st, cp, sp)])


def asked_kernel(page_len, heads, table_ref, context_ref, q_ref, out_ref, spread):
    most, rows = table_ref.shape
    steps, _, width = q_ref.shape
    block, head_dim = out_ref.shape[1:]
    per = width // head_dim // heads
    for s in range(steps):
        for h in range(heads * per):
            k, g = divmod(h, per)
            at = pl.ds(k * steps * per + s * per + g, rows, stride=block)
            spread[at, :] = q_ref[s, :, h * head_dim : (h + 1) * head_dim].astype(F32)
    for r in range(rows):
        out_ref[r] = spread[r * block : (r + 1) * block, :].astype(BF16)
    lane = lax.broadcasted_iota(I32, (block, LANES), 1)
    line = lax.broadcasted_iota(I32, (block, LANES), 0)
    request = jnp.zeros((block, LANES), I32)
    left = jnp.zeros((block, LANES), I32)
    for r in range(rows):
        context = context_ref[r]
        for j in range(most):
            here = lane == table_ref[j, r]
            request = jnp.where(here, r, request)
            left = jnp.where(here, jnp.clip(context - j * page_len, 0, page_len), left)
    out_ref[rows] = jnp.where(line == 0, request, left).astype(F32).astype(BF16)


def asked_queries(table, context, queries, page_len, heads, head_dim):
    steps, rows, width = queries.shape
    block = steps * width // head_dim
    return pl.pallas_call(
        functools.partial(asked_kernel, page_len, heads),
        out_shape=jax.ShapeDtypeStruct((rows + 1, block, head_dim), BF16),
        in_specs=[SMEM, SMEM, VMEM],
        out_specs=VMEM,
        scratch_shapes=[pltpu.VMEM((rows * block, head_dim), F32)],
        compiler_params=PARAMS,
        cost_estimate=pl.CostEstimate(flops=100_000, bytes_accessed=300_000, transcendentals=0),
        name="asked_queries",
    )(in_hbm(table), in_hbm(context), in_hbm(queries))


def read_scalar(x, pick):
    return jnp.max(jnp.where(pick, x, -2.0)).astype(I32)


def transposed_scores(queries, keys, group):
    turned = jnp.transpose(queries, (1, 0))
    chain = lax.broadcasted_iota(I32, (1, turned.shape[1]), 1) // group
    spread = [turned * jnp.where(chain == c, 1.0, 0.0).astype(BF16) for c in range(len(keys))]
    scores = jnp.dot(
        jnp.concatenate(keys, axis=1), jnp.concatenate(spread, axis=0), preferred_element_type=F32
    )
    return scores * (queries.shape[1] ** -0.5)


def weighted_values(weights, values):
    heads, head_dim = len(values), values[0].shape[1]
    group = weights.shape[0] // heads
    out = jnp.dot(weights, jnp.concatenate(values, axis=1), preferred_element_type=F32)
    parts = [out[k * group : (k + 1) * group, k * head_dim : (k + 1) * head_dim] for k in range(heads)]
    return jnp.concatenate(parts, axis=0)


def lane_values(scalars, lanes_each, shape):
    chain = lax.broadcasted_iota(I32, shape, 1) // lanes_each
    out = jnp.zeros(shape, I32)
    for i, x in enumerate(scalars):
        out = jnp.where(chain == i, x, out)
    return out


def local_kernel(
    page_len,
    heads,
    table_ref,
    context_ref,
    fill_ref,
    q_ref,
    new_ref,
    freq_ref,
    sign_ref,
    cache_ref,
    o_ref,
    stat_ref,
    kv,
    sems,
    kf,
    vf,
    position,
    where,
):
    rows, block, head_dim = q_ref.shape
    rows = rows - 1
    steps = new_ref.shape[0]
    most = table_ref.shape[0]
    group = block // heads
    per = group // steps
    together = LANES // block

    zeros = rows * most

    def copy(r, j):
        n = r * most + j
        return pltpu.make_async_copy(cache_ref.at[table_ref[j, r]], kv.at[n], sems.at[n])

    def seen_tokens(r, j):
        return jnp.minimum(fill_ref[table_ref[j, r]], context_ref[r] - j * page_len)

    for r in range(rows):
        for j in range(most):
            needed = seen_tokens(r, j) > 0
            where[r * most + j] = jnp.where(needed, r * most + j, zeros)
            pl.when(needed)(copy(r, j).start)
    kv[zeros] = jnp.zeros(kv.shape[1:], BF16)
    kf[...] = jnp.zeros_like(kf)
    vf[...] = jnp.zeros_like(vf)
    for r in range(rows):
        position[r : r + 1, :] = jnp.full((1, head_dim), context_ref[r], I32)
    for u in range(steps):
        angle = (position[...] + u).astype(F32) * freq_ref[...]
        cos, sin = jnp.cos(angle), jnp.sin(angle) * sign_ref[...]
        for k in range(heads):
            x = new_ref[u, :, k * head_dim : (k + 1) * head_dim].astype(F32)
            at = k * group + u
            kf[pl.ds(at, rows, stride=block), :] = x * cos + pltpu.roll(x, head_dim // 2, 1) * sin
            x = new_ref[u, :, (heads + k) * head_dim : (heads + k + 1) * head_dim].astype(F32)
            vf[pl.ds(at, rows, stride=block), :] = x
    token = lax.broadcasted_iota(I32, (page_len, LANES), 0)
    fresh = lax.broadcasted_iota(I32, (group, LANES), 0)
    step = lax.broadcasted_iota(I32, (group, LANES), 1) % group // per
    fresh_mask = (fresh <= step) & (fresh < steps)

    groups = [range(i * together, (i + 1) * together) for i in range(rows // together)]
    all_scores, all_weights = [], []
    for i, requests in enumerate(groups):
        if i % 2 == 0:
            for r in range(i * together, min(rows, (i + 2) * together)):
                for j in range(most):
                    pl.when(where[r * most + j] < zeros)(copy(r, j).wait)
        keys = []
        for r in requests:
            for k in range(heads):
                at = r * block + k * group
                pages = [kv[where[r * most + j], 0, k] for j in range(most)]
                keys.append(jnp.concatenate(pages + [kf[at : at + group, :].astype(BF16)], axis=0))
        queries = q_ref[i * together : (i + 1) * together].reshape(LANES, head_dim)
        all_scores.append(transposed_scores(queries, keys, group))
    for i, requests in enumerate(groups):
        mask = []
        for j in range(most):
            seen = [seen_tokens(r, j) for r in requests]
            mask.append(token < lane_values(seen, block, (1, LANES)))
        parts = [
            jnp.where(m, all_scores[i][n * page_len : n * page_len + m.shape[0]], -jnp.inf)
            for n, m in enumerate(mask + [fresh_mask])
        ]
        top = functools.reduce(jnp.maximum, [jnp.max(x, axis=0, keepdims=True) for x in parts])
        parts = [jnp.exp(x - top) for x in parts]
        total = functools.reduce(jnp.add, [jnp.sum(x, axis=0, keepdims=True) for x in parts])
        stats = jnp.concatenate(
            [parts[most], jnp.broadcast_to(top, (8, LANES)), jnp.broadcast_to(total, (8, LANES))], axis=0
        )
        stats = jnp.transpose(stats, (1, 0))
        stat_ref[i * LANES : (i + 1) * LANES, : stats.shape[1]] = stats
        weights = [jnp.transpose(x.astype(BF16), (1, 0)) for x in parts[:most]]
        weights.append(stats[:, :group].astype(BF16))
        all_weights.append(jnp.concatenate(weights, axis=1))
    for i, requests in enumerate(groups):
        for x, r in enumerate(requests):
            both = []
            for k in range(heads):
                at = r * block + k * group
                pages = [kv[where[r * most + j], 1, k] for j in range(most)]
                both.append(jnp.concatenate(pages + [vf[at : at + group, :].astype(BF16)], axis=0))
            both = weighted_values(all_weights[i][x * block : (x + 1) * block, :], both)
            o_ref[r * block : (r + 1) * block, :] = both


def local_attention(table, context, fills, queries, new_kv, cache_kv, tabs):
    rows, block, _ = queries.shape
    rows = rows - 1
    steps = new_kv.shape[0]
    slots, _, heads, page_len, head_dim = cache_kv.shape
    flat = (rows * block, head_dim)
    freq, sign = tabs[4:]
    return pl.pallas_call(
        functools.partial(local_kernel, page_len, heads),
        out_shape=[jax.ShapeDtypeStruct(flat, F32)] * 2,
        in_specs=[SMEM] * 3 + [VMEM] * 4 + [ANY],
        out_specs=[VMEM] * 2,
        scratch_shapes=[
            pltpu.VMEM((table.size + 1, 2, heads, page_len, head_dim), BF16),
            pltpu.SemaphoreType.DMA((table.size,)),
            pltpu.VMEM(flat, F32),
            pltpu.VMEM(flat, F32),
            pltpu.VMEM((rows, head_dim), I32),
            pltpu.SMEM((table.size,), I32),
        ],
        compiler_params=PARAMS,
        cost_estimate=pl.CostEstimate(flops=800_000_000, bytes_accessed=12_000_000, transcendentals=400_000),
        name="local_attention",
    )(
        *[in_hbm(x) for x in (table, context, fills)],
        queries,
        new_kv.reshape(steps, rows, 2 * heads * head_dim),
        *[in_hbm(x) for x in (freq, sign, cache_kv)],
    )


def pieces(x):
    high = x.astype(BF16).astype(F32)
    middle = (x - high).astype(BF16).astype(F32)
    return [high, middle, x - high - middle]


def arrived_kernel(npool, pair, me_ref, own_ref, *refs):
    blocks = refs[:npool]
    pages_ref, out_ref, queries = refs[npool:]
    items = npool * pair
    _, _, heads, page_len, head_dim = pages_ref.shape
    rows, block = blocks[0].shape[0] - 1, blocks[0].shape[1]
    group = block // heads
    together = LANES // block
    me = me_ref[0]
    owners = [owner_of(me, npool, apart, flip) for apart, flip in block_order(npool)]
    lane = lax.broadcasted_iota(I32, (1, LANES), 1)
    codes = [x[rows, :STAT_ROWS, :].astype(F32) for x in blocks]
    codes = [x[0:1] * CODE + x[1:2] for x in codes]
    places = [owners[x // pair] * pair + x % pair for x in range(items)]
    slots = [own_ref[2 * items + at] for at in places]
    read = [jnp.maximum(read_scalar(codes[x // pair], lane == slots[x]), 0) for x in range(items)]
    number = [own_ref[at] for at in places]
    seen = [jnp.minimum(code % CODE, own_ref[items + at]) for code, at in zip(read, places)]
    request = [jnp.where(slot >= 0, code // CODE, -1) for slot, code in zip(slots, read)]
    for x in range(items):
        queries[x * block : (x + 1) * block, :] = blocks[x // pair][read[x] // CODE]
    token = lax.broadcasted_iota(I32, (page_len, LANES), 0)
    groups = [range(i * together, (i + 1) * together) for i in range(items // together)]
    all_scores, all_weights = [], []
    for i, own in enumerate(groups):
        keys = [pages_ref[number[x], 0, k] for x in own for k in range(heads)]
        all_scores.append(transposed_scores(queries[i * LANES : (i + 1) * LANES, :], keys, group))
    for i, own in enumerate(groups):
        limit = lane_values([seen[x] for x in own], block, (1, LANES))
        scores = jnp.where(token < limit, all_scores[i], -jnp.inf)
        top = jnp.max(scores, axis=0, keepdims=True)
        top = jnp.where(top > -jnp.inf, top, 0.0)
        weights = jnp.exp(scores - top)
        stats = pieces(top) + pieces(jnp.sum(weights, axis=0, keepdims=True))
        stats.append(lane_values([request[x] for x in own], block, (1, LANES)).astype(F32))
        stats = jnp.concatenate(stats + [jnp.zeros((STAT_ROWS - len(stats), LANES), F32)], axis=0).astype(BF16)
        for place in sorted({x // pair for x in own}):
            out_ref[owners[place], pair * block : pair * block + STAT_ROWS, :] = stats
        all_weights.append(jnp.transpose(weights.astype(BF16), (1, 0)))
    for i, own in enumerate(groups):
        for c, x in enumerate(own):
            both = [pages_ref[number[x], 1, k] for k in range(heads)]
            both = weighted_values(all_weights[i][c * block : (c + 1) * block, :], both)
            at = (x % pair) * block
            out_ref[owners[x // pair], at : at + block, :] = both.astype(BF16)


def arrived_attention(me, own, blocks, arrived):
    npool = len(blocks)
    head_dim = arrived.shape[4]
    block = blocks[0].shape[1]
    items = own.shape[0] // 3
    pair = items // npool
    return pl.pallas_call(
        functools.partial(arrived_kernel, npool, pair),
        out_shape=jax.ShapeDtypeStruct((npool, pair * block + STAT_ROWS, head_dim), BF16),
        in_specs=[SMEM] * 2 + [VMEM] * (npool + 1),
        out_specs=VMEM,
        scratch_shapes=[pltpu.VMEM((items * block, head_dim), BF16)],
        compiler_params=PARAMS,
        cost_estimate=pl.CostEstimate(flops=200_000_000, bytes_accessed=4_000_000, transcendentals=70_000),
        name="arrived_attention",
    )(me, own, *blocks, arrived)


def merge_kernel(pair, heads, me_ref, core_ref, parts_ref, o_ref, stat_ref, out_ref, mixed, top, total, turned):
    del core_ref
    npool = parts_ref.shape[0]
    steps, rows, width = out_ref.shape
    head_dim = o_ref.shape[1]
    per = width // head_dim // heads
    group = steps * per
    block = heads * group
    me = me_ref[0]
    shape = top.shape
    mixed[...] = o_ref[...]
    top[...] = jnp.broadcast_to(stat_ref[:, group : group + 1], shape)
    total[...] = jnp.broadcast_to(stat_ref[:, group + 8 : group + 9], shape)
    tops, totals, readers = [], [], []
    chain = lax.broadcasted_iota(I32, (1, LANES), 1) // block
    for d in range(npool):
        x = parts_ref[d, pair * block : pair * block + STAT_ROWS, :].astype(F32)
        tops.append(x[0:1] + x[1:2] + x[2:3])
        totals.append(x[3:4] + x[4:5] + x[5:6])
        readers.append(x[6:7])
    empty = [jnp.zeros((LANES // 2 - npool, LANES), F32)]
    turned[...] = jnp.transpose(jnp.concatenate(tops + empty + totals + empty, axis=0), (1, 0))
    for d in range(npool):
        for p in range(pair):
            part = lax.rem(place_of(me, npool, d) * pair + p, LANES // block)
            r = read_scalar(readers[d], chain == part)
            there = r >= 0
            at = pl.ds(pl.multiple_of(jnp.maximum(r, 0) * block, block), block)
            lane = pl.ds(pl.multiple_of(part * block, block), block)
            m = jnp.broadcast_to(turned[lane, d : d + 1], (block, head_dim))
            l = jnp.broadcast_to(turned[lane, LANES // 2 + d : LANES // 2 + d + 1], (block, head_dim))
            seen = (l > 0.0) & there
            o = parts_ref[d, p * block : (p + 1) * block, :].astype(F32)
            old = top[at, :]
            new = jnp.where(seen, jnp.maximum(old, m), old)
            a = jnp.exp(old - new)
            b = jnp.where(seen, jnp.exp(m - new), 0.0)
            top[at, :] = new
            total[at, :] = total[at, :] * a + l * b
            mixed[at, :] = mixed[at, :] * a + o * b
    for s in range(steps):
        for h in range(heads * per):
            k, g = divmod(h, per)
            at = pl.ds(k * group + s * per + g, rows, stride=block)
            out_ref[s, :, h * head_dim : (h + 1) * head_dim] = (mixed[at, :] / total[at, :]).astype(BF16)


def merged(me, core, parts, local, shape, heads, pair):
    flat = local[0].shape
    return pl.pallas_call(
        functools.partial(merge_kernel, pair, heads),
        out_shape=jax.ShapeDtypeStruct(shape, BF16),
        in_specs=[SMEM] * 2 + [VMEM] * 3,
        out_specs=VMEM,
        scratch_shapes=[pltpu.VMEM(flat, F32)] * 3 + [pltpu.VMEM((LANES, LANES), F32)],
        compiler_params=PARAMS,
        cost_estimate=pl.CostEstimate(flops=2_000_000, bytes_accessed=1_500_000, transcendentals=100_000),
        name="merge",
    )(me, core, parts, *local)


def fetch_kernel(weight_ref, x_ref, weight_out, x_out, sems):
    chunks = sems.shape[0] - 1
    rows = weight_ref.shape[0] // chunks
    copies = []
    for i in range(chunks):
        at = pl.ds(i * rows, rows)
        copies.append(pltpu.make_async_copy(weight_ref.at[at], weight_out.at[at], sems.at[i]))
    copies.append(pltpu.make_async_copy(x_ref, x_out, sems.at[chunks]))
    for copy in copies:
        copy.start()
    for copy in copies:
        copy.wait()


def fetched(weight, x):
    return pl.pallas_call(
        fetch_kernel,
        out_shape=[pltpu.VMEM(weight.shape, weight.dtype), pltpu.VMEM(x.shape, x.dtype)],
        in_specs=[ANY, ANY],
        out_specs=[ANY, ANY],
        scratch_shapes=[pltpu.SemaphoreType.DMA((9,))],
        compiler_params=PARAMS,
        cost_estimate=pl.CostEstimate(flops=0, bytes_accessed=2 * weight.size * 2, transcendentals=0),
        name="fetch_weight",
    )(in_hbm(weight), x)


def rows_kernel(npool, me_ref, core_ref, *refs):
    blocks = refs[:npool]
    weight_ref, out_ref, lhs = refs[npool:]
    steps, rows, _ = blocks[0].shape
    every = npool * rows
    for x, (apart, flip) in enumerate(block_order(npool)):
        owner = owner_of(me_ref[0], npool, apart, flip)
        for s in range(steps):
            lhs[pl.ds(pl.multiple_of(s * every + owner * rows, rows), rows), :] = blocks[x][s]
    multiply(lhs, weight_ref, out_ref, 1 - core_ref[0])


def multiply(lhs, weight_ref, out_ref, which):
    steps, every, half = out_ref.shape
    tile = min(half, 256)
    for i in range(half // tile):
        at = pl.ds(pl.multiple_of(which * half + i * tile, LANES), tile)
        terms = jnp.dot(lhs[...], weight_ref[:, at], preferred_element_type=F32)
        for s in range(steps):
            out_ref[s, :, i * tile : (i + 1) * tile] = terms[s * every : (s + 1) * every].astype(out_ref.dtype)


def other_projection(me, core, blocks, weight):
    npool = len(blocks)
    steps, rows, width = blocks[0].shape
    half = weight.shape[1] // 2
    every = steps * npool * rows
    return pl.pallas_call(
        functools.partial(rows_kernel, npool),
        out_shape=[
            jax.ShapeDtypeStruct((steps, npool * rows, half), BF16),
            jax.ShapeDtypeStruct((every, width), BF16),
        ],
        in_specs=[SMEM] * 2 + [VMEM] * (npool + 1),
        out_specs=[VMEM] * 2,
        compiler_params=PARAMS,
        cost_estimate=pl.CostEstimate(flops=2 * every * width * half, bytes_accessed=4_000_000, transcendentals=0),
        name="project_other",
    )(me, core, *blocks, weight)


def own_kernel(core_ref, lhs, weight_ref, out_ref):
    multiply(lhs, weight_ref, out_ref, core_ref[0])


def own_projection(core, lhs, weight, steps):
    every, width = lhs.shape
    half = weight.shape[1] // 2
    return pl.pallas_call(
        own_kernel,
        out_shape=jax.ShapeDtypeStruct((steps, every // steps, half), F32),
        in_specs=[SMEM] + [VMEM] * 2,
        out_specs=VMEM,
        compiler_params=PARAMS,
        cost_estimate=pl.CostEstimate(flops=2 * every * width * half, bytes_accessed=4_000_000, transcendentals=0),
        name="project_own",
    )(core, lhs, weight)


def block_order(npool):
    return [(apart, flip) for flip in (0, 1) for apart in range(npool // 2)]


def owner_of(me, npool, apart, flip):
    half = npool // 2
    pair, side = me // 2, me % 2
    side = 1 - side if flip else side
    return lax.rem(pair + half - apart, half) * 2 + side


def place_of(me, npool, holder):
    half = npool // 2
    apart = lax.rem(holder // 2 - me // 2 + half, half)
    flip = lax.rem(me + holder, 2)
    return flip * half + apart


def in_hbm(x):
    return pltpu.with_memory_space_constraint(x, pltpu.HBM)


def gathered(x, npool, later=None):
    half = npool // 2
    later = x if later is None else later
    ahead = lambda x, by: lax.ppermute(x, "pool", [(i, (i + 2 * by) % npool) for i in range(npool)])
    across = lambda x: lax.ppermute(x, "pool", [(i, i ^ 1) for i in range(npool)])
    straight = [x] + [ahead(x if by == half // 2 else later, by) for by in range(1, half)]
    return straight + [across(y) for y in straight]


def swap_halves(x):
    return lax.ppermute(x, "tp", [(0, 1), (1, 0)])


def shards(
    prompt_kv,
    prompt_lengths,
    page_slot,
    cache_kv,
    cache_fill,
    page_table,
    context_lengths,
    queries,
    new_kv,
    out_weight,
):
    npool = lax.axis_size("pool")
    me = lax.axis_index("pool").astype(I32)
    pages, _, heads, page_len, head_dim = prompt_kv.shape
    cache_pages = cache_kv.shape[0]
    pair = (pages + npool - 1) // npool
    tabs = tables(page_len, head_dim, pages)
    me1, core1 = me[None], lax.axis_index("tp").astype(I32)[None]
    table = page_table.T

    asked = asked_queries(table, context_lengths, queries, page_len, heads, head_dim)
    asked_all = gathered(asked, npool)
    arrived, own = rotated_pages(prompt_kv, page_slot, prompt_lengths, tabs, npool, pair, cache_pages)
    local = local_attention(table, context_lengths, cache_fill, asked, new_kv, cache_kv, tabs)
    parts = arrived_attention(me1, own, asked_all, arrived)
    parts = lax.all_to_all(parts, "pool", split_axis=0, concat_axis=0, tiled=True)
    attention = merged(me1, core1, parts, local, queries.shape, heads, pair)
    weight, again = fetched(out_weight, attention)
    blocks = gathered(attention, npool, again)
    other_terms, lhs = other_projection(me1, core1, blocks, weight)
    other_terms = swap_halves(other_terms)
    terms = own_projection(core1, lhs, weight, queries.shape[0])
    return (terms + other_terms.astype(F32)).astype(BF16)


def solution(mesh):
    return jax.shard_map(
        shards,
        mesh=mesh,
        in_specs=(
            P(("group", "pool"), None, "tp", None, None),
            P(("group", "pool"), None),
            P(("group", "pool")),
            P(("group", "pool"), None, "tp", None, None),
            P(("group", "pool")),
            P(("group", "pool"), None),
            P(("group", "pool")),
            P(None, ("group", "pool"), "tp"),
            P(None, ("group", "pool"), None, "tp", None),
            P("tp", "pool"),
        ),
        out_specs=P(None, "group", ("pool", "tp")),
        check_vma=False,
    )
```

```python
import functools

import jax
import jax.numpy as jnp
import numpy as np
from jax import lax
from jax.experimental import pallas as pl
from jax.experimental.pallas import tpu as pltpu
from jax.sharding import PartitionSpec as P

ROPE_BASE = 500000.0
BF16, F32, I32 = jnp.bfloat16, jnp.float32, jnp.int32
SMEM = pl.BlockSpec(memory_space=pltpu.SMEM)
VMEM = pl.BlockSpec(memory_space=pltpu.VMEM)
ANY = pl.BlockSpec(memory_space=pl.ANY)
PARAMS = pltpu.CompilerParams(vmem_limit_bytes=24 * 2**20)
LANES = 128
STAT_ROWS = 16
CODE = 256


def tables(page_len, head_dim, pages):
    half = head_dim // 2
    freq = ROPE_BASE ** (-(np.arange(half) * 2.0) / head_dim)
    freq = np.concatenate([freq, freq])[None, :]
    sign = np.concatenate([-np.ones(half), np.ones(half)])[None, :]
    token = np.arange(page_len)[:, None] * freq
    first = np.arange(pages)[:, None] * page_len * freq
    out = (np.cos(token), sign * np.sin(token), np.cos(first), sign * np.sin(first), freq, sign)
    return [jnp.asarray(x, F32) for x in out]


def rope_kernel(
    npool, cache_pages, per, slot_ref, len_ref, pages_ref, ct_ref, st_ref, cp_ref, sp_ref, out_ref, own_ref, count
):
    _, _, heads, page_len, head_dim = pages_ref.shape

    @pl.when(pl.program_id(0) == 0)
    def _():
        items = own_ref.shape[0] // 3
        for e in range(npool):
            count[e] = 0
        for i in range(items):
            own_ref[i] = 0
            own_ref[items + i] = 0
            own_ref[2 * items + i] = -1
        for n in range(slot_ref.shape[0]):
            slot = slot_ref[n]
            target = slot // cache_pages
            at = target * (items // npool) + count[target]
            count[target] = count[target] + 1
            own_ref[at] = n
            own_ref[items + at] = page_place(len_ref, page_len, n)[1]
            own_ref[2 * items + at] = slot - target * cache_pages

    for i in range(per):
        number, _ = page_place(len_ref, page_len, pl.program_id(0) * per + i)
        c0, s0 = cp_ref[pl.ds(number, 1), :], sp_ref[pl.ds(number, 1), :]
        ct, st = ct_ref[...], st_ref[...]
        cos = c0 * ct - s0 * st
        sin = s0 * ct + c0 * st
        for k in range(heads):
            x = pages_ref[i, 0, k].astype(F32)
            out_ref[i, 0, k] = (x * cos + pltpu.roll(x, head_dim // 2, 1) * sin).astype(BF16)
            out_ref[i, 1, k] = pages_ref[i, 1, k]


def page_place(len_ref, page_len, n):
    begin = jnp.int32(0)
    number, fill = jnp.int32(0), jnp.int32(0)
    for q in range(len_ref.shape[1]):
        length = len_ref[0, q]
        count = (length + page_len - 1) // page_len
        here = (n >= begin) & (n < begin + count)
        number = jnp.where(here, n - begin, number)
        fill = jnp.where(here, jnp.clip(length - (n - begin) * page_len, 0, page_len), fill)
        begin = begin + count
    return number, fill


def rotated_pages(prompt_kv, page_slot, prompt_lengths, tabs, npool, pair, cache_pages):
    pages, _, heads, page_len, head_dim = prompt_kv.shape
    per = pages // 2
    ct, st, cp, sp, _, _ = tabs
    whole = lambda x: pl.BlockSpec(x.shape, lambda i: (0, 0))
    return pl.pallas_call(
        functools.partial(rope_kernel, npool, cache_pages, per),
        grid=(pages // per,),
        out_shape=[
            jax.ShapeDtypeStruct(prompt_kv.shape, BF16),
            jax.ShapeDtypeStruct((3 * npool * pair,), I32),
        ],
        in_specs=[
            SMEM,
            SMEM,
            pl.BlockSpec((per,) + prompt_kv.shape[1:], lambda i: (i, 0, 0, 0, 0)),
            whole(ct),
            whole(st),
            whole(cp),
            whole(sp),
        ],
        out_specs=[pl.BlockSpec((per,) + prompt_kv.shape[1:], lambda i: (i, 0, 0, 0, 0)), SMEM],
        scratch_shapes=[pltpu.SMEM((npool,), I32)],
        compiler_params=PARAMS,
        cost_estimate=pl.CostEstimate(flops=6_000_000, bytes_accessed=2_000_000, transcendentals=0),
        name="rope_pages",
    )(*[in_hbm(x) for x in (page_slot, prompt_lengths, prompt_kv, ct, st, cp, sp)])


def asked_kernel(page_len, heads, table_ref, context_ref, q_ref, out_ref, spread):
    most, rows = table_ref.shape
    steps, _, width = q_ref.shape
    block, head_dim = out_ref.shape[1:]
    per = width // head_dim // heads
    for s in range(steps):
        for h in range(heads * per):
            k, g = divmod(h, per)
            at = pl.ds(k * steps * per + s * per + g, rows, stride=block)
            spread[at, :] = q_ref[s, :, h * head_dim : (h + 1) * head_dim].astype(F32)
    for r in range(rows):
        out_ref[r] = spread[r * block : (r + 1) * block, :].astype(BF16)
    lane = lax.broadcasted_iota(I32, (block, LANES), 1)
    line = lax.broadcasted_iota(I32, (block, LANES), 0)
    request = jnp.zeros((block, LANES), I32)
    left = jnp.zeros((block, LANES), I32)
    for r in range(rows):
        context = context_ref[r]
        for j in range(most):
            here = lane == table_ref[j, r]
            request = jnp.where(here, r, request)
            left = jnp.where(here, jnp.clip(context - j * page_len, 0, page_len), left)
    out_ref[rows] = jnp.where(line == 0, request, left).astype(F32).astype(BF16)


def asked_queries(table, context, queries, page_len, heads, head_dim):
    steps, rows, width = queries.shape
    block = steps * width // head_dim
    return pl.pallas_call(
        functools.partial(asked_kernel, page_len, heads),
        out_shape=jax.ShapeDtypeStruct((rows + 1, block, head_dim), BF16),
        in_specs=[SMEM, SMEM, VMEM],
        out_specs=VMEM,
        scratch_shapes=[pltpu.VMEM((rows * block, head_dim), F32)],
        compiler_params=PARAMS,
        cost_estimate=pl.CostEstimate(flops=100_000, bytes_accessed=300_000, transcendentals=0),
        name="asked_queries",
    )(in_hbm(table), in_hbm(context), in_hbm(queries))


def read_scalar(x, pick):
    return jnp.max(jnp.where(pick, x, -2.0)).astype(I32)


def transposed_scores(queries, keys, group):
    turned = jnp.transpose(queries, (1, 0))
    chain = lax.broadcasted_iota(I32, (1, turned.shape[1]), 1) // group
    spread = [turned * jnp.where(chain == c, 1.0, 0.0).astype(BF16) for c in range(len(keys))]
    scores = jnp.dot(
        jnp.concatenate(keys, axis=1), jnp.concatenate(spread, axis=0), preferred_element_type=F32
    )
    return scores * (queries.shape[1] ** -0.5)


def weighted_values(weights, values):
    heads, head_dim = len(values), values[0].shape[1]
    group = weights.shape[0] // heads
    out = jnp.dot(weights, jnp.concatenate(values, axis=1), preferred_element_type=F32)
    parts = [out[k * group : (k + 1) * group, k * head_dim : (k + 1) * head_dim] for k in range(heads)]
    return jnp.concatenate(parts, axis=0)


def lane_values(scalars, lanes_each, shape):
    chain = lax.broadcasted_iota(I32, shape, 1) // lanes_each
    out = jnp.zeros(shape, I32)
    for i, x in enumerate(scalars):
        out = jnp.where(chain == i, x, out)
    return out


def local_kernel(
    page_len,
    heads,
    table_ref,
    context_ref,
    fill_ref,
    q_ref,
    new_ref,
    freq_ref,
    sign_ref,
    cache_ref,
    o_ref,
    stat_ref,
    kv,
    sems,
    kf,
    vf,
    position,
    where,
):
    rows, block, head_dim = q_ref.shape
    rows = rows - 1
    steps = new_ref.shape[0]
    most = table_ref.shape[0]
    group = block // heads
    per = group // steps
    together = LANES // block

    zeros = rows * most

    def copy(r, j):
        n = r * most + j
        return pltpu.make_async_copy(cache_ref.at[table_ref[j, r]], kv.at[n], sems.at[n])

    def seen_tokens(r, j):
        return jnp.minimum(fill_ref[table_ref[j, r]], context_ref[r] - j * page_len)

    for r in range(rows):
        for j in range(most):
            needed = seen_tokens(r, j) > 0
            where[r * most + j] = jnp.where(needed, r * most + j, zeros)
            pl.when(needed)(copy(r, j).start)
    kv[zeros] = jnp.zeros(kv.shape[1:], BF16)
    kf[...] = jnp.zeros_like(kf)
    vf[...] = jnp.zeros_like(vf)
    for r in range(rows):
        position[r : r + 1, :] = jnp.full((1, head_dim), context_ref[r], I32)
    for u in range(steps):
        angle = (position[...] + u).astype(F32) * freq_ref[...]
        cos, sin = jnp.cos(angle), jnp.sin(angle) * sign_ref[...]
        for k in range(heads):
            x = new_ref[u, :, k * head_dim : (k + 1) * head_dim].astype(F32)
            at = k * group + u
            kf[pl.ds(at, rows, stride=block), :] = x * cos + pltpu.roll(x, head_dim // 2, 1) * sin
            x = new_ref[u, :, (heads + k) * head_dim : (heads + k + 1) * head_dim].astype(F32)
            vf[pl.ds(at, rows, stride=block), :] = x
    token = lax.broadcasted_iota(I32, (page_len, LANES), 0)
    fresh = lax.broadcasted_iota(I32, (group, LANES), 0)
    step = lax.broadcasted_iota(I32, (group, LANES), 1) % group // per
    fresh_mask = (fresh <= step) & (fresh < steps)

    groups = [range(i * together, (i + 1) * together) for i in range(rows // together)]
    all_scores, all_weights = [], []
    for i, requests in enumerate(groups):
        if i % 2 == 0:
            for r in range(i * together, min(rows, (i + 2) * together)):
                for j in range(most):
                    pl.when(where[r * most + j] < zeros)(copy(r, j).wait)
        keys = []
        for r in requests:
            for k in range(heads):
                at = r * block + k * group
                pages = [kv[where[r * most + j], 0, k] for j in range(most)]
                keys.append(jnp.concatenate(pages + [kf[at : at + group, :].astype(BF16)], axis=0))
        queries = q_ref[i * together : (i + 1) * together].reshape(LANES, head_dim)
        all_scores.append(transposed_scores(queries, keys, group))
    for i, requests in enumerate(groups):
        mask = []
        for j in range(most):
            seen = [seen_tokens(r, j) for r in requests]
            mask.append(token < lane_values(seen, block, (1, LANES)))
        parts = [
            jnp.where(m, all_scores[i][n * page_len : n * page_len + m.shape[0]], -jnp.inf)
            for n, m in enumerate(mask + [fresh_mask])
        ]
        top = functools.reduce(jnp.maximum, [jnp.max(x, axis=0, keepdims=True) for x in parts])
        parts = [jnp.exp(x - top) for x in parts]
        total = functools.reduce(jnp.add, [jnp.sum(x, axis=0, keepdims=True) for x in parts])
        stats = jnp.concatenate(
            [parts[most], jnp.broadcast_to(top, (8, LANES)), jnp.broadcast_to(total, (8, LANES))], axis=0
        )
        stats = jnp.transpose(stats, (1, 0))
        stat_ref[i * LANES : (i + 1) * LANES, : stats.shape[1]] = stats
        weights = [jnp.transpose(x.astype(BF16), (1, 0)) for x in parts[:most]]
        weights.append(stats[:, :group].astype(BF16))
        all_weights.append(jnp.concatenate(weights, axis=1))
    for i, requests in enumerate(groups):
        for x, r in enumerate(requests):
            both = []
            for k in range(heads):
                at = r * block + k * group
                pages = [kv[where[r * most + j], 1, k] for j in range(most)]
                both.append(jnp.concatenate(pages + [vf[at : at + group, :].astype(BF16)], axis=0))
            both = weighted_values(all_weights[i][x * block : (x + 1) * block, :], both)
            o_ref[r * block : (r + 1) * block, :] = both


def local_attention(table, context, fills, queries, new_kv, cache_kv, tabs):
    rows, block, _ = queries.shape
    rows = rows - 1
    steps = new_kv.shape[0]
    slots, _, heads, page_len, head_dim = cache_kv.shape
    flat = (rows * block, head_dim)
    freq, sign = tabs[4:]
    return pl.pallas_call(
        functools.partial(local_kernel, page_len, heads),
        out_shape=[jax.ShapeDtypeStruct(flat, F32)] * 2,
        in_specs=[SMEM] * 3 + [VMEM] * 4 + [ANY],
        out_specs=[VMEM] * 2,
        scratch_shapes=[
            pltpu.VMEM((table.size + 1, 2, heads, page_len, head_dim), BF16),
            pltpu.SemaphoreType.DMA((table.size,)),
            pltpu.VMEM(flat, F32),
            pltpu.VMEM(flat, F32),
            pltpu.VMEM((rows, head_dim), I32),
            pltpu.SMEM((table.size,), I32),
        ],
        compiler_params=PARAMS,
        cost_estimate=pl.CostEstimate(flops=800_000_000, bytes_accessed=12_000_000, transcendentals=400_000),
        name="local_attention",
    )(
        *[in_hbm(x) for x in (table, context, fills)],
        queries,
        new_kv.reshape(steps, rows, 2 * heads * head_dim),
        *[in_hbm(x) for x in (freq, sign, cache_kv)],
    )


def pieces(x):
    high = x.astype(BF16).astype(F32)
    middle = (x - high).astype(BF16).astype(F32)
    return [high, middle, x - high - middle]


def arrived_kernel(npool, pair, me_ref, own_ref, *refs):
    blocks = refs[:npool]
    pages_ref, out_ref, queries = refs[npool:]
    items = npool * pair
    _, _, heads, page_len, head_dim = pages_ref.shape
    rows, block = blocks[0].shape[0] - 1, blocks[0].shape[1]
    group = block // heads
    together = LANES // block
    me = me_ref[0]
    owners = [owner_of(me, npool, apart, flip) for apart, flip in block_order(npool)]
    lane = lax.broadcasted_iota(I32, (1, LANES), 1)
    codes = [x[rows, :STAT_ROWS, :].astype(F32) for x in blocks]
    codes = [x[0:1] * CODE + x[1:2] for x in codes]
    places = [owners[x // pair] * pair + x % pair for x in range(items)]
    slots = [own_ref[2 * items + at] for at in places]
    read = [jnp.maximum(read_scalar(codes[x // pair], lane == slots[x]), 0) for x in range(items)]
    number = [own_ref[at] for at in places]
    seen = [jnp.minimum(code % CODE, own_ref[items + at]) for code, at in zip(read, places)]
    request = [jnp.where(slot >= 0, code // CODE, -1) for slot, code in zip(slots, read)]
    for x in range(items):
        queries[x * block : (x + 1) * block, :] = blocks[x // pair][read[x] // CODE]
    token = lax.broadcasted_iota(I32, (page_len, LANES), 0)
    groups = [range(i * together, (i + 1) * together) for i in range(items // together)]
    all_scores, all_weights = [], []
    for i, own in enumerate(groups):
        keys = [pages_ref[number[x], 0, k] for x in own for k in range(heads)]
        all_scores.append(transposed_scores(queries[i * LANES : (i + 1) * LANES, :], keys, group))
    for i, own in enumerate(groups):
        limit = lane_values([seen[x] for x in own], block, (1, LANES))
        scores = jnp.where(token < limit, all_scores[i], -jnp.inf)
        top = jnp.max(scores, axis=0, keepdims=True)
        top = jnp.where(top > -jnp.inf, top, 0.0)
        weights = jnp.exp(scores - top)
        stats = pieces(top) + pieces(jnp.sum(weights, axis=0, keepdims=True))
        stats.append(lane_values([request[x] for x in own], block, (1, LANES)).astype(F32))
        stats = jnp.concatenate(stats + [jnp.zeros((STAT_ROWS - len(stats), LANES), F32)], axis=0).astype(BF16)
        for place in sorted({x // pair for x in own}):
            out_ref[owners[place], pair * block : pair * block + STAT_ROWS, :] = stats
        all_weights.append(jnp.transpose(weights.astype(BF16), (1, 0)))
    for i, own in enumerate(groups):
        for c, x in enumerate(own):
            both = [pages_ref[number[x], 1, k] for k in range(heads)]
            both = weighted_values(all_weights[i][c * block : (c + 1) * block, :], both)
            at = (x % pair) * block
            out_ref[owners[x // pair], at : at + block, :] = both.astype(BF16)


def arrived_attention(me, own, blocks, arrived):
    npool = len(blocks)
    head_dim = arrived.shape[4]
    block = blocks[0].shape[1]
    items = own.shape[0] // 3
    pair = items // npool
    return pl.pallas_call(
        functools.partial(arrived_kernel, npool, pair),
        out_shape=jax.ShapeDtypeStruct((npool, pair * block + STAT_ROWS, head_dim), BF16),
        in_specs=[SMEM] * 2 + [VMEM] * (npool + 1),
        out_specs=VMEM,
        scratch_shapes=[pltpu.VMEM((items * block, head_dim), BF16)],
        compiler_params=PARAMS,
        cost_estimate=pl.CostEstimate(flops=200_000_000, bytes_accessed=4_000_000, transcendentals=70_000),
        name="arrived_attention",
    )(me, own, *blocks, arrived)


def merge_kernel(pair, heads, me_ref, core_ref, parts_ref, o_ref, stat_ref, out_ref, mixed, top, total, turned):
    del core_ref
    npool = parts_ref.shape[0]
    steps, rows, width = out_ref.shape
    head_dim = o_ref.shape[1]
    per = width // head_dim // heads
    group = steps * per
    block = heads * group
    me = me_ref[0]
    shape = top.shape
    mixed[...] = o_ref[...]
    top[...] = jnp.broadcast_to(stat_ref[:, group : group + 1], shape)
    total[...] = jnp.broadcast_to(stat_ref[:, group + 8 : group + 9], shape)
    tops, totals, readers = [], [], []
    chain = lax.broadcasted_iota(I32, (1, LANES), 1) // block
    for d in range(npool):
        x = parts_ref[d, pair * block : pair * block + STAT_ROWS, :].astype(F32)
        tops.append(x[0:1] + x[1:2] + x[2:3])
        totals.append(x[3:4] + x[4:5] + x[5:6])
        readers.append(x[6:7])
    empty = [jnp.zeros((LANES // 2 - npool, LANES), F32)]
    turned[...] = jnp.transpose(jnp.concatenate(tops + empty + totals + empty, axis=0), (1, 0))
    for d in range(npool):
        for p in range(pair):
            part = lax.rem(place_of(me, npool, d) * pair + p, LANES // block)
            r = read_scalar(readers[d], chain == part)
            there = r >= 0
            at = pl.ds(pl.multiple_of(jnp.maximum(r, 0) * block, block), block)
            lane = pl.ds(pl.multiple_of(part * block, block), block)
            m = jnp.broadcast_to(turned[lane, d : d + 1], (block, head_dim))
            l = jnp.broadcast_to(turned[lane, LANES // 2 + d : LANES // 2 + d + 1], (block, head_dim))
            seen = (l > 0.0) & there
            o = parts_ref[d, p * block : (p + 1) * block, :].astype(F32)
            old = top[at, :]
            new = jnp.where(seen, jnp.maximum(old, m), old)
            a = jnp.exp(old - new)
            b = jnp.where(seen, jnp.exp(m - new), 0.0)
            top[at, :] = new
            total[at, :] = total[at, :] * a + l * b
            mixed[at, :] = mixed[at, :] * a + o * b
    for s in range(steps):
        for h in range(heads * per):
            k, g = divmod(h, per)
            at = pl.ds(k * group + s * per + g, rows, stride=block)
            out_ref[s, :, h * head_dim : (h + 1) * head_dim] = (mixed[at, :] / total[at, :]).astype(BF16)


def merged(me, core, parts, local, shape, heads, pair):
    flat = local[0].shape
    return pl.pallas_call(
        functools.partial(merge_kernel, pair, heads),
        out_shape=jax.ShapeDtypeStruct(shape, BF16),
        in_specs=[SMEM] * 2 + [VMEM] * 3,
        out_specs=VMEM,
        scratch_shapes=[pltpu.VMEM(flat, F32)] * 3 + [pltpu.VMEM((LANES, LANES), F32)],
        compiler_params=PARAMS,
        cost_estimate=pl.CostEstimate(flops=2_000_000, bytes_accessed=1_500_000, transcendentals=100_000),
        name="merge",
    )(me, core, parts, *local)


def fetch_kernel(weight_ref, x_ref, weight_out, x_out, sems):
    chunks = sems.shape[0] - 1
    rows = weight_ref.shape[0] // chunks
    copies = []
    for i in range(chunks):
        at = pl.ds(i * rows, rows)
        copies.append(pltpu.make_async_copy(weight_ref.at[at], weight_out.at[at], sems.at[i]))
    copies.append(pltpu.make_async_copy(x_ref, x_out, sems.at[chunks]))
    for copy in copies:
        copy.start()
    for copy in copies:
        copy.wait()


def fetched(weight, x):
    return pl.pallas_call(
        fetch_kernel,
        out_shape=[pltpu.VMEM(weight.shape, weight.dtype), pltpu.VMEM(x.shape, x.dtype)],
        in_specs=[ANY, ANY],
        out_specs=[ANY, ANY],
        scratch_shapes=[pltpu.SemaphoreType.DMA((9,))],
        compiler_params=PARAMS,
        cost_estimate=pl.CostEstimate(flops=0, bytes_accessed=2 * weight.size * 2, transcendentals=0),
        name="fetch_weight",
    )(in_hbm(weight), x)


def rows_kernel(npool, me_ref, core_ref, *refs):
    blocks = refs[:npool]
    weight_ref, out_ref, lhs = refs[npool:]
    steps, rows, _ = blocks[0].shape
    every = npool * rows
    for x, (apart, flip) in enumerate(block_order(npool)):
        owner = owner_of(me_ref[0], npool, apart, flip)
        for s in range(steps):
            lhs[pl.ds(pl.multiple_of(s * every + owner * rows, rows), rows), :] = blocks[x][s]
    multiply(lhs, weight_ref, out_ref, 1 - core_ref[0])


def multiply(lhs, weight_ref, out_ref, which):
    steps, every, half = out_ref.shape
    tile = min(half, 256)
    for i in range(half // tile):
        at = pl.ds(pl.multiple_of(which * half + i * tile, LANES), tile)
        terms = jnp.dot(lhs[...], weight_ref[:, at], preferred_element_type=F32)
        for s in range(steps):
            out_ref[s, :, i * tile : (i + 1) * tile] = terms[s * every : (s + 1) * every].astype(out_ref.dtype)


def other_projection(me, core, blocks, weight):
    npool = len(blocks)
    steps, rows, width = blocks[0].shape
    half = weight.shape[1] // 2
    every = steps * npool * rows
    return pl.pallas_call(
        functools.partial(rows_kernel, npool),
        out_shape=[
            jax.ShapeDtypeStruct((steps, npool * rows, half), BF16),
            jax.ShapeDtypeStruct((every, width), BF16),
        ],
        in_specs=[SMEM] * 2 + [VMEM] * (npool + 1),
        out_specs=[VMEM] * 2,
        compiler_params=PARAMS,
        cost_estimate=pl.CostEstimate(flops=2 * every * width * half, bytes_accessed=4_000_000, transcendentals=0),
        name="project_other",
    )(me, core, *blocks, weight)


def own_kernel(core_ref, lhs, weight_ref, out_ref):
    multiply(lhs, weight_ref, out_ref, core_ref[0])


def own_projection(core, lhs, weight, steps):
    every, width = lhs.shape
    half = weight.shape[1] // 2
    return pl.pallas_call(
        own_kernel,
        out_shape=jax.ShapeDtypeStruct((steps, every // steps, half), F32),
        in_specs=[SMEM] + [VMEM] * 2,
        out_specs=VMEM,
        compiler_params=PARAMS,
        cost_estimate=pl.CostEstimate(flops=2 * every * width * half, bytes_accessed=4_000_000, transcendentals=0),
        name="project_own",
    )(core, lhs, weight)


def block_order(npool):
    return [(apart, flip) for flip in (0, 1) for apart in range(npool // 2)]


def owner_of(me, npool, apart, flip):
    half = npool // 2
    pair, side = me // 2, me % 2
    side = 1 - side if flip else side
    return lax.rem(pair + half - apart, half) * 2 + side


def place_of(me, npool, holder):
    half = npool // 2
    apart = lax.rem(holder // 2 - me // 2 + half, half)
    flip = lax.rem(me + holder, 2)
    return flip * half + apart


def in_hbm(x):
    return pltpu.with_memory_space_constraint(x, pltpu.HBM)


def gathered(x, npool, later=None):
    half = npool // 2
    later = x if later is None else later
    ahead = lambda x, by: lax.ppermute(x, "pool", [(i, (i + 2 * by) % npool) for i in range(npool)])
    across = lambda x: lax.ppermute(x, "pool", [(i, i ^ 1) for i in range(npool)])
    straight = [x] + [ahead(later if by == 1 else x, by) for by in range(1, half)]
    return straight + [across(y) for y in straight]


def swap_halves(x):
    return lax.ppermute(x, "tp", [(0, 1), (1, 0)])


def shards(
    prompt_kv,
    prompt_lengths,
    page_slot,
    cache_kv,
    cache_fill,
    page_table,
    context_lengths,
    queries,
    new_kv,
    out_weight,
):
    npool = lax.axis_size("pool")
    me = lax.axis_index("pool").astype(I32)
    pages, _, heads, page_len, head_dim = prompt_kv.shape
    cache_pages = cache_kv.shape[0]
    pair = (pages + npool - 1) // npool
    tabs = tables(page_len, head_dim, pages)
    me1, core1 = me[None], lax.axis_index("tp").astype(I32)[None]
    table = page_table.T

    asked = asked_queries(table, context_lengths, queries, page_len, heads, head_dim)
    asked_all = gathered(asked, npool)
    arrived, own = rotated_pages(prompt_kv, page_slot, prompt_lengths, tabs, npool, pair, cache_pages)
    local = local_attention(table, context_lengths, cache_fill, asked, new_kv, cache_kv, tabs)
    parts = arrived_attention(me1, own, asked_all, arrived)
    parts = lax.all_to_all(parts, "pool", split_axis=0, concat_axis=0, tiled=True)
    attention = merged(me1, core1, parts, local, queries.shape, heads, pair)
    weight, again = fetched(out_weight, attention)
    blocks = gathered(attention, npool, again)
    other_terms, lhs = other_projection(me1, core1, blocks, weight)
    other_terms = swap_halves(other_terms)
    terms = own_projection(core1, lhs, weight, queries.shape[0])
    return (terms + other_terms.astype(F32)).astype(BF16)


def solution(mesh):
    return jax.shard_map(
        shards,
        mesh=mesh,
        in_specs=(
            P(("group", "pool"), None, "tp", None, None),
            P(("group", "pool"), None),
            P(("group", "pool")),
            P(("group", "pool"), None, "tp", None, None),
            P(("group", "pool")),
            P(("group", "pool"), None),
            P(("group", "pool")),
            P(None, ("group", "pool"), "tp"),
            P(None, ("group", "pool"), None, "tp", None),
            P("tp", "pool"),
        ),
        out_specs=P(None, "group", ("pool", "tp")),
        check_vma=False,
    )
```

```python
import functools

import jax
import jax.numpy as jnp
import numpy as np
from jax import lax
from jax.experimental import pallas as pl
from jax.experimental.pallas import tpu as pltpu
from jax.sharding import PartitionSpec as P

ROPE_BASE = 500000.0
BF16, F32, I32 = jnp.bfloat16, jnp.float32, jnp.int32
SMEM = pl.BlockSpec(memory_space=pltpu.SMEM)
VMEM = pl.BlockSpec(memory_space=pltpu.VMEM)
ANY = pl.BlockSpec(memory_space=pl.ANY)
PARAMS = pltpu.CompilerParams(vmem_limit_bytes=24 * 2**20)
LANES = 128
STAT_ROWS = 16
CODE = 256


def tables(page_len, head_dim, pages):
    half = head_dim // 2
    freq = ROPE_BASE ** (-(np.arange(half) * 2.0) / head_dim)
    freq = np.concatenate([freq, freq])[None, :]
    sign = np.concatenate([-np.ones(half), np.ones(half)])[None, :]
    token = np.arange(page_len)[:, None] * freq
    first = np.arange(pages)[:, None] * page_len * freq
    out = (np.cos(token), sign * np.sin(token), np.cos(first), sign * np.sin(first), freq, sign)
    return [jnp.asarray(x, F32) for x in out]


def rope_kernel(
    npool, cache_pages, per, slot_ref, len_ref, pages_ref, ct_ref, st_ref, cp_ref, sp_ref, out_ref, own_ref, count
):
    _, _, heads, page_len, head_dim = pages_ref.shape

    @pl.when(pl.program_id(0) == 0)
    def _():
        items = own_ref.shape[0] // 3
        for e in range(npool):
            count[e] = 0
        for i in range(items):
            own_ref[i] = 0
            own_ref[items + i] = 0
            own_ref[2 * items + i] = -1
        for n in range(slot_ref.shape[0]):
            slot = slot_ref[n]
            target = slot // cache_pages
            at = target * (items // npool) + count[target]
            count[target] = count[target] + 1
            own_ref[at] = n
            own_ref[items + at] = page_place(len_ref, page_len, n)[1]
            own_ref[2 * items + at] = slot - target * cache_pages

    for i in range(per):
        number, _ = page_place(len_ref, page_len, pl.program_id(0) * per + i)
        c0, s0 = cp_ref[pl.ds(number, 1), :], sp_ref[pl.ds(number, 1), :]
        ct, st = ct_ref[...], st_ref[...]
        cos = c0 * ct - s0 * st
        sin = s0 * ct + c0 * st
        for k in range(heads):
            x = pages_ref[i, 0, k].astype(F32)
            out_ref[i, 0, k] = (x * cos + pltpu.roll(x, head_dim // 2, 1) * sin).astype(BF16)
            out_ref[i, 1, k] = pages_ref[i, 1, k]


def page_place(len_ref, page_len, n):
    begin = jnp.int32(0)
    number, fill = jnp.int32(0), jnp.int32(0)
    for q in range(len_ref.shape[1]):
        length = len_ref[0, q]
        count = (length + page_len - 1) // page_len
        here = (n >= begin) & (n < begin + count)
        number = jnp.where(here, n - begin, number)
        fill = jnp.where(here, jnp.clip(length - (n - begin) * page_len, 0, page_len), fill)
        begin = begin + count
    return number, fill


def rotated_pages(prompt_kv, page_slot, prompt_lengths, tabs, npool, pair, cache_pages):
    pages, _, heads, page_len, head_dim = prompt_kv.shape
    per = pages // 2
    ct, st, cp, sp, _, _ = tabs
    whole = lambda x: pl.BlockSpec(x.shape, lambda i: (0, 0))
    return pl.pallas_call(
        functools.partial(rope_kernel, npool, cache_pages, per),
        grid=(pages // per,),
        out_shape=[
            jax.ShapeDtypeStruct(prompt_kv.shape, BF16),
            jax.ShapeDtypeStruct((3 * npool * pair,), I32),
        ],
        in_specs=[
            SMEM,
            SMEM,
            pl.BlockSpec((per,) + prompt_kv.shape[1:], lambda i: (i, 0, 0, 0, 0)),
            whole(ct),
            whole(st),
            whole(cp),
            whole(sp),
        ],
        out_specs=[pl.BlockSpec((per,) + prompt_kv.shape[1:], lambda i: (i, 0, 0, 0, 0)), SMEM],
        scratch_shapes=[pltpu.SMEM((npool,), I32)],
        compiler_params=PARAMS,
        cost_estimate=pl.CostEstimate(flops=6_000_000, bytes_accessed=2_000_000, transcendentals=0),
        name="rope_pages",
    )(*[in_hbm(x) for x in (page_slot, prompt_lengths, prompt_kv, ct, st, cp, sp)])


def asked_kernel(page_len, heads, table_ref, context_ref, q_ref, out_ref, spread):
    most, rows = table_ref.shape
    steps, _, width = q_ref.shape
    block, head_dim = out_ref.shape[1:]
    per = width // head_dim // heads
    for s in range(steps):
        for h in range(heads * per):
            k, g = divmod(h, per)
            at = pl.ds(k * steps * per + s * per + g, rows, stride=block)
            spread[at, :] = q_ref[s, :, h * head_dim : (h + 1) * head_dim].astype(F32)
    for r in range(rows):
        out_ref[r] = spread[r * block : (r + 1) * block, :].astype(BF16)
    lane = lax.broadcasted_iota(I32, (block, LANES), 1)
    line = lax.broadcasted_iota(I32, (block, LANES), 0)
    request = jnp.zeros((block, LANES), I32)
    left = jnp.zeros((block, LANES), I32)
    for r in range(rows):
        context = context_ref[r]
        for j in range(most):
            here = lane == table_ref[j, r]
            request = jnp.where(here, r, request)
            left = jnp.where(here, jnp.clip(context - j * page_len, 0, page_len), left)
    out_ref[rows] = jnp.where(line == 0, request, left).astype(F32).astype(BF16)


def asked_queries(table, context, queries, page_len, heads, head_dim):
    steps, rows, width = queries.shape
    block = steps * width // head_dim
    return pl.pallas_call(
        functools.partial(asked_kernel, page_len, heads),
        out_shape=jax.ShapeDtypeStruct((rows + 1, block, head_dim), BF16),
        in_specs=[SMEM, SMEM, VMEM],
        out_specs=VMEM,
        scratch_shapes=[pltpu.VMEM((rows * block, head_dim), F32)],
        compiler_params=PARAMS,
        cost_estimate=pl.CostEstimate(flops=100_000, bytes_accessed=300_000, transcendentals=0),
        name="asked_queries",
    )(in_hbm(table), in_hbm(context), in_hbm(queries))


def read_scalar(x, pick):
    return jnp.max(jnp.where(pick, x, -2.0)).astype(I32)


def transposed_scores(queries, keys, group):
    turned = jnp.transpose(queries, (1, 0))
    chain = lax.broadcasted_iota(I32, (1, turned.shape[1]), 1) // group
    spread = [turned * jnp.where(chain == c, 1.0, 0.0).astype(BF16) for c in range(len(keys))]
    scores = jnp.dot(
        jnp.concatenate(keys, axis=1), jnp.concatenate(spread, axis=0), preferred_element_type=F32
    )
    return scores * (queries.shape[1] ** -0.5)


def weighted_values(weights, values):
    heads, head_dim = len(values), values[0].shape[1]
    group = weights.shape[0] // heads
    out = jnp.dot(weights, jnp.concatenate(values, axis=1), preferred_element_type=F32)
    parts = [out[k * group : (k + 1) * group, k * head_dim : (k + 1) * head_dim] for k in range(heads)]
    return jnp.concatenate(parts, axis=0)


def lane_values(scalars, lanes_each, shape):
    chain = lax.broadcasted_iota(I32, shape, 1) // lanes_each
    out = jnp.zeros(shape, I32)
    for i, x in enumerate(scalars):
        out = jnp.where(chain == i, x, out)
    return out


def local_kernel(
    page_len,
    heads,
    table_ref,
    context_ref,
    fill_ref,
    q_ref,
    new_ref,
    freq_ref,
    sign_ref,
    cache_ref,
    o_ref,
    stat_ref,
    kv,
    sems,
    kf,
    vf,
    position,
    where,
):
    rows, block, head_dim = q_ref.shape
    rows = rows - 1
    steps = new_ref.shape[0]
    most = table_ref.shape[0]
    group = block // heads
    per = group // steps
    together = LANES // block

    zeros = rows * most

    def copy(r, j):
        n = r * most + j
        return pltpu.make_async_copy(cache_ref.at[table_ref[j, r]], kv.at[n], sems.at[n])

    def seen_tokens(r, j):
        return jnp.minimum(fill_ref[table_ref[j, r]], context_ref[r] - j * page_len)

    for r in range(rows):
        for j in range(most):
            needed = seen_tokens(r, j) > 0
            where[r * most + j] = jnp.where(needed, r * most + j, zeros)
            pl.when(needed)(copy(r, j).start)
    kv[zeros] = jnp.zeros(kv.shape[1:], BF16)
    kf[...] = jnp.zeros_like(kf)
    vf[...] = jnp.zeros_like(vf)
    for r in range(rows):
        position[r : r + 1, :] = jnp.full((1, head_dim), context_ref[r], I32)
    for u in range(steps):
        angle = (position[...] + u).astype(F32) * freq_ref[...]
        cos, sin = jnp.cos(angle), jnp.sin(angle) * sign_ref[...]
        for k in range(heads):
            x = new_ref[u, :, k * head_dim : (k + 1) * head_dim].astype(F32)
            at = k * group + u
            kf[pl.ds(at, rows, stride=block), :] = x * cos + pltpu.roll(x, head_dim // 2, 1) * sin
            x = new_ref[u, :, (heads + k) * head_dim : (heads + k + 1) * head_dim].astype(F32)
            vf[pl.ds(at, rows, stride=block), :] = x
    token = lax.broadcasted_iota(I32, (page_len, LANES), 0)
    fresh = lax.broadcasted_iota(I32, (group, LANES), 0)
    step = lax.broadcasted_iota(I32, (group, LANES), 1) % group // per
    fresh_mask = (fresh <= step) & (fresh < steps)

    groups = [range(i * together, (i + 1) * together) for i in range(rows // together)]
    all_scores, all_weights = [], []
    for i, requests in enumerate(groups):
        if i % 2 == 0:
            for r in range(i * together, min(rows, (i + 2) * together)):
                for j in range(most):
                    pl.when(where[r * most + j] < zeros)(copy(r, j).wait)
        keys = []
        for r in requests:
            for k in range(heads):
                at = r * block + k * group
                pages = [kv[where[r * most + j], 0, k] for j in range(most)]
                keys.append(jnp.concatenate(pages + [kf[at : at + group, :].astype(BF16)], axis=0))
        queries = q_ref[i * together : (i + 1) * together].reshape(LANES, head_dim)
        all_scores.append(transposed_scores(queries, keys, group))
    for i, requests in enumerate(groups):
        mask = []
        for j in range(most):
            seen = [seen_tokens(r, j) for r in requests]
            mask.append(token < lane_values(seen, block, (1, LANES)))
        parts = [
            jnp.where(m, all_scores[i][n * page_len : n * page_len + m.shape[0]], -jnp.inf)
            for n, m in enumerate(mask + [fresh_mask])
        ]
        top = functools.reduce(jnp.maximum, [jnp.max(x, axis=0, keepdims=True) for x in parts])
        parts = [jnp.exp(x - top) for x in parts]
        total = functools.reduce(jnp.add, [jnp.sum(x, axis=0, keepdims=True) for x in parts])
        stats = jnp.concatenate(
            [parts[most], jnp.broadcast_to(top, (8, LANES)), jnp.broadcast_to(total, (8, LANES))], axis=0
        )
        stats = jnp.transpose(stats, (1, 0))
        stat_ref[i * LANES : (i + 1) * LANES, : stats.shape[1]] = stats
        weights = [jnp.transpose(x.astype(BF16), (1, 0)) for x in parts[:most]]
        weights.append(stats[:, :group].astype(BF16))
        all_weights.append(jnp.concatenate(weights, axis=1))
    for i, requests in enumerate(groups):
        for x, r in enumerate(requests):
            both = []
            for k in range(heads):
                at = r * block + k * group
                pages = [kv[where[r * most + j], 1, k] for j in range(most)]
                both.append(jnp.concatenate(pages + [vf[at : at + group, :].astype(BF16)], axis=0))
            both = weighted_values(all_weights[i][x * block : (x + 1) * block, :], both)
            o_ref[r * block : (r + 1) * block, :] = both


def local_attention(table, context, fills, queries, new_kv, cache_kv, tabs):
    rows, block, _ = queries.shape
    rows = rows - 1
    steps = new_kv.shape[0]
    slots, _, heads, page_len, head_dim = cache_kv.shape
    flat = (rows * block, head_dim)
    freq, sign = tabs[4:]
    return pl.pallas_call(
        functools.partial(local_kernel, page_len, heads),
        out_shape=[jax.ShapeDtypeStruct(flat, F32)] * 2,
        in_specs=[SMEM] * 3 + [VMEM] * 4 + [ANY],
        out_specs=[VMEM] * 2,
        scratch_shapes=[
            pltpu.VMEM((table.size + 1, 2, heads, page_len, head_dim), BF16),
            pltpu.SemaphoreType.DMA((table.size,)),
            pltpu.VMEM(flat, F32),
            pltpu.VMEM(flat, F32),
            pltpu.VMEM((rows, head_dim), I32),
            pltpu.SMEM((table.size,), I32),
        ],
        compiler_params=PARAMS,
        cost_estimate=pl.CostEstimate(flops=800_000_000, bytes_accessed=12_000_000, transcendentals=400_000),
        name="local_attention",
    )(
        *[in_hbm(x) for x in (table, context, fills)],
        queries,
        new_kv.reshape(steps, rows, 2 * heads * head_dim),
        *[in_hbm(x) for x in (freq, sign, cache_kv)],
    )


def pieces(x):
    high = x.astype(BF16).astype(F32)
    middle = (x - high).astype(BF16).astype(F32)
    return [high, middle, x - high - middle]


def arrived_kernel(npool, pair, me_ref, own_ref, *refs):
    blocks = refs[:npool]
    pages_ref, out_ref, queries = refs[npool:]
    items = npool * pair
    _, _, heads, page_len, head_dim = pages_ref.shape
    rows, block = blocks[0].shape[0] - 1, blocks[0].shape[1]
    group = block // heads
    together = LANES // block
    me = me_ref[0]
    owners = [owner_of(me, npool, apart, flip) for apart, flip in block_order(npool)]
    lane = lax.broadcasted_iota(I32, (1, LANES), 1)
    codes = [x[rows, :STAT_ROWS, :].astype(F32) for x in blocks]
    codes = [x[0:1] * CODE + x[1:2] for x in codes]
    places = [owners[x // pair] * pair + x % pair for x in range(items)]
    slots = [own_ref[2 * items + at] for at in places]
    read = [jnp.maximum(read_scalar(codes[x // pair], lane == slots[x]), 0) for x in range(items)]
    number = [own_ref[at] for at in places]
    seen = [jnp.minimum(code % CODE, own_ref[items + at]) for code, at in zip(read, places)]
    request = [jnp.where(slot >= 0, code // CODE, -1) for slot, code in zip(slots, read)]
    for x in range(items):
        queries[x * block : (x + 1) * block, :] = blocks[x // pair][read[x] // CODE]
    token = lax.broadcasted_iota(I32, (page_len, LANES), 0)
    groups = [range(i * together, (i + 1) * together) for i in range(items // together)]
    all_scores, all_weights = [], []
    for i, own in enumerate(groups):
        keys = [pages_ref[number[x], 0, k] for x in own for k in range(heads)]
        all_scores.append(transposed_scores(queries[i * LANES : (i + 1) * LANES, :], keys, group))
    for i, own in enumerate(groups):
        limit = lane_values([seen[x] for x in own], block, (1, LANES))
        scores = jnp.where(token < limit, all_scores[i], -jnp.inf)
        top = jnp.max(scores, axis=0, keepdims=True)
        top = jnp.where(top > -jnp.inf, top, 0.0)
        weights = jnp.exp(scores - top)
        stats = pieces(top) + pieces(jnp.sum(weights, axis=0, keepdims=True))
        stats.append(lane_values([request[x] for x in own], block, (1, LANES)).astype(F32))
        stats = jnp.concatenate(stats + [jnp.zeros((STAT_ROWS - len(stats), LANES), F32)], axis=0).astype(BF16)
        for place in sorted({x // pair for x in own}):
            out_ref[owners[place], pair * block : pair * block + STAT_ROWS, :] = stats
        all_weights.append(jnp.transpose(weights.astype(BF16), (1, 0)))
    for i, own in enumerate(groups):
        for c, x in enumerate(own):
            both = [pages_ref[number[x], 1, k] for k in range(heads)]
            both = weighted_values(all_weights[i][c * block : (c + 1) * block, :], both)
            at = (x % pair) * block
            out_ref[owners[x // pair], at : at + block, :] = both.astype(BF16)


def arrived_attention(me, own, blocks, arrived):
    npool = len(blocks)
    head_dim = arrived.shape[4]
    block = blocks[0].shape[1]
    items = own.shape[0] // 3
    pair = items // npool
    return pl.pallas_call(
        functools.partial(arrived_kernel, npool, pair),
        out_shape=jax.ShapeDtypeStruct((npool, pair * block + STAT_ROWS, head_dim), BF16),
        in_specs=[SMEM] * 2 + [VMEM] * (npool + 1),
        out_specs=VMEM,
        scratch_shapes=[pltpu.VMEM((items * block, head_dim), BF16)],
        compiler_params=PARAMS,
        cost_estimate=pl.CostEstimate(flops=200_000_000, bytes_accessed=4_000_000, transcendentals=70_000),
        name="arrived_attention",
    )(me, own, *blocks, arrived)


def merge_kernel(pair, heads, me_ref, core_ref, parts_ref, o_ref, stat_ref, out_ref, mixed, top, total, turned):
    del core_ref
    npool = parts_ref.shape[0]
    steps, rows, width = out_ref.shape
    head_dim = o_ref.shape[1]
    per = width // head_dim // heads
    group = steps * per
    block = heads * group
    me = me_ref[0]
    shape = top.shape
    mixed[...] = o_ref[...]
    top[...] = jnp.broadcast_to(stat_ref[:, group : group + 1], shape)
    total[...] = jnp.broadcast_to(stat_ref[:, group + 8 : group + 9], shape)
    tops, totals, readers = [], [], []
    chain = lax.broadcasted_iota(I32, (1, LANES), 1) // block
    for d in range(npool):
        x = parts_ref[d, pair * block : pair * block + STAT_ROWS, :].astype(F32)
        tops.append(x[0:1] + x[1:2] + x[2:3])
        totals.append(x[3:4] + x[4:5] + x[5:6])
        readers.append(x[6:7])
    empty = [jnp.zeros((LANES // 2 - npool, LANES), F32)]
    turned[...] = jnp.transpose(jnp.concatenate(tops + empty + totals + empty, axis=0), (1, 0))
    for d in range(npool):
        for p in range(pair):
            part = lax.rem(place_of(me, npool, d) * pair + p, LANES // block)
            r = read_scalar(readers[d], chain == part)
            there = r >= 0
            at = pl.ds(pl.multiple_of(jnp.maximum(r, 0) * block, block), block)
            lane = pl.ds(pl.multiple_of(part * block, block), block)
            m = jnp.broadcast_to(turned[lane, d : d + 1], (block, head_dim))
            l = jnp.broadcast_to(turned[lane, LANES // 2 + d : LANES // 2 + d + 1], (block, head_dim))
            seen = (l > 0.0) & there
            o = parts_ref[d, p * block : (p + 1) * block, :].astype(F32)
            old = top[at, :]
            new = jnp.where(seen, jnp.maximum(old, m), old)
            a = jnp.exp(old - new)
            b = jnp.where(seen, jnp.exp(m - new), 0.0)
            top[at, :] = new
            total[at, :] = total[at, :] * a + l * b
            mixed[at, :] = mixed[at, :] * a + o * b
    for s in range(steps):
        for h in range(heads * per):
            k, g = divmod(h, per)
            at = pl.ds(k * group + s * per + g, rows, stride=block)
            out_ref[s, :, h * head_dim : (h + 1) * head_dim] = (mixed[at, :] / total[at, :]).astype(BF16)


def merged(me, core, parts, local, shape, heads, pair):
    flat = local[0].shape
    return pl.pallas_call(
        functools.partial(merge_kernel, pair, heads),
        out_shape=jax.ShapeDtypeStruct(shape, BF16),
        in_specs=[SMEM] * 2 + [VMEM] * 3,
        out_specs=VMEM,
        scratch_shapes=[pltpu.VMEM(flat, F32)] * 3 + [pltpu.VMEM((LANES, LANES), F32)],
        compiler_params=PARAMS,
        cost_estimate=pl.CostEstimate(flops=2_000_000, bytes_accessed=1_500_000, transcendentals=100_000),
        name="merge",
    )(me, core, parts, *local)


def fetch_kernel(first, weight_ref, x_ref, weight_out, x_out, sems):
    chunks = sems.shape[0] - 1
    rows = weight_out.shape[0] // chunks
    copies = []
    for i in range(chunks):
        at = pl.ds(i * rows, rows)
        copies.append(pltpu.make_async_copy(weight_ref.at[pl.ds(first + i * rows, rows)], weight_out.at[at], sems.at[i]))
    copies.append(pltpu.make_async_copy(x_ref, x_out, sems.at[chunks]))
    for copy in copies:
        copy.start()
    for copy in copies:
        copy.wait()


def fetched(weight, x, part):
    return pl.pallas_call(
        functools.partial(fetch_kernel, part * weight.shape[0] // 2),
        out_shape=[pltpu.VMEM((weight.shape[0] // 2, weight.shape[1]), weight.dtype), pltpu.VMEM(x.shape, x.dtype)],
        in_specs=[ANY, ANY],
        out_specs=[ANY, ANY],
        scratch_shapes=[pltpu.SemaphoreType.DMA((9,))],
        compiler_params=PARAMS,
        cost_estimate=pl.CostEstimate(flops=0, bytes_accessed=weight.size * 2, transcendentals=0),
        name="fetch_weight",
    )(in_hbm(weight), x)


def rows_kernel(npool, me_ref, core_ref, *refs):
    blocks = refs[:npool]
    *weights, out_ref, lhs = refs[npool:]
    steps, rows, _ = blocks[0].shape
    every = npool * rows
    for x, (apart, flip) in enumerate(block_order(npool)):
        owner = owner_of(me_ref[0], npool, apart, flip)
        for s in range(steps):
            lhs[pl.ds(pl.multiple_of(s * every + owner * rows, rows), rows), :] = blocks[x][s]
    multiply(lhs, weights, out_ref, 1 - core_ref[0])


def multiply(lhs, weights, out_ref, which):
    steps, every, half = out_ref.shape
    tile = min(half, 256)
    for i in range(half // tile):
        at = pl.ds(pl.multiple_of(which * half + i * tile, LANES), tile)
        depth = weights[0].shape[0]
        terms = jnp.dot(lhs[:, :depth], weights[0][:, at], preferred_element_type=F32)
        terms = terms + jnp.dot(lhs[:, depth:], weights[1][:, at], preferred_element_type=F32)
        for s in range(steps):
            out_ref[s, :, i * tile : (i + 1) * tile] = terms[s * every : (s + 1) * every].astype(out_ref.dtype)


def other_projection(me, core, blocks, weight):
    npool = len(blocks)
    steps, rows, width = blocks[0].shape
    half = weight[0].shape[1] // 2
    every = steps * npool * rows
    return pl.pallas_call(
        functools.partial(rows_kernel, npool),
        out_shape=[
            jax.ShapeDtypeStruct((steps, npool * rows, half), BF16),
            jax.ShapeDtypeStruct((every, width), BF16),
        ],
        in_specs=[SMEM] * 2 + [VMEM] * (npool + 2),
        out_specs=[VMEM] * 2,
        compiler_params=PARAMS,
        cost_estimate=pl.CostEstimate(flops=2 * every * width * half, bytes_accessed=4_000_000, transcendentals=0),
        name="project_other",
    )(me, core, *blocks, *weight)


def own_kernel(core_ref, lhs, low, high, out_ref):
    multiply(lhs, (low, high), out_ref, core_ref[0])


def own_projection(core, lhs, weight, steps):
    every, width = lhs.shape
    half = weight[0].shape[1] // 2
    return pl.pallas_call(
        own_kernel,
        out_shape=jax.ShapeDtypeStruct((steps, every // steps, half), F32),
        in_specs=[SMEM] + [VMEM] * 3,
        out_specs=VMEM,
        compiler_params=PARAMS,
        cost_estimate=pl.CostEstimate(flops=2 * every * width * half, bytes_accessed=4_000_000, transcendentals=0),
        name="project_own",
    )(core, lhs, *weight)


def block_order(npool):
    return [(apart, flip) for flip in (0, 1) for apart in range(npool // 2)]


def owner_of(me, npool, apart, flip):
    half = npool // 2
    pair, side = me // 2, me % 2
    side = 1 - side if flip else side
    return lax.rem(pair + half - apart, half) * 2 + side


def place_of(me, npool, holder):
    half = npool // 2
    apart = lax.rem(holder // 2 - me // 2 + half, half)
    flip = lax.rem(me + holder, 2)
    return flip * half + apart


def in_hbm(x):
    return pltpu.with_memory_space_constraint(x, pltpu.HBM)


def gathered(x, npool, later=None, last=None):
    half = npool // 2
    later = x if later is None else later
    last = later if last is None else last
    ahead = lambda x, by: lax.ppermute(x, "pool", [(i, (i + 2 * by) % npool) for i in range(npool)])
    across = lambda x: lax.ppermute(x, "pool", [(i, i ^ 1) for i in range(npool)])
    straight = [x] + [ahead(x if by == half // 2 else last if by == 1 else later, by) for by in range(1, half)]
    return straight + [across(y) for y in straight]


def swap_halves(x):
    return lax.ppermute(x, "tp", [(0, 1), (1, 0)])


def shards(
    prompt_kv,
    prompt_lengths,
    page_slot,
    cache_kv,
    cache_fill,
    page_table,
    context_lengths,
    queries,
    new_kv,
    out_weight,
):
    npool = lax.axis_size("pool")
    me = lax.axis_index("pool").astype(I32)
    pages, _, heads, page_len, head_dim = prompt_kv.shape
    cache_pages = cache_kv.shape[0]
    pair = (pages + npool - 1) // npool
    tabs = tables(page_len, head_dim, pages)
    me1, core1 = me[None], lax.axis_index("tp").astype(I32)[None]
    table = page_table.T

    asked = asked_queries(table, context_lengths, queries, page_len, heads, head_dim)
    asked_all = gathered(asked, npool)
    arrived, own = rotated_pages(prompt_kv, page_slot, prompt_lengths, tabs, npool, pair, cache_pages)
    local = local_attention(table, context_lengths, cache_fill, asked, new_kv, cache_kv, tabs)
    parts = arrived_attention(me1, own, asked_all, arrived)
    parts = lax.all_to_all(parts, "pool", split_axis=0, concat_axis=0, tiled=True)
    attention = merged(me1, core1, parts, local, queries.shape, heads, pair)
    low, again = fetched(out_weight, attention, 0)
    high, last = fetched(out_weight, again, 1)
    weight = (low, high)
    blocks = gathered(attention, npool, again, last)
    other_terms, lhs = other_projection(me1, core1, blocks, weight)
    other_terms = swap_halves(other_terms)
    terms = own_projection(core1, lhs, weight, queries.shape[0])
    return (terms + other_terms.astype(F32)).astype(BF16)


def solution(mesh):
    return jax.shard_map(
        shards,
        mesh=mesh,
        in_specs=(
            P(("group", "pool"), None, "tp", None, None),
            P(("group", "pool"), None),
            P(("group", "pool")),
            P(("group", "pool"), None, "tp", None, None),
            P(("group", "pool")),
            P(("group", "pool"), None),
            P(("group", "pool")),
            P(None, ("group", "pool"), "tp"),
            P(None, ("group", "pool"), None, "tp", None),
            P("tp", "pool"),
        ),
        out_specs=P(None, "group", ("pool", "tp")),
        check_vma=False,
    )
```
